32 devices in a mesh: leaf: 8 (over z, core), vec: 4 (over y, x).
Axes of the slice: x: 2, y: 2, z: 4, core: 2. Of those that a mesh axis runs over, the one named last changes fastest.
Arguments:
- points: bfloat16 [128, 3, 256], P('leaf'), may hold values from 0 to 1
- probe_vectors: bfloat16 [128, 256, 256], P('leaf', 'vec'), may hold values from -6 to 6
- neighbours: int32 [128, 16], P('leaf'), may hold values from -1 to 127, as said below
- leaf_pivots: int32 [128, 64], P('leaf'), may hold values from 0 to 255, as said below
- leaf_inverse: float32 [128, 64, 64], P('leaf'), as said below
- local_pivots: int32 [120, 64], P('leaf'), may hold values from 0 to 127, as said below
- local_inverse: float32 [120, 64, 64], P('leaf'), as said below
- upper_pivots: int32 [7, 64], replicated, may hold values from 0 to 127, as said below
- upper_inverse: float32 [7, 64, 64], replicated, as said below
Outputs:
- leaf_interp: float32 [128, 256, 64], P('leaf')
- local_interp: float32 [120, 128, 64], P('leaf')
- upper_interp: float32 [8, 3, 128, 64], P('leaf')
- top_sketch: float32 [8, 256, 64], P('leaf', 'vec')
The draws below stay inside these ranges and needn't reach their ends.
Inputs may be any that keep to these rules, and one draw needn't show every extreme that they name: Entry 0 of neighbours[i] is i; then come distinct clusters j != i with |j - i| <= 16, then -1 to the end. The first cluster of each group of 16 lists the cluster before it in entry 1, and the last one lists the cluster after it there, where those exist. A list holds at least 4 clusters, and some lists hold 16. `leaf_pivots`: each row holds 64 distinct row numbers. `local_pivots`: each row holds 64 distinct row numbers. `upper_pivots`: each row holds 64 distinct row numbers. `leaf_inverse`: diagonal entries lie in 0.5 to 1.5. `local_inverse`: diagonal entries lie in 0.5 to 1.5. `upper_inverse`: diagonal entries lie in 0.5 to 1.5.
All inputs are finite; a program needn't handle non-finite values.
Results may differ from the reference program's by a relative error of at most 0.0013.
Values may be sent and summed in bfloat16 or wider, within the bound.
No kernel may reach another device: no remote copies, remote signals or barrier semaphores. Data moves between devices by JAX's collectives and lax.ppermute only.
A program may use at most 64 MiB of HBM per device.

```python
import jax
import jax.numpy as jnp
from jax import lax

P_SIZE = 256
K = 64
S = 256
NB = 16
LEVELS_LOCAL = 4
UPL = 3
LEAF_DEV = 16
CLUSTERS = 128
LOCAL_NODES = 120
UNODES = 7


def pivot_rows(key, node_count, row_total):
    scores = jax.random.randint(key, (node_count, row_total), 0, 2 ** 16) * row_total + jnp.arange(row_total, dtype=jnp.int32)[None, :]
    ranking = jnp.argsort(scores, axis=1)
    return ranking[:, :K].astype(jnp.int32)


def inverse_blocks(key, node_count):
    first_key, second_key = jax.random.split(key)
    diagonal = jax.random.uniform(first_key, (node_count, K), jnp.float32, 0.5, 1.5)
    off_part = jax.random.normal(second_key, (node_count, K, K), jnp.float32) * (0.3 / K ** 0.5)
    identity = jnp.eye(K, dtype=jnp.float32)
    return off_part * (1.0 - identity) + identity * diagonal[:, :, None]


def draw_neighbours(key, part):
    window = 2 * LEAF_DEV + 1
    offsets = jnp.arange(window, dtype=jnp.int32) - LEAF_DEV
    cluster = jnp.arange(CLUSTERS, dtype=jnp.int32)
    target = cluster[:, None] + offsets[None, :]
    in_range = (target >= 0) & (target < CLUSTERS) & (offsets[None, :] != 0)
    group_place = cluster % LEAF_DEV
    forced = jnp.where((group_place == 0) & (cluster > 0), cluster - 1, -1)
    forced = jnp.where((group_place == LEAF_DEV - 1) & (cluster < CLUSTERS - 1) & (forced < 0), cluster + 1, forced)
    first_key, second_key = jax.random.split(key)
    scores = jax.random.randint(first_key, (CLUSTERS, window), 0, 2 ** 16) * window + jnp.arange(window, dtype=jnp.int32)[None, :]
    scores = jnp.where(target == forced[:, None], -1, scores)
    scores = jnp.where(in_range, scores, 2 ** 30)
    ranking = jnp.argsort(scores, axis=1)[:, :NB - 1]
    chosen = jnp.take_along_axis(target, ranking, axis=1)
    counts = jax.random.randint(second_key, (CLUSTERS,), max(1, NB // 4), NB + 1)
    counts = jnp.where(cluster % 5 == 0, NB, counts)
    counts = jnp.where(forced >= 0, jnp.maximum(counts, 2), counts)
    slot_index = jnp.arange(NB - 1, dtype=jnp.int32)[None, :]
    listed = jnp.where(slot_index < counts[:, None] - 1, chosen, -1)
    return jnp.concatenate([cluster[:, None], listed], axis=1).astype(jnp.int32)


def draw_leaf_pivots(key, part):
    return pivot_rows(jax.random.fold_in(key, 11), CLUSTERS, P_SIZE)


def draw_local_pivots(key, part):
    return pivot_rows(jax.random.fold_in(key, 12), LOCAL_NODES, 2 * K)


def draw_upper_pivots(key, part):
    return pivot_rows(jax.random.fold_in(key, 13), UNODES, 2 * K)


def draw_leaf_inverse(key, part):
    return inverse_blocks(jax.random.fold_in(key, 21), CLUSTERS)


def draw_local_inverse(key, part):
    return inverse_blocks(jax.random.fold_in(key, 22), LOCAL_NODES)


def draw_upper_inverse(key, part):
    return inverse_blocks(jax.random.fold_in(key, 23), UNODES)


def level_of(rng, extent, shards, smallest, largest):
    def one(dim, shards_of):
        draws = jax.random.uniform(jax.random.fold_in(jax.random.fold_in(rng, 6), dim), (shards_of,), jnp.float32, smallest / len(shards), largest / len(shards))
        return jnp.repeat(jnp.exp(draws), extent[dim] // shards_of).reshape((-1,) + (1,) * (len(extent) - dim - 1))

    factor_of = one(*shards[0])
    for cut in shards[1:]:
        factor_of = factor_of * one(*cut)
    return factor_of


def gaussian(rng, extent, scale, limit, shards=(), kind=jnp.bfloat16):
    array = jax.random.normal(rng, extent, jnp.float32) * scale
    if len(shards) > 0:
        array = level_of(rng, extent, shards, -0.22, 0.18) * array
    return jnp.clip(array, min=-limit, max=limit).astype(kind)


def setup_inputs(seed: int = 0) -> dict:
    key_of = jax.random.split(jax.random.key(seed), 10)
    points = jnp.clip(1.0 * jax.random.uniform(key_of[0], (CLUSTERS, 3, P_SIZE), jnp.float32) ** level_of(key_of[0], (CLUSTERS, 3, P_SIZE), ((0, 8),), -0.2, 0.2), 0.0, 1.0).astype(jnp.bfloat16)
    probe_vectors = gaussian(key_of[1], (CLUSTERS, S, P_SIZE), 1.0, 6.0, ((0, 8), (1, 4)))
    neighbours = draw_neighbours(jax.random.fold_in(key_of[9], 71), 0)
    leaf_pivots = draw_leaf_pivots(jax.random.fold_in(key_of[9], 71), 0)
    leaf_inverse = draw_leaf_inverse(jax.random.fold_in(key_of[9], 71), 0)
    local_pivots = draw_local_pivots(jax.random.fold_in(key_of[9], 71), 0)
    local_inverse = draw_local_inverse(jax.random.fold_in(key_of[9], 71), 0)
    upper_pivots = draw_upper_pivots(jax.random.fold_in(key_of[9], 71), 0)
    upper_inverse = draw_upper_inverse(jax.random.fold_in(key_of[9], 71), 0)
    return {"points": points, "probe_vectors": probe_vectors, "neighbours": neighbours, "leaf_pivots": leaf_pivots, "leaf_inverse": leaf_inverse, "local_pivots": local_pivots, "local_inverse": local_inverse, "upper_pivots": upper_pivots, "upper_inverse": upper_inverse}


SOFTEN = 0.0009
EPSILON = 1e-06

def kernel_tile(near_points, far_points):
    near_xyz = near_points.astype(jnp.float32)
    far_xyz = far_points.astype(jnp.float32)
    distance = SOFTEN + jnp.zeros((near_xyz.shape[0], near_xyz.shape[2], far_xyz.shape[2]), jnp.float32)
    for coordinate in range(3):
        offset_gap = near_xyz[:, coordinate, :, None] - far_xyz[:, coordinate, None, :]
        distance = distance + offset_gap * offset_gap
    return 1.0 / (64.0 * jnp.sqrt(distance))

def interpolate(sketch, pivots, inverse, column_total):
    rows = sketch.shape[2]
    index_grid = jnp.broadcast_to(pivots[:, None, :], (sketch.shape[0], sketch.shape[1], pivots.shape[1]))
    chosen = jnp.take_along_axis(sketch, index_grid, axis=2)
    gram_rows = jnp.einsum('nsp,nsk->npk', sketch, chosen, precision=lax.Precision.HIGHEST)
    squares = lax.optimization_barrier(jnp.sum(sketch * sketch, axis=(1, 2)))
    mean_sq = squares / (rows * column_total) + EPSILON
    interp_map = jnp.einsum('npl,nlk->npk', gram_rows, inverse, precision=lax.Precision.HIGHEST)
    interp_map = interp_map / (column_total * mean_sq)[:, None, None]
    upward = jnp.einsum('nsp,npk->nsk', sketch, interp_map, precision=lax.Precision.HIGHEST)
    upward = upward / jnp.sqrt(mean_sq)[:, None, None]
    return (interp_map, upward)

def pair_children(upward):
    node_count = upward.shape[0] // 2
    paired = upward.reshape(node_count, 2, upward.shape[1], upward.shape[2])
    paired = jnp.transpose(paired, (0, 2, 1, 3))
    return paired.reshape(node_count, upward.shape[1], 2 * upward.shape[2])

def near_sketch(points, probe_vectors, neighbours):
    block_count = CLUSTERS // LEAF_DEV

    def one_block(inputs):
        block_points, block_lists = inputs

        def add_slot(slot_index, running):
            listed = lax.dynamic_slice_in_dim(block_lists, slot_index, 1, 1)[:, 0]
            present = listed >= 0
            safe_index = jnp.maximum(listed, 0).astype(jnp.int32)
            kernel_block = kernel_tile(block_points, points[safe_index])
            kernel_block = jnp.where(present[:, None, None], kernel_block, 0.0).astype(jnp.bfloat16)
            far_vectors = probe_vectors[safe_index].astype(jnp.float32)
            return running + jnp.einsum('nsq,npq->nsp', far_vectors, kernel_block.astype(jnp.float32))
        start = jnp.zeros((LEAF_DEV, S, P_SIZE), jnp.float32)
        return lax.fori_loop(0, NB, add_slot, start)
    result = lax.map(one_block, (points.reshape(block_count, LEAF_DEV, 3, P_SIZE), neighbours.reshape(block_count, LEAF_DEV, NB)))
    return result.reshape(CLUSTERS, S, P_SIZE)

def reference(points, probe_vectors, neighbours, leaf_pivots, leaf_inverse, local_pivots, local_inverse, upper_pivots, upper_inverse):
    sketch = near_sketch(points, probe_vectors, neighbours)
    leaf_interp, upward = interpolate(sketch, leaf_pivots, leaf_inverse, S)
    group_count = CLUSTERS // LEAF_DEV
    grouped_pivots = local_pivots.reshape(group_count, LEAF_DEV - 1, K)
    grouped_inverse = local_inverse.reshape(group_count, LEAF_DEV - 1, K, K)
    pieces = []
    offset = 0
    for tier_index in range(LEVELS_LOCAL):
        node_count = LEAF_DEV >> tier_index + 1
        node_pivots = grouped_pivots[:, offset:offset + node_count].reshape(-1, K)
        node_inverse = grouped_inverse[:, offset:offset + node_count].reshape(-1, K, K)
        interp_map, upward = interpolate(pair_children(upward), node_pivots, node_inverse, S)
        pieces.append(interp_map.reshape(group_count, node_count, 2 * K, K))
        offset = offset + node_count
    local_interp = jnp.concatenate(pieces, axis=1).reshape(group_count * (LEAF_DEV - 1), 2 * K, K)
    heap_offset = 0
    upper_maps = []
    for tier_index in range(UPL):
        node_count = group_count >> tier_index + 1
        interp_map, upward = interpolate(pair_children(upward), upper_pivots[heap_offset:heap_offset + node_count], upper_inverse[heap_offset:heap_offset + node_count], S)
        upper_maps.append(jnp.repeat(interp_map, 2 ** (tier_index + 1), axis=0))
        heap_offset = heap_offset + node_count
    upper_interp = jnp.stack(upper_maps, axis=1)
    top_sketch = jnp.repeat(upward, 2 ** UPL, axis=0)
    return (leaf_interp, local_interp, upper_interp, top_sketch)
```

```python
import functools

import jax
import jax.numpy as jnp
from jax import lax
from jax.experimental import pallas as pl
from jax.experimental.pallas import tpu as pltpu
from jax.sharding import PartitionSpec as P

UPL = 3

SOFTEN = 0.0009
EPSILON = 1e-06
VMEM_BYTES = 48 * 1024 * 1024
VMEM = pltpu.MemorySpace.VMEM
SMEM = pltpu.MemorySpace.SMEM


def nt(a, b):
    return lax.dot_general(a, b, (((1,), (1,)), ((), ())), preferred_element_type=jnp.float32)


def nn(a, b):
    return lax.dot_general(a, b, (((1,), (0,)), ((), ())), preferred_element_type=jnp.float32)


def split(a):
    high = a.astype(jnp.bfloat16)
    low = (a - high.astype(jnp.float32)).astype(jnp.bfloat16)
    return high, low


def stacked_split(a):
    high, low = split(a)
    return jnp.concatenate([high, low], axis=0)


def halves(a):
    rows = a.shape[0] // 2
    return a[:rows] + a[rows:]


def near_kernel(tiers, share, count, has_start, halo, own, scaled, refs):
    refs = list(refs)
    nb_ref, points_ref = refs[:2]
    refs = refs[2:]
    probe_ref = refs.pop(0) if own else None
    if halo:
        before_points, after_points, before_probe, after_probe = refs[:4]
        refs = refs[4:]
    start_ref = refs.pop(0) if has_start else None
    outs = [refs.pop(0) for _ in range(len(tiers) if scaled else 1)]
    far, vectors, near, total, tile_a, tile_b, codes = refs

    me = lax.axis_index("vec")
    first = lax.axis_index("leaf") * count
    slots = nb_ref.shape[1]
    rows = len(tiers) * share

    for cluster in range(count):
        far[count + cluster, 0:3, :] = points_ref[cluster].astype(jnp.float32)
    if halo:
        for cluster in range(count):
            far[cluster, 0:3, :] = before_points[cluster].astype(jnp.float32)
            far[2 * count + cluster, 0:3, :] = after_points[cluster].astype(jnp.float32)
        vectors[0:count] = before_probe[...]
        vectors[2 * count : 3 * count] = after_probe[...]
    if own:
        vectors[count : 2 * count] = probe_ref[...]

    codes[0] = rows * 64 + count
    filled = jnp.int32(1)
    for place, tier in enumerate(tiers):
        for part in range(share):
            row = place * share + part
            cluster = (me ^ tier) * share + part

            def add_code(slot, filled, row=row, cluster=cluster):
                listed = nb_ref[cluster, slot]
                position = listed - first + count
                inside = (position >= count) & (position < 2 * count)
                if own and halo:
                    wanted = listed >= 0
                elif own:
                    wanted = (listed >= 0) & inside
                else:
                    wanted = (listed >= 0) & jnp.logical_not(inside)
                codes[filled] = row * 64 + jnp.clip(position, 0, 3 * count - 1)
                return filled + wanted.astype(jnp.int32)

            for slot in range(slots):
                filled = add_code(slot, filled)

    lanes = near.shape[3]
    for place, tier in enumerate(tiers):
        for part in range(share):
            row = place * share + part
            cluster = (me ^ tier) * share + part
            turned = jnp.transpose(far[count + cluster])
            for coordinate in range(3):
                near[row, coordinate] = jnp.broadcast_to(
                    turned[:, coordinate : coordinate + 1], (turned.shape[0], lanes)
                )
    near[rows] = near[0]
    if has_start:
        total[0:rows] = start_ref[...]
        total[rows] = jnp.zeros(total.shape[1:], jnp.float32)
    else:
        total[...] = jnp.zeros(total.shape, jnp.float32)
    tile_b[...] = jnp.zeros(tile_b.shape, tile_b.dtype)
    codes[filled] = rows * 64 + count
    codes[filled + 1] = rows * 64 + count

    size = tile_a.shape[0]

    def multiply(code, tile):
        row = code // 64
        position = code % 64
        total[row] = total[row] + nt(vectors[position], tile[...])

    def evaluate(code, tile):
        row = code // 64
        position = code % 64
        for lane in range(0, size, lanes):
            there = [
                jnp.broadcast_to(
                    far[position, coordinate : coordinate + 1, lane : lane + lanes], (16, lanes)
                )
                for coordinate in range(3)
            ]
            for top in range(0, size, 16):
                distance = SOFTEN
                for coordinate in range(3):
                    gap = near[row, coordinate, top : top + 16, :] - there[coordinate]
                    distance = distance + gap * gap
                tile[top : top + 16, lane : lane + lanes] = lax.rsqrt(distance).astype(
                    jnp.bfloat16
                )

    def step(index, carry):
        code_0 = codes[2 * index]
        code_1 = codes[2 * index + 1]
        code_2 = codes[2 * index + 2]
        multiply(code_0, tile_b)
        evaluate(code_1, tile_a)
        multiply(code_1, tile_a)
        evaluate(code_2, tile_b)
        return carry

    steps = filled // 2
    lax.fori_loop(0, steps, step, 0)
    multiply(codes[2 * steps], tile_b)

    if scaled:
        for place, out in enumerate(outs):
            out[...] = (total[place * share : (place + 1) * share] * 0.015625).astype(out.dtype)
    else:
        outs[0][...] = total[0:rows]


def near_field(tiers, share, nb, points, probe, halo, start, scaled):
    count, columns, size = points.shape[0], (probe if probe is not None else halo[2]).shape[1], points.shape[2]
    rows = len(tiers) * share
    operands = [nb, points]
    if probe is not None:
        operands.append(probe)
    if halo is not None:
        operands.extend(halo)
    if start is not None:
        operands.append(start)
    if scaled:
        outs = [jax.ShapeDtypeStruct((share, columns, size), jnp.bfloat16)] * len(tiers)
    else:
        outs = [jax.ShapeDtypeStruct((rows, columns, size), jnp.float32)]
    body = functools.partial(
        near_kernel, tiers, share, count, start is not None, halo is not None, probe is not None, scaled
    )
    blocks = rows * 6
    return pl.pallas_call(
        lambda *refs: body(refs),
        out_shape=outs,
        in_specs=[pl.BlockSpec(memory_space=SMEM)]
        + [pl.BlockSpec(memory_space=VMEM)] * (len(operands) - 1),
        out_specs=[pl.BlockSpec(memory_space=VMEM)] * len(outs),
        scratch_shapes=[
            pltpu.VMEM((3 * count, 8, size), jnp.float32),
            pltpu.VMEM((3 * count, columns, size), jnp.bfloat16),
            pltpu.VMEM((rows + 1, 3, size, 128), jnp.float32),
            pltpu.VMEM((rows + 1, columns, size), jnp.float32),
            pltpu.VMEM((size, size), jnp.bfloat16),
            pltpu.VMEM((size, size), jnp.bfloat16),
            pltpu.SMEM((rows * nb.shape[1] + 4,), jnp.int32),
        ],
        compiler_params=pltpu.CompilerParams(vmem_limit_bytes=VMEM_BYTES),
        cost_estimate=pl.CostEstimate(
            flops=blocks * size * size * (2 * columns + 10),
            bytes_accessed=8 * rows * columns * size,
            transcendentals=blocks * size * size,
        ),
    )(*operands)


def pivot_factor(pivots, inverse, width):
    chosen = (
        lax.broadcasted_iota(jnp.int32, (width, pivots.shape[1]), 0) == pivots
    ).astype(jnp.bfloat16)
    return nt(stacked_split(jnp.transpose(inverse)), chosen).astype(jnp.bfloat16)


def leaf_node(sketch, pivots, inverse):
    factor = pivot_factor(pivots, inverse, sketch.shape[1])
    wide = sketch.astype(jnp.float32)
    mean_sq = jnp.sum(wide * wide, keepdims=True) / (sketch.shape[0] * sketch.shape[1]) + EPSILON
    scale = 1.0 / (sketch.shape[0] * mean_sq)
    picked = halves(nt(factor, sketch))
    raw = halves(nn(stacked_split(picked), sketch))
    interp = raw * scale
    upward = halves(nt(stacked_split(raw), sketch)) * (scale * lax.rsqrt(mean_sq))
    return interp, upward


def tree_node(sketch, pivots, inverse):
    width, columns = sketch.shape
    factor = pivot_factor(pivots, inverse, width)
    mean_sq = jnp.sum(sketch * sketch, keepdims=True) / (width * columns) + EPSILON
    scale = 1.0 / (columns * mean_sq)
    parts = stacked_split(sketch)
    picked = halves(nn(jnp.concatenate([factor, factor], axis=1), parts))
    raw = halves(nt(stacked_split(picked), parts))
    raw = raw[:, :width] + raw[:, width:]
    interp = raw * scale
    both = stacked_split(raw)
    upward = halves(nn(jnp.concatenate([both, both], axis=1), parts)) * (scale * lax.rsqrt(mean_sq))
    return interp, upward


def device_kernel(
    share,
    group,
    rank,
    own,
    *refs,
):
    parts = group // share
    arrived = refs[: parts - 1]
    pivots, inverse, local_pivots, local_inverse, pack, up_out, sketch, ups = refs[parts - 1 :]
    me = lax.axis_index("vec")
    columns = own.shape[1]
    size = own.shape[2]
    for tier, piece in enumerate((own,) + tuple(arrived)):
        place = pl.ds(pl.multiple_of((me ^ tier) * columns, columns), columns)
        for cluster in range(share):
            sketch[cluster, place, :] = piece[cluster]
    for cluster in range(share):
        row = me * share + cluster
        interp, upward = leaf_node(sketch[cluster], pivots[pl.ds(row, 1), :], inverse[row])
        pack[cluster * rank : (cluster + 1) * rank, :] = interp
        ups[cluster * rank : (cluster + 1) * rank, :] = upward
    level_first, nodes, packed = 0, share // 2, 0
    level_nodes = group // 2
    while nodes >= 1:
        results = []
        for node in range(nodes):
            row = level_first + me * nodes + node
            interp, upward = tree_node(
                ups[2 * node * rank : 2 * (node + 1) * rank, :],
                local_pivots[pl.ds(row, 1), :],
                local_inverse[row],
            )
            top = (share + packed // 2) * rank
            side = (packed % 2) * 2 * rank
            pack[top : top + rank, side : side + 2 * rank] = interp
            results.append(upward)
            packed += 1
        for node, upward in enumerate(results):
            ups[node * rank : (node + 1) * rank, :] = upward
        level_first += level_nodes
        level_nodes //= 2
        nodes //= 2
    up_out[...] = ups[0:rank, :]


def group_kernel(share, group, rank, own, *refs):
    parts = group // share
    arrived = refs[: parts - 1]
    local_pivots, local_inverse, interps, up_out, ups = refs[parts - 1 :]
    me = lax.axis_index("vec")
    for tier, piece in enumerate((own,) + tuple(arrived)):
        ups[pl.ds(pl.multiple_of((me ^ tier) * rank, rank), rank), :] = piece[...]
    row = group - parts
    done = 0
    nodes = parts // 2
    while nodes >= 1:
        results = []
        for node in range(nodes):
            interp, upward = tree_node(
                ups[2 * node * rank : 2 * (node + 1) * rank, :],
                local_pivots[row : row + 1, :],
                local_inverse[row],
            )
            interps[done] = interp
            results.append(upward)
            row += 1
            done += 1
        for node, upward in enumerate(results):
            ups[node * rank : (node + 1) * rank, :] = upward
        nodes //= 2
    up_out[...] = ups[0:rank, :]


def upper_kernel(tier, heap_first, last, rank, own, arrived, pivots, inverse, *refs):
    refs = list(refs)
    if last:
        earlier = [refs.pop(0) for _ in range(tier)]
        interps, top, ups, turned = refs
    else:
        interp_out, up_out, ups = refs
    me = lax.axis_index("leaf")
    side = (me >> tier) & 1
    ups[pl.ds(pl.multiple_of(side * rank, rank), rank), :] = own[...]
    ups[pl.ds(pl.multiple_of((1 - side) * rank, rank), rank), :] = arrived[...]
    node = heap_first + (me >> (tier + 1))
    interp, upward = tree_node(ups[...], pivots[pl.ds(node, 1), :], inverse[node])
    if last:
        for index, ref in enumerate(earlier):
            interps[index] = ref[...]
        interps[tier] = interp
        turned[...] = jnp.transpose(upward)
        columns = top.shape[0]
        place = lax.axis_index("vec") * columns
        top[...] = turned[pl.ds(pl.multiple_of(place, columns), columns), :]
    else:
        interp_out[...] = interp
        up_out[...] = upward


def place_kernel(share, group, rank, own, *refs):
    parts = group // share
    arrived = refs[: parts - 1]
    joined, leaf_out, local_out = refs[parts - 1 :]
    me = lax.axis_index("vec")
    for tier, piece in enumerate((own,) + tuple(arrived)):
        device = me ^ tier
        for cluster in range(share):
            leaf_out[device * share + cluster] = piece[cluster * rank : (cluster + 1) * rank, :]
        level_first, nodes, packed = 0, share // 2, 0
        level_nodes = group // 2
        while nodes >= 1:
            for node in range(nodes):
                top = (share + packed // 2) * rank
                side = (packed % 2) * 2 * rank
                local_out[level_first + device * nodes + node] = piece[
                    top : top + rank, side : side + 2 * rank
                ]
                packed += 1
            level_first += level_nodes
            level_nodes //= 2
            nodes //= 2
    for index in range(parts - 1):
        local_out[group - parts + index] = joined[index]


def call(body, outs, scratch, operands, flops=0):
    return pl.pallas_call(
        body,
        out_shape=outs,
        in_specs=[pl.BlockSpec(memory_space=VMEM)] * len(operands),
        out_specs=jax.tree.map(lambda _: pl.BlockSpec(memory_space=VMEM), outs),
        scratch_shapes=scratch,
        compiler_params=pltpu.CompilerParams(vmem_limit_bytes=VMEM_BYTES),
        cost_estimate=pl.CostEstimate(
            flops=flops, bytes_accessed=sum(o.size * o.dtype.itemsize for o in operands), transcendentals=0
        ),
    )(*operands)


def f32(*shape):
    return jax.ShapeDtypeStruct(shape, jnp.float32)


def on_device(
    points,
    probe_vectors,
    neighbours,
    leaf_pivots,
    leaf_inverse,
    local_pivots,
    local_inverse,
    upper_pivots,
    upper_inverse,
):
    group, columns, size = probe_vectors.shape
    rank = leaf_pivots.shape[1]
    leaf_total = lax.axis_size("leaf")
    parts = lax.axis_size("vec")
    share = group // parts
    total_columns = columns * parts

    up = [(i, i + 1) for i in range(leaf_total - 1)]
    down = [(j, i) for i, j in up]
    halo = (
        lax.ppermute(points, "leaf", up),
        lax.ppermute(points, "leaf", down),
        lax.ppermute(probe_vectors, "leaf", up),
        lax.ppermute(probe_vectors, "leaf", down),
    )

    def vec_send(array, tier):
        return lax.ppermute(array, "vec", [(i, i ^ tier) for i in range(parts)])

    away = list(range(parts - 1, 0, -1))
    started = near_field(away, share, neighbours, points, probe_vectors, None, None, False)[0]
    sent = near_field(away, share, neighbours, points, None, halo, started, True)
    arrived = {tier: vec_send(array, tier) for tier, array in zip(away, sent)}
    kept = near_field([0], share, neighbours, points, probe_vectors, halo, None, True)[0]

    pack_rows = share * rank + (share // 2) * rank
    pack, own_up = call(
        functools.partial(device_kernel, share, group, rank),
        (f32(pack_rows, size), f32(rank, total_columns)),
        [
            pltpu.VMEM((share, total_columns, size), jnp.bfloat16),
            pltpu.VMEM((share * rank, total_columns), jnp.float32),
        ],
        [kept]
        + [arrived[tier] for tier in range(1, parts)]
        + [leaf_pivots, leaf_inverse, local_pivots, local_inverse],
    )
    joined, own_up = call(
        functools.partial(group_kernel, share, group, rank),
        (f32(parts - 1, rank, 2 * rank), f32(rank, total_columns)),
        [pltpu.VMEM((parts * rank, total_columns), jnp.float32)],
        [own_up]
        + [vec_send(own_up, tier) for tier in range(1, parts)]
        + [local_pivots, local_inverse],
    )
    pack, own_up = lax.optimization_barrier((pack, own_up))
    others = [vec_send(pack, tier) for tier in range(1, parts)]

    heap_first = 0
    maps = []
    for tier in range(UPL):
        last = tier == UPL - 1
        partner = lax.ppermute(own_up, "leaf", [(i, i ^ (1 << tier)) for i in range(leaf_total)])
        outs = (f32(rank, 2 * rank), f32(rank, total_columns))
        scratch = [pltpu.VMEM((2 * rank, total_columns), jnp.float32)]
        operands = [own_up, partner, upper_pivots, upper_inverse]
        if last:
            outs = (f32(UPL, rank, 2 * rank), f32(columns, rank))
            scratch.append(pltpu.VMEM((total_columns, rank), jnp.float32))
            operands += maps
        first, own_up = call(
            functools.partial(upper_kernel, tier, heap_first, last, rank), outs, scratch, operands
        )
        maps.append(first)
        heap_first += leaf_total >> (tier + 1)
    leaf_map, local_map = call(
        functools.partial(place_kernel, share, group, rank),
        (f32(group, rank, size), f32(group - 1, rank, 2 * rank)),
        [],
        [pack] + others + [joined],
    )
    return (
        jnp.swapaxes(leaf_map, 1, 2),
        jnp.swapaxes(local_map, 1, 2),
        jnp.swapaxes(first, 1, 2)[None],
        own_up[None],
    )


def solution(mesh):
    placed = (
        P("leaf", None, None),
        P("leaf", "vec", None),
        P("leaf", None),
        P("leaf", None),
        P("leaf", None, None),
        P("leaf", None),
        P("leaf", None, None),
        P(),
        P(),
    )
    return jax.shard_map(
        on_device,
        mesh=mesh,
        in_specs=placed,
        out_specs=(
            P("leaf", None, None),
            P("leaf", None, None),
            P("leaf", None, None, None),
            P("leaf", "vec", None),
        ),
        check_vma=False,
    )
```

```python
import functools

import jax
import jax.numpy as jnp
from jax import lax
from jax.experimental import pallas as pl
from jax.experimental.pallas import tpu as pltpu
from jax.sharding import PartitionSpec as P

UPL = 3

SOFTEN = 0.0009
EPSILON = 1e-06
VMEM_BYTES = 48 * 1024 * 1024
VMEM = pltpu.MemorySpace.VMEM
SMEM = pltpu.MemorySpace.SMEM


def nt(a, b):
    return lax.dot_general(a, b, (((1,), (1,)), ((), ())), preferred_element_type=jnp.float32)


def nn(a, b):
    return lax.dot_general(a, b, (((1,), (0,)), ((), ())), preferred_element_type=jnp.float32)


def split(a):
    high = a.astype(jnp.bfloat16)
    low = (a - high.astype(jnp.float32)).astype(jnp.bfloat16)
    return high, low


def stacked_split(a):
    high, low = split(a)
    return jnp.concatenate([high, low], axis=0)


def halves(a):
    rows = a.shape[0] // 2
    return a[:rows] + a[rows:]


def coordinates(points, extra):
    row = lax.broadcasted_iota(jnp.int32, (8, points.shape[1]), 0)
    padded = jnp.concatenate(
        [points.astype(jnp.float32), jnp.full((5, points.shape[1]), 0.5, jnp.float32)], axis=0
    )
    centred = padded - 0.5
    high, low = [part.astype(jnp.float32) for part in split(centred)]
    norm = jnp.sum(centred * centred, axis=0, keepdims=True) + extra
    first, rest = [part.astype(jnp.float32) for part in split(norm)]
    second, third = [part.astype(jnp.float32) for part in split(norm - first)]
    norms = jnp.where(row == 0, first, jnp.where(row == 1, second, jnp.where(row == 2, third, 0.0)))
    return high, low, norms, jnp.where(row < 3, 1.0, 0.0)


def near_kernel(tiers, share, count, has_start, halo, own, scaled, refs):
    refs = list(refs)
    nb_ref, points_ref = refs[:2]
    refs = refs[2:]
    probe_ref = refs.pop(0) if own else None
    if halo:
        before_points, after_points, before_probe, after_probe = refs[:4]
        refs = refs[4:]
    start_ref = refs.pop(0) if has_start else None
    outs = [refs.pop(0) for _ in range(len(tiers) if scaled else 1)]
    far, vectors, near, total, tile_a, tile_b, codes = refs

    me = lax.axis_index("vec")
    first = lax.axis_index("leaf") * count
    slots = nb_ref.shape[1]
    rows = len(tiers) * share

    vacant = jnp.zeros((far.shape[1] - 48, far.shape[2]), far.dtype)
    for place, group_points in enumerate(
        (before_points, points_ref, after_points) if halo else (None, points_ref, None)
    ):
        if group_points is None:
            continue
        for cluster in range(count):
            high, low, norm, one = coordinates(group_points[cluster], SOFTEN)
            far[place * count + cluster, 0:48, :] = jnp.concatenate(
                [-2.0 * high, -2.0 * low, -2.0 * high, -2.0 * low, one, norm], axis=0
            ).astype(far.dtype)
            far[place * count + cluster, 48:, :] = vacant
    if halo:
        vectors[0:count] = before_probe[...]
        vectors[2 * count : 3 * count] = after_probe[...]
    if own:
        vectors[count : 2 * count] = probe_ref[...]

    codes[0] = rows * 64 + count
    filled = jnp.int32(1)
    for place, tier in enumerate(tiers):
        for part in range(share):
            row = place * share + part
            cluster = (me ^ tier) * share + part

            def add_code(slot, filled, row=row, cluster=cluster):
                listed = nb_ref[cluster, slot]
                position = listed - first + count
                inside = (position >= count) & (position < 2 * count)
                if own and halo:
                    wanted = listed >= 0
                elif own:
                    wanted = (listed >= 0) & inside
                else:
                    wanted = (listed >= 0) & jnp.logical_not(inside)
                codes[filled] = row * 64 + jnp.clip(position, 0, 3 * count - 1)
                return filled + wanted.astype(jnp.int32)

            for slot in range(slots):
                filled = add_code(slot, filled)

    for place, tier in enumerate(tiers):
        for part in range(share):
            row = place * share + part
            cluster = (me ^ tier) * share + part
            high, low, norm, one = coordinates(points_ref[cluster], 0.0)
            vacant = jnp.zeros((near.shape[2] - 48, high.shape[1]), jnp.float32)
            near[row] = jnp.transpose(
                jnp.concatenate([high, high, low, low, norm, one, vacant], axis=0)
            ).astype(near.dtype)
    near[rows] = near[0]
    if has_start:
        total[0:rows] = start_ref[...]
        total[rows] = jnp.zeros(total.shape[1:], jnp.float32)
    else:
        total[...] = jnp.zeros(total.shape, jnp.float32)
    tile_b[...] = jnp.zeros(tile_b.shape, tile_b.dtype)
    codes[filled] = rows * 64 + count
    codes[filled + 1] = rows * 64 + count

    size = tile_a.shape[0]

    def multiply(code, tile):
        row = code // 64
        position = code % 64
        total[row] = total[row] + nt(vectors[position], tile[...])

    def evaluate(code, tile):
        row = code // 64
        position = code % 64
        for top in range(0, size, 64):
            distance = nn(near[row, top : top + 64, :], far[position])
            tile[top : top + 64, :] = lax.rsqrt(distance).astype(jnp.bfloat16)

    def step(index, carry):
        code_0 = codes[2 * index]
        code_1 = codes[2 * index + 1]
        code_2 = codes[2 * index + 2]
        multiply(code_0, tile_b)
        evaluate(code_1, tile_a)
        multiply(code_1, tile_a)
        evaluate(code_2, tile_b)
        return carry

    steps = filled // 2
    lax.fori_loop(0, steps, step, 0)
    multiply(codes[2 * steps], tile_b)

    if scaled:
        for place, out in enumerate(outs):
            out[...] = (total[place * share : (place + 1) * share] * 0.015625).astype(out.dtype)
    else:
        outs[0][...] = total[0:rows]


def near_field(tiers, share, nb, points, probe, halo, start, scaled):
    count, columns, size = points.shape[0], (probe if probe is not None else halo[2]).shape[1], points.shape[2]
    rows = len(tiers) * share
    operands = [nb, points]
    if probe is not None:
        operands.append(probe)
    if halo is not None:
        operands.extend(halo)
    if start is not None:
        operands.append(start)
    if scaled:
        outs = [jax.ShapeDtypeStruct((share, columns, size), jnp.bfloat16)] * len(tiers)
    else:
        outs = [jax.ShapeDtypeStruct((rows, columns, size), jnp.float32)]
    body = functools.partial(
        near_kernel, tiers, share, count, start is not None, halo is not None, probe is not None, scaled
    )
    blocks = rows * 6
    return pl.pallas_call(
        lambda *refs: body(refs),
        out_shape=outs,
        in_specs=[pl.BlockSpec(memory_space=SMEM)]
        + [pl.BlockSpec(memory_space=VMEM)] * (len(operands) - 1),
        out_specs=[pl.BlockSpec(memory_space=VMEM)] * len(outs),
        scratch_shapes=[
            pltpu.VMEM((3 * count, 128, size), jnp.bfloat16),
            pltpu.VMEM((3 * count, columns, size), jnp.bfloat16),
            pltpu.VMEM((rows + 1, size, 128), jnp.bfloat16),
            pltpu.VMEM((rows + 1, columns, size), jnp.float32),
            pltpu.VMEM((size, size), jnp.bfloat16),
            pltpu.VMEM((size, size), jnp.bfloat16),
            pltpu.SMEM((rows * nb.shape[1] + 4,), jnp.int32),
        ],
        compiler_params=pltpu.CompilerParams(vmem_limit_bytes=VMEM_BYTES),
        cost_estimate=pl.CostEstimate(
            flops=blocks * size * size * (2 * columns + 10),
            bytes_accessed=8 * rows * columns * size,
            transcendentals=blocks * size * size,
        ),
    )(*operands)


def pivot_factor(pivots, inverse, width):
    chosen = (
        lax.broadcasted_iota(jnp.int32, (width, pivots.shape[1]), 0) == pivots
    ).astype(jnp.bfloat16)
    return nt(stacked_split(jnp.transpose(inverse)), chosen).astype(jnp.bfloat16)


def leaf_node(sketch, pivots, inverse):
    factor = pivot_factor(pivots, inverse, sketch.shape[1])
    wide = sketch.astype(jnp.float32)
    mean_sq = jnp.sum(wide * wide, keepdims=True) / (sketch.shape[0] * sketch.shape[1]) + EPSILON
    scale = 1.0 / (sketch.shape[0] * mean_sq)
    picked = halves(nt(factor, sketch))
    raw = halves(nn(stacked_split(picked), sketch))
    interp = raw * scale
    upward = halves(nt(stacked_split(raw), sketch)) * (scale * lax.rsqrt(mean_sq))
    return interp, upward


def tree_node(sketch, pivots, inverse):
    width, columns = sketch.shape
    factor = pivot_factor(pivots, inverse, width)
    mean_sq = jnp.sum(sketch * sketch, keepdims=True) / (width * columns) + EPSILON
    scale = 1.0 / (columns * mean_sq)
    parts = stacked_split(sketch)
    picked = halves(nn(jnp.concatenate([factor, factor], axis=1), parts))
    raw = halves(nt(stacked_split(picked), parts))
    raw = raw[:, :width] + raw[:, width:]
    interp = raw * scale
    both = stacked_split(raw)
    upward = halves(nn(jnp.concatenate([both, both], axis=1), parts)) * (scale * lax.rsqrt(mean_sq))
    return interp, upward


def device_kernel(
    share,
    group,
    rank,
    own,
    *refs,
):
    parts = group // share
    arrived = refs[: parts - 1]
    pivots, inverse, local_pivots, local_inverse, pack, up_out, sketch, ups = refs[parts - 1 :]
    me = lax.axis_index("vec")
    columns = own.shape[1]
    size = own.shape[2]
    for tier, piece in enumerate((own,) + tuple(arrived)):
        place = pl.ds(pl.multiple_of((me ^ tier) * columns, columns), columns)
        for cluster in range(share):
            sketch[cluster, place, :] = piece[cluster]
    for cluster in range(share):
        row = me * share + cluster
        interp, upward = leaf_node(sketch[cluster], pivots[pl.ds(row, 1), :], inverse[row])
        pack[cluster * rank : (cluster + 1) * rank, :] = interp
        ups[cluster * rank : (cluster + 1) * rank, :] = upward
    level_first, nodes, packed = 0, share // 2, 0
    level_nodes = group // 2
    while nodes >= 1:
        results = []
        for node in range(nodes):
            row = level_first + me * nodes + node
            interp, upward = tree_node(
                ups[2 * node * rank : 2 * (node + 1) * rank, :],
                local_pivots[pl.ds(row, 1), :],
                local_inverse[row],
            )
            top = (share + packed // 2) * rank
            side = (packed % 2) * 2 * rank
            pack[top : top + rank, side : side + 2 * rank] = interp
            results.append(upward)
            packed += 1
        for node, upward in enumerate(results):
            ups[node * rank : (node + 1) * rank, :] = upward
        level_first += level_nodes
        level_nodes //= 2
        nodes //= 2
    up_out[...] = ups[0:rank, :]


def group_kernel(share, group, rank, own, *refs):
    parts = group // share
    arrived = refs[: parts - 1]
    local_pivots, local_inverse, interps, up_out, ups = refs[parts - 1 :]
    me = lax.axis_index("vec")
    for tier, piece in enumerate((own,) + tuple(arrived)):
        ups[pl.ds(pl.multiple_of((me ^ tier) * rank, rank), rank), :] = piece[...]
    row = group - parts
    done = 0
    nodes = parts // 2
    while nodes >= 1:
        results = []
        for node in range(nodes):
            interp, upward = tree_node(
                ups[2 * node * rank : 2 * (node + 1) * rank, :],
                local_pivots[row : row + 1, :],
                local_inverse[row],
            )
            interps[done] = interp
            results.append(upward)
            row += 1
            done += 1
        for node, upward in enumerate(results):
            ups[node * rank : (node + 1) * rank, :] = upward
        nodes //= 2
    up_out[...] = ups[0:rank, :]


def upper_kernel(tier, heap_first, last, rank, own, arrived, pivots, inverse, *refs):
    refs = list(refs)
    if last:
        earlier = [refs.pop(0) for _ in range(tier)]
        interps, top, ups, turned = refs
    else:
        interp_out, up_out, ups = refs
    me = lax.axis_index("leaf")
    side = (me >> tier) & 1
    ups[pl.ds(pl.multiple_of(side * rank, rank), rank), :] = own[...]
    ups[pl.ds(pl.multiple_of((1 - side) * rank, rank), rank), :] = arrived[...]
    node = heap_first + (me >> (tier + 1))
    interp, upward = tree_node(ups[...], pivots[pl.ds(node, 1), :], inverse[node])
    if last:
        for index, ref in enumerate(earlier):
            interps[index] = ref[...]
        interps[tier] = interp
        turned[...] = jnp.transpose(upward)
        columns = top.shape[0]
        place = lax.axis_index("vec") * columns
        top[...] = turned[pl.ds(pl.multiple_of(place, columns), columns), :]
    else:
        interp_out[...] = interp
        up_out[...] = upward


def place_kernel(share, group, rank, own, *refs):
    parts = group // share
    arrived = refs[: parts - 1]
    joined, leaf_out, local_out = refs[parts - 1 :]
    me = lax.axis_index("vec")
    for tier, piece in enumerate((own,) + tuple(arrived)):
        device = me ^ tier
        for cluster in range(share):
            leaf_out[device * share + cluster] = piece[cluster * rank : (cluster + 1) * rank, :]
        level_first, nodes, packed = 0, share // 2, 0
        level_nodes = group // 2
        while nodes >= 1:
            for node in range(nodes):
                top = (share + packed // 2) * rank
                side = (packed % 2) * 2 * rank
                local_out[level_first + device * nodes + node] = piece[
                    top : top + rank, side : side + 2 * rank
                ]
                packed += 1
            level_first += level_nodes
            level_nodes //= 2
            nodes //= 2
    for index in range(parts - 1):
        local_out[group - parts + index] = joined[index]


def call(body, outs, scratch, operands, flops=0):
    return pl.pallas_call(
        body,
        out_shape=outs,
        in_specs=[pl.BlockSpec(memory_space=VMEM)] * len(operands),
        out_specs=jax.tree.map(lambda _: pl.BlockSpec(memory_space=VMEM), outs),
        scratch_shapes=scratch,
        compiler_params=pltpu.CompilerParams(vmem_limit_bytes=VMEM_BYTES),
        cost_estimate=pl.CostEstimate(
            flops=flops, bytes_accessed=sum(o.size * o.dtype.itemsize for o in operands), transcendentals=0
        ),
    )(*operands)


def f32(*shape):
    return jax.ShapeDtypeStruct(shape, jnp.float32)


def on_device(
    points,
    probe_vectors,
    neighbours,
    leaf_pivots,
    leaf_inverse,
    local_pivots,
    local_inverse,
    upper_pivots,
    upper_inverse,
):
    group, columns, size = probe_vectors.shape
    rank = leaf_pivots.shape[1]
    leaf_total = lax.axis_size("leaf")
    parts = lax.axis_size("vec")
    share = group // parts
    total_columns = columns * parts

    up = [(i, i + 1) for i in range(leaf_total - 1)]
    down = [(j, i) for i, j in up]
    halo = (
        lax.ppermute(points, "leaf", up),
        lax.ppermute(points, "leaf", down),
        lax.ppermute(probe_vectors, "leaf", up),
        lax.ppermute(probe_vectors, "leaf", down),
    )

    def vec_send(array, tier):
        return lax.ppermute(array, "vec", [(i, i ^ tier) for i in range(parts)])

    away = list(range(parts - 1, 0, -1))
    started = near_field(away, share, neighbours, points, probe_vectors, None, None, False)[0]
    sent = near_field(away, share, neighbours, points, None, halo, started, True)
    arrived = {tier: vec_send(array, tier) for tier, array in zip(away, sent)}
    kept = near_field([0], share, neighbours, points, probe_vectors, halo, None, True)[0]

    pack_rows = share * rank + (share // 2) * rank
    pack, own_up = call(
        functools.partial(device_kernel, share, group, rank),
        (f32(pack_rows, size), f32(rank, total_columns)),
        [
            pltpu.VMEM((share, total_columns, size), jnp.bfloat16),
            pltpu.VMEM((share * rank, total_columns), jnp.float32),
        ],
        [kept]
        + [arrived[tier] for tier in range(1, parts)]
        + [leaf_pivots, leaf_inverse, local_pivots, local_inverse],
    )
    joined, own_up = call(
        functools.partial(group_kernel, share, group, rank),
        (f32(parts - 1, rank, 2 * rank), f32(rank, total_columns)),
        [pltpu.VMEM((parts * rank, total_columns), jnp.float32)],
        [own_up]
        + [vec_send(own_up, tier) for tier in range(1, parts)]
        + [local_pivots, local_inverse],
    )
    pack, own_up = lax.optimization_barrier((pack, own_up))
    others = [vec_send(pack, tier) for tier in range(1, parts)]

    heap_first = 0
    maps = []
    for tier in range(UPL):
        last = tier == UPL - 1
        partner = lax.ppermute(own_up, "leaf", [(i, i ^ (1 << tier)) for i in range(leaf_total)])
        outs = (f32(rank, 2 * rank), f32(rank, total_columns))
        scratch = [pltpu.VMEM((2 * rank, total_columns), jnp.float32)]
        operands = [own_up, partner, upper_pivots, upper_inverse]
        if last:
            outs = (f32(UPL, rank, 2 * rank), f32(columns, rank))
            scratch.append(pltpu.VMEM((total_columns, rank), jnp.float32))
            operands += maps
        first, own_up = call(
            functools.partial(upper_kernel, tier, heap_first, last, rank), outs, scratch, operands
        )
        maps.append(first)
        heap_first += leaf_total >> (tier + 1)
    leaf_map, local_map = call(
        functools.partial(place_kernel, share, group, rank),
        (f32(group, rank, size), f32(group - 1, rank, 2 * rank)),
        [],
        [pack] + others + [joined],
    )
    return (
        jnp.swapaxes(leaf_map, 1, 2),
        jnp.swapaxes(local_map, 1, 2),
        jnp.swapaxes(first, 1, 2)[None],
        own_up[None],
    )


def solution(mesh):
    placed = (
        P("leaf", None, None),
        P("leaf", "vec", None),
        P("leaf", None),
        P("leaf", None),
        P("leaf", None, None),
        P("leaf", None),
        P("leaf", None, None),
        P(),
        P(),
    )
    return jax.shard_map(
        on_device,
        mesh=mesh,
        in_specs=placed,
        out_specs=(
            P("leaf", None, None),
            P("leaf", None, None),
            P("leaf", None, None, None),
            P("leaf", "vec", None),
        ),
        check_vma=False,
    )
```

```python
import functools

import jax
import jax.numpy as jnp
from jax import lax
from jax.experimental import pallas as pl
from jax.experimental.pallas import tpu as pltpu
from jax.sharding import PartitionSpec as P

UPL = 3

SOFTEN = 0.0009
EPSILON = 1e-06
FLIGHT = 4
VMEM_BYTES = 48 * 1024 * 1024
VMEM = pltpu.MemorySpace.VMEM
SMEM = pltpu.MemorySpace.SMEM


def nt(a, b):
    return lax.dot_general(a, b, (((1,), (1,)), ((), ())), preferred_element_type=jnp.float32)


def nn(a, b):
    return lax.dot_general(a, b, (((1,), (0,)), ((), ())), preferred_element_type=jnp.float32)


def split(a):
    high = a.astype(jnp.bfloat16)
    low = (a - high.astype(jnp.float32)).astype(jnp.bfloat16)
    return high, low


def stacked_split(a):
    high, low = split(a)
    return jnp.concatenate([high, low], axis=0)


def halves(a):
    rows = a.shape[0] // 2
    return a[:rows] + a[rows:]


def coordinates(points, extra):
    row = lax.broadcasted_iota(jnp.int32, (8, points.shape[1]), 0)
    padded = jnp.concatenate(
        [points.astype(jnp.float32), jnp.full((5, points.shape[1]), 0.5, jnp.float32)], axis=0
    )
    centred = padded - 0.5
    high, low = [part.astype(jnp.float32) for part in split(centred)]
    norm = jnp.sum(centred * centred, axis=0, keepdims=True) + extra
    first, rest = [part.astype(jnp.float32) for part in split(norm)]
    second, third = [part.astype(jnp.float32) for part in split(norm - first)]
    norms = jnp.where(row == 0, first, jnp.where(row == 1, second, jnp.where(row == 2, third, 0.0)))
    return high, low, norms, jnp.where(row < 3, 1.0, 0.0)


def near_kernel(tiers, share, count, has_start, halo, own, scaled, refs):
    refs = list(refs)
    nb_ref, points_ref = refs[:2]
    refs = refs[2:]
    probe_ref = refs.pop(0) if own else None
    if halo:
        before_points, after_points, before_probe, after_probe = refs[:4]
        refs = refs[4:]
    start_ref = refs.pop(0) if has_start else None
    outs = [refs.pop(0) for _ in range(len(tiers) if scaled else 1)]
    far, vectors, near, total, tiles, codes = refs
    flight = tiles.shape[0]

    me = lax.axis_index("vec")
    first = lax.axis_index("leaf") * count
    slots = nb_ref.shape[1]
    rows = len(tiers) * share

    vacant = jnp.zeros((far.shape[1] - 48, far.shape[2]), far.dtype)
    for place, group_points in enumerate(
        (before_points, points_ref, after_points) if halo else (None, points_ref, None)
    ):
        if group_points is None:
            continue
        for cluster in range(count):
            high, low, norm, one = coordinates(group_points[cluster], SOFTEN)
            far[place * count + cluster, 0:48, :] = jnp.concatenate(
                [-2.0 * high, -2.0 * low, -2.0 * high, -2.0 * low, one, norm], axis=0
            ).astype(far.dtype)
            far[place * count + cluster, 48:, :] = vacant
    if halo:
        vectors[0:count] = before_probe[...]
        vectors[2 * count : 3 * count] = after_probe[...]
    if own:
        vectors[count : 2 * count] = probe_ref[...]

    for way in range(flight):
        codes[way] = rows * 64 + count
    filled = jnp.int32(flight)
    for place, tier in enumerate(tiers):
        for part in range(share):
            row = place * share + part
            cluster = (me ^ tier) * share + part

            def add_code(slot, filled, row=row, cluster=cluster):
                listed = nb_ref[cluster, slot]
                position = listed - first + count
                inside = (position >= count) & (position < 2 * count)
                if own and halo:
                    wanted = listed >= 0
                elif own:
                    wanted = (listed >= 0) & inside
                else:
                    wanted = (listed >= 0) & jnp.logical_not(inside)
                codes[filled] = row * 64 + jnp.clip(position, 0, 3 * count - 1)
                return filled + wanted.astype(jnp.int32)

            for slot in range(slots):
                filled = add_code(slot, filled)

    for place, tier in enumerate(tiers):
        for part in range(share):
            row = place * share + part
            cluster = (me ^ tier) * share + part
            high, low, norm, one = coordinates(points_ref[cluster], 0.0)
            vacant = jnp.zeros((near.shape[2] - 48, high.shape[1]), jnp.float32)
            near[row] = jnp.transpose(
                jnp.concatenate([high, high, low, low, norm, one, vacant], axis=0)
            ).astype(near.dtype)
    near[rows] = near[0]
    if has_start:
        total[0:rows] = start_ref[...]
        total[rows] = jnp.zeros(total.shape[1:], jnp.float32)
    else:
        total[...] = jnp.zeros(total.shape, jnp.float32)
    tiles[...] = jnp.zeros(tiles.shape, tiles.dtype)
    for way in range(flight):
        codes[filled + way] = rows * 64 + count

    size = tiles.shape[1]

    def multiply(code, tile):
        row = code // 64
        position = code % 64
        total[row] = total[row] + nt(vectors[position], tile[...])

    def evaluate(code, tile):
        row = code // 64
        position = code % 64
        for top in range(0, size, 128):
            distance = nn(near[row, top : top + 128, :], far[position])
            tile[top : top + 128, :] = lax.rsqrt(distance).astype(jnp.bfloat16)

    def step(index, carry):
        for way in range(flight):
            multiply(codes[index * flight + way], tiles.at[way])
            evaluate(codes[(index + 1) * flight + way], tiles.at[way])
        return carry

    steps = (filled - 1) // flight
    lax.fori_loop(0, steps, step, 0)
    for way in range(flight):
        multiply(codes[steps * flight + way], tiles.at[way])

    if scaled:
        for place, out in enumerate(outs):
            out[...] = (total[place * share : (place + 1) * share] * 0.015625).astype(out.dtype)
    else:
        outs[0][...] = total[0:rows]


def near_field(tiers, share, nb, points, probe, halo, start, scaled):
    count, columns, size = points.shape[0], (probe if probe is not None else halo[2]).shape[1], points.shape[2]
    rows = len(tiers) * share
    operands = [nb, points]
    if probe is not None:
        operands.append(probe)
    if halo is not None:
        operands.extend(halo)
    if start is not None:
        operands.append(start)
    if scaled:
        outs = [jax.ShapeDtypeStruct((share, columns, size), jnp.bfloat16)] * len(tiers)
    else:
        outs = [jax.ShapeDtypeStruct((rows, columns, size), jnp.float32)]
    body = functools.partial(
        near_kernel, tiers, share, count, start is not None, halo is not None, probe is not None, scaled
    )
    blocks = rows * 6
    return pl.pallas_call(
        lambda *refs: body(refs),
        out_shape=outs,
        in_specs=[pl.BlockSpec(memory_space=SMEM)]
        + [pl.BlockSpec(memory_space=VMEM)] * (len(operands) - 1),
        out_specs=[pl.BlockSpec(memory_space=VMEM)] * len(outs),
        scratch_shapes=[
            pltpu.VMEM((3 * count, 128, size), jnp.bfloat16),
            pltpu.VMEM((3 * count, columns, size), jnp.bfloat16),
            pltpu.VMEM((rows + 1, size, 128), jnp.bfloat16),
            pltpu.VMEM((rows + 1, columns, size), jnp.float32),
            pltpu.VMEM((FLIGHT, size, size), jnp.bfloat16),
            pltpu.SMEM((rows * nb.shape[1] + 2 * FLIGHT,), jnp.int32),
        ],
        compiler_params=pltpu.CompilerParams(vmem_limit_bytes=VMEM_BYTES),
        cost_estimate=pl.CostEstimate(
            flops=blocks * size * size * (2 * columns + 10),
            bytes_accessed=8 * rows * columns * size,
            transcendentals=blocks * size * size,
        ),
    )(*operands)


def pivot_factor(pivots, inverse, width):
    chosen = (
        lax.broadcasted_iota(jnp.int32, (width, pivots.shape[1]), 0) == pivots
    ).astype(jnp.bfloat16)
    return nt(stacked_split(jnp.transpose(inverse)), chosen).astype(jnp.bfloat16)


def leaf_node(sketch, pivots, inverse):
    factor = pivot_factor(pivots, inverse, sketch.shape[1])
    wide = sketch.astype(jnp.float32)
    mean_sq = jnp.sum(wide * wide, keepdims=True) / (sketch.shape[0] * sketch.shape[1]) + EPSILON
    scale = 1.0 / (sketch.shape[0] * mean_sq)
    picked = halves(nt(factor, sketch))
    raw = halves(nn(stacked_split(picked), sketch))
    interp = raw * scale
    upward = halves(nt(stacked_split(raw), sketch)) * (scale * lax.rsqrt(mean_sq))
    return interp, upward


def tree_node(sketch, pivots, inverse):
    width, columns = sketch.shape
    factor = pivot_factor(pivots, inverse, width)
    mean_sq = jnp.sum(sketch * sketch, keepdims=True) / (width * columns) + EPSILON
    scale = 1.0 / (columns * mean_sq)
    parts = stacked_split(sketch)
    picked = halves(nn(jnp.concatenate([factor, factor], axis=1), parts))
    raw = halves(nt(stacked_split(picked), parts))
    raw = raw[:, :width] + raw[:, width:]
    interp = raw * scale
    both = stacked_split(raw)
    upward = halves(nn(jnp.concatenate([both, both], axis=1), parts)) * (scale * lax.rsqrt(mean_sq))
    return interp, upward


def device_kernel(
    share,
    group,
    rank,
    own,
    *refs,
):
    parts = group // share
    arrived = refs[: parts - 1]
    pivots, inverse, local_pivots, local_inverse, pack, up_out, sketch, ups = refs[parts - 1 :]
    me = lax.axis_index("vec")
    columns = own.shape[1]
    size = own.shape[2]
    for tier, piece in enumerate((own,) + tuple(arrived)):
        place = pl.ds(pl.multiple_of((me ^ tier) * columns, columns), columns)
        for cluster in range(share):
            sketch[cluster, place, :] = piece[cluster]
    for cluster in range(share):
        row = me * share + cluster
        interp, upward = leaf_node(sketch[cluster], pivots[pl.ds(row, 1), :], inverse[row])
        pack[cluster * rank : (cluster + 1) * rank, :] = interp
        ups[cluster * rank : (cluster + 1) * rank, :] = upward
    level_first, nodes, packed = 0, share // 2, 0
    level_nodes = group // 2
    while nodes >= 1:
        results = []
        for node in range(nodes):
            row = level_first + me * nodes + node
            interp, upward = tree_node(
                ups[2 * node * rank : 2 * (node + 1) * rank, :],
                local_pivots[pl.ds(row, 1), :],
                local_inverse[row],
            )
            top = (share + packed // 2) * rank
            side = (packed % 2) * 2 * rank
            pack[top : top + rank, side : side + 2 * rank] = interp
            results.append(upward)
            packed += 1
        for node, upward in enumerate(results):
            ups[node * rank : (node + 1) * rank, :] = upward
        level_first += level_nodes
        level_nodes //= 2
        nodes //= 2
    up_out[...] = ups[0:rank, :]


def group_kernel(share, group, rank, own, *refs):
    parts = group // share
    arrived = refs[: parts - 1]
    local_pivots, local_inverse, interps, up_out, ups = refs[parts - 1 :]
    me = lax.axis_index("vec")
    for tier, piece in enumerate((own,) + tuple(arrived)):
        ups[pl.ds(pl.multiple_of((me ^ tier) * rank, rank), rank), :] = piece[...]
    row = group - parts
    done = 0
    nodes = parts // 2
    while nodes >= 1:
        results = []
        for node in range(nodes):
            interp, upward = tree_node(
                ups[2 * node * rank : 2 * (node + 1) * rank, :],
                local_pivots[row : row + 1, :],
                local_inverse[row],
            )
            interps[done] = interp
            results.append(upward)
            row += 1
            done += 1
        for node, upward in enumerate(results):
            ups[node * rank : (node + 1) * rank, :] = upward
        nodes //= 2
    up_out[...] = ups[0:rank, :]


def upper_kernel(tier, heap_first, last, rank, own, arrived, pivots, inverse, *refs):
    refs = list(refs)
    if last:
        earlier = [refs.pop(0) for _ in range(tier)]
        interps, top, ups, turned = refs
    else:
        interp_out, up_out, ups = refs
    me = lax.axis_index("leaf")
    side = (me >> tier) & 1
    ups[pl.ds(pl.multiple_of(side * rank, rank), rank), :] = own[...]
    ups[pl.ds(pl.multiple_of((1 - side) * rank, rank), rank), :] = arrived[...]
    node = heap_first + (me >> (tier + 1))
    interp, upward = tree_node(ups[...], pivots[pl.ds(node, 1), :], inverse[node])
    if last:
        for index, ref in enumerate(earlier):
            interps[index] = ref[...]
        interps[tier] = interp
        turned[...] = jnp.transpose(upward)
        columns = top.shape[0]
        place = lax.axis_index("vec") * columns
        top[...] = turned[pl.ds(pl.multiple_of(place, columns), columns), :]
    else:
        interp_out[...] = interp
        up_out[...] = upward


def place_kernel(share, group, rank, own, *refs):
    parts = group // share
    arrived = refs[: parts - 1]
    joined, leaf_out, local_out = refs[parts - 1 :]
    me = lax.axis_index("vec")
    for tier, piece in enumerate((own,) + tuple(arrived)):
        device = me ^ tier
        for cluster in range(share):
            leaf_out[device * share + cluster] = piece[cluster * rank : (cluster + 1) * rank, :]
        level_first, nodes, packed = 0, share // 2, 0
        level_nodes = group // 2
        while nodes >= 1:
            for node in range(nodes):
                top = (share + packed // 2) * rank
                side = (packed % 2) * 2 * rank
                local_out[level_first + device * nodes + node] = piece[
                    top : top + rank, side : side + 2 * rank
                ]
                packed += 1
            level_first += level_nodes
            level_nodes //= 2
            nodes //= 2
    for index in range(parts - 1):
        local_out[group - parts + index] = joined[index]


def call(body, outs, scratch, operands, flops=0):
    return pl.pallas_call(
        body,
        out_shape=outs,
        in_specs=[pl.BlockSpec(memory_space=VMEM)] * len(operands),
        out_specs=jax.tree.map(lambda _: pl.BlockSpec(memory_space=VMEM), outs),
        scratch_shapes=scratch,
        compiler_params=pltpu.CompilerParams(vmem_limit_bytes=VMEM_BYTES),
        cost_estimate=pl.CostEstimate(
            flops=flops, bytes_accessed=sum(o.size * o.dtype.itemsize for o in operands), transcendentals=0
        ),
    )(*operands)


def f32(*shape):
    return jax.ShapeDtypeStruct(shape, jnp.float32)


def on_device(
    points,
    probe_vectors,
    neighbours,
    leaf_pivots,
    leaf_inverse,
    local_pivots,
    local_inverse,
    upper_pivots,
    upper_inverse,
):
    group, columns, size = probe_vectors.shape
    rank = leaf_pivots.shape[1]
    leaf_total = lax.axis_size("leaf")
    parts = lax.axis_size("vec")
    share = group // parts
    total_columns = columns * parts

    up = [(i, i + 1) for i in range(leaf_total - 1)]
    down = [(j, i) for i, j in up]
    halo = (
        lax.ppermute(points, "leaf", up),
        lax.ppermute(points, "leaf", down),
        lax.ppermute(probe_vectors, "leaf", up),
        lax.ppermute(probe_vectors, "leaf", down),
    )

    def vec_send(array, tier):
        return lax.ppermute(array, "vec", [(i, i ^ tier) for i in range(parts)])

    away = list(range(parts - 1, 0, -1))
    started = near_field(away, share, neighbours, points, probe_vectors, None, None, False)[0]
    sent = near_field(away, share, neighbours, points, None, halo, started, True)
    arrived = {tier: vec_send(array, tier) for tier, array in zip(away, sent)}
    kept = near_field([0], share, neighbours, points, probe_vectors, halo, None, True)[0]

    pack_rows = share * rank + (share // 2) * rank
    pack, own_up = call(
        functools.partial(device_kernel, share, group, rank),
        (f32(pack_rows, size), f32(rank, total_columns)),
        [
            pltpu.VMEM((share, total_columns, size), jnp.bfloat16),
            pltpu.VMEM((share * rank, total_columns), jnp.float32),
        ],
        [kept]
        + [arrived[tier] for tier in range(1, parts)]
        + [leaf_pivots, leaf_inverse, local_pivots, local_inverse],
    )
    joined, own_up = call(
        functools.partial(group_kernel, share, group, rank),
        (f32(parts - 1, rank, 2 * rank), f32(rank, total_columns)),
        [pltpu.VMEM((parts * rank, total_columns), jnp.float32)],
        [own_up]
        + [vec_send(own_up, tier) for tier in range(1, parts)]
        + [local_pivots, local_inverse],
    )
    pack, own_up = lax.optimization_barrier((pack, own_up))
    others = [vec_send(pack, tier) for tier in range(1, parts)]

    heap_first = 0
    maps = []
    for tier in range(UPL):
        last = tier == UPL - 1
        partner = lax.ppermute(own_up, "leaf", [(i, i ^ (1 << tier)) for i in range(leaf_total)])
        outs = (f32(rank, 2 * rank), f32(rank, total_columns))
        scratch = [pltpu.VMEM((2 * rank, total_columns), jnp.float32)]
        operands = [own_up, partner, upper_pivots, upper_inverse]
        if last:
            outs = (f32(UPL, rank, 2 * rank), f32(columns, rank))
            scratch.append(pltpu.VMEM((total_columns, rank), jnp.float32))
            operands += maps
        first, own_up = call(
            functools.partial(upper_kernel, tier, heap_first, last, rank), outs, scratch, operands
        )
        maps.append(first)
        heap_first += leaf_total >> (tier + 1)
    leaf_map, local_map = call(
        functools.partial(place_kernel, share, group, rank),
        (f32(group, rank, size), f32(group - 1, rank, 2 * rank)),
        [],
        [pack] + others + [joined],
    )
    return (
        jnp.swapaxes(leaf_map, 1, 2),
        jnp.swapaxes(local_map, 1, 2),
        jnp.swapaxes(first, 1, 2)[None],
        own_up[None],
    )


def solution(mesh):
    placed = (
        P("leaf", None, None),
        P("leaf", "vec", None),
        P("leaf", None),
        P("leaf", None),
        P("leaf", None, None),
        P("leaf", None),
        P("leaf", None, None),
        P(),
        P(),
    )
    return jax.shard_map(
        on_device,
        mesh=mesh,
        in_specs=placed,
        out_specs=(
            P("leaf", None, None),
            P("leaf", None, None),
            P("leaf", None, None, None),
            P("leaf", "vec", None),
        ),
        check_vma=False,
    )
```

```python
import functools

import jax
import jax.numpy as jnp
from jax import lax
from jax.experimental import pallas as pl
from jax.experimental.pallas import tpu as pltpu
from jax.sharding import PartitionSpec as P

UPL = 3

SOFTEN = 0.0009
EPSILON = 1e-06
FLIGHT = 4
VMEM_BYTES = 48 * 1024 * 1024
VMEM = pltpu.MemorySpace.VMEM
SMEM = pltpu.MemorySpace.SMEM


def nt(a, b):
    return lax.dot_general(a, b, (((1,), (1,)), ((), ())), preferred_element_type=jnp.float32)


def nn(a, b):
    return lax.dot_general(a, b, (((1,), (0,)), ((), ())), preferred_element_type=jnp.float32)


def split(a):
    high = a.astype(jnp.bfloat16)
    low = (a - high.astype(jnp.float32)).astype(jnp.bfloat16)
    return high, low


def stacked_split(a):
    high, low = split(a)
    return jnp.concatenate([high, low], axis=0)


def halves(a):
    rows = a.shape[0] // 2
    return a[:rows] + a[rows:]


def coordinates(points, extra):
    row = lax.broadcasted_iota(jnp.int32, (8, points.shape[1]), 0)
    padded = jnp.concatenate(
        [points, jnp.full((5, points.shape[1]), 0.5, jnp.float32)], axis=0
    )
    centred = padded - 0.5
    high, low = [part.astype(jnp.float32) for part in split(centred)]
    norm = jnp.sum(centred * centred, axis=0, keepdims=True) + extra
    first, rest = [part.astype(jnp.float32) for part in split(norm)]
    second, third = [part.astype(jnp.float32) for part in split(norm - first)]
    norms = jnp.where(row == 0, first, jnp.where(row == 1, second, jnp.where(row == 2, third, 0.0)))
    return high, low, norms, jnp.where(row < 3, 1.0, 0.0)


def near_kernel(tiers, share, count, has_start, halo, own, scaled, refs):
    refs = list(refs)
    nb_ref, points_ref = refs[:2]
    refs = refs[2:]
    probe_ref = refs.pop(0) if own else None
    if halo:
        before, after = refs[:2]
        refs = refs[2:]
    start_ref = refs.pop(0) if has_start else None
    outs = [refs.pop(0) for _ in range(len(tiers) if scaled else 1)]
    far, vectors, near, total, tiles, codes = refs
    flight = tiles.shape[0]

    me = lax.axis_index("vec")
    first = lax.axis_index("leaf") * count
    slots = nb_ref.shape[1]
    rows = len(tiers) * share

    vacant = jnp.zeros((far.shape[1] - 48, far.shape[2]), far.dtype)
    columns = vectors.shape[1]
    for place, source in enumerate((before, points_ref, after) if halo else (None, points_ref, None)):
        if source is None:
            continue
        for cluster in range(count):
            if place == 1:
                listed_points = source[cluster].astype(jnp.float32)
            else:
                listed_points = source[cluster, columns:, :].astype(jnp.float32)[0:3]
            high, low, norm, one = coordinates(listed_points, SOFTEN)
            far[place * count + cluster, 0:48, :] = jnp.concatenate(
                [-2.0 * high, -2.0 * low, -2.0 * high, -2.0 * low, one, norm], axis=0
            ).astype(far.dtype)
            far[place * count + cluster, 48:, :] = vacant
    if halo:
        vectors[0:count] = before[:, 0:columns, :]
        vectors[2 * count : 3 * count] = after[:, 0:columns, :]
    if own:
        vectors[count : 2 * count] = probe_ref[...]

    for way in range(flight):
        codes[way] = rows * 64 + count
    filled = jnp.int32(flight)
    for place, tier in enumerate(tiers):
        for part in range(share):
            row = place * share + part
            cluster = (me ^ tier) * share + part

            def add_code(slot, filled, row=row, cluster=cluster):
                listed = nb_ref[cluster, slot]
                position = listed - first + count
                inside = (position >= count) & (position < 2 * count)
                if own and halo:
                    wanted = listed >= 0
                elif own:
                    wanted = (listed >= 0) & inside
                else:
                    wanted = (listed >= 0) & jnp.logical_not(inside)
                codes[filled] = row * 64 + jnp.clip(position, 0, 3 * count - 1)
                return filled + wanted.astype(jnp.int32)

            for slot in range(slots):
                filled = add_code(slot, filled)

    for place, tier in enumerate(tiers):
        for part in range(share):
            row = place * share + part
            cluster = (me ^ tier) * share + part
            high, low, norm, one = coordinates(points_ref[cluster].astype(jnp.float32), 0.0)
            vacant = jnp.zeros((near.shape[2] - 48, high.shape[1]), jnp.float32)
            near[row] = jnp.transpose(
                jnp.concatenate([high, high, low, low, norm, one, vacant], axis=0)
            ).astype(near.dtype)
    near[rows] = near[0]
    if has_start:
        total[0:rows] = start_ref[...]
        total[rows] = jnp.zeros(total.shape[1:], jnp.float32)
    else:
        total[...] = jnp.zeros(total.shape, jnp.float32)
    tiles[...] = jnp.zeros(tiles.shape, tiles.dtype)
    for way in range(flight):
        codes[filled + way] = rows * 64 + count

    size = tiles.shape[1]

    def multiply(code, tile):
        row = code // 64
        position = code % 64
        total[row] = total[row] + nt(vectors[position], tile[...])

    def evaluate(code, tile):
        row = code // 64
        position = code % 64
        for top in range(0, size, 128):
            distance = nn(near[row, top : top + 128, :], far[position])
            tile[top : top + 128, :] = lax.rsqrt(distance).astype(jnp.bfloat16)

    def step(index, carry):
        for way in range(flight):
            multiply(codes[index * flight + way], tiles.at[way])
            evaluate(codes[(index + 1) * flight + way], tiles.at[way])
        return carry

    steps = (filled - 1) // flight
    lax.fori_loop(0, steps, step, 0)
    for way in range(flight):
        multiply(codes[steps * flight + way], tiles.at[way])

    if scaled:
        for place, out in enumerate(outs):
            out[...] = (total[place * share : (place + 1) * share] * 0.015625).astype(out.dtype)
    else:
        outs[0][...] = total[0:rows]


def join_kernel(points, probe, joined):
    count, columns, size = probe.shape
    joined[:, 0:columns, :] = probe[...]
    vacant = jnp.zeros((joined.shape[1] - columns - 3, size), jnp.float32)
    for cluster in range(count):
        joined[cluster, columns:, :] = jnp.concatenate(
            [points[cluster].astype(jnp.float32), vacant], axis=0
        ).astype(joined.dtype)


def near_field(tiers, share, columns, nb, points, probe, halo, start, scaled):
    count, size = points.shape[0], points.shape[2]
    rows = len(tiers) * share
    operands = [nb, points]
    if probe is not None:
        operands.append(probe)
    if halo is not None:
        operands.extend(halo)
    if start is not None:
        operands.append(start)
    if scaled:
        outs = [jax.ShapeDtypeStruct((share, columns, size), jnp.bfloat16)] * len(tiers)
    else:
        outs = [jax.ShapeDtypeStruct((rows, columns, size), jnp.float32)]
    body = functools.partial(
        near_kernel, tiers, share, count, start is not None, halo is not None, probe is not None, scaled
    )
    blocks = rows * 6
    return pl.pallas_call(
        lambda *refs: body(refs),
        out_shape=outs,
        in_specs=[pl.BlockSpec(memory_space=SMEM)]
        + [pl.BlockSpec(memory_space=VMEM)] * (len(operands) - 1),
        out_specs=[pl.BlockSpec(memory_space=VMEM)] * len(outs),
        scratch_shapes=[
            pltpu.VMEM((3 * count, 128, size), jnp.bfloat16),
            pltpu.VMEM((3 * count, columns, size), jnp.bfloat16),
            pltpu.VMEM((rows + 1, size, 128), jnp.bfloat16),
            pltpu.VMEM((rows + 1, columns, size), jnp.float32),
            pltpu.VMEM((FLIGHT, size, size), jnp.bfloat16),
            pltpu.SMEM((rows * nb.shape[1] + 2 * FLIGHT,), jnp.int32),
        ],
        compiler_params=pltpu.CompilerParams(vmem_limit_bytes=VMEM_BYTES),
        cost_estimate=pl.CostEstimate(
            flops=blocks * size * size * (2 * columns + 10),
            bytes_accessed=8 * rows * columns * size,
            transcendentals=blocks * size * size,
        ),
    )(*operands)


def pivot_factor(pivots, inverse, width):
    chosen = (
        lax.broadcasted_iota(jnp.int32, (width, pivots.shape[1]), 0) == pivots
    ).astype(jnp.bfloat16)
    return nt(stacked_split(jnp.transpose(inverse)), chosen).astype(jnp.bfloat16)


def leaf_node(sketch, pivots, inverse):
    factor = pivot_factor(pivots, inverse, sketch.shape[1])
    wide = sketch.astype(jnp.float32)
    mean_sq = jnp.sum(wide * wide, keepdims=True) / (sketch.shape[0] * sketch.shape[1]) + EPSILON
    scale = 1.0 / (sketch.shape[0] * mean_sq)
    picked = halves(nt(factor, sketch))
    raw = halves(nn(stacked_split(picked), sketch))
    interp = raw * scale
    upward = halves(nt(stacked_split(raw), sketch)) * (scale * lax.rsqrt(mean_sq))
    return interp, upward


def tree_node(sketch, pivots, inverse):
    width, columns = sketch.shape
    factor = pivot_factor(pivots, inverse, width)
    mean_sq = jnp.sum(sketch * sketch, keepdims=True) / (width * columns) + EPSILON
    scale = 1.0 / (columns * mean_sq)
    parts = stacked_split(sketch)
    picked = halves(nn(jnp.concatenate([factor, factor], axis=1), parts))
    raw = halves(nt(stacked_split(picked), parts))
    raw = raw[:, :width] + raw[:, width:]
    interp = raw * scale
    both = stacked_split(raw)
    upward = halves(nn(jnp.concatenate([both, both], axis=1), parts)) * (scale * lax.rsqrt(mean_sq))
    return interp, upward


def device_kernel(
    share,
    group,
    rank,
    own,
    *refs,
):
    parts = group // share
    arrived = refs[: parts - 1]
    pivots, inverse, local_pivots, local_inverse, pack, up_out, sketch, ups = refs[parts - 1 :]
    me = lax.axis_index("vec")
    columns = own.shape[1]
    size = own.shape[2]
    for tier, piece in enumerate((own,) + tuple(arrived)):
        place = pl.ds(pl.multiple_of((me ^ tier) * columns, columns), columns)
        for cluster in range(share):
            sketch[cluster, place, :] = piece[cluster]
    for cluster in range(share):
        row = me * share + cluster
        interp, upward = leaf_node(sketch[cluster], pivots[pl.ds(row, 1), :], inverse[row])
        pack[cluster * rank : (cluster + 1) * rank, :] = interp
        ups[cluster * rank : (cluster + 1) * rank, :] = upward
    level_first, nodes, packed = 0, share // 2, 0
    level_nodes = group // 2
    while nodes >= 1:
        results = []
        for node in range(nodes):
            row = level_first + me * nodes + node
            interp, upward = tree_node(
                ups[2 * node * rank : 2 * (node + 1) * rank, :],
                local_pivots[pl.ds(row, 1), :],
                local_inverse[row],
            )
            top = (share + packed // 2) * rank
            side = (packed % 2) * 2 * rank
            pack[top : top + rank, side : side + 2 * rank] = interp
            results.append(upward)
            packed += 1
        for node, upward in enumerate(results):
            ups[node * rank : (node + 1) * rank, :] = upward
        level_first += level_nodes
        level_nodes //= 2
        nodes //= 2
    up_out[...] = ups[0:rank, :]


def group_kernel(share, group, rank, own, *refs):
    parts = group // share
    arrived = refs[: parts - 1]
    local_pivots, local_inverse, interps, up_out, ups = refs[parts - 1 :]
    me = lax.axis_index("vec")
    for tier, piece in enumerate((own,) + tuple(arrived)):
        ups[pl.ds(pl.multiple_of((me ^ tier) * rank, rank), rank), :] = piece[...]
    row = group - parts
    done = 0
    nodes = parts // 2
    while nodes >= 1:
        results = []
        for node in range(nodes):
            interp, upward = tree_node(
                ups[2 * node * rank : 2 * (node + 1) * rank, :],
                local_pivots[row : row + 1, :],
                local_inverse[row],
            )
            interps[done] = interp
            results.append(upward)
            row += 1
            done += 1
        for node, upward in enumerate(results):
            ups[node * rank : (node + 1) * rank, :] = upward
        nodes //= 2
    up_out[...] = ups[0:rank, :]


def upper_kernel(tier, heap_first, last, rank, own, arrived, pivots, inverse, *refs):
    refs = list(refs)
    if last:
        earlier = [refs.pop(0) for _ in range(tier)]
        interps, top, ups, turned = refs
    else:
        interp_out, up_out, ups = refs
    me = lax.axis_index("leaf")
    side = (me >> tier) & 1
    ups[pl.ds(pl.multiple_of(side * rank, rank), rank), :] = own[...]
    ups[pl.ds(pl.multiple_of((1 - side) * rank, rank), rank), :] = arrived[...]
    node = heap_first + (me >> (tier + 1))
    interp, upward = tree_node(ups[...], pivots[pl.ds(node, 1), :], inverse[node])
    if last:
        for index, ref in enumerate(earlier):
            interps[index] = ref[...]
        interps[tier] = interp
        turned[...] = jnp.transpose(upward)
        columns = top.shape[0]
        place = lax.axis_index("vec") * columns
        top[...] = turned[pl.ds(pl.multiple_of(place, columns), columns), :]
    else:
        interp_out[...] = interp
        up_out[...] = upward


def place_kernel(share, group, rank, own, *refs):
    parts = group // share
    arrived = refs[: parts - 1]
    joined, leaf_out, local_out = refs[parts - 1 :]
    me = lax.axis_index("vec")
    for tier, piece in enumerate((own,) + tuple(arrived)):
        device = me ^ tier
        for cluster in range(share):
            leaf_out[device * share + cluster] = piece[cluster * rank : (cluster + 1) * rank, :]
        level_first, nodes, packed = 0, share // 2, 0
        level_nodes = group // 2
        while nodes >= 1:
            for node in range(nodes):
                top = (share + packed // 2) * rank
                side = (packed % 2) * 2 * rank
                local_out[level_first + device * nodes + node] = piece[
                    top : top + rank, side : side + 2 * rank
                ]
                packed += 1
            level_first += level_nodes
            level_nodes //= 2
            nodes //= 2
    for index in range(parts - 1):
        local_out[group - parts + index] = joined[index]


def call(body, outs, scratch, operands, flops=0):
    return pl.pallas_call(
        body,
        out_shape=outs,
        in_specs=[pl.BlockSpec(memory_space=VMEM)] * len(operands),
        out_specs=jax.tree.map(lambda _: pl.BlockSpec(memory_space=VMEM), outs),
        scratch_shapes=scratch,
        compiler_params=pltpu.CompilerParams(vmem_limit_bytes=VMEM_BYTES),
        cost_estimate=pl.CostEstimate(
            flops=flops, bytes_accessed=sum(o.size * o.dtype.itemsize for o in operands), transcendentals=0
        ),
    )(*operands)


def f32(*shape):
    return jax.ShapeDtypeStruct(shape, jnp.float32)


def on_device(
    points,
    probe_vectors,
    neighbours,
    leaf_pivots,
    leaf_inverse,
    local_pivots,
    local_inverse,
    upper_pivots,
    upper_inverse,
):
    group, columns, size = probe_vectors.shape
    rank = leaf_pivots.shape[1]
    leaf_total = lax.axis_size("leaf")
    parts = lax.axis_size("vec")
    share = group // parts
    total_columns = columns * parts

    up = [(i, i + 1) for i in range(leaf_total - 1)]
    down = [(j, i) for i, j in up]
    joined = call(
        join_kernel,
        jax.ShapeDtypeStruct((group, columns + 16, size), jnp.bfloat16),
        [],
        [points, probe_vectors],
    )
    halo = (lax.ppermute(joined, "leaf", up), lax.ppermute(joined, "leaf", down))

    def vec_send(array, tier):
        return lax.ppermute(array, "vec", [(i, i ^ tier) for i in range(parts)])

    away = list(range(parts - 1, 0, -1))
    started = near_field(away, share, columns, neighbours, points, probe_vectors, None, None, False)[0]
    sent = near_field(away, share, columns, neighbours, points, None, halo, started, True)
    arrived = {tier: vec_send(array, tier) for tier, array in zip(away, sent)}
    kept = near_field([0], share, columns, neighbours, points, probe_vectors, halo, None, True)[0]

    pack_rows = share * rank + (share // 2) * rank
    pack, own_up = call(
        functools.partial(device_kernel, share, group, rank),
        (f32(pack_rows, size), f32(rank, total_columns)),
        [
            pltpu.VMEM((share, total_columns, size), jnp.bfloat16),
            pltpu.VMEM((share * rank, total_columns), jnp.float32),
        ],
        [kept]
        + [arrived[tier] for tier in range(1, parts)]
        + [leaf_pivots, leaf_inverse, local_pivots, local_inverse],
    )
    joined, own_up = call(
        functools.partial(group_kernel, share, group, rank),
        (f32(parts - 1, rank, 2 * rank), f32(rank, total_columns)),
        [pltpu.VMEM((parts * rank, total_columns), jnp.float32)],
        [own_up]
        + [vec_send(own_up, tier) for tier in range(1, parts)]
        + [local_pivots, local_inverse],
    )
    pack, own_up = lax.optimization_barrier((pack, own_up))
    others = [vec_send(pack, tier) for tier in range(1, parts)]

    heap_first = 0
    maps = []
    for tier in range(UPL):
        last = tier == UPL - 1
        partner = lax.ppermute(own_up, "leaf", [(i, i ^ (1 << tier)) for i in range(leaf_total)])
        outs = (f32(rank, 2 * rank), f32(rank, total_columns))
        scratch = [pltpu.VMEM((2 * rank, total_columns), jnp.float32)]
        operands = [own_up, partner, upper_pivots, upper_inverse]
        if last:
            outs = (f32(UPL, rank, 2 * rank), f32(columns, rank))
            scratch.append(pltpu.VMEM((total_columns, rank), jnp.float32))
            operands += maps
        first, own_up = call(
            functools.partial(upper_kernel, tier, heap_first, last, rank), outs, scratch, operands
        )
        maps.append(first)
        heap_first += leaf_total >> (tier + 1)
    leaf_map, local_map = call(
        functools.partial(place_kernel, share, group, rank),
        (f32(group, rank, size), f32(group - 1, rank, 2 * rank)),
        [],
        [pack] + others + [joined],
    )
    return (
        jnp.swapaxes(leaf_map, 1, 2),
        jnp.swapaxes(local_map, 1, 2),
        jnp.swapaxes(first, 1, 2)[None],
        own_up[None],
    )


def solution(mesh):
    placed = (
        P("leaf", None, None),
        P("leaf", "vec", None),
        P("leaf", None),
        P("leaf", None),
        P("leaf", None, None),
        P("leaf", None),
        P("leaf", None, None),
        P(),
        P(),
    )
    return jax.shard_map(
        on_device,
        mesh=mesh,
        in_specs=placed,
        out_specs=(
            P("leaf", None, None),
            P("leaf", None, None),
            P("leaf", None, None, None),
            P("leaf", "vec", None),
        ),
        check_vma=False,
    )
```

```python
import functools

import jax
import jax.numpy as jnp
from jax import lax
from jax.experimental import pallas as pl
from jax.experimental.pallas import tpu as pltpu
from jax.sharding import PartitionSpec as P

UPL = 3

SOFTEN = 0.0009
EPSILON = 1e-06
FLIGHT = 4
VMEM_BYTES = 48 * 1024 * 1024
VMEM = pltpu.MemorySpace.VMEM
SMEM = pltpu.MemorySpace.SMEM


def nt(a, b):
    return lax.dot_general(a, b, (((1,), (1,)), ((), ())), preferred_element_type=jnp.float32)


def nn(a, b):
    return lax.dot_general(a, b, (((1,), (0,)), ((), ())), preferred_element_type=jnp.float32)


def split(a):
    high = a.astype(jnp.bfloat16)
    low = (a - high.astype(jnp.float32)).astype(jnp.bfloat16)
    return high, low


def stacked_split(a):
    high, low = split(a)
    return jnp.concatenate([high, low], axis=0)


def halves(a):
    rows = a.shape[0] // 2
    return a[:rows] + a[rows:]


def coordinates(points, extra):
    row = lax.broadcasted_iota(jnp.int32, (8, points.shape[1]), 0)
    padded = jnp.concatenate(
        [points, jnp.full((5, points.shape[1]), 0.5, jnp.float32)], axis=0
    )
    centred = padded - 0.5
    high, low = [part.astype(jnp.float32) for part in split(centred)]
    norm = jnp.sum(centred * centred, axis=0, keepdims=True) + extra
    first, rest = [part.astype(jnp.float32) for part in split(norm)]
    second, third = [part.astype(jnp.float32) for part in split(norm - first)]
    norms = jnp.where(row == 0, first, jnp.where(row == 1, second, jnp.where(row == 2, third, 0.0)))
    return high, low, norms, jnp.where(row < 3, 1.0, 0.0)


def near_kernel(tiers, share, count, has_start, halo, own, scaled, refs):
    refs = list(refs)
    nb_ref, points_ref = refs[:2]
    refs = refs[2:]
    probe_ref = refs.pop(0) if own else None
    if halo:
        before, after = refs[:2]
        refs = refs[2:]
    start_ref = refs.pop(0) if has_start else None
    outs = [refs.pop(0)]
    far, vectors, near, total, tiles, codes = refs
    flight = tiles.shape[0]

    me = lax.axis_index("vec")
    first = lax.axis_index("leaf") * count
    slots = nb_ref.shape[1]
    rows = len(tiers) * share

    vacant = jnp.zeros((far.shape[1] - 48, far.shape[2]), far.dtype)
    columns = vectors.shape[1]
    for place, source in enumerate((before, points_ref, after) if halo else (None, points_ref, None)):
        if source is None:
            continue
        for cluster in range(count):
            if place == 1:
                listed_points = source[cluster].astype(jnp.float32)
            else:
                listed_points = source[cluster, columns:, :].astype(jnp.float32)[0:3]
            high, low, norm, one = coordinates(listed_points, SOFTEN)
            far[place * count + cluster, 0:48, :] = jnp.concatenate(
                [-2.0 * high, -2.0 * low, -2.0 * high, -2.0 * low, one, norm], axis=0
            ).astype(far.dtype)
            far[place * count + cluster, 48:, :] = vacant
    if halo:
        vectors[0:count] = before[:, 0:columns, :]
        vectors[2 * count : 3 * count] = after[:, 0:columns, :]
    if own:
        vectors[count : 2 * count] = probe_ref[...]

    for way in range(flight):
        codes[way] = rows * 64 + count
    filled = jnp.int32(flight)
    for place, tier in enumerate(tiers):
        for part in range(share):
            row = place * share + part
            cluster = (me ^ tier) * share + part

            def add_code(slot, filled, row=row, cluster=cluster):
                listed = nb_ref[cluster, slot]
                position = listed - first + count
                inside = (position >= count) & (position < 2 * count)
                if own and halo:
                    wanted = listed >= 0
                elif own:
                    wanted = (listed >= 0) & inside
                else:
                    wanted = (listed >= 0) & jnp.logical_not(inside)
                codes[filled] = row * 64 + jnp.clip(position, 0, 3 * count - 1)
                return filled + wanted.astype(jnp.int32)

            for slot in range(slots):
                filled = add_code(slot, filled)

    for place, tier in enumerate(tiers):
        for part in range(share):
            row = place * share + part
            cluster = (me ^ tier) * share + part
            high, low, norm, one = coordinates(points_ref[cluster].astype(jnp.float32), 0.0)
            vacant = jnp.zeros((near.shape[2] - 48, high.shape[1]), jnp.float32)
            near[row] = jnp.transpose(
                jnp.concatenate([high, high, low, low, norm, one, vacant], axis=0)
            ).astype(near.dtype)
    near[rows] = near[0]
    if has_start:
        total[0:rows] = start_ref[...]
        total[rows] = jnp.zeros(total.shape[1:], jnp.float32)
    else:
        total[...] = jnp.zeros(total.shape, jnp.float32)
    tiles[...] = jnp.zeros(tiles.shape, tiles.dtype)
    for way in range(flight):
        codes[filled + way] = rows * 64 + count

    size = tiles.shape[1]

    def multiply(code, tile):
        row = code // 64
        position = code % 64
        total[row] = total[row] + nt(vectors[position], tile[...])

    def evaluate(code, tile):
        row = code // 64
        position = code % 64
        for top in range(0, size, 128):
            distance = nn(near[row, top : top + 128, :], far[position])
            tile[top : top + 128, :] = lax.rsqrt(distance).astype(jnp.bfloat16)

    def step(index, carry):
        for way in range(flight):
            multiply(codes[index * flight + way], tiles.at[way])
            evaluate(codes[(index + 1) * flight + way], tiles.at[way])
        return carry

    steps = (filled - 1) // flight
    lax.fori_loop(0, steps, step, 0)
    for way in range(flight):
        multiply(codes[steps * flight + way], tiles.at[way])

    out = outs[0]
    if not scaled:
        out[...] = total[0:rows]
    elif len(tiers) == 1:
        out[...] = (total[0:share] * 0.015625).astype(out.dtype)
    else:
        for place, tier in enumerate(tiers):
            part = total[place * share : (place + 1) * share]
            out[me ^ tier] = (part * 0.015625).astype(out.dtype)
        out[me] = jnp.zeros(out.shape[1:], out.dtype)


def join_kernel(points, probe, joined):
    count, columns, size = probe.shape
    joined[:, 0:columns, :] = probe[...]
    vacant = jnp.zeros((joined.shape[1] - columns - 3, size), jnp.float32)
    for cluster in range(count):
        joined[cluster, columns:, :] = jnp.concatenate(
            [points[cluster].astype(jnp.float32), vacant], axis=0
        ).astype(joined.dtype)


def near_field(tiers, share, columns, nb, points, probe, halo, start, scaled):
    count, size = points.shape[0], points.shape[2]
    rows = len(tiers) * share
    operands = [nb, points]
    if probe is not None:
        operands.append(probe)
    if halo is not None:
        operands.extend(halo)
    if start is not None:
        operands.append(start)
    if scaled and len(tiers) > 1:
        outs = [jax.ShapeDtypeStruct((len(tiers) + 1, share, columns, size), jnp.bfloat16)]
    elif scaled:
        outs = [jax.ShapeDtypeStruct((share, columns, size), jnp.bfloat16)]
    else:
        outs = [jax.ShapeDtypeStruct((rows, columns, size), jnp.float32)]
    body = functools.partial(
        near_kernel, tiers, share, count, start is not None, halo is not None, probe is not None, scaled
    )
    blocks = rows * 6
    return pl.pallas_call(
        lambda *refs: body(refs),
        out_shape=outs,
        in_specs=[pl.BlockSpec(memory_space=SMEM)]
        + [pl.BlockSpec(memory_space=VMEM)] * (len(operands) - 1),
        out_specs=[pl.BlockSpec(memory_space=VMEM)] * len(outs),
        scratch_shapes=[
            pltpu.VMEM((3 * count, 128, size), jnp.bfloat16),
            pltpu.VMEM((3 * count, columns, size), jnp.bfloat16),
            pltpu.VMEM((rows + 1, size, 128), jnp.bfloat16),
            pltpu.VMEM((rows + 1, columns, size), jnp.float32),
            pltpu.VMEM((FLIGHT, size, size), jnp.bfloat16),
            pltpu.SMEM((rows * nb.shape[1] + 2 * FLIGHT,), jnp.int32),
        ],
        compiler_params=pltpu.CompilerParams(vmem_limit_bytes=VMEM_BYTES),
        cost_estimate=pl.CostEstimate(
            flops=blocks * size * size * (2 * columns + 10),
            bytes_accessed=8 * rows * columns * size,
            transcendentals=blocks * size * size,
        ),
    )(*operands)


def pivot_factor(pivots, inverse, width):
    chosen = (
        lax.broadcasted_iota(jnp.int32, (width, pivots.shape[1]), 0) == pivots
    ).astype(jnp.bfloat16)
    return nt(stacked_split(jnp.transpose(inverse)), chosen).astype(jnp.bfloat16)


def leaf_node(sketch, pivots, inverse):
    factor = pivot_factor(pivots, inverse, sketch.shape[1])
    wide = sketch.astype(jnp.float32)
    mean_sq = jnp.sum(wide * wide, keepdims=True) / (sketch.shape[0] * sketch.shape[1]) + EPSILON
    scale = 1.0 / (sketch.shape[0] * mean_sq)
    picked = halves(nt(factor, sketch))
    raw = halves(nn(stacked_split(picked), sketch))
    interp = raw * scale
    upward = halves(nt(stacked_split(raw), sketch)) * (scale * lax.rsqrt(mean_sq))
    return interp, upward


def tree_node(sketch, pivots, inverse):
    width, columns = sketch.shape
    factor = pivot_factor(pivots, inverse, width)
    mean_sq = jnp.sum(sketch * sketch, keepdims=True) / (width * columns) + EPSILON
    scale = 1.0 / (columns * mean_sq)
    parts = stacked_split(sketch)
    picked = halves(nn(jnp.concatenate([factor, factor], axis=1), parts))
    raw = halves(nt(stacked_split(picked), parts))
    raw = raw[:, :width] + raw[:, width:]
    interp = raw * scale
    both = stacked_split(raw)
    upward = halves(nn(jnp.concatenate([both, both], axis=1), parts)) * (scale * lax.rsqrt(mean_sq))
    return interp, upward


def device_kernel(
    share,
    group,
    rank,
    own,
    arrived,
    pivots,
    inverse,
    local_pivots,
    local_inverse,
    pack,
    up_out,
    sketch,
    ups,
):
    parts = group // share
    me = lax.axis_index("vec")
    columns = own.shape[1]
    size = own.shape[2]
    place = pl.ds(pl.multiple_of(me * columns, columns), columns)
    for cluster in range(share):
        for part in range(parts):
            sketch[cluster, part * columns : (part + 1) * columns, :] = arrived[part, cluster]
        sketch[cluster, place, :] = own[cluster]
    for cluster in range(share):
        row = me * share + cluster
        interp, upward = leaf_node(sketch[cluster], pivots[pl.ds(row, 1), :], inverse[row])
        pack[cluster * rank : (cluster + 1) * rank, :] = interp
        ups[cluster * rank : (cluster + 1) * rank, :] = upward
    level_first, nodes, packed = 0, share // 2, 0
    level_nodes = group // 2
    while nodes >= 1:
        results = []
        for node in range(nodes):
            row = level_first + me * nodes + node
            interp, upward = tree_node(
                ups[2 * node * rank : 2 * (node + 1) * rank, :],
                local_pivots[pl.ds(row, 1), :],
                local_inverse[row],
            )
            top = (share + packed // 2) * rank
            side = (packed % 2) * 2 * rank
            pack[top : top + rank, side : side + 2 * rank] = interp
            results.append(upward)
            packed += 1
        for node, upward in enumerate(results):
            ups[node * rank : (node + 1) * rank, :] = upward
        level_first += level_nodes
        level_nodes //= 2
        nodes //= 2
    for part in range(parts):
        up_out[part] = ups[0:rank, :]


def group_kernel(share, group, rank, arrived, local_pivots, local_inverse, interps, up_out, ups):
    parts = group // share
    for part in range(parts):
        ups[part * rank : (part + 1) * rank, :] = arrived[part]
    row = group - parts
    done = 0
    nodes = parts // 2
    while nodes >= 1:
        results = []
        for node in range(nodes):
            interp, upward = tree_node(
                ups[2 * node * rank : 2 * (node + 1) * rank, :],
                local_pivots[row : row + 1, :],
                local_inverse[row],
            )
            interps[done] = interp
            results.append(upward)
            row += 1
            done += 1
        for node, upward in enumerate(results):
            ups[node * rank : (node + 1) * rank, :] = upward
        nodes //= 2
    up_out[...] = ups[0:rank, :]


def upper_kernel(tier, heap_first, last, rank, own, arrived, pivots, inverse, *refs):
    refs = list(refs)
    if last:
        earlier = [refs.pop(0) for _ in range(tier)]
        interps, top, ups, turned = refs
    else:
        interp_out, up_out, ups = refs
    me = lax.axis_index("leaf")
    side = (me >> tier) & 1
    ups[pl.ds(pl.multiple_of(side * rank, rank), rank), :] = own[...]
    ups[pl.ds(pl.multiple_of((1 - side) * rank, rank), rank), :] = arrived[...]
    node = heap_first + (me >> (tier + 1))
    interp, upward = tree_node(ups[...], pivots[pl.ds(node, 1), :], inverse[node])
    if last:
        for index, ref in enumerate(earlier):
            interps[index] = ref[...]
        interps[tier] = interp
        turned[...] = jnp.transpose(upward)
        columns = top.shape[0]
        place = lax.axis_index("vec") * columns
        top[...] = turned[pl.ds(pl.multiple_of(place, columns), columns), :]
    else:
        interp_out[...] = interp
        up_out[...] = upward


def place_kernel(share, group, rank, own, *refs):
    parts = group // share
    arrived = refs[: parts - 1]
    joined, leaf_out, local_out = refs[parts - 1 :]
    me = lax.axis_index("vec")
    for tier, piece in enumerate((own,) + tuple(arrived)):
        device = me ^ tier
        for cluster in range(share):
            leaf_out[device * share + cluster] = piece[cluster * rank : (cluster + 1) * rank, :]
        level_first, nodes, packed = 0, share // 2, 0
        level_nodes = group // 2
        while nodes >= 1:
            for node in range(nodes):
                top = (share + packed // 2) * rank
                side = (packed % 2) * 2 * rank
                local_out[level_first + device * nodes + node] = piece[
                    top : top + rank, side : side + 2 * rank
                ]
                packed += 1
            level_first += level_nodes
            level_nodes //= 2
            nodes //= 2
    for index in range(parts - 1):
        local_out[group - parts + index] = joined[index]


def call(body, outs, scratch, operands, flops=0):
    return pl.pallas_call(
        body,
        out_shape=outs,
        in_specs=[pl.BlockSpec(memory_space=VMEM)] * len(operands),
        out_specs=jax.tree.map(lambda _: pl.BlockSpec(memory_space=VMEM), outs),
        scratch_shapes=scratch,
        compiler_params=pltpu.CompilerParams(vmem_limit_bytes=VMEM_BYTES),
        cost_estimate=pl.CostEstimate(
            flops=flops, bytes_accessed=sum(o.size * o.dtype.itemsize for o in operands), transcendentals=0
        ),
    )(*operands)


def f32(*shape):
    return jax.ShapeDtypeStruct(shape, jnp.float32)


def on_device(
    points,
    probe_vectors,
    neighbours,
    leaf_pivots,
    leaf_inverse,
    local_pivots,
    local_inverse,
    upper_pivots,
    upper_inverse,
):
    group, columns, size = probe_vectors.shape
    rank = leaf_pivots.shape[1]
    leaf_total = lax.axis_size("leaf")
    parts = lax.axis_size("vec")
    share = group // parts
    total_columns = columns * parts

    up = [(i, i + 1) for i in range(leaf_total - 1)]
    down = [(j, i) for i, j in up]
    joined = call(
        join_kernel,
        jax.ShapeDtypeStruct((group, columns + 16, size), jnp.bfloat16),
        [],
        [points, probe_vectors],
    )
    halo = (lax.ppermute(joined, "leaf", up), lax.ppermute(joined, "leaf", down))

    def vec_send(array, tier):
        return lax.ppermute(array, "vec", [(i, i ^ tier) for i in range(parts)])

    def vec_swap(array):
        return lax.all_to_all(array, "vec", 0, 0, tiled=True)

    away = list(range(parts - 1, 0, -1))
    started = near_field(away, share, columns, neighbours, points, probe_vectors, None, None, False)[0]
    sent = near_field(away, share, columns, neighbours, points, None, halo, started, True)[0]
    arrived = vec_swap(sent)
    kept = near_field([0], share, columns, neighbours, points, probe_vectors, halo, None, True)[0]

    pack_rows = share * rank + (share // 2) * rank
    pack, own_up = call(
        functools.partial(device_kernel, share, group, rank),
        (f32(pack_rows, size), f32(parts, rank, total_columns)),
        [
            pltpu.VMEM((share, total_columns, size), jnp.bfloat16),
            pltpu.VMEM((share * rank, total_columns), jnp.float32),
        ],
        [kept, arrived, leaf_pivots, leaf_inverse, local_pivots, local_inverse],
    )
    joined, own_up = call(
        functools.partial(group_kernel, share, group, rank),
        (f32(parts - 1, rank, 2 * rank), f32(rank, total_columns)),
        [pltpu.VMEM((parts * rank, total_columns), jnp.float32)],
        [vec_swap(own_up), local_pivots, local_inverse],
    )
    pack, own_up = lax.optimization_barrier((pack, own_up))
    others = [vec_send(pack, tier) for tier in range(1, parts)]

    heap_first = 0
    maps = []
    for tier in range(UPL):
        last = tier == UPL - 1
        partner = lax.ppermute(own_up, "leaf", [(i, i ^ (1 << tier)) for i in range(leaf_total)])
        outs = (f32(rank, 2 * rank), f32(rank, total_columns))
        scratch = [pltpu.VMEM((2 * rank, total_columns), jnp.float32)]
        operands = [own_up, partner, upper_pivots, upper_inverse]
        if last:
            outs = (f32(UPL, rank, 2 * rank), f32(columns, rank))
            scratch.append(pltpu.VMEM((total_columns, rank), jnp.float32))
            operands += maps
        first, own_up = call(
            functools.partial(upper_kernel, tier, heap_first, last, rank), outs, scratch, operands
        )
        maps.append(first)
        heap_first += leaf_total >> (tier + 1)
    leaf_map, local_map = call(
        functools.partial(place_kernel, share, group, rank),
        (f32(group, rank, size), f32(group - 1, rank, 2 * rank)),
        [],
        [pack] + others + [joined],
    )
    return (
        jnp.swapaxes(leaf_map, 1, 2),
        jnp.swapaxes(local_map, 1, 2),
        jnp.swapaxes(first, 1, 2)[None],
        own_up[None],
    )


def solution(mesh):
    placed = (
        P("leaf", None, None),
        P("leaf", "vec", None),
        P("leaf", None),
        P("leaf", None),
        P("leaf", None, None),
        P("leaf", None),
        P("leaf", None, None),
        P(),
        P(),
    )
    return jax.shard_map(
        on_device,
        mesh=mesh,
        in_specs=placed,
        out_specs=(
            P("leaf", None, None),
            P("leaf", None, None),
            P("leaf", None, None, None),
            P("leaf", "vec", None),
        ),
        check_vma=False,
    )
```

```python
import functools

import jax
import jax.numpy as jnp
from jax import lax
from jax.experimental import pallas as pl
from jax.experimental.pallas import tpu as pltpu
from jax.sharding import PartitionSpec as P

UPL = 3

SOFTEN = 0.0009
EPSILON = 1e-06
FLIGHT = 4
DEPTH = 128
VMEM_BYTES = 20 * 1024 * 1024
VMEM = pltpu.MemorySpace.VMEM
SMEM = pltpu.MemorySpace.SMEM


def nt(a, b):
    return lax.dot_general(a, b, (((1,), (1,)), ((), ())), preferred_element_type=jnp.float32)


def nn(a, b):
    return lax.dot_general(a, b, (((1,), (0,)), ((), ())), preferred_element_type=jnp.float32)


def split(a):
    high = a.astype(jnp.bfloat16)
    low = (a - high.astype(jnp.float32)).astype(jnp.bfloat16)
    return high, low


def stacked_split(a):
    high, low = split(a)
    return jnp.concatenate([high, low], axis=0)


def halves(a):
    rows = a.shape[0] // 2
    return a[:rows] + a[rows:]


def coordinates(points, extra):
    row = lax.broadcasted_iota(jnp.int32, (8, points.shape[1]), 0)
    padded = jnp.concatenate(
        [points, jnp.full((5, points.shape[1]), 0.5, jnp.float32)], axis=0
    )
    centred = padded - 0.5
    high, low = [part.astype(jnp.float32) for part in split(centred)]
    norm = jnp.sum(centred * centred, axis=0, keepdims=True) + extra
    first, rest = [part.astype(jnp.float32) for part in split(norm)]
    second, third = [part.astype(jnp.float32) for part in split(norm - first)]
    norms = jnp.where(row == 0, first, jnp.where(row == 1, second, jnp.where(row == 2, third, 0.0)))
    return high, low, norms, jnp.where(row < 3, 1.0, 0.0)


def far_features(points):
    high, low, norm, one = coordinates(points, SOFTEN)
    vacant = jnp.zeros((DEPTH - 48, points.shape[1]), jnp.float32)
    return jnp.concatenate(
        [-2.0 * high, -2.0 * low, -2.0 * high, -2.0 * low, one, norm, vacant], axis=0
    ).astype(jnp.bfloat16)


def near_features(points):
    high, low, norm, one = coordinates(points, 0.0)
    vacant = jnp.zeros((DEPTH - 48, points.shape[1]), jnp.float32)
    return jnp.transpose(
        jnp.concatenate([high, high, low, low, norm, one, vacant], axis=0)
    ).astype(jnp.bfloat16)


def add_blocks(share, tiers, base, wanted, nb_ref, far, vectors, near, total, tiles, codes):
    me = lax.axis_index("vec")
    count, slots = nb_ref.shape
    first = lax.axis_index("leaf") * count
    flight, size = tiles.shape[0], tiles.shape[1]
    idle = count * 64

    for way in range(flight):
        codes[way] = idle
    filled = jnp.int32(flight)
    for tier in tiers:
        for part in range(share):
            cluster = (me ^ tier) * share + part
            for slot in range(slots):
                listed = nb_ref[cluster, slot]
                position = listed - first + count
                codes[filled] = cluster * 64 + position - base
                filled += ((listed >= 0) & wanted(position, count)).astype(jnp.int32)
    for way in range(flight):
        codes[filled + way] = idle
    tiles[...] = jnp.zeros(tiles.shape, tiles.dtype)

    def multiply(code, tile):
        row = code // 64
        total[row] = total[row] + nt(vectors[code % 64], tile[...])

    def evaluate(code, tile):
        row = code // 64
        position = code % 64
        for top in range(0, size, 128):
            distance = nn(near[row, top : top + 128, :], far[position])
            tile[top : top + 128, :] = lax.rsqrt(distance).astype(jnp.bfloat16)

    def step(index, carry):
        for way in range(flight):
            multiply(codes[index * flight + way], tiles.at[way])
            evaluate(codes[(index + 1) * flight + way], tiles.at[way])
        return carry

    steps = (filled - 1) // flight
    lax.fori_loop(0, steps, step, 0)
    for way in range(flight):
        multiply(codes[steps * flight + way], tiles.at[way])


def inside(position, count):
    return (position >= count) & (position < 2 * count)


def outside(position, count):
    return (position < count) | (position >= 2 * count)


def anywhere(position, count):
    return position >= 0


def own_kernel(share, tiers, nb_ref, points, probe, total, far, near, tiles, codes):
    count = points.shape[0]
    for cluster in range(count):
        here = points[cluster].astype(jnp.float32)
        far[cluster] = far_features(here)
        near[cluster] = near_features(here)
    near[count] = near[0]
    total[...] = jnp.zeros(total.shape, total.dtype)
    add_blocks(share, tiers, count, inside, nb_ref, far, probe, near, total, tiles, codes)


def halo_kernel(share, tiers, nb_ref, probe, before, after, own_far, near, start, *refs):
    outs = refs[: len(tiers)]
    far, vectors, total, tiles, codes = refs[len(tiers) :]
    count, columns, _ = probe.shape
    me = lax.axis_index("vec")
    for place, source in ((0, before), (2, after)):
        for cluster in range(count):
            far[place * count + cluster] = far_features(
                source[cluster, columns:, :].astype(jnp.float32)[0:3]
            )
        vectors[place * count : (place + 1) * count] = source[:, 0:columns, :]
    far[count : 2 * count] = own_far[...]
    vectors[count : 2 * count] = probe[...]
    total[...] = start[...]
    add_blocks(share, tiers, 0, outside, nb_ref, far, vectors, near, total, tiles, codes)
    for tier, out in zip(tiers, outs):
        part = total[pl.ds((me ^ tier) * share, share)]
        out[...] = (part * 0.015625).astype(out.dtype)


def kept_kernel(share, nb_ref, far, vectors, near, out, total, tiles, codes):
    mine = pl.ds(lax.axis_index("vec") * share, share)
    total[mine] = jnp.zeros((share,) + total.shape[1:], total.dtype)
    add_blocks(share, (0,), 0, anywhere, nb_ref, far, vectors, near, total, tiles, codes)
    out[...] = (total[mine] * 0.015625).astype(out.dtype)


def join_kernel(points, probe, joined):
    count, columns, size = probe.shape
    joined[:, 0:columns, :] = probe[...]
    vacant = jnp.zeros((joined.shape[1] - columns - 3, size), jnp.float32)
    for cluster in range(count):
        joined[cluster, columns:, :] = jnp.concatenate(
            [points[cluster].astype(jnp.float32), vacant], axis=0
        ).astype(joined.dtype)


def near_call(body, outs, scratch, operands, rows, per_row):
    nb, size = operands[0], outs[0].shape[-1]
    blocks = rows * per_row
    return pl.pallas_call(
        body,
        out_shape=outs,
        in_specs=[pl.BlockSpec(memory_space=SMEM)]
        + [pl.BlockSpec(memory_space=VMEM)] * (len(operands) - 1),
        out_specs=[pl.BlockSpec(memory_space=VMEM)] * len(outs),
        scratch_shapes=scratch
        + [
            pltpu.VMEM((FLIGHT, size, size), jnp.bfloat16),
            pltpu.SMEM((rows * nb.shape[1] + 2 * FLIGHT,), jnp.int32),
        ],
        compiler_params=pltpu.CompilerParams(vmem_limit_bytes=VMEM_BYTES),
        cost_estimate=pl.CostEstimate(
            flops=blocks * size * size * 256,
            bytes_accessed=sum(o.size * o.dtype.itemsize for o in operands),
            transcendentals=blocks * size * size,
        ),
    )(*operands)


def pivot_factor(pivots, inverse, width):
    chosen = (
        lax.broadcasted_iota(jnp.int32, (width, pivots.shape[1]), 0) == pivots
    ).astype(jnp.bfloat16)
    return nt(stacked_split(jnp.transpose(inverse)), chosen).astype(jnp.bfloat16)


def leaf_node(sketch, pivots, inverse):
    factor = pivot_factor(pivots, inverse, sketch.shape[1])
    wide = sketch.astype(jnp.float32)
    mean_sq = jnp.sum(wide * wide, keepdims=True) / (sketch.shape[0] * sketch.shape[1]) + EPSILON
    scale = 1.0 / (sketch.shape[0] * mean_sq)
    picked = halves(nt(factor, sketch))
    raw = halves(nn(stacked_split(picked), sketch))
    interp = raw * scale
    upward = halves(nt(stacked_split(raw), sketch)) * (scale * lax.rsqrt(mean_sq))
    return interp, upward


def tree_node(sketch, pivots, inverse):
    width, columns = sketch.shape
    factor = pivot_factor(pivots, inverse, width)
    mean_sq = jnp.sum(sketch * sketch, keepdims=True) / (width * columns) + EPSILON
    scale = 1.0 / (columns * mean_sq)
    parts = stacked_split(sketch)
    picked = halves(nn(jnp.concatenate([factor, factor], axis=1), parts))
    raw = halves(nt(stacked_split(picked), parts))
    raw = raw[:, :width] + raw[:, width:]
    interp = raw * scale
    both = stacked_split(raw)
    upward = halves(nn(jnp.concatenate([both, both], axis=1), parts)) * (scale * lax.rsqrt(mean_sq))
    return interp, upward


def device_kernel(
    share,
    group,
    rank,
    own,
    *refs,
):
    parts = group // share
    arrived = refs[: parts - 1]
    pivots, inverse, local_pivots, local_inverse, pack, up_out, sketch, ups = refs[parts - 1 :]
    me = lax.axis_index("vec")
    columns = own.shape[1]
    size = own.shape[2]
    for tier, piece in enumerate((own,) + tuple(arrived)):
        place = pl.ds(pl.multiple_of((me ^ tier) * columns, columns), columns)
        for cluster in range(share):
            sketch[cluster, place, :] = piece[cluster]
    for cluster in range(share):
        row = me * share + cluster
        interp, upward = leaf_node(sketch[cluster], pivots[pl.ds(row, 1), :], inverse[row])
        pack[cluster * rank : (cluster + 1) * rank, :] = interp
        ups[cluster * rank : (cluster + 1) * rank, :] = upward
    level_first, nodes, packed = 0, share // 2, 0
    level_nodes = group // 2
    while nodes >= 1:
        results = []
        for node in range(nodes):
            row = level_first + me * nodes + node
            interp, upward = tree_node(
                ups[2 * node * rank : 2 * (node + 1) * rank, :],
                local_pivots[pl.ds(row, 1), :],
                local_inverse[row],
            )
            top = (share + packed // 2) * rank
            side = (packed % 2) * 2 * rank
            pack[top : top + rank, side : side + 2 * rank] = interp
            results.append(upward)
            packed += 1
        for node, upward in enumerate(results):
            ups[node * rank : (node + 1) * rank, :] = upward
        level_first += level_nodes
        level_nodes //= 2
        nodes //= 2
    for slab in range(up_out.shape[0]):
        width = up_out.shape[2]
        up_out[slab] = ups[0:rank, slab * width : (slab + 1) * width]


def join_rows(bit, parts, group):
    def below(level, node):
        if level < 0:
            return []
        inner = below(level - 1, 2 * node) + below(level - 1, 2 * node + 1)
        return inner + [group - (parts >> level) + node]

    return below(bit, 0)


def pair_kernel(bit, parts, group, rank, slabs, own, arrived, pivots, inverse, *refs):
    *outs, ups = refs
    interps = outs[0]
    held, width = own.shape[0] - slabs, own.shape[2]
    ahead = slabs if len(outs) == 1 else 0
    me = lax.axis_index("vec")
    side = (me >> bit) & 1
    for piece, half in ((own, side), (arrived, 1 - side)):
        place = pl.ds(pl.multiple_of(half * rank, rank), rank)
        for slab in range(slabs):
            ups[place, slab * width : (slab + 1) * width] = piece[slab]
        for index in range(held):
            interps[ahead + half * held + index] = piece[slabs + index]
    row = group - (parts >> bit) + (me >> (bit + 1))
    interp, upward = tree_node(ups[...], pivots[pl.ds(row, 1), :], inverse[row])
    interps[ahead + 2 * held] = interp
    if len(outs) == 1:
        for slab in range(slabs):
            interps[slab] = upward[:, slab * width : (slab + 1) * width]
    else:
        outs[1][...] = upward


def upper_kernel(tier, heap_first, last, rank, own, arrived, pivots, inverse, *refs):
    refs = list(refs)
    if last:
        earlier = [refs.pop(0) for _ in range(tier)]
        interps, top, ups, turned = refs
    else:
        interp_out, up_out, ups = refs
    me = lax.axis_index("leaf")
    side = (me >> tier) & 1
    ups[pl.ds(pl.multiple_of(side * rank, rank), rank), :] = own[...]
    ups[pl.ds(pl.multiple_of((1 - side) * rank, rank), rank), :] = arrived[...]
    node = heap_first + (me >> (tier + 1))
    interp, upward = tree_node(ups[...], pivots[pl.ds(node, 1), :], inverse[node])
    if last:
        for index, ref in enumerate(earlier):
            interps[index] = ref[...]
        interps[tier] = interp
        turned[...] = jnp.transpose(upward)
        columns = top.shape[0]
        place = lax.axis_index("vec") * columns
        top[...] = turned[pl.ds(pl.multiple_of(place, columns), columns), :]
    else:
        interp_out[...] = interp
        up_out[...] = upward


def place_kernel(share, group, rank, own, *refs):
    parts = group // share
    arrived = refs[: parts - 1]
    joined, leaf_out, local_out = refs[parts - 1 :]
    me = lax.axis_index("vec")
    for tier, piece in enumerate((own,) + tuple(arrived)):
        device = me ^ tier
        for cluster in range(share):
            leaf_out[device * share + cluster] = piece[cluster * rank : (cluster + 1) * rank, :]
        level_first, nodes, packed = 0, share // 2, 0
        level_nodes = group // 2
        while nodes >= 1:
            for node in range(nodes):
                top = (share + packed // 2) * rank
                side = (packed % 2) * 2 * rank
                local_out[level_first + device * nodes + node] = piece[
                    top : top + rank, side : side + 2 * rank
                ]
                packed += 1
            level_first += level_nodes
            level_nodes //= 2
            nodes //= 2
    for index, row in enumerate(join_rows(parts.bit_length() - 2, parts, group)):
        local_out[row] = joined[index]


def call(body, outs, scratch, operands, flops=0):
    return pl.pallas_call(
        body,
        out_shape=outs,
        in_specs=[pl.BlockSpec(memory_space=VMEM)] * len(operands),
        out_specs=jax.tree.map(lambda _: pl.BlockSpec(memory_space=VMEM), outs),
        scratch_shapes=scratch,
        compiler_params=pltpu.CompilerParams(vmem_limit_bytes=VMEM_BYTES),
        cost_estimate=pl.CostEstimate(
            flops=flops, bytes_accessed=sum(o.size * o.dtype.itemsize for o in operands), transcendentals=0
        ),
    )(*operands)


def f32(*shape):
    return jax.ShapeDtypeStruct(shape, jnp.float32)


def on_device(
    points,
    probe_vectors,
    neighbours,
    leaf_pivots,
    leaf_inverse,
    local_pivots,
    local_inverse,
    upper_pivots,
    upper_inverse,
):
    group, columns, size = probe_vectors.shape
    rank = leaf_pivots.shape[1]
    leaf_total = lax.axis_size("leaf")
    parts = lax.axis_size("vec")
    share = group // parts
    total_columns = columns * parts

    up = [(i, i + 1) for i in range(leaf_total - 1)]
    down = [(j, i) for i, j in up]
    joined = call(
        join_kernel,
        jax.ShapeDtypeStruct((group, columns + 16, size), jnp.bfloat16),
        [],
        [points, probe_vectors],
    )
    halo = (lax.ppermute(joined, "leaf", up), lax.ppermute(joined, "leaf", down))

    def vec_send(array, tier):
        return lax.ppermute(array, "vec", [(i, i ^ tier) for i in range(parts)])

    away = list(range(parts - 1, 0, -1))
    sent_rows = (parts - 1) * share

    def bf16(*shape):
        return jax.ShapeDtypeStruct(shape, jnp.bfloat16)

    started, own_far, near = near_call(
        functools.partial(own_kernel, share, away),
        [f32(group + 1, columns, size), bf16(group, DEPTH, size), bf16(group + 1, size, DEPTH)],
        [],
        [neighbours, points, probe_vectors],
        sent_rows,
        6,
    )
    *sent, far, vectors = near_call(
        functools.partial(halo_kernel, share, away),
        [bf16(share, columns, size)] * len(away)
        + [bf16(3 * group, DEPTH, size), bf16(3 * group, columns, size)],
        [pltpu.VMEM((group + 1, columns, size), jnp.float32)],
        [neighbours, probe_vectors, *halo, own_far, near, started],
        sent_rows,
        6,
    )
    arrived = {tier: vec_send(array, tier) for tier, array in zip(away, sent)}
    kept = near_call(
        functools.partial(kept_kernel, share),
        [bf16(share, columns, size)],
        [pltpu.VMEM((group + 1, columns, size), jnp.float32)],
        [neighbours, far, vectors, near],
        share,
        12,
    )[0]

    pack_rows = share * rank + (share // 2) * rank
    slabs = total_columns // (2 * rank)
    pack, state = call(
        functools.partial(device_kernel, share, group, rank),
        (f32(pack_rows, size), f32(slabs, rank, 2 * rank)),
        [
            pltpu.VMEM((share, total_columns, size), jnp.bfloat16),
            pltpu.VMEM((share * rank, total_columns), jnp.float32),
        ],
        [kept]
        + [arrived[tier] for tier in range(1, parts)]
        + [leaf_pivots, leaf_inverse, local_pivots, local_inverse],
    )
    waiting = list(range(1, parts))
    others = {}

    def send_pack(after, number):
        for tier in waiting[:number]:
            held_pack, after = lax.optimization_barrier((pack, after))
            others[tier] = vec_send(held_pack, tier)
        del waiting[:number]
        return after

    rounds = parts.bit_length() - 1
    for bit in range(rounds):
        partner = vec_send(state, 1 << bit)
        nodes = (2 << bit) - 1
        if bit < rounds - 1:
            outs = [f32(slabs + nodes, rank, 2 * rank)]
        else:
            outs = [f32(nodes, rank, 2 * rank), f32(rank, total_columns)]
        *interps, state = call(
            functools.partial(pair_kernel, bit, parts, group, rank, slabs),
            outs,
            [pltpu.VMEM((2 * rank, total_columns), jnp.float32)],
            [state, partner, local_pivots, local_inverse],
        )
        state = send_pack(state, 1)
    joined, own_up = interps[0], state

    heap_first = 0
    maps = []
    for tier in range(UPL):
        last = tier == UPL - 1
        partner = lax.ppermute(own_up, "leaf", [(i, i ^ (1 << tier)) for i in range(leaf_total)])
        outs = (f32(rank, 2 * rank), f32(rank, total_columns))
        scratch = [pltpu.VMEM((2 * rank, total_columns), jnp.float32)]
        operands = [own_up, partner, upper_pivots, upper_inverse]
        if last:
            outs = (f32(UPL, rank, 2 * rank), f32(columns, rank))
            scratch.append(pltpu.VMEM((total_columns, rank), jnp.float32))
            operands += maps
        first, own_up = call(
            functools.partial(upper_kernel, tier, heap_first, last, rank), outs, scratch, operands
        )
        if not last:
            own_up = send_pack(own_up, parts)
        maps.append(first)
        heap_first += leaf_total >> (tier + 1)
    leaf_map, local_map = call(
        functools.partial(place_kernel, share, group, rank),
        (f32(group, rank, size), f32(group - 1, rank, 2 * rank)),
        [],
        [pack] + [others[tier] for tier in range(1, parts)] + [joined],
    )
    return (
        jnp.swapaxes(leaf_map, 1, 2),
        jnp.swapaxes(local_map, 1, 2),
        jnp.swapaxes(first, 1, 2)[None],
        own_up[None],
    )


def solution(mesh):
    placed = (
        P("leaf", None, None),
        P("leaf", "vec", None),
        P("leaf", None),
        P("leaf", None),
        P("leaf", None, None),
        P("leaf", None),
        P("leaf", None, None),
        P(),
        P(),
    )
    return jax.shard_map(
        on_device,
        mesh=mesh,
        in_specs=placed,
        out_specs=(
            P("leaf", None, None),
            P("leaf", None, None),
            P("leaf", None, None, None),
            P("leaf", "vec", None),
        ),
        check_vma=False,
    )
```

```python
import functools

import jax
import jax.numpy as jnp
from jax import lax
from jax.experimental import pallas as pl
from jax.experimental.pallas import tpu as pltpu
from jax.sharding import PartitionSpec as P

UPL = 3

SOFTEN = 0.0009
EPSILON = 1e-06
FLIGHT = 8
DEPTH = 128
VMEM_BYTES = 20 * 1024 * 1024
VMEM = pltpu.MemorySpace.VMEM
SMEM = pltpu.MemorySpace.SMEM


def nt(a, b):
    return lax.dot_general(a, b, (((1,), (1,)), ((), ())), preferred_element_type=jnp.float32)


def nn(a, b):
    return lax.dot_general(a, b, (((1,), (0,)), ((), ())), preferred_element_type=jnp.float32)


def split(a):
    high = a.astype(jnp.bfloat16)
    low = (a - high.astype(jnp.float32)).astype(jnp.bfloat16)
    return high, low


def stacked_split(a):
    high, low = split(a)
    return jnp.concatenate([high, low], axis=0)


def halves(a):
    rows = a.shape[0] // 2
    return a[:rows] + a[rows:]


def coordinates(points, extra):
    row = lax.broadcasted_iota(jnp.int32, (8, points.shape[1]), 0)
    padded = jnp.concatenate(
        [points, jnp.full((5, points.shape[1]), 0.5, jnp.float32)], axis=0
    )
    centred = padded - 0.5
    high, low = [part.astype(jnp.float32) for part in split(centred)]
    norm = jnp.sum(centred * centred, axis=0, keepdims=True) + extra
    first, rest = [part.astype(jnp.float32) for part in split(norm)]
    second, third = [part.astype(jnp.float32) for part in split(norm - first)]
    norms = jnp.where(row == 0, first, jnp.where(row == 1, second, jnp.where(row == 2, third, 0.0)))
    return high, low, norms, jnp.where(row < 3, 1.0, 0.0)


def far_features(points):
    high, low, norm, one = coordinates(points, SOFTEN)
    vacant = jnp.zeros((DEPTH - 48, points.shape[1]), jnp.float32)
    return jnp.concatenate(
        [-2.0 * high, -2.0 * low, -2.0 * high, -2.0 * low, one, norm, vacant], axis=0
    ).astype(jnp.bfloat16)


def near_features(points):
    high, low, norm, one = coordinates(points, 0.0)
    vacant = jnp.zeros((DEPTH - 48, points.shape[1]), jnp.float32)
    return jnp.transpose(
        jnp.concatenate([high, high, low, low, norm, one, vacant], axis=0)
    ).astype(jnp.bfloat16)


def add_blocks(share, tiers, base, wanted, nb_ref, far, vectors, near, total, tiles, codes):
    me = lax.axis_index("vec")
    count, slots = nb_ref.shape
    first = lax.axis_index("leaf") * count
    flight, size = tiles.shape[0], tiles.shape[1]
    idle = count * 64

    for way in range(flight):
        codes[way] = idle
    filled = jnp.int32(flight)
    for tier in tiers:
        for part in range(share):
            cluster = (me ^ tier) * share + part
            for slot in range(slots):
                listed = nb_ref[cluster, slot]
                position = listed - first + count
                codes[filled] = cluster * 64 + position - base
                filled += ((listed >= 0) & wanted(position, count)).astype(jnp.int32)
    for way in range(flight):
        codes[filled + way] = idle
    tiles[...] = jnp.zeros(tiles.shape, tiles.dtype)

    def multiply(code, tile):
        row = code // 64
        total[row] = total[row] + nt(vectors[code % 64], tile[...])

    def evaluate(code, tile):
        row = code // 64
        position = code % 64
        for top in range(0, size, 128):
            distance = nn(near[row, top : top + 128, :], far[position])
            tile[top : top + 128, :] = lax.rsqrt(distance).astype(jnp.bfloat16)

    def step(index, carry):
        for way in range(flight):
            multiply(codes[index * flight + way], tiles.at[way])
            evaluate(codes[(index + 1) * flight + way], tiles.at[way])
        return carry

    steps = (filled - 1) // flight
    lax.fori_loop(0, steps, step, 0)
    for way in range(flight):
        multiply(codes[steps * flight + way], tiles.at[way])


def inside(position, count):
    return (position >= count) & (position < 2 * count)


def outside(position, count):
    return (position < count) | (position >= 2 * count)


def anywhere(position, count):
    return position >= 0


def own_kernel(share, tiers, nb_ref, points, probe, total, far, near, tiles, codes):
    count = points.shape[0]
    for cluster in range(count):
        here = points[cluster].astype(jnp.float32)
        far[cluster] = far_features(here)
        near[cluster] = near_features(here)
    near[count] = near[0]
    total[...] = jnp.zeros(total.shape, total.dtype)
    add_blocks(share, tiers, count, inside, nb_ref, far, probe, near, total, tiles, codes)


def halo_kernel(share, tiers, nb_ref, probe, before, after, own_far, near, start, *refs):
    outs = refs[: len(tiers)]
    far, vectors, total, tiles, codes = refs[len(tiers) :]
    count, columns, _ = probe.shape
    me = lax.axis_index("vec")
    for place, source in ((0, before), (2, after)):
        for cluster in range(count):
            far[place * count + cluster] = far_features(
                source[cluster, columns:, :].astype(jnp.float32)[0:3]
            )
        vectors[place * count : (place + 1) * count] = source[:, 0:columns, :]
    far[count : 2 * count] = own_far[...]
    vectors[count : 2 * count] = probe[...]
    total[...] = start[...]
    add_blocks(share, tiers, 0, outside, nb_ref, far, vectors, near, total, tiles, codes)
    for tier, out in zip(tiers, outs):
        part = total[pl.ds((me ^ tier) * share, share)]
        out[...] = (part * 0.015625).astype(out.dtype)


def kept_kernel(share, nb_ref, far, vectors, near, out, total, tiles, codes):
    mine = pl.ds(lax.axis_index("vec") * share, share)
    total[mine] = jnp.zeros((share,) + total.shape[1:], total.dtype)
    add_blocks(share, (0,), 0, anywhere, nb_ref, far, vectors, near, total, tiles, codes)
    out[...] = (total[mine] * 0.015625).astype(out.dtype)


def join_kernel(points, probe, joined):
    count, columns, size = probe.shape
    joined[:, 0:columns, :] = probe[...]
    vacant = jnp.zeros((joined.shape[1] - columns - 3, size), jnp.float32)
    for cluster in range(count):
        joined[cluster, columns:, :] = jnp.concatenate(
            [points[cluster].astype(jnp.float32), vacant], axis=0
        ).astype(joined.dtype)


def near_call(body, outs, scratch, operands, rows, per_row):
    nb, size = operands[0], outs[0].shape[-1]
    blocks = rows * per_row
    return pl.pallas_call(
        body,
        out_shape=outs,
        in_specs=[pl.BlockSpec(memory_space=SMEM)]
        + [pl.BlockSpec(memory_space=VMEM)] * (len(operands) - 1),
        out_specs=[pl.BlockSpec(memory_space=VMEM)] * len(outs),
        scratch_shapes=scratch
        + [
            pltpu.VMEM((FLIGHT, size, size), jnp.bfloat16),
            pltpu.SMEM((rows * nb.shape[1] + 2 * FLIGHT,), jnp.int32),
        ],
        compiler_params=pltpu.CompilerParams(vmem_limit_bytes=VMEM_BYTES),
        cost_estimate=pl.CostEstimate(
            flops=blocks * size * size * 256,
            bytes_accessed=sum(o.size * o.dtype.itemsize for o in operands),
            transcendentals=blocks * size * size,
        ),
    )(*operands)


def pivot_factor(pivots, inverse, width):
    chosen = (
        lax.broadcasted_iota(jnp.int32, (width, pivots.shape[1]), 0) == pivots
    ).astype(jnp.bfloat16)
    return nt(stacked_split(jnp.transpose(inverse)), chosen).astype(jnp.bfloat16)


def leaf_node(sketch, pivots, inverse):
    factor = pivot_factor(pivots, inverse, sketch.shape[1])
    wide = sketch.astype(jnp.float32)
    mean_sq = jnp.sum(wide * wide, keepdims=True) / (sketch.shape[0] * sketch.shape[1]) + EPSILON
    scale = 1.0 / (sketch.shape[0] * mean_sq)
    picked = halves(nt(factor, sketch))
    raw = halves(nn(stacked_split(picked), sketch))
    interp = raw * scale
    upward = halves(nt(stacked_split(raw), sketch)) * (scale * lax.rsqrt(mean_sq))
    return interp, upward


def tree_node(sketch, pivots, inverse):
    width, columns = sketch.shape
    factor = pivot_factor(pivots, inverse, width)
    mean_sq = jnp.sum(sketch * sketch, keepdims=True) / (width * columns) + EPSILON
    scale = 1.0 / (columns * mean_sq)
    parts = stacked_split(sketch)
    picked = halves(nn(jnp.concatenate([factor, factor], axis=1), parts))
    raw = halves(nt(stacked_split(picked), parts))
    raw = raw[:, :width] + raw[:, width:]
    interp = raw * scale
    both = stacked_split(raw)
    upward = halves(nn(jnp.concatenate([both, both], axis=1), parts)) * (scale * lax.rsqrt(mean_sq))
    return interp, upward


def device_kernel(
    share,
    group,
    rank,
    own,
    *refs,
):
    parts = group // share
    arrived = refs[: parts - 1]
    pivots, inverse, local_pivots, local_inverse, pack, up_out, up_sent, sketch, ups = refs[
        parts - 1 :
    ]
    me = lax.axis_index("vec")
    columns = own.shape[1]
    size = own.shape[2]
    for tier, piece in enumerate((own,) + tuple(arrived)):
        place = pl.ds(pl.multiple_of((me ^ tier) * columns, columns), columns)
        for cluster in range(share):
            sketch[cluster, place, :] = piece[cluster]
    for cluster in range(share):
        row = me * share + cluster
        interp, upward = leaf_node(sketch[cluster], pivots[pl.ds(row, 1), :], inverse[row])
        pack[cluster * rank : (cluster + 1) * rank, :] = interp
        ups[cluster * rank : (cluster + 1) * rank, :] = upward
    level_first, nodes, packed = 0, share // 2, 0
    level_nodes = group // 2
    while nodes >= 1:
        results = []
        for node in range(nodes):
            row = level_first + me * nodes + node
            interp, upward = tree_node(
                ups[2 * node * rank : 2 * (node + 1) * rank, :],
                local_pivots[pl.ds(row, 1), :],
                local_inverse[row],
            )
            top = (share + packed // 2) * rank
            side = (packed % 2) * 2 * rank
            pack[top : top + rank, side : side + 2 * rank] = interp
            results.append(upward)
            packed += 1
        for node, upward in enumerate(results):
            ups[node * rank : (node + 1) * rank, :] = upward
        level_first += level_nodes
        level_nodes //= 2
        nodes //= 2
    up_out[...] = ups[0:rank, :]
    up_sent[...] = ups[0:rank, :].astype(up_sent.dtype)


def group_kernel(share, group, rank, own, *refs):
    parts = group // share
    arrived = refs[: parts - 1]
    local_pivots, local_inverse, interps, up_out, ups = refs[parts - 1 :]
    me = lax.axis_index("vec")
    for tier, piece in enumerate((own,) + tuple(arrived)):
        place = pl.ds(pl.multiple_of((me ^ tier) * rank, rank), rank)
        ups[place, :] = piece[...].astype(ups.dtype)
    row = group - parts
    done = 0
    nodes = parts // 2
    while nodes >= 1:
        results = []
        for node in range(nodes):
            interp, upward = tree_node(
                ups[2 * node * rank : 2 * (node + 1) * rank, :],
                local_pivots[row : row + 1, :],
                local_inverse[row],
            )
            interps[done] = interp
            results.append(upward)
            row += 1
            done += 1
        for node, upward in enumerate(results):
            ups[node * rank : (node + 1) * rank, :] = upward
        nodes //= 2
    up_out[...] = ups[0:rank, :]


def sibling_kernel(rank, own, arrived, pivots, inverse, interp_out, up_out, ups):
    me = lax.axis_index("leaf")
    side = me & 1
    ups[pl.ds(pl.multiple_of(side * rank, rank), rank), :] = own[...]
    ups[pl.ds(pl.multiple_of((1 - side) * rank, rank), rank), :] = arrived[...]
    node = me >> 1
    interp, upward = tree_node(ups[...], pivots[pl.ds(node, 1), :], inverse[node])
    interp_out[...] = interp
    up_out[...] = upward


def top_kernel(rank, heap_first, first, own, *refs):
    leaves = 1 << (UPL - 1)
    arrived = refs[: leaves - 1]
    pivots, inverse, interps, top, ups, maps, turned = refs[leaves - 1 :]
    me = lax.axis_index("leaf")
    mine = (me >> 1) & (leaves - 1)
    for tier, piece in enumerate((own,) + tuple(arrived)):
        ups[pl.ds(pl.multiple_of((mine ^ tier) * rank, rank), rank), :] = piece[...]
    interps[0] = first[...]
    nodes = leaves // 2
    for level in range(1, UPL):
        results = []
        for node in range(nodes):
            row = heap_first[level] + (me >> UPL) * nodes + node
            interp, upward = tree_node(
                ups[2 * node * rank : 2 * (node + 1) * rank, :],
                pivots[pl.ds(row, 1), :],
                inverse[row],
            )
            maps[node] = interp
            results.append(upward)
        for node, upward in enumerate(results):
            ups[node * rank : (node + 1) * rank, :] = upward
        interps[level] = maps[mine >> level]
        nodes //= 2
    turned[...] = jnp.transpose(ups[0:rank, :])
    columns = top.shape[0]
    place = pl.multiple_of(lax.axis_index("vec") * columns, columns)
    top[...] = turned[pl.ds(place, columns), :]


def place_kernel(share, group, rank, own, *refs):
    parts = group // share
    arrived = refs[: parts - 1]
    joined, leaf_out, local_out = refs[parts - 1 :]
    me = lax.axis_index("vec")
    for tier, piece in enumerate((own,) + tuple(arrived)):
        device = me ^ tier
        for cluster in range(share):
            leaf_out[device * share + cluster] = piece[cluster * rank : (cluster + 1) * rank, :]
        level_first, nodes, packed = 0, share // 2, 0
        level_nodes = group // 2
        while nodes >= 1:
            for node in range(nodes):
                top = (share + packed // 2) * rank
                side = (packed % 2) * 2 * rank
                local_out[level_first + device * nodes + node] = piece[
                    top : top + rank, side : side + 2 * rank
                ]
                packed += 1
            level_first += level_nodes
            level_nodes //= 2
            nodes //= 2
    for index in range(parts - 1):
        local_out[group - parts + index] = joined[index]


def copy_kernel(source, copied):
    copied[...] = source[...]


def call(body, outs, scratch, operands, flops=0):
    return pl.pallas_call(
        body,
        out_shape=outs,
        in_specs=[pl.BlockSpec(memory_space=VMEM)] * len(operands),
        out_specs=jax.tree.map(lambda _: pl.BlockSpec(memory_space=VMEM), outs),
        scratch_shapes=scratch,
        compiler_params=pltpu.CompilerParams(vmem_limit_bytes=VMEM_BYTES),
        cost_estimate=pl.CostEstimate(
            flops=flops, bytes_accessed=sum(o.size * o.dtype.itemsize for o in operands), transcendentals=0
        ),
    )(*operands)


def f32(*shape):
    return jax.ShapeDtypeStruct(shape, jnp.float32)


def on_device(
    points,
    probe_vectors,
    neighbours,
    leaf_pivots,
    leaf_inverse,
    local_pivots,
    local_inverse,
    upper_pivots,
    upper_inverse,
):
    group, columns, size = probe_vectors.shape
    rank = leaf_pivots.shape[1]
    leaf_total = lax.axis_size("leaf")
    parts = lax.axis_size("vec")
    share = group // parts
    total_columns = columns * parts

    up = [(i, i + 1) for i in range(leaf_total - 1)]
    down = [(j, i) for i, j in up]
    joined = call(
        join_kernel,
        jax.ShapeDtypeStruct((group, columns + 16, size), jnp.bfloat16),
        [],
        [points, probe_vectors],
    )
    halo = (lax.ppermute(joined, "leaf", up), lax.ppermute(joined, "leaf", down))

    def vec_send(array, tier):
        return lax.ppermute(array, "vec", [(i, i ^ tier) for i in range(parts)])

    away = list(range(parts - 1, 0, -1))
    sent_rows = (parts - 1) * share

    def bf16(*shape):
        return jax.ShapeDtypeStruct(shape, jnp.bfloat16)

    started, own_far, near = near_call(
        functools.partial(own_kernel, share, away),
        [f32(group + 1, columns, size), bf16(group, DEPTH, size), bf16(group + 1, size, DEPTH)],
        [],
        [neighbours, points, probe_vectors],
        sent_rows,
        6,
    )
    *sent, far, vectors = near_call(
        functools.partial(halo_kernel, share, away),
        [bf16(share, columns, size)] * len(away)
        + [bf16(3 * group, DEPTH, size), bf16(3 * group, columns, size)],
        [pltpu.VMEM((group + 1, columns, size), jnp.float32)],
        [neighbours, probe_vectors, *halo, own_far, near, started],
        sent_rows,
        6,
    )
    arrived = {tier: vec_send(array, tier) for tier, array in zip(away, sent)}
    kept = near_call(
        functools.partial(kept_kernel, share),
        [bf16(share, columns, size)],
        [pltpu.VMEM((group + 1, columns, size), jnp.float32)],
        [neighbours, far, vectors, near],
        share,
        12,
    )[0]

    pack_rows = share * rank + (share // 2) * rank
    pack, own_up, sent_up = call(
        functools.partial(device_kernel, share, group, rank),
        (f32(pack_rows, size), f32(rank, total_columns), bf16(rank, total_columns)),
        [
            pltpu.VMEM((share, total_columns, size), jnp.bfloat16),
            pltpu.VMEM((share * rank, total_columns), jnp.float32),
        ],
        [kept]
        + [arrived[tier] for tier in range(1, parts)]
        + [leaf_pivots, leaf_inverse, local_pivots, local_inverse],
    )
    near_ups = [vec_send(sent_up, tier) for tier in range(1, parts)]
    ready = call(copy_kernel, f32(pack_rows, size), [], [pack])
    others = [vec_send(ready, tier) for tier in range(1, parts)]
    joined, own_up = call(
        functools.partial(group_kernel, share, group, rank),
        (f32(parts - 1, rank, 2 * rank), f32(rank, total_columns)),
        [pltpu.VMEM((parts * rank, total_columns), jnp.float32)],
        [own_up] + near_ups + [local_pivots, local_inverse],
    )

    def leaf_send(array, flip):
        return lax.ppermute(array, "leaf", [(i, i ^ flip) for i in range(leaf_total)])

    first, own_up = call(
        functools.partial(sibling_kernel, rank),
        (f32(rank, 2 * rank), f32(rank, total_columns)),
        [pltpu.VMEM((2 * rank, total_columns), jnp.float32)],
        [own_up, leaf_send(own_up, 1), upper_pivots, upper_inverse],
    )
    heap_first = [0]
    for tier in range(1, UPL):
        heap_first.append(heap_first[-1] + (leaf_total >> tier))
    leaves = 1 << (UPL - 1)
    maps, top = call(
        functools.partial(top_kernel, rank, heap_first),
        (f32(UPL, rank, 2 * rank), f32(columns, rank)),
        [
            pltpu.VMEM((leaves * rank, total_columns), jnp.float32),
            pltpu.VMEM((leaves // 2, rank, 2 * rank), jnp.float32),
            pltpu.VMEM((total_columns, rank), jnp.float32),
        ],
        [first, own_up]
        + [leaf_send(own_up, 2 * tier) for tier in range(1, leaves)]
        + [upper_pivots, upper_inverse],
    )
    leaf_map, local_map = call(
        functools.partial(place_kernel, share, group, rank),
        (f32(group, rank, size), f32(group - 1, rank, 2 * rank)),
        [],
        [pack] + others + [joined],
    )
    return (
        jnp.swapaxes(leaf_map, 1, 2),
        jnp.swapaxes(local_map, 1, 2),
        jnp.swapaxes(maps, 1, 2)[None],
        top[None],
    )


def solution(mesh):
    placed = (
        P("leaf", None, None),
        P("leaf", "vec", None),
        P("leaf", None),
        P("leaf", None),
        P("leaf", None, None),
        P("leaf", None),
        P("leaf", None, None),
        P(),
        P(),
    )
    return jax.shard_map(
        on_device,
        mesh=mesh,
        in_specs=placed,
        out_specs=(
            P("leaf", None, None),
            P("leaf", None, None),
            P("leaf", None, None, None),
            P("leaf", "vec", None),
        ),
        check_vma=False,
    )
```

```python
import functools

import jax
import jax.numpy as jnp
from jax import lax
from jax.experimental import pallas as pl
from jax.experimental.pallas import tpu as pltpu
from jax.sharding import PartitionSpec as P

UPL = 3

SOFTEN = 0.0009
EPSILON = 1e-06
FLIGHT = 8
DEPTH = 128
ROUND_FLOPS = 850_000_000
VMEM_BYTES = 20 * 1024 * 1024
VMEM = pltpu.MemorySpace.VMEM
SMEM = pltpu.MemorySpace.SMEM


def nt(a, b):
    return lax.dot_general(a, b, (((1,), (1,)), ((), ())), preferred_element_type=jnp.float32)


def nn(a, b):
    return lax.dot_general(a, b, (((1,), (0,)), ((), ())), preferred_element_type=jnp.float32)


def split(a):
    high = a.astype(jnp.bfloat16)
    low = (a - high.astype(jnp.float32)).astype(jnp.bfloat16)
    return high, low


def stacked_split(a):
    high, low = split(a)
    return jnp.concatenate([high, low], axis=0)


def halves(a):
    rows = a.shape[0] // 2
    return a[:rows] + a[rows:]


def coordinates(points, extra):
    row = lax.broadcasted_iota(jnp.int32, (8, points.shape[1]), 0)
    padded = jnp.concatenate(
        [points, jnp.full((5, points.shape[1]), 0.5, jnp.float32)], axis=0
    )
    centred = padded - 0.5
    high, low = [part.astype(jnp.float32) for part in split(centred)]
    norm = jnp.sum(centred * centred, axis=0, keepdims=True) + extra
    first, rest = [part.astype(jnp.float32) for part in split(norm)]
    second, third = [part.astype(jnp.float32) for part in split(norm - first)]
    norms = jnp.where(row == 0, first, jnp.where(row == 1, second, jnp.where(row == 2, third, 0.0)))
    return high, low, norms, jnp.where(row < 3, 1.0, 0.0)


def far_features(points):
    high, low, norm, one = coordinates(points, SOFTEN)
    vacant = jnp.zeros((DEPTH - 48, points.shape[1]), jnp.float32)
    return jnp.concatenate(
        [-2.0 * high, -2.0 * low, -2.0 * high, -2.0 * low, one, norm, vacant], axis=0
    ).astype(jnp.bfloat16)


def near_features(points):
    high, low, norm, one = coordinates(points, 0.0)
    vacant = jnp.zeros((DEPTH - 48, points.shape[1]), jnp.float32)
    return jnp.transpose(
        jnp.concatenate([high, high, low, low, norm, one, vacant], axis=0)
    ).astype(jnp.bfloat16)


def add_blocks(share, tiers, base, wanted, nb_ref, far, vectors, near, total, tiles, codes):
    me = lax.axis_index("vec")
    count, slots = nb_ref.shape
    first = lax.axis_index("leaf") * count
    flight, size = tiles.shape[0], tiles.shape[1]
    idle = count * 64

    for way in range(flight):
        codes[way] = idle
    filled = jnp.int32(flight)
    for tier in tiers:
        for part in range(share):
            cluster = (me ^ tier) * share + part
            for slot in range(slots):
                listed = nb_ref[cluster, slot]
                position = listed - first + count
                codes[filled] = cluster * 64 + position - base
                filled += ((listed >= 0) & wanted(position, count)).astype(jnp.int32)
    for way in range(flight):
        codes[filled + way] = idle
    tiles[...] = jnp.zeros(tiles.shape, tiles.dtype)

    def multiply(code, tile):
        row = code // 64
        total[row] = total[row] + nt(vectors[code % 64], tile[...])

    def evaluate(code, tile):
        row = code // 64
        position = code % 64
        for top in range(0, size, 128):
            distance = nn(near[row, top : top + 128, :], far[position])
            tile[top : top + 128, :] = jnp.exp2(-0.5 * jnp.log2(distance)).astype(
                jnp.bfloat16
            )

    def step(index, carry):
        for way in range(flight):
            multiply(codes[index * flight + way], tiles.at[way])
            evaluate(codes[(index + 1) * flight + way], tiles.at[way])
        return carry

    steps = (filled - 1) // flight
    lax.fori_loop(0, steps, step, 0)
    for way in range(flight):
        multiply(codes[steps * flight + way], tiles.at[way])


def inside(position, count):
    return (position >= count) & (position < 2 * count)


def outside(position, count):
    return (position < count) | (position >= 2 * count)


def anywhere(position, count):
    return position >= 0


def own_kernel(share, tiers, nb_ref, points, probe, total, far, near, tiles, codes):
    count = points.shape[0]
    for cluster in range(count):
        here = points[cluster].astype(jnp.float32)
        far[cluster] = far_features(here)
        near[cluster] = near_features(here)
    near[count] = near[0]
    total[...] = jnp.zeros(total.shape, total.dtype)
    add_blocks(share, tiers, count, inside, nb_ref, far, probe, near, total, tiles, codes)


def halo_kernel(share, tiers, nb_ref, probe, before, after, own_far, near, start, *refs):
    outs = refs[: len(tiers)]
    far, vectors, total, tiles, codes = refs[len(tiers) :]
    count, columns, _ = probe.shape
    me = lax.axis_index("vec")
    for place, source in ((0, before), (2, after)):
        for cluster in range(count):
            far[place * count + cluster] = far_features(
                source[cluster, columns:, :].astype(jnp.float32)[0:3]
            )
        vectors[place * count : (place + 1) * count] = source[:, 0:columns, :]
    far[count : 2 * count] = own_far[...]
    vectors[count : 2 * count] = probe[...]
    total[...] = start[...]
    add_blocks(share, tiers, 0, outside, nb_ref, far, vectors, near, total, tiles, codes)
    for tier, out in zip(tiers, outs):
        part = total[pl.ds((me ^ tier) * share, share)]
        out[...] = (part * 0.015625).astype(out.dtype)


def kept_kernel(share, nb_ref, far, vectors, near, out, total, tiles, codes):
    mine = pl.ds(lax.axis_index("vec") * share, share)
    total[mine] = jnp.zeros((share,) + total.shape[1:], total.dtype)
    add_blocks(share, (0,), 0, anywhere, nb_ref, far, vectors, near, total, tiles, codes)
    out[...] = (total[mine] * 0.015625).astype(out.dtype)


def join_kernel(points, probe, joined):
    count, columns, size = probe.shape
    joined[:, 0:columns, :] = probe[...]
    vacant = jnp.zeros((joined.shape[1] - columns - 3, size), jnp.float32)
    for cluster in range(count):
        joined[cluster, columns:, :] = jnp.concatenate(
            [points[cluster].astype(jnp.float32), vacant], axis=0
        ).astype(joined.dtype)


def near_call(body, outs, scratch, operands, rows, per_row):
    nb, size = operands[0], outs[0].shape[-1]
    blocks = rows * per_row
    return pl.pallas_call(
        body,
        out_shape=outs,
        in_specs=[pl.BlockSpec(memory_space=SMEM)]
        + [pl.BlockSpec(memory_space=VMEM)] * (len(operands) - 1),
        out_specs=[pl.BlockSpec(memory_space=VMEM)] * len(outs),
        scratch_shapes=scratch
        + [
            pltpu.VMEM((FLIGHT, size, size), jnp.bfloat16),
            pltpu.SMEM((rows * nb.shape[1] + 2 * FLIGHT,), jnp.int32),
        ],
        compiler_params=pltpu.CompilerParams(vmem_limit_bytes=VMEM_BYTES),
        cost_estimate=pl.CostEstimate(
            flops=blocks * size * size * 256,
            bytes_accessed=sum(o.size * o.dtype.itemsize for o in operands),
            transcendentals=blocks * size * size,
        ),
    )(*operands)


def pivot_factor(pivots, inverse, width):
    chosen = (
        lax.broadcasted_iota(jnp.int32, (width, pivots.shape[1]), 0) == pivots
    ).astype(jnp.bfloat16)
    return nt(stacked_split(jnp.transpose(inverse)), chosen).astype(jnp.bfloat16)


def leaf_node(sketch, pivots, inverse):
    factor = pivot_factor(pivots, inverse, sketch.shape[1])
    wide = sketch.astype(jnp.float32)
    mean_sq = jnp.sum(wide * wide, keepdims=True) / (sketch.shape[0] * sketch.shape[1]) + EPSILON
    scale = 1.0 / (sketch.shape[0] * mean_sq)
    picked = halves(nt(factor, sketch))
    raw = halves(nn(stacked_split(picked), sketch))
    interp = raw * scale
    upward = halves(nt(stacked_split(raw), sketch)) * (scale * lax.rsqrt(mean_sq))
    return interp, upward


def tree_node(sketch, pivots, inverse):
    width, columns = sketch.shape
    factor = pivot_factor(pivots, inverse, width)
    mean_sq = jnp.sum(sketch * sketch, keepdims=True) / (width * columns) + EPSILON
    scale = 1.0 / (columns * mean_sq)
    parts = stacked_split(sketch)
    picked = halves(nn(jnp.concatenate([factor, factor], axis=1), parts))
    raw = halves(nt(stacked_split(picked), parts))
    raw = raw[:, :width] + raw[:, width:]
    interp = raw * scale
    both = stacked_split(raw)
    upward = halves(nn(jnp.concatenate([both, both], axis=1), parts)) * (scale * lax.rsqrt(mean_sq))
    return interp, upward


def device_kernel(
    share,
    group,
    rank,
    own,
    *refs,
):
    parts = group // share
    arrived = refs[: parts - 1]
    pivots, inverse, local_pivots, local_inverse, pack, up_out, sketch, ups = refs[parts - 1 :]
    me = lax.axis_index("vec")
    columns = own.shape[1]
    size = own.shape[2]
    for tier, piece in enumerate((own,) + tuple(arrived)):
        place = pl.ds(pl.multiple_of((me ^ tier) * columns, columns), columns)
        for cluster in range(share):
            sketch[cluster, place, :] = piece[cluster]
    for cluster in range(share):
        row = me * share + cluster
        interp, upward = leaf_node(sketch[cluster], pivots[pl.ds(row, 1), :], inverse[row])
        pack[cluster * rank : (cluster + 1) * rank, :] = interp
        ups[cluster * rank : (cluster + 1) * rank, :] = upward
    level_first, nodes, packed = 0, share // 2, 0
    level_nodes = group // 2
    while nodes >= 1:
        results = []
        for node in range(nodes):
            row = level_first + me * nodes + node
            interp, upward = tree_node(
                ups[2 * node * rank : 2 * (node + 1) * rank, :],
                local_pivots[pl.ds(row, 1), :],
                local_inverse[row],
            )
            top = (share + packed // 2) * rank
            side = (packed % 2) * 2 * rank
            pack[top : top + rank, side : side + 2 * rank] = interp
            results.append(upward)
            packed += 1
        for node, upward in enumerate(results):
            ups[node * rank : (node + 1) * rank, :] = upward
        level_first += level_nodes
        level_nodes //= 2
        nodes //= 2
    up_out[...] = ups[0:rank, :]


def group_kernel(share, group, rank, own, *refs):
    parts = group // share
    arrived = refs[: parts - 1]
    local_pivots, local_inverse, interps, up_out, ups = refs[parts - 1 :]
    me = lax.axis_index("vec")
    for tier, piece in enumerate((own,) + tuple(arrived)):
        ups[pl.ds(pl.multiple_of((me ^ tier) * rank, rank), rank), :] = piece[...]
    row = group - parts
    done = 0
    nodes = parts // 2
    while nodes >= 1:
        results = []
        for node in range(nodes):
            interp, upward = tree_node(
                ups[2 * node * rank : 2 * (node + 1) * rank, :],
                local_pivots[row : row + 1, :],
                local_inverse[row],
            )
            interps[done] = interp
            results.append(upward)
            row += 1
            done += 1
        for node, upward in enumerate(results):
            ups[node * rank : (node + 1) * rank, :] = upward
        nodes //= 2
    up_out[...] = ups[0:rank, :]


def upper_kernel(tier, heap_first, last, rank, own, arrived, pivots, inverse, *refs):
    refs = list(refs)
    if last:
        earlier = [refs.pop(0) for _ in range(tier)]
        interps, top, ups, turned = refs
    else:
        interp_out, up_out, ups = refs
    me = lax.axis_index("leaf")
    side = (me >> tier) & 1
    ups[pl.ds(pl.multiple_of(side * rank, rank), rank), :] = own[...]
    ups[pl.ds(pl.multiple_of((1 - side) * rank, rank), rank), :] = arrived[...]
    node = heap_first + (me >> (tier + 1))
    interp, upward = tree_node(ups[...], pivots[pl.ds(node, 1), :], inverse[node])
    if last:
        for index, ref in enumerate(earlier):
            interps[index] = ref[...]
        interps[tier] = interp
        turned[...] = jnp.transpose(upward)
        columns = top.shape[0]
        place = lax.axis_index("vec") * columns
        top[...] = turned[pl.ds(pl.multiple_of(place, columns), columns), :]
    else:
        interp_out[...] = interp
        up_out[...] = upward


def place_kernel(share, group, rank, own, *refs):
    parts = group // share
    arrived = refs[: parts - 1]
    joined, leaf_out, local_out = refs[parts - 1 :]
    me = lax.axis_index("vec")
    for tier, piece in enumerate((own,) + tuple(arrived)):
        device = me ^ tier
        for cluster in range(share):
            leaf_out[device * share + cluster] = piece[cluster * rank : (cluster + 1) * rank, :]
        level_first, nodes, packed = 0, share // 2, 0
        level_nodes = group // 2
        while nodes >= 1:
            for node in range(nodes):
                top = (share + packed // 2) * rank
                side = (packed % 2) * 2 * rank
                local_out[level_first + device * nodes + node] = piece[
                    top : top + rank, side : side + 2 * rank
                ]
                packed += 1
            level_first += level_nodes
            level_nodes //= 2
            nodes //= 2
    for index in range(parts - 1):
        local_out[group - parts + index] = joined[index]


def call(body, outs, scratch, operands, flops=0):
    return pl.pallas_call(
        body,
        out_shape=outs,
        in_specs=[pl.BlockSpec(memory_space=VMEM)] * len(operands),
        out_specs=jax.tree.map(lambda _: pl.BlockSpec(memory_space=VMEM), outs),
        scratch_shapes=scratch,
        compiler_params=pltpu.CompilerParams(vmem_limit_bytes=VMEM_BYTES),
        cost_estimate=pl.CostEstimate(
            flops=flops, bytes_accessed=sum(o.size * o.dtype.itemsize for o in operands), transcendentals=0
        ),
    )(*operands)


def f32(*shape):
    return jax.ShapeDtypeStruct(shape, jnp.float32)


def on_device(
    points,
    probe_vectors,
    neighbours,
    leaf_pivots,
    leaf_inverse,
    local_pivots,
    local_inverse,
    upper_pivots,
    upper_inverse,
):
    group, columns, size = probe_vectors.shape
    rank = leaf_pivots.shape[1]
    leaf_total = lax.axis_size("leaf")
    parts = lax.axis_size("vec")
    share = group // parts
    total_columns = columns * parts

    up = [(i, i + 1) for i in range(leaf_total - 1)]
    down = [(j, i) for i, j in up]
    joined = call(
        join_kernel,
        jax.ShapeDtypeStruct((group, columns + 16, size), jnp.bfloat16),
        [],
        [points, probe_vectors],
    )
    halo = (lax.ppermute(joined, "leaf", up), lax.ppermute(joined, "leaf", down))

    def vec_send(array, tier):
        return lax.ppermute(array, "vec", [(i, i ^ tier) for i in range(parts)])

    away = list(range(parts - 1, 0, -1))
    sent_rows = (parts - 1) * share

    def bf16(*shape):
        return jax.ShapeDtypeStruct(shape, jnp.bfloat16)

    started, own_far, near = near_call(
        functools.partial(own_kernel, share, away),
        [f32(group + 1, columns, size), bf16(group, DEPTH, size), bf16(group + 1, size, DEPTH)],
        [],
        [neighbours, points, probe_vectors],
        sent_rows,
        6,
    )
    *sent, far, vectors = near_call(
        functools.partial(halo_kernel, share, away),
        [bf16(share, columns, size)] * len(away)
        + [bf16(3 * group, DEPTH, size), bf16(3 * group, columns, size)],
        [pltpu.VMEM((group + 1, columns, size), jnp.float32)],
        [neighbours, probe_vectors, *halo, own_far, near, started],
        sent_rows,
        6,
    )
    arrived = {tier: vec_send(array, tier) for tier, array in zip(away, sent)}
    kept = near_call(
        functools.partial(kept_kernel, share),
        [bf16(share, columns, size)],
        [pltpu.VMEM((group + 1, columns, size), jnp.float32)],
        [neighbours, far, vectors, near],
        share,
        12,
    )[0]

    pack_rows = share * rank + (share // 2) * rank
    pack, own_up = call(
        functools.partial(device_kernel, share, group, rank),
        (f32(pack_rows, size), f32(rank, total_columns)),
        [
            pltpu.VMEM((share, total_columns, size), jnp.bfloat16),
            pltpu.VMEM((share * rank, total_columns), jnp.float32),
        ],
        [kept]
        + [arrived[tier] for tier in range(1, parts)]
        + [leaf_pivots, leaf_inverse, local_pivots, local_inverse],
    )
    near_ups = [vec_send(own_up, tier) for tier in range(1, parts)]
    joined, own_up = call(
        functools.partial(group_kernel, share, group, rank),
        (f32(parts - 1, rank, 2 * rank), f32(rank, total_columns)),
        [pltpu.VMEM((parts * rank, total_columns), jnp.float32)],
        [own_up] + near_ups + [local_pivots, local_inverse],
    )

    pack, own_up = lax.optimization_barrier((pack, own_up))
    others = [vec_send(pack, tier) for tier in range(1, parts)]

    heap_first = 0
    maps = []
    for tier in range(UPL):
        last = tier == UPL - 1
        partner = lax.ppermute(own_up, "leaf", [(i, i ^ (1 << tier)) for i in range(leaf_total)])
        outs = (f32(rank, 2 * rank), f32(rank, total_columns))
        scratch = [pltpu.VMEM((2 * rank, total_columns), jnp.float32)]
        operands = [own_up, partner, upper_pivots, upper_inverse]
        if last:
            outs = (f32(UPL, rank, 2 * rank), f32(columns, rank))
            scratch.append(pltpu.VMEM((total_columns, rank), jnp.float32))
            operands += maps
        first, own_up = call(
            functools.partial(upper_kernel, tier, heap_first, last, rank),
            outs,
            scratch,
            operands,
            flops=ROUND_FLOPS,
        )
        maps.append(first)
        heap_first += leaf_total >> (tier + 1)
    leaf_map, local_map = call(
        functools.partial(place_kernel, share, group, rank),
        (f32(group, rank, size), f32(group - 1, rank, 2 * rank)),
        [],
        [pack] + others + [joined],
    )
    return (
        jnp.swapaxes(leaf_map, 1, 2),
        jnp.swapaxes(local_map, 1, 2),
        jnp.swapaxes(first, 1, 2)[None],
        own_up[None],
    )


def solution(mesh):
    placed = (
        P("leaf", None, None),
        P("leaf", "vec", None),
        P("leaf", None),
        P("leaf", None),
        P("leaf", None, None),
        P("leaf", None),
        P("leaf", None, None),
        P(),
        P(),
    )
    return jax.shard_map(
        on_device,
        mesh=mesh,
        in_specs=placed,
        out_specs=(
            P("leaf", None, None),
            P("leaf", None, None),
            P("leaf", None, None, None),
            P("leaf", "vec", None),
        ),
        check_vma=False,
    )
```

```python
import functools

import jax
import jax.numpy as jnp
from jax import lax
from jax.experimental import pallas as pl
from jax.experimental.pallas import tpu as pltpu
from jax.sharding import PartitionSpec as P

UPL = 3

SOFTEN = 0.0009
EPSILON = 1e-06
FLIGHT = 8
DEPTH = 128
LATE = (2,)
ROUND_FLOPS = 400_000_000
VMEM_BYTES = 20 * 1024 * 1024
VMEM = pltpu.MemorySpace.VMEM
SMEM = pltpu.MemorySpace.SMEM


def nt(a, b):
    return lax.dot_general(a, b, (((1,), (1,)), ((), ())), preferred_element_type=jnp.float32)


def nn(a, b):
    return lax.dot_general(a, b, (((1,), (0,)), ((), ())), preferred_element_type=jnp.float32)


def split(a):
    high = a.astype(jnp.bfloat16)
    low = (a - high.astype(jnp.float32)).astype(jnp.bfloat16)
    return high, low


def stacked_split(a):
    high, low = split(a)
    return jnp.concatenate([high, low], axis=0)


def halves(a):
    rows = a.shape[0] // 2
    return a[:rows] + a[rows:]


def coordinates(points, extra):
    row = lax.broadcasted_iota(jnp.int32, (8, points.shape[1]), 0)
    padded = jnp.concatenate(
        [points, jnp.full((5, points.shape[1]), 0.5, jnp.float32)], axis=0
    )
    centred = padded - 0.5
    high, low = [part.astype(jnp.float32) for part in split(centred)]
    norm = jnp.sum(centred * centred, axis=0, keepdims=True) + extra
    first, rest = [part.astype(jnp.float32) for part in split(norm)]
    second, third = [part.astype(jnp.float32) for part in split(norm - first)]
    norms = jnp.where(row == 0, first, jnp.where(row == 1, second, jnp.where(row == 2, third, 0.0)))
    return high, low, norms, jnp.where(row < 3, 1.0, 0.0)


def far_features(points):
    high, low, norm, one = coordinates(points, SOFTEN)
    vacant = jnp.zeros((DEPTH - 48, points.shape[1]), jnp.float32)
    return jnp.concatenate(
        [-2.0 * high, -2.0 * low, -2.0 * high, -2.0 * low, one, norm, vacant], axis=0
    ).astype(jnp.bfloat16)


def near_features(points):
    high, low, norm, one = coordinates(points, 0.0)
    vacant = jnp.zeros((DEPTH - 48, points.shape[1]), jnp.float32)
    return jnp.transpose(
        jnp.concatenate([high, high, low, low, norm, one, vacant], axis=0)
    ).astype(jnp.bfloat16)


def add_blocks(share, tiers, base, wanted, nb_ref, far, vectors, near, total, tiles, codes):
    me = lax.axis_index("vec")
    count, slots = nb_ref.shape
    first = lax.axis_index("leaf") * count
    flight, size = tiles.shape[0], tiles.shape[1]
    idle = count * 64

    for way in range(flight):
        codes[way] = idle
    filled = jnp.int32(flight)
    for tier in tiers:
        for part in range(share):
            cluster = (me ^ tier) * share + part
            for slot in range(slots):
                listed = nb_ref[cluster, slot]
                position = listed - first + count
                codes[filled] = cluster * 64 + position - base
                filled += ((listed >= 0) & wanted(position, count)).astype(jnp.int32)
    for way in range(flight):
        codes[filled + way] = idle
    tiles[...] = jnp.zeros(tiles.shape, tiles.dtype)

    def multiply(code, tile):
        row = code // 64
        total[row] = total[row] + nt(vectors[code % 64], tile[...])

    def evaluate(code, tile):
        row = code // 64
        position = code % 64
        for top in range(0, size, 128):
            distance = nn(near[row, top : top + 128, :], far[position])
            tile[top : top + 128, :] = lax.rsqrt(distance).astype(jnp.bfloat16)

    def step(index, carry):
        for way in range(flight):
            multiply(codes[index * flight + way], tiles.at[way])
            evaluate(codes[(index + 1) * flight + way], tiles.at[way])
        return carry

    steps = (filled - 1) // flight
    lax.fori_loop(0, steps, step, 0)
    for way in range(flight):
        multiply(codes[steps * flight + way], tiles.at[way])


def inside(position, count):
    return (position >= count) & (position < 2 * count)


def outside(position, count):
    return (position < count) | (position >= 2 * count)


def anywhere(position, count):
    return position >= 0


def own_kernel(share, tiers, nb_ref, points, probe, total, far, near, tiles, codes):
    count = points.shape[0]
    for cluster in range(count):
        here = points[cluster].astype(jnp.float32)
        far[cluster] = far_features(here)
        near[cluster] = near_features(here)
    near[count] = near[0]
    total[...] = jnp.zeros(total.shape, total.dtype)
    add_blocks(share, tiers, count, inside, nb_ref, far, probe, near, total, tiles, codes)


def halo_kernel(share, tiers, nb_ref, probe, before, after, own_far, near, start, *refs):
    outs = refs[: len(tiers)]
    far, vectors, total, tiles, codes = refs[len(tiers) :]
    count, columns, _ = probe.shape
    me = lax.axis_index("vec")
    for place, source in ((0, before), (2, after)):
        for cluster in range(count):
            far[place * count + cluster] = far_features(
                source[cluster, columns:, :].astype(jnp.float32)[0:3]
            )
        vectors[place * count : (place + 1) * count] = source[:, 0:columns, :]
    far[count : 2 * count] = own_far[...]
    vectors[count : 2 * count] = probe[...]
    total[...] = start[...]
    add_blocks(share, tiers, 0, outside, nb_ref, far, vectors, near, total, tiles, codes)
    for tier, out in zip(tiers, outs):
        part = total[pl.ds((me ^ tier) * share, share)]
        out[...] = (part * 0.015625).astype(out.dtype)


def kept_kernel(share, nb_ref, far, vectors, near, out, total, tiles, codes):
    mine = pl.ds(lax.axis_index("vec") * share, share)
    total[mine] = jnp.zeros((share,) + total.shape[1:], total.dtype)
    add_blocks(share, (0,), 0, anywhere, nb_ref, far, vectors, near, total, tiles, codes)
    out[...] = (total[mine] * 0.015625).astype(out.dtype)


def join_kernel(points, probe, joined):
    count, columns, size = probe.shape
    joined[:, 0:columns, :] = probe[...]
    vacant = jnp.zeros((joined.shape[1] - columns - 3, size), jnp.float32)
    for cluster in range(count):
        joined[cluster, columns:, :] = jnp.concatenate(
            [points[cluster].astype(jnp.float32), vacant], axis=0
        ).astype(joined.dtype)


def near_call(body, outs, scratch, operands, rows, per_row):
    nb, size = operands[0], outs[0].shape[-1]
    blocks = rows * per_row
    return pl.pallas_call(
        body,
        out_shape=outs,
        in_specs=[pl.BlockSpec(memory_space=SMEM)]
        + [pl.BlockSpec(memory_space=VMEM)] * (len(operands) - 1),
        out_specs=[pl.BlockSpec(memory_space=VMEM)] * len(outs),
        scratch_shapes=scratch
        + [
            pltpu.VMEM((FLIGHT, size, size), jnp.bfloat16),
            pltpu.SMEM((rows * nb.shape[1] + 2 * FLIGHT,), jnp.int32),
        ],
        compiler_params=pltpu.CompilerParams(vmem_limit_bytes=VMEM_BYTES),
        cost_estimate=pl.CostEstimate(
            flops=blocks * size * size * 256,
            bytes_accessed=sum(o.size * o.dtype.itemsize for o in operands),
            transcendentals=blocks * size * size,
        ),
    )(*operands)


def pivot_factor(pivots, inverse, width):
    chosen = (
        lax.broadcasted_iota(jnp.int32, (width, pivots.shape[1]), 0) == pivots
    ).astype(jnp.bfloat16)
    return nt(stacked_split(jnp.transpose(inverse)), chosen).astype(jnp.bfloat16)


def leaf_node(sketch, pivots, inverse):
    factor = pivot_factor(pivots, inverse, sketch.shape[1])
    wide = sketch.astype(jnp.float32)
    mean_sq = jnp.sum(wide * wide, keepdims=True) / (sketch.shape[0] * sketch.shape[1]) + EPSILON
    scale = 1.0 / (sketch.shape[0] * mean_sq)
    picked = halves(nt(factor, sketch))
    raw = halves(nn(stacked_split(picked), sketch))
    interp = raw * scale
    upward = halves(nt(stacked_split(raw), sketch)) * (scale * lax.rsqrt(mean_sq))
    return interp, upward


def tree_node(sketch, pivots, inverse):
    width, columns = sketch.shape
    factor = pivot_factor(pivots, inverse, width)
    mean_sq = jnp.sum(sketch * sketch, keepdims=True) / (width * columns) + EPSILON
    scale = 1.0 / (columns * mean_sq)
    parts = stacked_split(sketch)
    picked = halves(nn(jnp.concatenate([factor, factor], axis=1), parts))
    raw = halves(nt(stacked_split(picked), parts))
    raw = raw[:, :width] + raw[:, width:]
    interp = raw * scale
    both = stacked_split(raw)
    upward = halves(nn(jnp.concatenate([both, both], axis=1), parts)) * (scale * lax.rsqrt(mean_sq))
    return interp, upward


def device_kernel(
    share,
    group,
    rank,
    own,
    *refs,
):
    parts = group // share
    arrived = refs[: parts - 1]
    pivots, inverse, local_pivots, local_inverse, pack, up_out, sketch, ups = refs[parts - 1 :]
    me = lax.axis_index("vec")
    columns = own.shape[1]
    size = own.shape[2]
    for tier, piece in enumerate((own,) + tuple(arrived)):
        place = pl.ds(pl.multiple_of((me ^ tier) * columns, columns), columns)
        for cluster in range(share):
            sketch[cluster, place, :] = piece[cluster]
    for cluster in range(share):
        row = me * share + cluster
        interp, upward = leaf_node(sketch[cluster], pivots[pl.ds(row, 1), :], inverse[row])
        pack[cluster * rank : (cluster + 1) * rank, :] = interp
        ups[cluster * rank : (cluster + 1) * rank, :] = upward
    level_first, nodes, packed = 0, share // 2, 0
    level_nodes = group // 2
    while nodes >= 1:
        results = []
        for node in range(nodes):
            row = level_first + me * nodes + node
            interp, upward = tree_node(
                ups[2 * node * rank : 2 * (node + 1) * rank, :],
                local_pivots[pl.ds(row, 1), :],
                local_inverse[row],
            )
            top = (share + packed // 2) * rank
            side = (packed % 2) * 2 * rank
            pack[top : top + rank, side : side + 2 * rank] = interp
            results.append(upward)
            packed += 1
        for node, upward in enumerate(results):
            ups[node * rank : (node + 1) * rank, :] = upward
        level_first += level_nodes
        level_nodes //= 2
        nodes //= 2
    up_out[...] = ups[0:rank, :]


def group_kernel(share, group, rank, own, *refs):
    parts = group // share
    arrived = refs[: parts - 1]
    local_pivots, local_inverse, interps, up_out, ups = refs[parts - 1 :]
    me = lax.axis_index("vec")
    for tier, piece in enumerate((own,) + tuple(arrived)):
        ups[pl.ds(pl.multiple_of((me ^ tier) * rank, rank), rank), :] = piece[...]
    row = group - parts
    done = 0
    nodes = parts // 2
    while nodes >= 1:
        results = []
        for node in range(nodes):
            interp, upward = tree_node(
                ups[2 * node * rank : 2 * (node + 1) * rank, :],
                local_pivots[row : row + 1, :],
                local_inverse[row],
            )
            interps[done] = interp
            results.append(upward)
            row += 1
            done += 1
        for node, upward in enumerate(results):
            ups[node * rank : (node + 1) * rank, :] = upward
        nodes //= 2
    up_out[...] = ups[0:rank, :]


def upper_kernel(tier, heap_first, last, rank, own, arrived, pivots, inverse, *refs):
    refs = list(refs)
    if last:
        earlier = [refs.pop(0) for _ in range(tier)]
        interps, top, ups, turned = refs
    else:
        interp_out, up_out, ups = refs
    me = lax.axis_index("leaf")
    side = (me >> tier) & 1
    ups[pl.ds(pl.multiple_of(side * rank, rank), rank), :] = own[...]
    ups[pl.ds(pl.multiple_of((1 - side) * rank, rank), rank), :] = arrived[...]
    node = heap_first + (me >> (tier + 1))
    interp, upward = tree_node(ups[...], pivots[pl.ds(node, 1), :], inverse[node])
    if last:
        for index, ref in enumerate(earlier):
            interps[index] = ref[...]
        interps[tier] = interp
        turned[...] = jnp.transpose(upward)
        columns = top.shape[0]
        place = lax.axis_index("vec") * columns
        top[...] = turned[pl.ds(pl.multiple_of(place, columns), columns), :]
    else:
        interp_out[...] = interp
        up_out[...] = upward


def place_kernel(share, group, rank, own, *refs):
    parts = group // share
    arrived = refs[: parts - 1]
    joined, leaf_out, local_out = refs[parts - 1 :]
    me = lax.axis_index("vec")
    for tier, piece in enumerate((own,) + tuple(arrived)):
        device = me ^ tier
        for cluster in range(share):
            leaf_out[device * share + cluster] = piece[cluster * rank : (cluster + 1) * rank, :]
        level_first, nodes, packed = 0, share // 2, 0
        level_nodes = group // 2
        while nodes >= 1:
            for node in range(nodes):
                top = (share + packed // 2) * rank
                side = (packed % 2) * 2 * rank
                local_out[level_first + device * nodes + node] = piece[
                    top : top + rank, side : side + 2 * rank
                ]
                packed += 1
            level_first += level_nodes
            level_nodes //= 2
            nodes //= 2
    for index in range(parts - 1):
        local_out[group - parts + index] = joined[index]


def call(body, outs, scratch, operands, flops=0):
    return pl.pallas_call(
        body,
        out_shape=outs,
        in_specs=[pl.BlockSpec(memory_space=VMEM)] * len(operands),
        out_specs=jax.tree.map(lambda _: pl.BlockSpec(memory_space=VMEM), outs),
        scratch_shapes=scratch,
        compiler_params=pltpu.CompilerParams(vmem_limit_bytes=VMEM_BYTES),
        cost_estimate=pl.CostEstimate(
            flops=flops, bytes_accessed=sum(o.size * o.dtype.itemsize for o in operands), transcendentals=0
        ),
    )(*operands)


def f32(*shape):
    return jax.ShapeDtypeStruct(shape, jnp.float32)


def on_device(
    points,
    probe_vectors,
    neighbours,
    leaf_pivots,
    leaf_inverse,
    local_pivots,
    local_inverse,
    upper_pivots,
    upper_inverse,
):
    group, columns, size = probe_vectors.shape
    rank = leaf_pivots.shape[1]
    leaf_total = lax.axis_size("leaf")
    parts = lax.axis_size("vec")
    share = group // parts
    total_columns = columns * parts

    up = [(i, i + 1) for i in range(leaf_total - 1)]
    down = [(j, i) for i, j in up]
    joined = call(
        join_kernel,
        jax.ShapeDtypeStruct((group, columns + 16, size), jnp.bfloat16),
        [],
        [points, probe_vectors],
    )
    halo = (lax.ppermute(joined, "leaf", up), lax.ppermute(joined, "leaf", down))

    def vec_send(array, tier):
        return lax.ppermute(array, "vec", [(i, i ^ tier) for i in range(parts)])

    away = list(range(parts - 1, 0, -1))
    sent_rows = (parts - 1) * share

    def bf16(*shape):
        return jax.ShapeDtypeStruct(shape, jnp.bfloat16)

    started, own_far, near = near_call(
        functools.partial(own_kernel, share, away),
        [f32(group + 1, columns, size), bf16(group, DEPTH, size), bf16(group + 1, size, DEPTH)],
        [],
        [neighbours, points, probe_vectors],
        sent_rows,
        6,
    )
    *sent, far, vectors = near_call(
        functools.partial(halo_kernel, share, away),
        [bf16(share, columns, size)] * len(away)
        + [bf16(3 * group, DEPTH, size), bf16(3 * group, columns, size)],
        [pltpu.VMEM((group + 1, columns, size), jnp.float32)],
        [neighbours, probe_vectors, *halo, own_far, near, started],
        sent_rows,
        6,
    )
    arrived = {tier: vec_send(array, tier) for tier, array in zip(away, sent)}
    kept = near_call(
        functools.partial(kept_kernel, share),
        [bf16(share, columns, size)],
        [pltpu.VMEM((group + 1, columns, size), jnp.float32)],
        [neighbours, far, vectors, near],
        share,
        12,
    )[0]

    pack_rows = share * rank + (share // 2) * rank
    pack, own_up = call(
        functools.partial(device_kernel, share, group, rank),
        (f32(pack_rows, size), f32(rank, total_columns)),
        [
            pltpu.VMEM((share, total_columns, size), jnp.bfloat16),
            pltpu.VMEM((share * rank, total_columns), jnp.float32),
        ],
        [kept]
        + [arrived[tier] for tier in range(1, parts)]
        + [leaf_pivots, leaf_inverse, local_pivots, local_inverse],
    )
    near_ups = [vec_send(own_up, tier) for tier in range(1, parts)]
    joined, own_up = call(
        functools.partial(group_kernel, share, group, rank),
        (f32(parts - 1, rank, 2 * rank), f32(rank, total_columns)),
        [pltpu.VMEM((parts * rank, total_columns), jnp.float32)],
        [own_up] + near_ups + [local_pivots, local_inverse],
    )

    later, own_up = lax.optimization_barrier((pack, own_up))
    late = LATE if parts > max(LATE) else ()
    others = [vec_send(later if tier in late else pack, tier) for tier in range(1, parts)]

    heap_first = 0
    maps = []
    for tier in range(UPL):
        last = tier == UPL - 1
        partner = lax.ppermute(own_up, "leaf", [(i, i ^ (1 << tier)) for i in range(leaf_total)])
        outs = (f32(rank, 2 * rank), f32(rank, total_columns))
        scratch = [pltpu.VMEM((2 * rank, total_columns), jnp.float32)]
        operands = [own_up, partner, upper_pivots, upper_inverse]
        if last:
            outs = (f32(UPL, rank, 2 * rank), f32(columns, rank))
            scratch.append(pltpu.VMEM((total_columns, rank), jnp.float32))
            operands += maps
        first, own_up = call(
            functools.partial(upper_kernel, tier, heap_first, last, rank),
            outs,
            scratch,
            operands,
            flops=ROUND_FLOPS,
        )
        maps.append(first)
        heap_first += leaf_total >> (tier + 1)
    leaf_map, local_map = call(
        functools.partial(place_kernel, share, group, rank),
        (f32(group, rank, size), f32(group - 1, rank, 2 * rank)),
        [],
        [pack] + others + [joined],
    )
    return (
        jnp.swapaxes(leaf_map, 1, 2),
        jnp.swapaxes(local_map, 1, 2),
        jnp.swapaxes(first, 1, 2)[None],
        own_up[None],
    )


def solution(mesh):
    placed = (
        P("leaf", None, None),
        P("leaf", "vec", None),
        P("leaf", None),
        P("leaf", None),
        P("leaf", None, None),
        P("leaf", None),
        P("leaf", None, None),
        P(),
        P(),
    )
    return jax.shard_map(
        on_device,
        mesh=mesh,
        in_specs=placed,
        out_specs=(
            P("leaf", None, None),
            P("leaf", None, None),
            P("leaf", None, None, None),
            P("leaf", "vec", None),
        ),
        check_vma=False,
    )
```

```python
import functools

import jax
import jax.numpy as jnp
from jax import lax
from jax.experimental import pallas as pl
from jax.experimental.pallas import tpu as pltpu
from jax.sharding import PartitionSpec as P

UPL = 3

SOFTEN = 0.0009
EPSILON = 1e-06
FLIGHT = 8
DEPTH = 128
CHUNK = 256
LATE = (2,)
ROUND_FLOPS = 400_000_000
VMEM_BYTES = 20 * 1024 * 1024
VMEM = pltpu.MemorySpace.VMEM
SMEM = pltpu.MemorySpace.SMEM


def nt(a, b):
    return lax.dot_general(a, b, (((1,), (1,)), ((), ())), preferred_element_type=jnp.float32)


def nn(a, b):
    return lax.dot_general(a, b, (((1,), (0,)), ((), ())), preferred_element_type=jnp.float32)


def split(a):
    high = a.astype(jnp.bfloat16)
    low = (a - high.astype(jnp.float32)).astype(jnp.bfloat16)
    return high, low


def stacked_split(a):
    high, low = split(a)
    return jnp.concatenate([high, low], axis=0)


def halves(a):
    rows = a.shape[0] // 2
    return a[:rows] + a[rows:]


def coordinates(points, extra):
    row = lax.broadcasted_iota(jnp.int32, (8, points.shape[1]), 0)
    padded = jnp.concatenate(
        [points, jnp.full((5, points.shape[1]), 0.5, jnp.float32)], axis=0
    )
    centred = padded - 0.5
    high, low = [part.astype(jnp.float32) for part in split(centred)]
    norm = jnp.sum(centred * centred, axis=0, keepdims=True) + extra
    first, rest = [part.astype(jnp.float32) for part in split(norm)]
    second, third = [part.astype(jnp.float32) for part in split(norm - first)]
    norms = jnp.where(row == 0, first, jnp.where(row == 1, second, jnp.where(row == 2, third, 0.0)))
    return high, low, norms, jnp.where(row < 3, 1.0, 0.0)


def far_features(points):
    high, low, norm, one = coordinates(points, SOFTEN)
    vacant = jnp.zeros((DEPTH - 48, points.shape[1]), jnp.float32)
    return jnp.concatenate(
        [-2.0 * high, -2.0 * low, -2.0 * high, -2.0 * low, one, norm, vacant], axis=0
    ).astype(jnp.bfloat16)


def near_features(points):
    high, low, norm, one = coordinates(points, 0.0)
    vacant = jnp.zeros((DEPTH - 48, points.shape[1]), jnp.float32)
    return jnp.transpose(
        jnp.concatenate([high, high, low, low, norm, one, vacant], axis=0)
    ).astype(jnp.bfloat16)


def add_blocks(share, tiers, base, wanted, nb_ref, far, vectors, near, total, tiles, codes):
    me = lax.axis_index("vec")
    count, slots = nb_ref.shape
    first = lax.axis_index("leaf") * count
    flight, size = tiles.shape[0], tiles.shape[1]
    columns = total.shape[1]
    idle = count * 64

    for way in range(flight):
        codes[way] = idle
    filled = jnp.int32(flight)
    for tier in tiers:
        for part in range(share):
            cluster = (me ^ tier) * share + part
            for slot in range(slots):
                listed = nb_ref[cluster, slot]
                position = listed - first + count
                codes[filled] = cluster * 64 + position - base
                filled += ((listed >= 0) & wanted(position, count)).astype(jnp.int32)
    for way in range(flight):
        codes[filled + way] = idle
    tiles[...] = jnp.zeros(tiles.shape, tiles.dtype)

    def multiply(code, tile):
        row = code // 64
        total[row] = total[row] + nt(vectors[code % 64, 0:columns, :], tile[...])

    def evaluate(code, tile):
        row = code // 64
        position = code % 64
        for top in range(0, size, CHUNK):
            distance = nn(near[row, top : top + CHUNK, :], far[position])
            tile[top : top + CHUNK, :] = lax.rsqrt(distance).astype(jnp.bfloat16)

    def step(index, carry):
        for way in range(flight):
            multiply(codes[index * flight + way], tiles.at[way])
            evaluate(codes[(index + 1) * flight + way], tiles.at[way])
        return carry

    steps = (filled - 1) // flight
    lax.fori_loop(0, steps, step, 0)
    for way in range(flight):
        multiply(codes[steps * flight + way], tiles.at[way])


def inside(position, count):
    return (position >= count) & (position < 2 * count)


def outside(position, count):
    return (position < count) | (position >= 2 * count)


def anywhere(position, count):
    return position >= 0


def own_kernel(share, tiers, nb_ref, joined, total, far, near, tiles, codes):
    count, columns = joined.shape[0], total.shape[1]
    for cluster in range(count):
        here = joined[cluster, columns:, :].astype(jnp.float32)[0:3]
        far[cluster] = far_features(here)
        near[cluster] = near_features(here)
    near[count] = near[0]
    total[...] = jnp.zeros(total.shape, total.dtype)
    add_blocks(share, tiers, count, inside, nb_ref, far, joined, near, total, tiles, codes)


def halo_kernel(share, tiers, nb_ref, joined, before, after, own_far, near, start, *refs):
    outs = refs[: len(tiers)]
    far, vectors, total, tiles, codes = refs[len(tiers) :]
    count, columns = joined.shape[0], start.shape[1]
    me = lax.axis_index("vec")
    for place, source in ((0, before), (2, after)):
        for cluster in range(count):
            far[place * count + cluster] = far_features(
                source[cluster, columns:, :].astype(jnp.float32)[0:3]
            )
        vectors[place * count : (place + 1) * count] = source[:, 0:columns, :]
    far[count : 2 * count] = own_far[...]
    vectors[count : 2 * count] = joined[:, 0:columns, :]
    total[...] = start[...]
    add_blocks(share, tiers, 0, outside, nb_ref, far, vectors, near, total, tiles, codes)
    for tier, out in zip(tiers, outs):
        part = total[pl.ds((me ^ tier) * share, share)]
        out[...] = (part * 0.015625).astype(out.dtype)


def kept_kernel(share, nb_ref, far, vectors, near, out, total, tiles, codes):
    mine = pl.ds(lax.axis_index("vec") * share, share)
    total[mine] = jnp.zeros((share,) + total.shape[1:], total.dtype)
    add_blocks(share, (0,), 0, anywhere, nb_ref, far, vectors, near, total, tiles, codes)
    out[...] = (total[mine] * 0.015625).astype(out.dtype)


def join_kernel(points, probe, joined):
    count, columns, size = probe.shape
    joined[:, 0:columns, :] = probe[...]
    vacant = jnp.zeros((joined.shape[1] - columns - 3, size), jnp.float32)
    for cluster in range(count):
        joined[cluster, columns:, :] = jnp.concatenate(
            [points[cluster].astype(jnp.float32), vacant], axis=0
        ).astype(joined.dtype)


def near_call(body, outs, scratch, operands, rows, per_row):
    nb, size = operands[0], outs[0].shape[-1]
    blocks = rows * per_row
    return pl.pallas_call(
        body,
        out_shape=outs,
        in_specs=[pl.BlockSpec(memory_space=SMEM)]
        + [pl.BlockSpec(memory_space=VMEM)] * (len(operands) - 1),
        out_specs=[pl.BlockSpec(memory_space=VMEM)] * len(outs),
        scratch_shapes=scratch
        + [
            pltpu.VMEM((FLIGHT, size, size), jnp.bfloat16),
            pltpu.SMEM((rows * nb.shape[1] + 2 * FLIGHT,), jnp.int32),
        ],
        compiler_params=pltpu.CompilerParams(vmem_limit_bytes=VMEM_BYTES),
        cost_estimate=pl.CostEstimate(
            flops=blocks * size * size * 256,
            bytes_accessed=sum(o.size * o.dtype.itemsize for o in operands),
            transcendentals=blocks * size * size,
        ),
    )(*operands)


def pivot_factor(pivots, inverse, width):
    chosen = (
        lax.broadcasted_iota(jnp.int32, (width, pivots.shape[1]), 0) == pivots
    ).astype(jnp.bfloat16)
    return nt(stacked_split(jnp.transpose(inverse)), chosen).astype(jnp.bfloat16)


def leaf_node(sketch, pivots, inverse):
    factor = pivot_factor(pivots, inverse, sketch.shape[1])
    wide = sketch.astype(jnp.float32)
    mean_sq = jnp.sum(wide * wide, keepdims=True) / (sketch.shape[0] * sketch.shape[1]) + EPSILON
    scale = 1.0 / (sketch.shape[0] * mean_sq)
    picked = halves(nt(factor, sketch))
    raw = halves(nn(stacked_split(picked), sketch))
    interp = raw * scale
    upward = halves(nt(stacked_split(raw), sketch)) * (scale * lax.rsqrt(mean_sq))
    return interp, upward


def tree_node(sketch, pivots, inverse):
    width, columns = sketch.shape
    factor = pivot_factor(pivots, inverse, width)
    mean_sq = jnp.sum(sketch * sketch, keepdims=True) / (width * columns) + EPSILON
    scale = 1.0 / (columns * mean_sq)
    parts = stacked_split(sketch)
    picked = halves(nn(jnp.concatenate([factor, factor], axis=1), parts))
    raw = halves(nt(stacked_split(picked), parts))
    raw = raw[:, :width] + raw[:, width:]
    interp = raw * scale
    both = stacked_split(raw)
    upward = halves(nn(jnp.concatenate([both, both], axis=1), parts)) * (scale * lax.rsqrt(mean_sq))
    return interp, upward


def device_kernel(
    share,
    group,
    rank,
    own,
    *refs,
):
    parts = group // share
    arrived = refs[: parts - 1]
    pivots, inverse, local_pivots, local_inverse, pack, up_out, sketch, ups = refs[parts - 1 :]
    me = lax.axis_index("vec")
    columns = own.shape[1]
    size = own.shape[2]
    for tier, piece in enumerate((own,) + tuple(arrived)):
        place = pl.ds(pl.multiple_of((me ^ tier) * columns, columns), columns)
        for cluster in range(share):
            sketch[cluster, place, :] = piece[cluster]
    for cluster in range(share):
        row = me * share + cluster
        interp, upward = leaf_node(sketch[cluster], pivots[pl.ds(row, 1), :], inverse[row])
        pack[cluster] = interp
        ups[cluster * rank : (cluster + 1) * rank, :] = upward
    level_first, nodes, packed = 0, share // 2, 0
    level_nodes = group // 2
    while nodes >= 1:
        results = []
        for node in range(nodes):
            row = level_first + me * nodes + node
            interp, upward = tree_node(
                ups[2 * node * rank : 2 * (node + 1) * rank, :],
                local_pivots[pl.ds(row, 1), :],
                local_inverse[row],
            )
            side = (packed % 2) * 2 * rank
            pack[share + packed // 2, :, side : side + 2 * rank] = interp
            results.append(upward)
            packed += 1
        for node, upward in enumerate(results):
            ups[node * rank : (node + 1) * rank, :] = upward
        level_first += level_nodes
        level_nodes //= 2
        nodes //= 2
    up_out[...] = ups[0:rank, :]


def group_kernel(share, group, rank, own, *refs):
    parts = group // share
    arrived = refs[: parts - 1]
    local_pivots, local_inverse, interps, up_out, ups = refs[parts - 1 :]
    me = lax.axis_index("vec")
    for tier, piece in enumerate((own,) + tuple(arrived)):
        ups[pl.ds(pl.multiple_of((me ^ tier) * rank, rank), rank), :] = piece[...]
    row = group - parts
    done = 0
    nodes = parts // 2
    while nodes >= 1:
        results = []
        for node in range(nodes):
            interp, upward = tree_node(
                ups[2 * node * rank : 2 * (node + 1) * rank, :],
                local_pivots[row : row + 1, :],
                local_inverse[row],
            )
            interps[done] = interp
            results.append(upward)
            row += 1
            done += 1
        for node, upward in enumerate(results):
            ups[node * rank : (node + 1) * rank, :] = upward
        nodes //= 2
    up_out[...] = ups[0:rank, :]


def upper_node(tier, heap_first, rank, own, arrived, pivots, inverse, ups):
    me = lax.axis_index("leaf")
    side = (me >> tier) & 1
    ups[pl.ds(pl.multiple_of(side * rank, rank), rank), :] = own[...]
    ups[pl.ds(pl.multiple_of((1 - side) * rank, rank), rank), :] = arrived[...]
    node = heap_first + (me >> (tier + 1))
    return tree_node(ups[...], pivots[pl.ds(node, 1), :], inverse[node])


def upper_kernel(tier, heap_first, rank, own, arrived, pivots, inverse, interp_out, up_out, ups):
    interp, upward = upper_node(tier, heap_first, rank, own, arrived, pivots, inverse, ups)
    interp_out[...] = interp
    up_out[...] = upward


def finish_kernel(tier, heap_first, share, group, rank, own, arrived, pivots, inverse, *refs):
    parts = group // share
    refs = list(refs)
    earlier = [refs.pop(0) for _ in range(tier)]
    packs = [refs.pop(0) for _ in range(parts)]
    joined, interps, top, leaf_out, local_out, ups, turned, sems = refs
    me = lax.axis_index("vec")
    copies = []

    def put(source, target):
        copies.append(pltpu.make_async_copy(source, target, sems.at[len(copies)]))
        copies[-1].start()

    for flip, piece in enumerate(packs):
        device = me ^ flip
        put(piece.at[0:share], leaf_out.at[pl.ds(device * share, share)])
        level_first, nodes, packed = 0, share // 2, 0
        level_nodes = group // 2
        while nodes >= 1:
            for node in range(nodes):
                side = (packed % 2) * 2 * rank
                put(
                    piece.at[share + packed // 2, :, side : side + 2 * rank],
                    local_out.at[level_first + device * nodes + node],
                )
                packed += 1
            level_first += level_nodes
            level_nodes //= 2
            nodes //= 2
    put(joined, local_out.at[group - parts : group - 1])

    interp, upward = upper_node(tier, heap_first, rank, own, arrived, pivots, inverse, ups)
    for index, ref in enumerate(earlier):
        interps[index] = ref[...]
    interps[tier] = interp
    turned[...] = jnp.transpose(upward)
    columns = top.shape[0]
    place = pl.multiple_of(me * columns, columns)
    top[...] = turned[pl.ds(place, columns), :]
    for copy in copies:
        copy.wait()


def call(body, outs, scratch, operands, flops=0, anywhere_in=0, anywhere_out=0):
    fixed = pl.BlockSpec(memory_space=VMEM)
    free = pl.BlockSpec(memory_space=pl.ANY)
    return pl.pallas_call(
        body,
        out_shape=outs,
        in_specs=[fixed] * (len(operands) - anywhere_in) + [free] * anywhere_in,
        out_specs=[fixed] * (len(outs) - anywhere_out) + [free] * anywhere_out,
        scratch_shapes=scratch,
        compiler_params=pltpu.CompilerParams(vmem_limit_bytes=VMEM_BYTES),
        cost_estimate=pl.CostEstimate(
            flops=flops, bytes_accessed=sum(o.size * o.dtype.itemsize for o in operands), transcendentals=0
        ),
    )(*operands)


def f32(*shape):
    return jax.ShapeDtypeStruct(shape, jnp.float32)


def on_device(
    points,
    probe_vectors,
    neighbours,
    leaf_pivots,
    leaf_inverse,
    local_pivots,
    local_inverse,
    upper_pivots,
    upper_inverse,
):
    group, columns, size = probe_vectors.shape
    rank = leaf_pivots.shape[1]
    leaf_total = lax.axis_size("leaf")
    parts = lax.axis_size("vec")
    share = group // parts
    total_columns = columns * parts

    up = [(i, i + 1) for i in range(leaf_total - 1)]
    down = [(j, i) for i, j in up]
    joined = call(
        join_kernel,
        [jax.ShapeDtypeStruct((group, columns + 16, size), jnp.bfloat16)],
        [],
        [points, probe_vectors],
    )[0]
    halo = (lax.ppermute(joined, "leaf", up), lax.ppermute(joined, "leaf", down))

    def vec_send(array, tier):
        return lax.ppermute(array, "vec", [(i, i ^ tier) for i in range(parts)])

    away = list(range(parts - 1, 0, -1))
    sent_rows = (parts - 1) * share

    def bf16(*shape):
        return jax.ShapeDtypeStruct(shape, jnp.bfloat16)

    started, own_far, near = near_call(
        functools.partial(own_kernel, share, away),
        [f32(group + 1, columns, size), bf16(group, DEPTH, size), bf16(group + 1, size, DEPTH)],
        [],
        [neighbours, joined],
        sent_rows,
        6,
    )
    *sent, far, vectors = near_call(
        functools.partial(halo_kernel, share, away),
        [bf16(share, columns, size)] * len(away)
        + [bf16(3 * group, DEPTH, size), bf16(3 * group, columns, size)],
        [pltpu.VMEM((group + 1, columns, size), jnp.float32)],
        [neighbours, joined, *halo, own_far, near, started],
        sent_rows,
        6,
    )
    arrived = {tier: vec_send(array, tier) for tier, array in zip(away, sent)}
    kept = near_call(
        functools.partial(kept_kernel, share),
        [bf16(share, columns, size)],
        [pltpu.VMEM((group + 1, columns, size), jnp.float32)],
        [neighbours, far, vectors, near],
        share,
        12,
    )[0]

    slabs = share + share // 2
    pack, own_up = call(
        functools.partial(device_kernel, share, group, rank),
        (f32(slabs, rank, size), f32(rank, total_columns)),
        [
            pltpu.VMEM((share, total_columns, size), jnp.bfloat16),
            pltpu.VMEM((share * rank, total_columns), jnp.float32),
        ],
        [kept]
        + [arrived[tier] for tier in range(1, parts)]
        + [leaf_pivots, leaf_inverse, local_pivots, local_inverse],
    )
    near_ups = [vec_send(own_up, tier) for tier in range(1, parts)]
    joined, own_up = call(
        functools.partial(group_kernel, share, group, rank),
        (f32(parts - 1, rank, 2 * rank), f32(rank, total_columns)),
        [pltpu.VMEM((parts * rank, total_columns), jnp.float32)],
        [own_up] + near_ups + [local_pivots, local_inverse],
    )

    later, own_up = lax.optimization_barrier((pack, own_up))
    late = LATE if parts > max(LATE) else ()
    others = [vec_send(later if tier in late else pack, tier) for tier in range(1, parts)]

    heap_first = 0
    maps = []
    for tier in range(UPL):
        partner = lax.ppermute(own_up, "leaf", [(i, i ^ (1 << tier)) for i in range(leaf_total)])
        operands = [own_up, partner, upper_pivots, upper_inverse]
        ups = pltpu.VMEM((2 * rank, total_columns), jnp.float32)
        if tier < UPL - 1:
            interp, own_up = call(
                functools.partial(upper_kernel, tier, heap_first, rank),
                [f32(rank, 2 * rank), f32(rank, total_columns)],
                [ups],
                operands,
                flops=ROUND_FLOPS,
            )
            maps.append(interp)
            heap_first += leaf_total >> (tier + 1)
    upper_map, top, leaf_map, local_map = call(
        functools.partial(finish_kernel, UPL - 1, heap_first, share, group, rank),
        [
            f32(UPL, rank, 2 * rank),
            f32(columns, rank),
            f32(group, rank, size),
            f32(group - 1, rank, 2 * rank),
        ],
        [
            ups,
            pltpu.VMEM((total_columns, rank), jnp.float32),
            pltpu.SemaphoreType.DMA((parts * share + 1,)),
        ],
        operands + maps + [pack] + others + [joined],
        flops=ROUND_FLOPS,
        anywhere_in=parts + 1,
        anywhere_out=2,
    )
    return (
        jnp.swapaxes(leaf_map, 1, 2),
        jnp.swapaxes(local_map, 1, 2),
        jnp.swapaxes(upper_map, 1, 2)[None],
        top[None],
    )


def solution(mesh):
    placed = (
        P("leaf", None, None),
        P("leaf", "vec", None),
        P("leaf", None),
        P("leaf", None),
        P("leaf", None, None),
        P("leaf", None),
        P("leaf", None, None),
        P(),
        P(),
    )
    return jax.shard_map(
        on_device,
        mesh=mesh,
        in_specs=placed,
        out_specs=(
            P("leaf", None, None),
            P("leaf", None, None),
            P("leaf", None, None, None),
            P("leaf", "vec", None),
        ),
        check_vma=False,
    )
```

```python
import functools

import jax
import jax.numpy as jnp
from jax import lax
from jax.experimental import pallas as pl
from jax.experimental.pallas import tpu as pltpu
from jax.sharding import PartitionSpec as P

UPL = 3

SOFTEN = 0.0009
EPSILON = 1e-06
FLIGHT = 8
DEPTH = 128
CHUNK = 256
LATE = (2,)
ROUND_FLOPS = 400_000_000
VMEM_BYTES = 20 * 1024 * 1024
VMEM = pltpu.MemorySpace.VMEM


def nt(a, b):
    return lax.dot_general(a, b, (((1,), (1,)), ((), ())), preferred_element_type=jnp.float32)


def nn(a, b):
    return lax.dot_general(a, b, (((1,), (0,)), ((), ())), preferred_element_type=jnp.float32)


def split(a):
    high = a.astype(jnp.bfloat16)
    low = (a - high.astype(jnp.float32)).astype(jnp.bfloat16)
    return high, low


def stacked_split(a):
    high, low = split(a)
    return jnp.concatenate([high, low], axis=0)


def halves(a):
    rows = a.shape[0] // 2
    return a[:rows] + a[rows:]


def coordinates(points, extra):
    row = lax.broadcasted_iota(jnp.int32, (8, points.shape[1]), 0)
    padded = jnp.concatenate(
        [points, jnp.full((5, points.shape[1]), 0.5, jnp.float32)], axis=0
    )
    centred = padded - 0.5
    high, low = [part.astype(jnp.float32) for part in split(centred)]
    norm = jnp.sum(centred * centred, axis=0, keepdims=True) + extra
    first, rest = [part.astype(jnp.float32) for part in split(norm)]
    second, third = [part.astype(jnp.float32) for part in split(norm - first)]
    norms = jnp.where(row == 0, first, jnp.where(row == 1, second, jnp.where(row == 2, third, 0.0)))
    return high, low, norms, jnp.where(row < 3, 1.0, 0.0)


def far_features(points):
    high, low, norm, one = coordinates(points, SOFTEN)
    vacant = jnp.zeros((DEPTH - 48, points.shape[1]), jnp.float32)
    return jnp.concatenate(
        [-2.0 * high, -2.0 * low, -2.0 * high, -2.0 * low, one, norm, vacant], axis=0
    ).astype(jnp.bfloat16)


def near_features(points):
    high, low, norm, one = coordinates(points, 0.0)
    vacant = jnp.zeros((DEPTH - 48, points.shape[1]), jnp.float32)
    return jnp.transpose(
        jnp.concatenate([high, high, low, low, norm, one, vacant], axis=0)
    ).astype(jnp.bfloat16)


def add_blocks(share, tiers, base, wanted, lists, far, vectors, near, total, tiles, codes):
    lists.wait()
    nb_ref = lists.dst_ref
    me = lax.axis_index("vec")
    count, slots = nb_ref.shape
    first = lax.axis_index("leaf") * count
    flight, size = tiles.shape[0], tiles.shape[1]
    columns = total.shape[2]
    idle = count * 64

    for way in range(flight):
        codes[way] = idle
    filled = jnp.int32(flight)
    for tier in tiers:
        for part in range(share):
            cluster = (me ^ tier) * share + part
            for slot in range(slots):
                listed = nb_ref[cluster, slot]
                position = listed - first + count
                codes[filled] = cluster * 64 + position - base
                filled += ((listed >= 0) & wanted(position, count)).astype(jnp.int32)
    for way in range(flight):
        codes[filled + way] = idle
    tiles[...] = jnp.zeros(tiles.shape, tiles.dtype)

    def multiply(code, tile):
        row = code // 64
        total[row] = total[row] + nt(tile[...], vectors[code % 64, 0:columns, :])

    def evaluate(code, tile):
        row = code // 64
        position = code % 64
        for top in range(0, size, CHUNK):
            distance = nn(near[row, top : top + CHUNK, :], far[position])
            tile[top : top + CHUNK, :] = lax.rsqrt(distance).astype(jnp.bfloat16)

    def step(index, carry):
        for way in range(flight):
            multiply(codes[index * flight + way], tiles.at[way])
            evaluate(codes[(index + 1) * flight + way], tiles.at[way])
        return carry

    steps = (filled - 1) // flight
    lax.fori_loop(0, steps, step, 0)
    for way in range(flight):
        multiply(codes[steps * flight + way], tiles.at[way])


def finished(total, dtype):
    return jnp.transpose(total * 0.015625).astype(dtype)


def inside(position, count):
    return (position >= count) & (position < 2 * count)


def outside(position, count):
    return (position < count) | (position >= 2 * count)


def anywhere(position, count):
    return position >= 0


def read_lists(nb, nb_ref, sem):
    copy = pltpu.make_async_copy(nb, nb_ref, sem)
    copy.start()
    return copy


def own_kernel(share, tiers, nb, joined, total, far, near, tiles, codes, nb_ref, sem):
    lists = read_lists(nb, nb_ref, sem)
    count, columns = joined.shape[0], total.shape[2]
    for cluster in range(count):
        here = joined[cluster, columns:, :].astype(jnp.float32)[0:3]
        far[cluster] = far_features(here)
        near[cluster] = near_features(here)
    near[count] = near[0]
    total[...] = jnp.zeros(total.shape, total.dtype)
    add_blocks(share, tiers, count, inside, lists, far, joined, near, total, tiles, codes)


def halo_kernel(share, tiers, nb, joined, before, after, own_far, near, start, *refs):
    outs = refs[: len(tiers)]
    far, vectors, total, tiles, codes, nb_ref, sem = refs[len(tiers) :]
    lists = read_lists(nb, nb_ref, sem)
    count, columns = joined.shape[0], start.shape[2]
    me = lax.axis_index("vec")
    for place, source in ((0, before), (2, after)):
        for cluster in range(count):
            far[place * count + cluster] = far_features(
                source[cluster, columns:, :].astype(jnp.float32)[0:3]
            )
        vectors[place * count : (place + 1) * count] = source[:, 0:columns, :]
    far[count : 2 * count] = own_far[...]
    vectors[count : 2 * count] = joined[:, 0:columns, :]
    total[...] = start[...]
    add_blocks(share, tiers, 0, outside, lists, far, vectors, near, total, tiles, codes)
    for tier, out in zip(tiers, outs):
        for part in range(share):
            out[part] = finished(total[(me ^ tier) * share + part], out.dtype)


def kept_kernel(share, nb, far, vectors, near, out, total, tiles, codes, nb_ref, sem):
    lists = read_lists(nb, nb_ref, sem)
    first = lax.axis_index("vec") * share
    total[pl.ds(first, share)] = jnp.zeros((share,) + total.shape[1:], total.dtype)
    add_blocks(share, (0,), 0, anywhere, lists, far, vectors, near, total, tiles, codes)
    for part in range(share):
        out[part] = finished(total[first + part], out.dtype)


def join_kernel(points, probe, joined):
    count, columns, size = probe.shape
    joined[:, 0:columns, :] = probe[...]
    vacant = jnp.zeros((joined.shape[1] - columns - 3, size), jnp.float32)
    for cluster in range(count):
        joined[cluster, columns:, :] = jnp.concatenate(
            [points[cluster].astype(jnp.float32), vacant], axis=0
        ).astype(joined.dtype)


def near_call(body, outs, scratch, operands, size, rows, per_row):
    nb = operands[0]
    blocks = rows * per_row
    return pl.pallas_call(
        body,
        out_shape=outs,
        in_specs=[pl.BlockSpec(memory_space=pl.ANY)]
        + [pl.BlockSpec(memory_space=VMEM)] * (len(operands) - 1),
        out_specs=[pl.BlockSpec(memory_space=VMEM)] * len(outs),
        scratch_shapes=scratch
        + [
            pltpu.VMEM((FLIGHT, size, size), jnp.bfloat16),
            pltpu.SMEM((rows * nb.shape[1] + 2 * FLIGHT,), jnp.int32),
            pltpu.SMEM(nb.shape, jnp.int32),
            pltpu.SemaphoreType.DMA,
        ],
        compiler_params=pltpu.CompilerParams(vmem_limit_bytes=VMEM_BYTES),
        cost_estimate=pl.CostEstimate(
            flops=blocks * size * size * 256,
            bytes_accessed=sum(o.size * o.dtype.itemsize for o in operands),
            transcendentals=blocks * size * size,
        ),
    )(*operands)


def pivot_factor(pivots, inverse, width):
    chosen = (
        lax.broadcasted_iota(jnp.int32, (width, pivots.shape[1]), 0) == pivots
    ).astype(jnp.bfloat16)
    return nt(stacked_split(jnp.transpose(inverse)), chosen).astype(jnp.bfloat16)


def leaf_node(sketch, pivots, inverse):
    factor = pivot_factor(pivots, inverse, sketch.shape[1])
    wide = sketch.astype(jnp.float32)
    mean_sq = jnp.sum(wide * wide, keepdims=True) / (sketch.shape[0] * sketch.shape[1]) + EPSILON
    scale = 1.0 / (sketch.shape[0] * mean_sq)
    picked = halves(nt(factor, sketch))
    raw = halves(nn(stacked_split(picked), sketch))
    interp = raw * scale
    upward = halves(nt(stacked_split(raw), sketch)) * (scale * lax.rsqrt(mean_sq))
    return interp, upward


def tree_node(sketch, pivots, inverse):
    width, columns = sketch.shape
    factor = pivot_factor(pivots, inverse, width)
    mean_sq = jnp.sum(sketch * sketch, keepdims=True) / (width * columns) + EPSILON
    scale = 1.0 / (columns * mean_sq)
    parts = stacked_split(sketch)
    picked = halves(nn(jnp.concatenate([factor, factor], axis=1), parts))
    raw = halves(nt(stacked_split(picked), parts))
    raw = raw[:, :width] + raw[:, width:]
    interp = raw * scale
    both = stacked_split(raw)
    upward = halves(nn(jnp.concatenate([both, both], axis=1), parts)) * (scale * lax.rsqrt(mean_sq))
    return interp, upward


def device_kernel(
    share,
    group,
    rank,
    own,
    *refs,
):
    parts = group // share
    arrived = refs[: parts - 1]
    pivots, inverse, local_pivots, local_inverse, pack, up_out, sketch, ups = refs[parts - 1 :]
    me = lax.axis_index("vec")
    columns = own.shape[1]
    size = own.shape[2]
    for tier, piece in enumerate((own,) + tuple(arrived)):
        place = pl.ds(pl.multiple_of((me ^ tier) * columns, columns), columns)
        for cluster in range(share):
            sketch[cluster, place, :] = piece[cluster]
    for cluster in range(share):
        row = me * share + cluster
        interp, upward = leaf_node(sketch[cluster], pivots[pl.ds(row, 1), :], inverse[row])
        pack[cluster] = interp
        ups[cluster * rank : (cluster + 1) * rank, :] = upward
    level_first, nodes, packed = 0, share // 2, 0
    level_nodes = group // 2
    while nodes >= 1:
        results = []
        for node in range(nodes):
            row = level_first + me * nodes + node
            interp, upward = tree_node(
                ups[2 * node * rank : 2 * (node + 1) * rank, :],
                local_pivots[pl.ds(row, 1), :],
                local_inverse[row],
            )
            side = (packed % 2) * 2 * rank
            pack[share + packed // 2, :, side : side + 2 * rank] = interp
            results.append(upward)
            packed += 1
        for node, upward in enumerate(results):
            ups[node * rank : (node + 1) * rank, :] = upward
        level_first += level_nodes
        level_nodes //= 2
        nodes //= 2
    up_out[...] = ups[0:rank, :]


def group_kernel(share, group, rank, own, *refs):
    parts = group // share
    arrived = refs[: parts - 1]
    local_pivots, local_inverse, interps, up_out, ups = refs[parts - 1 :]
    me = lax.axis_index("vec")
    for tier, piece in enumerate((own,) + tuple(arrived)):
        ups[pl.ds(pl.multiple_of((me ^ tier) * rank, rank), rank), :] = piece[...]
    row = group - parts
    done = 0
    nodes = parts // 2
    while nodes >= 1:
        results = []
        for node in range(nodes):
            interp, upward = tree_node(
                ups[2 * node * rank : 2 * (node + 1) * rank, :],
                local_pivots[row : row + 1, :],
                local_inverse[row],
            )
            interps[done] = interp
            results.append(upward)
            row += 1
            done += 1
        for node, upward in enumerate(results):
            ups[node * rank : (node + 1) * rank, :] = upward
        nodes //= 2
    up_out[...] = ups[0:rank, :]


def upper_node(tier, heap_first, rank, own, arrived, pivots, inverse, ups):
    me = lax.axis_index("leaf")
    side = (me >> tier) & 1
    ups[pl.ds(pl.multiple_of(side * rank, rank), rank), :] = own[...]
    ups[pl.ds(pl.multiple_of((1 - side) * rank, rank), rank), :] = arrived[...]
    node = heap_first + (me >> (tier + 1))
    return tree_node(ups[...], pivots[pl.ds(node, 1), :], inverse[node])


def upper_kernel(tier, heap_first, rank, own, arrived, pivots, inverse, interp_out, up_out, ups):
    interp, upward = upper_node(tier, heap_first, rank, own, arrived, pivots, inverse, ups)
    interp_out[...] = interp
    up_out[...] = upward


def finish_kernel(tier, heap_first, share, group, rank, own, arrived, pivots, inverse, *refs):
    parts = group // share
    refs = list(refs)
    earlier = [refs.pop(0) for _ in range(tier)]
    packs = [refs.pop(0) for _ in range(parts)]
    joined, interps, top, leaf_out, local_out, ups, turned, sems = refs
    me = lax.axis_index("vec")
    copies = []

    def put(source, target):
        copies.append(pltpu.make_async_copy(source, target, sems.at[len(copies)]))
        copies[-1].start()

    for flip, piece in enumerate(packs):
        device = me ^ flip
        put(piece.at[0:share], leaf_out.at[pl.ds(device * share, share)])
        level_first, nodes, packed = 0, share // 2, 0
        level_nodes = group // 2
        while nodes >= 1:
            for node in range(nodes):
                side = (packed % 2) * 2 * rank
                put(
                    piece.at[share + packed // 2, :, side : side + 2 * rank],
                    local_out.at[level_first + device * nodes + node],
                )
                packed += 1
            level_first += level_nodes
            level_nodes //= 2
            nodes //= 2
    put(joined, local_out.at[group - parts : group - 1])

    interp, upward = upper_node(tier, heap_first, rank, own, arrived, pivots, inverse, ups)
    for index, ref in enumerate(earlier):
        interps[index] = ref[...]
    interps[tier] = interp
    turned[...] = jnp.transpose(upward)
    columns = top.shape[0]
    place = pl.multiple_of(me * columns, columns)
    top[...] = turned[pl.ds(place, columns), :]
    for copy in copies:
        copy.wait()


def call(body, outs, scratch, operands, flops=0, anywhere_in=0, anywhere_out=0):
    fixed = pl.BlockSpec(memory_space=VMEM)
    free = pl.BlockSpec(memory_space=pl.ANY)
    return pl.pallas_call(
        body,
        out_shape=outs,
        in_specs=[fixed] * (len(operands) - anywhere_in) + [free] * anywhere_in,
        out_specs=[fixed] * (len(outs) - anywhere_out) + [free] * anywhere_out,
        scratch_shapes=scratch,
        compiler_params=pltpu.CompilerParams(vmem_limit_bytes=VMEM_BYTES),
        cost_estimate=pl.CostEstimate(
            flops=flops, bytes_accessed=sum(o.size * o.dtype.itemsize for o in operands), transcendentals=0
        ),
    )(*operands)


def f32(*shape):
    return jax.ShapeDtypeStruct(shape, jnp.float32)


def on_device(
    points,
    probe_vectors,
    neighbours,
    leaf_pivots,
    leaf_inverse,
    local_pivots,
    local_inverse,
    upper_pivots,
    upper_inverse,
):
    group, columns, size = probe_vectors.shape
    rank = leaf_pivots.shape[1]
    leaf_total = lax.axis_size("leaf")
    parts = lax.axis_size("vec")
    share = group // parts
    total_columns = columns * parts

    up = [(i, i + 1) for i in range(leaf_total - 1)]
    down = [(j, i) for i, j in up]
    joined = call(
        join_kernel,
        [jax.ShapeDtypeStruct((group, columns + 16, size), jnp.bfloat16)],
        [],
        [points, probe_vectors],
    )[0]
    halo = (lax.ppermute(joined, "leaf", up), lax.ppermute(joined, "leaf", down))

    def vec_send(array, tier):
        return lax.ppermute(array, "vec", [(i, i ^ tier) for i in range(parts)])

    away = list(range(parts - 1, 0, -1))
    sent_rows = (parts - 1) * share

    def bf16(*shape):
        return jax.ShapeDtypeStruct(shape, jnp.bfloat16)

    started, own_far, near = near_call(
        functools.partial(own_kernel, share, away),
        [f32(group + 1, size, columns), bf16(group, DEPTH, size), bf16(group + 1, size, DEPTH)],
        [],
        [neighbours, joined],
        size,
        sent_rows,
        6,
    )
    *sent, far, vectors = near_call(
        functools.partial(halo_kernel, share, away),
        [bf16(share, columns, size)] * len(away)
        + [bf16(3 * group, DEPTH, size), bf16(3 * group, columns, size)],
        [pltpu.VMEM((group + 1, size, columns), jnp.float32)],
        [neighbours, joined, *halo, own_far, near, started],
        size,
        sent_rows,
        6,
    )
    arrived = {tier: vec_send(array, tier) for tier, array in zip(away, sent)}
    kept = near_call(
        functools.partial(kept_kernel, share),
        [bf16(share, columns, size)],
        [pltpu.VMEM((group + 1, size, columns), jnp.float32)],
        [neighbours, far, vectors, near],
        size,
        share,
        12,
    )[0]

    slabs = share + share // 2
    pack, own_up = call(
        functools.partial(device_kernel, share, group, rank),
        (f32(slabs, rank, size), f32(rank, total_columns)),
        [
            pltpu.VMEM((share, total_columns, size), jnp.bfloat16),
            pltpu.VMEM((share * rank, total_columns), jnp.float32),
        ],
        [kept]
        + [arrived[tier] for tier in range(1, parts)]
        + [leaf_pivots, leaf_inverse, local_pivots, local_inverse],
    )
    near_ups = [vec_send(own_up, tier) for tier in range(1, parts)]
    joined, own_up = call(
        functools.partial(group_kernel, share, group, rank),
        (f32(parts - 1, rank, 2 * rank), f32(rank, total_columns)),
        [pltpu.VMEM((parts * rank, total_columns), jnp.float32)],
        [own_up] + near_ups + [local_pivots, local_inverse],
    )

    later, own_up = lax.optimization_barrier((pack, own_up))
    late = LATE if parts > max(LATE) else ()
    others = [vec_send(later if tier in late else pack, tier) for tier in range(1, parts)]

    heap_first = 0
    maps = []
    for tier in range(UPL):
        partner = lax.ppermute(own_up, "leaf", [(i, i ^ (1 << tier)) for i in range(leaf_total)])
        operands = [own_up, partner, upper_pivots, upper_inverse]
        ups = pltpu.VMEM((2 * rank, total_columns), jnp.float32)
        if tier < UPL - 1:
            interp, own_up = call(
                functools.partial(upper_kernel, tier, heap_first, rank),
                [f32(rank, 2 * rank), f32(rank, total_columns)],
                [ups],
                operands,
                flops=ROUND_FLOPS,
            )
            maps.append(interp)
            heap_first += leaf_total >> (tier + 1)
    upper_map, top, leaf_map, local_map = call(
        functools.partial(finish_kernel, UPL - 1, heap_first, share, group, rank),
        [
            f32(UPL, rank, 2 * rank),
            f32(columns, rank),
            f32(group, rank, size),
            f32(group - 1, rank, 2 * rank),
        ],
        [
            ups,
            pltpu.VMEM((total_columns, rank), jnp.float32),
            pltpu.SemaphoreType.DMA((parts * share + 1,)),
        ],
        operands + maps + [pack] + others + [joined],
        flops=ROUND_FLOPS,
        anywhere_in=parts + 1,
        anywhere_out=2,
    )
    return (
        jnp.swapaxes(leaf_map, 1, 2),
        jnp.swapaxes(local_map, 1, 2),
        jnp.swapaxes(upper_map, 1, 2)[None],
        top[None],
    )


def solution(mesh):
    placed = (
        P("leaf", None, None),
        P("leaf", "vec", None),
        P("leaf", None),
        P("leaf", None),
        P("leaf", None, None),
        P("leaf", None),
        P("leaf", None, None),
        P(),
        P(),
    )
    return jax.shard_map(
        on_device,
        mesh=mesh,
        in_specs=placed,
        out_specs=(
            P("leaf", None, None),
            P("leaf", None, None),
            P("leaf", None, None, None),
            P("leaf", "vec", None),
        ),
        check_vma=False,
    )
```

```python
import functools

import jax
import jax.numpy as jnp
from jax import lax
from jax.experimental import pallas as pl
from jax.experimental.pallas import tpu as pltpu
from jax.sharding import PartitionSpec as P

UPL = 3

SOFTEN = 0.0009
EPSILON = 1e-06
FLIGHT = 8
DEPTH = 64
CHUNK = 256
LATE = (2,)
ROUND_FLOPS = 400_000_000
VMEM_BYTES = 20 * 1024 * 1024
VMEM = pltpu.MemorySpace.VMEM


def nt(a, b):
    return lax.dot_general(a, b, (((1,), (1,)), ((), ())), preferred_element_type=jnp.float32)


def nn(a, b):
    return lax.dot_general(a, b, (((1,), (0,)), ((), ())), preferred_element_type=jnp.float32)


def split(a):
    high = a.astype(jnp.bfloat16)
    low = (a - high.astype(jnp.float32)).astype(jnp.bfloat16)
    return high, low


def stacked_split(a):
    high, low = split(a)
    return jnp.concatenate([high, low], axis=0)


def halves(a):
    rows = a.shape[0] // 2
    return a[:rows] + a[rows:]


def coordinates(points, extra):
    row = lax.broadcasted_iota(jnp.int32, (8, points.shape[1]), 0)
    padded = jnp.concatenate(
        [points, jnp.full((5, points.shape[1]), 0.5, jnp.float32)], axis=0
    )
    centred = padded - 0.5
    high, low = [part.astype(jnp.float32) for part in split(centred)]
    norm = jnp.sum(centred * centred, axis=0, keepdims=True) + extra
    first, rest = [part.astype(jnp.float32) for part in split(norm)]
    second, third = [part.astype(jnp.float32) for part in split(norm - first)]
    norms = jnp.where(row == 0, first, jnp.where(row == 1, second, jnp.where(row == 2, third, 0.0)))
    return high, low, norms, jnp.where(row < 3, 1.0, 0.0)


def far_features(points):
    high, low, norm, one = coordinates(points, SOFTEN)
    vacant = jnp.zeros((DEPTH - 48, points.shape[1]), jnp.float32)
    return jnp.concatenate(
        [-2.0 * high, -2.0 * low, -2.0 * high, -2.0 * low, one, norm, vacant], axis=0
    ).astype(jnp.bfloat16)


def near_features(points):
    high, low, norm, one = coordinates(points, 0.0)
    vacant = jnp.zeros((DEPTH - 48, points.shape[1]), jnp.float32)
    return jnp.transpose(
        jnp.concatenate([high, high, low, low, norm, one, vacant], axis=0)
    ).astype(jnp.bfloat16)


def add_blocks(share, tiers, base, wanted, lists, far, vectors, near, total, tiles, codes):
    lists.wait()
    nb_ref = lists.dst_ref
    me = lax.axis_index("vec")
    count, slots = nb_ref.shape
    first = lax.axis_index("leaf") * count
    flight, size = tiles.shape[0], tiles.shape[1]
    columns = total.shape[1]
    idle = count * 64

    for way in range(flight):
        codes[way] = idle
    filled = jnp.int32(flight)
    for tier in tiers:
        for part in range(share):
            cluster = (me ^ tier) * share + part
            for slot in range(slots):
                listed = nb_ref[cluster, slot]
                position = listed - first + count
                codes[filled] = cluster * 64 + position - base
                filled += ((listed >= 0) & wanted(position, count)).astype(jnp.int32)
    for way in range(flight):
        codes[filled + way] = idle
    tiles[...] = jnp.zeros(tiles.shape, tiles.dtype)

    def multiply(code, tile):
        row = code // 64
        total[row] = total[row] + nt(vectors[code % 64, 0:columns, :], tile[...])

    def evaluate(code, tile):
        row = code // 64
        position = code % 64
        for top in range(0, size, CHUNK):
            distance = nn(near[row, top : top + CHUNK, :], far[position])
            tile[top : top + CHUNK, :] = lax.rsqrt(distance).astype(jnp.bfloat16)

    def step(index, carry):
        for way in range(flight):
            multiply(codes[index * flight + way], tiles.at[way])
            evaluate(codes[(index + 1) * flight + way], tiles.at[way])
        return carry

    steps = (filled - 1) // flight
    lax.fori_loop(0, steps, step, 0)
    for way in range(flight):
        multiply(codes[steps * flight + way], tiles.at[way])


def finished(total, dtype):
    return (total * 0.015625).astype(dtype)


def inside(position, count):
    return (position >= count) & (position < 2 * count)


def outside(position, count):
    return (position < count) | (position >= 2 * count)


def anywhere(position, count):
    return position >= 0


def read_lists(nb, nb_ref, sem):
    copy = pltpu.make_async_copy(nb, nb_ref, sem)
    copy.start()
    return copy


def own_kernel(share, tiers, nb, joined, total, far, near, tiles, codes, nb_ref, sem):
    lists = read_lists(nb, nb_ref, sem)
    count, columns = joined.shape[0], total.shape[1]
    for cluster in range(count):
        here = joined[cluster, columns:, :].astype(jnp.float32)[0:3]
        far[cluster] = far_features(here)
        near[cluster] = near_features(here)
    near[count] = near[0]
    total[...] = jnp.zeros(total.shape, total.dtype)
    add_blocks(share, tiers, count, inside, lists, far, joined, near, total, tiles, codes)


def halo_kernel(share, tiers, nb, joined, before, after, own_far, near, start, *refs):
    outs = refs[: len(tiers)]
    far, vectors, total, tiles, codes, nb_ref, sem = refs[len(tiers) :]
    lists = read_lists(nb, nb_ref, sem)
    count, columns = joined.shape[0], start.shape[1]
    me = lax.axis_index("vec")
    for place, source in ((0, before), (2, after)):
        for cluster in range(count):
            far[place * count + cluster] = far_features(
                source[cluster, columns:, :].astype(jnp.float32)[0:3]
            )
        vectors[place * count : (place + 1) * count] = source[:, 0:columns, :]
    far[count : 2 * count] = own_far[...]
    vectors[count : 2 * count] = joined[:, 0:columns, :]
    total[...] = start[...]
    add_blocks(share, tiers, 0, outside, lists, far, vectors, near, total, tiles, codes)
    for tier, out in zip(tiers, outs):
        for part in range(share):
            out[part] = finished(total[(me ^ tier) * share + part], out.dtype)


def kept_kernel(share, nb, far, vectors, near, out, total, tiles, codes, nb_ref, sem):
    lists = read_lists(nb, nb_ref, sem)
    first = lax.axis_index("vec") * share
    total[pl.ds(first, share)] = jnp.zeros((share,) + total.shape[1:], total.dtype)
    add_blocks(share, (0,), 0, anywhere, lists, far, vectors, near, total, tiles, codes)
    for part in range(share):
        out[part] = finished(total[first + part], out.dtype)


def join_kernel(points, probe, joined):
    count, columns, size = probe.shape
    joined[:, 0:columns, :] = probe[...]
    vacant = jnp.zeros((joined.shape[1] - columns - 3, size), jnp.float32)
    for cluster in range(count):
        joined[cluster, columns:, :] = jnp.concatenate(
            [points[cluster].astype(jnp.float32), vacant], axis=0
        ).astype(joined.dtype)


def near_call(body, outs, scratch, operands, size, rows, per_row):
    nb = operands[0]
    blocks = rows * per_row
    return pl.pallas_call(
        body,
        out_shape=outs,
        in_specs=[pl.BlockSpec(memory_space=pl.ANY)]
        + [pl.BlockSpec(memory_space=VMEM)] * (len(operands) - 1),
        out_specs=[pl.BlockSpec(memory_space=VMEM)] * len(outs),
        scratch_shapes=scratch
        + [
            pltpu.VMEM((FLIGHT, size, size), jnp.bfloat16),
            pltpu.SMEM((rows * nb.shape[1] + 2 * FLIGHT,), jnp.int32),
            pltpu.SMEM(nb.shape, jnp.int32),
            pltpu.SemaphoreType.DMA,
        ],
        compiler_params=pltpu.CompilerParams(vmem_limit_bytes=VMEM_BYTES),
        cost_estimate=pl.CostEstimate(
            flops=blocks * size * size * 256,
            bytes_accessed=sum(o.size * o.dtype.itemsize for o in operands),
            transcendentals=blocks * size * size,
        ),
    )(*operands)


def pivot_factor(pivots, inverse, width):
    chosen = (
        lax.broadcasted_iota(jnp.int32, (width, pivots.shape[1]), 0) == pivots
    ).astype(jnp.bfloat16)
    return nt(stacked_split(jnp.transpose(inverse)), chosen).astype(jnp.bfloat16)


def leaf_node(sketch, pivots, inverse):
    factor = pivot_factor(pivots, inverse, sketch.shape[1])
    wide = sketch.astype(jnp.float32)
    mean_sq = jnp.sum(wide * wide, keepdims=True) / (sketch.shape[0] * sketch.shape[1]) + EPSILON
    scale = 1.0 / (sketch.shape[0] * mean_sq)
    picked = halves(nt(factor, sketch))
    raw = halves(nn(stacked_split(picked), sketch))
    interp = raw * scale
    upward = halves(nt(stacked_split(raw), sketch)) * (scale * lax.rsqrt(mean_sq))
    return interp, upward


def tree_node(sketch, pivots, inverse):
    width, columns = sketch.shape
    factor = pivot_factor(pivots, inverse, width)
    mean_sq = jnp.sum(sketch * sketch, keepdims=True) / (width * columns) + EPSILON
    scale = 1.0 / (columns * mean_sq)
    parts = stacked_split(sketch)
    picked = halves(nn(jnp.concatenate([factor, factor], axis=1), parts))
    raw = halves(nt(stacked_split(picked), parts))
    raw = raw[:, :width] + raw[:, width:]
    interp = raw * scale
    both = stacked_split(raw)
    upward = halves(nn(jnp.concatenate([both, both], axis=1), parts)) * (scale * lax.rsqrt(mean_sq))
    return interp, upward


def device_kernel(
    share,
    group,
    rank,
    own,
    *refs,
):
    parts = group // share
    arrived = refs[: parts - 1]
    pivots, inverse, local_pivots, local_inverse, pack, up_out, sketch, ups = refs[parts - 1 :]
    me = lax.axis_index("vec")
    columns = own.shape[1]
    size = own.shape[2]
    for tier, piece in enumerate((own,) + tuple(arrived)):
        place = pl.ds(pl.multiple_of((me ^ tier) * columns, columns), columns)
        for cluster in range(share):
            sketch[cluster, place, :] = piece[cluster]
    for cluster in range(share):
        row = me * share + cluster
        interp, upward = leaf_node(sketch[cluster], pivots[pl.ds(row, 1), :], inverse[row])
        pack[cluster] = interp
        ups[cluster * rank : (cluster + 1) * rank, :] = upward
    level_first, nodes, packed = 0, share // 2, 0
    level_nodes = group // 2
    while nodes >= 1:
        results = []
        for node in range(nodes):
            row = level_first + me * nodes + node
            interp, upward = tree_node(
                ups[2 * node * rank : 2 * (node + 1) * rank, :],
                local_pivots[pl.ds(row, 1), :],
                local_inverse[row],
            )
            side = (packed % 2) * 2 * rank
            pack[share + packed // 2, :, side : side + 2 * rank] = interp
            results.append(upward)
            packed += 1
        for node, upward in enumerate(results):
            ups[node * rank : (node + 1) * rank, :] = upward
        level_first += level_nodes
        level_nodes //= 2
        nodes //= 2
    up_out[...] = ups[0:rank, :]


def group_kernel(share, group, rank, own, *refs):
    parts = group // share
    arrived = refs[: parts - 1]
    local_pivots, local_inverse, interps, up_out, ups = refs[parts - 1 :]
    me = lax.axis_index("vec")
    for tier, piece in enumerate((own,) + tuple(arrived)):
        ups[pl.ds(pl.multiple_of((me ^ tier) * rank, rank), rank), :] = piece[...]
    row = group - parts
    done = 0
    nodes = parts // 2
    while nodes >= 1:
        results = []
        for node in range(nodes):
            interp, upward = tree_node(
                ups[2 * node * rank : 2 * (node + 1) * rank, :],
                local_pivots[row : row + 1, :],
                local_inverse[row],
            )
            interps[done] = interp
            results.append(upward)
            row += 1
            done += 1
        for node, upward in enumerate(results):
            ups[node * rank : (node + 1) * rank, :] = upward
        nodes //= 2
    up_out[...] = ups[0:rank, :]


def upper_node(tier, heap_first, rank, own, arrived, pivots, inverse, ups):
    me = lax.axis_index("leaf")
    side = (me >> tier) & 1
    ups[pl.ds(pl.multiple_of(side * rank, rank), rank), :] = own[...]
    ups[pl.ds(pl.multiple_of((1 - side) * rank, rank), rank), :] = arrived[...]
    node = heap_first + (me >> (tier + 1))
    return tree_node(ups[...], pivots[pl.ds(node, 1), :], inverse[node])


def upper_kernel(tier, heap_first, rank, own, arrived, pivots, inverse, interp_out, up_out, ups):
    interp, upward = upper_node(tier, heap_first, rank, own, arrived, pivots, inverse, ups)
    interp_out[...] = interp
    up_out[...] = upward


def place_copies(flips, packs, share, group, rank, leaf_out, local_out, sems):
    me = lax.axis_index("vec")
    moves = []
    for flip, piece in zip(flips, packs):
        device = me ^ flip
        moves.append((piece.at[0:share], leaf_out.at[pl.ds(device * share, share)]))
        level_first, nodes, packed = 0, share // 2, 0
        level_nodes = group // 2
        while nodes >= 1:
            for node in range(nodes):
                side = (packed % 2) * 2 * rank
                source = piece.at[share + packed // 2, :, side : side + 2 * rank]
                moves.append((source, local_out.at[level_first + device * nodes + node]))
                packed += 1
            level_first += level_nodes
            level_nodes //= 2
            nodes //= 2
    return [
        pltpu.make_async_copy(source, target, sems.at[index])
        for index, (source, target) in enumerate(moves)
    ]


def place_kernel(flips, share, group, rank, *refs):
    packs, (joined, leaf_out, local_out, sems) = refs[: len(flips)], refs[len(flips) :]
    copies = place_copies(flips, packs, share, group, rank, leaf_out, local_out, sems)
    rows = joined.shape[0]
    target = local_out.at[group - 1 - rows : group - 1]
    copies.append(pltpu.make_async_copy(joined, target, sems.at[len(copies)]))
    for copy in copies:
        copy.start()
    for copy in copies:
        copy.wait()


def finish_kernel(tier, heap_first, flips, share, group, rank, own, arrived, pivots, inverse, *refs):
    earlier, refs = refs[:tier], refs[tier:]
    packs, refs = refs[: len(flips)], refs[len(flips) :]
    _, _, interps, top, leaf_out, local_out, ups, turned, sems = refs
    copies = place_copies(flips, packs, share, group, rank, leaf_out, local_out, sems)
    for copy in copies:
        copy.start()
    interp, upward = upper_node(tier, heap_first, rank, own, arrived, pivots, inverse, ups)
    for index, ref in enumerate(earlier):
        interps[index] = ref[...]
    interps[tier] = interp
    turned[...] = jnp.transpose(upward)
    columns = top.shape[0]
    place = pl.multiple_of(lax.axis_index("vec") * columns, columns)
    top[...] = turned[pl.ds(place, columns), :]
    for copy in copies:
        copy.wait()


def call(body, outs, scratch, operands, flops=0, anywhere_in=0, anywhere_out=0, aliases=None):
    fixed = pl.BlockSpec(memory_space=VMEM)
    free = pl.BlockSpec(memory_space=pl.ANY)
    return pl.pallas_call(
        body,
        out_shape=outs,
        in_specs=[fixed] * (len(operands) - anywhere_in) + [free] * anywhere_in,
        out_specs=[fixed] * (len(outs) - anywhere_out) + [free] * anywhere_out,
        scratch_shapes=scratch,
        input_output_aliases=aliases or {},
        compiler_params=pltpu.CompilerParams(vmem_limit_bytes=VMEM_BYTES),
        cost_estimate=pl.CostEstimate(
            flops=flops, bytes_accessed=sum(o.size * o.dtype.itemsize for o in operands), transcendentals=0
        ),
    )(*operands)


def f32(*shape):
    return jax.ShapeDtypeStruct(shape, jnp.float32)


def on_device(
    points,
    probe_vectors,
    neighbours,
    leaf_pivots,
    leaf_inverse,
    local_pivots,
    local_inverse,
    upper_pivots,
    upper_inverse,
):
    group, columns, size = probe_vectors.shape
    rank = leaf_pivots.shape[1]
    leaf_total = lax.axis_size("leaf")
    parts = lax.axis_size("vec")
    share = group // parts
    total_columns = columns * parts

    up = [(i, i + 1) for i in range(leaf_total - 1)]
    down = [(j, i) for i, j in up]
    joined = call(
        join_kernel,
        [jax.ShapeDtypeStruct((group, columns + 16, size), jnp.bfloat16)],
        [],
        [points, probe_vectors],
    )[0]
    halo = (lax.ppermute(joined, "leaf", up), lax.ppermute(joined, "leaf", down))

    def vec_send(array, tier):
        return lax.ppermute(array, "vec", [(i, i ^ tier) for i in range(parts)])

    away = list(range(parts - 1, 0, -1))
    sent_rows = (parts - 1) * share

    def bf16(*shape):
        return jax.ShapeDtypeStruct(shape, jnp.bfloat16)

    started, own_far, near = near_call(
        functools.partial(own_kernel, share, away),
        [f32(group + 1, columns, size), bf16(group, DEPTH, size), bf16(group + 1, size, DEPTH)],
        [],
        [neighbours, joined],
        size,
        sent_rows,
        6,
    )
    *sent, far, vectors = near_call(
        functools.partial(halo_kernel, share, away),
        [bf16(share, columns, size)] * len(away)
        + [bf16(3 * group, DEPTH, size), bf16(3 * group, columns, size)],
        [pltpu.VMEM((group + 1, columns, size), jnp.float32)],
        [neighbours, joined, *halo, own_far, near, started],
        size,
        sent_rows,
        6,
    )
    arrived = {tier: vec_send(array, tier) for tier, array in zip(away, sent)}
    kept = near_call(
        functools.partial(kept_kernel, share),
        [bf16(share, columns, size)],
        [pltpu.VMEM((group + 1, columns, size), jnp.float32)],
        [neighbours, far, vectors, near],
        size,
        share,
        12,
    )[0]

    slabs = share + share // 2
    pack, own_up = call(
        functools.partial(device_kernel, share, group, rank),
        (f32(slabs, rank, size), f32(rank, total_columns)),
        [
            pltpu.VMEM((share, total_columns, size), jnp.bfloat16),
            pltpu.VMEM((share * rank, total_columns), jnp.float32),
        ],
        [kept]
        + [arrived[tier] for tier in range(1, parts)]
        + [leaf_pivots, leaf_inverse, local_pivots, local_inverse],
    )
    near_ups = [vec_send(own_up, tier) for tier in range(1, parts)]
    joined, own_up = call(
        functools.partial(group_kernel, share, group, rank),
        (f32(parts - 1, rank, 2 * rank), f32(rank, total_columns)),
        [pltpu.VMEM((parts * rank, total_columns), jnp.float32)],
        [own_up] + near_ups + [local_pivots, local_inverse],
    )

    later, own_up = lax.optimization_barrier((pack, own_up))
    late = LATE if parts > max(LATE) else ()
    others = [vec_send(later if tier in late else pack, tier) for tier in range(1, parts)]

    heap_first = 0
    maps = []
    for tier in range(UPL):
        partner = lax.ppermute(own_up, "leaf", [(i, i ^ (1 << tier)) for i in range(leaf_total)])
        operands = [own_up, partner, upper_pivots, upper_inverse]
        ups = pltpu.VMEM((2 * rank, total_columns), jnp.float32)
        if tier < UPL - 1:
            interp, own_up = call(
                functools.partial(upper_kernel, tier, heap_first, rank),
                [f32(rank, 2 * rank), f32(rank, total_columns)],
                [ups],
                operands,
                flops=ROUND_FLOPS,
            )
            maps.append(interp)
            heap_first += leaf_total >> (tier + 1)
    early = [flip for flip in range(parts) if flip not in late]
    packs = [pack] + others
    leaf_map, local_map = call(
        functools.partial(place_kernel, early, share, group, rank),
        [f32(group, rank, size), f32(group - 1, rank, 2 * rank)],
        [pltpu.SemaphoreType.DMA((len(early) * share + 1,))],
        [packs[flip] for flip in early] + [joined],
        flops=ROUND_FLOPS,
        anywhere_in=len(early) + 1,
        anywhere_out=2,
    )
    operands += maps + [packs[flip] for flip in late] + [leaf_map, local_map]
    upper_map, top, leaf_map, local_map = call(
        functools.partial(finish_kernel, UPL - 1, heap_first, late, share, group, rank),
        [
            f32(UPL, rank, 2 * rank),
            f32(columns, rank),
            f32(group, rank, size),
            f32(group - 1, rank, 2 * rank),
        ],
        [
            ups,
            pltpu.VMEM((total_columns, rank), jnp.float32),
            pltpu.SemaphoreType.DMA((max(1, len(late) * share),)),
        ],
        operands,
        flops=ROUND_FLOPS,
        anywhere_in=len(late) + 2,
        anywhere_out=2,
        aliases={len(operands) - 2: 2, len(operands) - 1: 3},
    )
    return (
        jnp.swapaxes(leaf_map, 1, 2),
        jnp.swapaxes(local_map, 1, 2),
        jnp.swapaxes(upper_map, 1, 2)[None],
        top[None],
    )


def solution(mesh):
    placed = (
        P("leaf", None, None),
        P("leaf", "vec", None),
        P("leaf", None),
        P("leaf", None),
        P("leaf", None, None),
        P("leaf", None),
        P("leaf", None, None),
        P(),
        P(),
    )
    return jax.shard_map(
        on_device,
        mesh=mesh,
        in_specs=placed,
        out_specs=(
            P("leaf", None, None),
            P("leaf", None, None),
            P("leaf", None, None, None),
            P("leaf", "vec", None),
        ),
        check_vma=False,
    )
```

```python
import functools

import jax
import jax.numpy as jnp
from jax import lax
from jax.experimental import pallas as pl
from jax.experimental.pallas import tpu as pltpu
from jax.sharding import PartitionSpec as P

UPL = 3

SOFTEN = 0.0009
EPSILON = 1e-06
FLIGHT = 8
DEPTH = 128
CHUNK = 256
LATE = (2,)
ROUND_FLOPS = 400_000_000
VMEM_BYTES = 20 * 1024 * 1024
VMEM = pltpu.MemorySpace.VMEM
SMEM = pltpu.MemorySpace.SMEM


def nt(a, b):
    return lax.dot_general(a, b, (((1,), (1,)), ((), ())), preferred_element_type=jnp.float32)


def nn(a, b):
    return lax.dot_general(a, b, (((1,), (0,)), ((), ())), preferred_element_type=jnp.float32)


def split(a):
    high = a.astype(jnp.bfloat16)
    low = (a - high.astype(jnp.float32)).astype(jnp.bfloat16)
    return high, low


def stacked_split(a):
    high, low = split(a)
    return jnp.concatenate([high, low], axis=0)


def halves(a):
    rows = a.shape[0] // 2
    return a[:rows] + a[rows:]


def coordinates(points, extra):
    row = lax.broadcasted_iota(jnp.int32, (8, points.shape[1]), 0)
    padded = jnp.concatenate(
        [points, jnp.full((5, points.shape[1]), 0.5, jnp.float32)], axis=0
    )
    centred = padded - 0.5
    high, low = [part.astype(jnp.float32) for part in split(centred)]
    norm = jnp.sum(centred * centred, axis=0, keepdims=True) + extra
    first, rest = [part.astype(jnp.float32) for part in split(norm)]
    second, third = [part.astype(jnp.float32) for part in split(norm - first)]
    norms = jnp.where(row == 0, first, jnp.where(row == 1, second, jnp.where(row == 2, third, 0.0)))
    return high, low, norms, jnp.where(row < 3, 1.0, 0.0)


def far_features(points):
    high, low, norm, one = coordinates(points, SOFTEN)
    vacant = jnp.zeros((DEPTH - 48, points.shape[1]), jnp.float32)
    return jnp.concatenate(
        [-2.0 * high, -2.0 * low, -2.0 * high, -2.0 * low, one, norm, vacant], axis=0
    ).astype(jnp.bfloat16)


def near_features(points):
    high, low, norm, one = coordinates(points, 0.0)
    vacant = jnp.zeros((DEPTH - 48, points.shape[1]), jnp.float32)
    return jnp.transpose(
        jnp.concatenate([high, high, low, low, norm, one, vacant], axis=0)
    ).astype(jnp.bfloat16)


def add_blocks(share, tiers, base, wanted, nb_ref, far, vectors, near, total, tiles, codes):
    me = lax.axis_index("vec")
    count, slots = nb_ref.shape
    first = lax.axis_index("leaf") * count
    flight, size = tiles.shape[0], tiles.shape[1]
    columns = total.shape[1]
    idle = count * 64

    for way in range(flight):
        codes[way] = idle
    filled = jnp.int32(flight)
    for tier in tiers:
        for part in range(share):
            cluster = (me ^ tier) * share + part
            shift = cluster * 64 + count - base - first
            for slot in range(slots):
                listed = nb_ref[cluster, slot]
                codes[filled] = listed + shift
                filled += wanted(listed, first, count).astype(jnp.int32)
    for way in range(flight):
        codes[filled + way] = idle
    tiles[...] = jnp.zeros(tiles.shape, tiles.dtype)

    def multiply(code, tile):
        row = code // 64
        total[row] = total[row] + nt(vectors[code % 64, 0:columns, :], tile[...])

    def evaluate(code, tile):
        row = code // 64
        position = code % 64
        for top in range(0, size, CHUNK):
            distance = nn(near[row, top : top + CHUNK, :], far[position])
            tile[top : top + CHUNK, :] = lax.rsqrt(distance).astype(jnp.bfloat16)

    def step(index, carry):
        for way in range(flight):
            multiply(codes[index * flight + way], tiles.at[way])
            evaluate(codes[(index + 1) * flight + way], tiles.at[way])
        return carry

    steps = (filled - 1) // flight
    lax.fori_loop(0, steps, step, 0)
    for way in range(flight):
        multiply(codes[steps * flight + way], tiles.at[way])


def inside(listed, first, count):
    return (listed >= first) & (listed < first + count)


def outside(listed, first, count):
    return (listed >= 0) & ((listed < first) | (listed >= first + count))


def anywhere(listed, first, count):
    return listed >= 0


def own_kernel(share, tiers, nb_ref, joined, total, far, near, tiles, codes):
    count, columns = joined.shape[0], total.shape[1]
    for cluster in range(count):
        here = joined[cluster, columns:, :].astype(jnp.float32)[0:3]
        far[cluster] = far_features(here)
        near[cluster] = near_features(here)
    near[count] = near[0]
    total[...] = jnp.zeros(total.shape, total.dtype)
    add_blocks(share, tiers, count, inside, nb_ref, far, joined, near, total, tiles, codes)


def halo_kernel(share, tiers, nb_ref, joined, before, after, own_far, near, start, *refs):
    outs = refs[: len(tiers)]
    far, vectors, total, tiles, codes = refs[len(tiers) :]
    count, columns = joined.shape[0], start.shape[1]
    me = lax.axis_index("vec")
    for place, source in ((0, before), (2, after)):
        for cluster in range(count):
            far[place * count + cluster] = far_features(
                source[cluster, columns:, :].astype(jnp.float32)[0:3]
            )
        vectors[place * count : (place + 1) * count] = source[:, 0:columns, :]
    far[count : 2 * count] = own_far[...]
    vectors[count : 2 * count] = joined[:, 0:columns, :]
    total[...] = start[...]
    add_blocks(share, tiers, 0, outside, nb_ref, far, vectors, near, total, tiles, codes)
    for tier, out in zip(tiers, outs):
        part = total[pl.ds((me ^ tier) * share, share)]
        out[...] = (part * 0.015625).astype(out.dtype)


def kept_kernel(share, nb_ref, far, vectors, near, out, total, tiles, codes):
    mine = pl.ds(lax.axis_index("vec") * share, share)
    total[mine] = jnp.zeros((share,) + total.shape[1:], total.dtype)
    add_blocks(share, (0,), 0, anywhere, nb_ref, far, vectors, near, total, tiles, codes)
    out[...] = (total[mine] * 0.015625).astype(out.dtype)


def join_kernel(points, probe, joined):
    count, columns, size = probe.shape
    joined[:, 0:columns, :] = probe[...]
    vacant = jnp.zeros((joined.shape[1] - columns - 3, size), jnp.float32)
    for cluster in range(count):
        joined[cluster, columns:, :] = jnp.concatenate(
            [points[cluster].astype(jnp.float32), vacant], axis=0
        ).astype(joined.dtype)


def near_call(body, outs, scratch, operands, rows, per_row):
    nb, size = operands[0], outs[0].shape[-1]
    blocks = rows * per_row
    return pl.pallas_call(
        body,
        out_shape=outs,
        in_specs=[pl.BlockSpec(memory_space=SMEM)]
        + [pl.BlockSpec(memory_space=VMEM)] * (len(operands) - 1),
        out_specs=[pl.BlockSpec(memory_space=VMEM)] * len(outs),
        scratch_shapes=scratch
        + [
            pltpu.VMEM((FLIGHT, size, size), jnp.bfloat16),
            pltpu.SMEM((rows * nb.shape[1] + 2 * FLIGHT,), jnp.int32),
        ],
        compiler_params=pltpu.CompilerParams(vmem_limit_bytes=VMEM_BYTES),
        cost_estimate=pl.CostEstimate(
            flops=blocks * size * size * 256,
            bytes_accessed=sum(o.size * o.dtype.itemsize for o in operands),
            transcendentals=blocks * size * size,
        ),
    )(*operands)


def pivot_factor(pivots, inverse, width):
    chosen = (
        lax.broadcasted_iota(jnp.int32, (width, pivots.shape[1]), 0) == pivots
    ).astype(jnp.bfloat16)
    return nt(stacked_split(jnp.transpose(inverse)), chosen).astype(jnp.bfloat16)


def leaf_node(sketch, factor):
    wide = sketch.astype(jnp.float32)
    mean_sq = jnp.sum(wide * wide, keepdims=True) / (sketch.shape[0] * sketch.shape[1]) + EPSILON
    scale = 1.0 / (sketch.shape[0] * mean_sq)
    picked = halves(nt(factor, sketch))
    raw = halves(nn(stacked_split(picked), sketch))
    interp = raw * scale
    upward = halves(nt(stacked_split(raw), sketch)) * (scale * lax.rsqrt(mean_sq))
    return interp, upward


def tree_node(sketch, factor):
    width, columns = sketch.shape
    mean_sq = jnp.sum(sketch * sketch, keepdims=True) / (width * columns) + EPSILON
    scale = 1.0 / (columns * mean_sq)
    parts = stacked_split(sketch)
    picked = halves(nn(jnp.concatenate([factor, factor], axis=1), parts))
    raw = halves(nt(stacked_split(picked), parts))
    raw = raw[:, :width] + raw[:, width:]
    interp = raw * scale
    both = stacked_split(raw)
    upward = halves(nn(jnp.concatenate([both, both], axis=1), parts)) * (scale * lax.rsqrt(mean_sq))
    return interp, upward


def own_nodes(share, group, me):
    rows, level_first, nodes = [], 0, share // 2
    while nodes >= 1:
        rows += [level_first + me * nodes + node for node in range(nodes)]
        level_first += (group // share) * nodes
        nodes //= 2
    return rows


def factor_kernel(
    share,
    leaf_total,
    leaf_pivots,
    leaf_inverse,
    local_pivots,
    local_inverse,
    upper_pivots,
    upper_inverse,
    _,
    leaf_out,
    own_out,
    group_out,
    upper_out,
):
    me = lax.axis_index("vec")
    group = leaf_pivots.shape[0]

    def put(out, index, pivots, inverse, row):
        out[index] = pivot_factor(pivots[pl.ds(row, 1), :], inverse[row], out.shape[2])

    for cluster in range(share):
        put(leaf_out, cluster, leaf_pivots, leaf_inverse, me * share + cluster)
    for index, row in enumerate(own_nodes(share, group, me)):
        put(own_out, index, local_pivots, local_inverse, row)
    for index in range(group // share - 1):
        put(group_out, index, local_pivots, local_inverse, group - group // share + index)
    heap_first = 0
    for tier in range(UPL):
        node = heap_first + (lax.axis_index("leaf") >> (tier + 1))
        put(upper_out, tier, upper_pivots, upper_inverse, node)
        heap_first += leaf_total >> (tier + 1)


def device_kernel(share, group, rank, own, *refs):
    parts = group // share
    arrived, refs = refs[: parts - 1], refs[parts - 1 :]
    leaf_factors, own_factors, pack, up_out, sketch, ups = refs
    me = lax.axis_index("vec")
    columns = own.shape[1]
    width = 2 * rank
    for tier, piece in enumerate((own,) + tuple(arrived)):
        place = pl.ds(pl.multiple_of((me ^ tier) * columns, columns), columns)
        for cluster in range(share):
            sketch[cluster, place, :] = piece[cluster]
    for cluster in range(share):
        interp, upward = leaf_node(sketch[cluster], leaf_factors[cluster])
        pack[cluster * rank : (cluster + 1) * rank, :] = interp
        ups[cluster * rank : (cluster + 1) * rank, :] = upward
    nodes, packed = share // 2, 0
    while nodes >= 1:
        results = []
        for node in range(nodes):
            interp, upward = tree_node(
                ups[2 * node * rank : 2 * (node + 1) * rank, :], own_factors[packed]
            )
            for lane, source, top, height in pack_places(packed, share, rank):
                pack[top : top + height, lane : lane + width] = interp[source : source + height]
            results.append(upward)
            packed += 1
        for node, upward in enumerate(results):
            ups[node * rank : (node + 1) * rank, :] = upward
        nodes //= 2
    up_out[...] = ups[0:rank, :]


def pack_places(index, share, rank):
    top = share * rank + index // 2 * rank
    if index < share - 2:
        return [(index % 2 * 2 * rank, 0, top, rank)]
    return [(0, 0, top, rank // 2), (2 * rank, rank // 2, top, rank // 2)]


def group_kernel(share, group, rank, own, *refs):
    parts = group // share
    arrived, refs = refs[: parts - 1], refs[parts - 1 :]
    factors, interps, up_out, ups = refs
    me = lax.axis_index("vec")
    for tier, piece in enumerate((own,) + tuple(arrived)):
        ups[pl.ds(pl.multiple_of((me ^ tier) * rank, rank), rank), :] = piece[...]
    done = 0
    nodes = parts // 2
    while nodes >= 1:
        results = []
        for node in range(nodes):
            interp, upward = tree_node(
                ups[2 * node * rank : 2 * (node + 1) * rank, :], factors[done]
            )
            interps[done * rank : (done + 1) * rank, :] = interp
            results.append(upward)
            done += 1
        for node, upward in enumerate(results):
            ups[node * rank : (node + 1) * rank, :] = upward
        nodes //= 2
    up_out[...] = ups[0:rank, :]


def upper_node(tier, rank, own, arrived, factors, ups):
    side = (lax.axis_index("leaf") >> tier) & 1
    ups[pl.ds(pl.multiple_of(side * rank, rank), rank), :] = own[...]
    ups[pl.ds(pl.multiple_of((1 - side) * rank, rank), rank), :] = arrived[...]
    return tree_node(ups[...], factors[tier])


def upper_kernel(tier, rank, own, arrived, factors, interp_out, up_out, ups):
    interp, upward = upper_node(tier, rank, own, arrived, factors, ups)
    interp_out[...] = interp
    up_out[...] = upward


def finish_kernel(tier, share, group, rank, own, arrived, factors, *refs):
    parts = group // share
    earlier, refs = refs[:tier], refs[tier:]
    packs, refs = refs[:parts], refs[parts:]
    joined, interps, top, leaf_out, local_out, ups, turned, sems = refs
    me = lax.axis_index("vec")
    copies = []

    def put(source, target):
        copies.append(pltpu.make_async_copy(source, target, sems.at[len(copies)]))
        copies[-1].start()

    def rows_at(start, height):
        return pl.ds(pl.multiple_of(start, height), height)

    for flip, piece in enumerate(packs):
        device = me ^ flip
        leaves = share * rank
        put(piece.at[0:leaves], leaf_out.at[rows_at(device * leaves, leaves)])
        for index, row in enumerate(own_nodes(share, group, device)):
            for lane, source, start, height in pack_places(index, share, rank):
                put(
                    piece.at[start : start + height, lane : lane + 2 * rank],
                    local_out.at[rows_at(row * rank + source, height)],
                )
    put(joined, local_out.at[(group - parts) * rank : (group - 1) * rank])

    interp, upward = upper_node(tier, rank, own, arrived, factors, ups)
    for index, ref in enumerate(earlier):
        interps[index] = ref[...]
    interps[tier] = interp
    turned[...] = jnp.transpose(upward)
    columns = top.shape[0]
    place = pl.multiple_of(me * columns, columns)
    top[...] = turned[pl.ds(place, columns), :]
    for copy in copies:
        copy.wait()


def call(body, outs, scratch, operands, flops=0, anywhere_in=0, anywhere_out=0):
    fixed = pl.BlockSpec(memory_space=VMEM)
    free = pl.BlockSpec(memory_space=pl.ANY)
    return pl.pallas_call(
        body,
        out_shape=outs,
        in_specs=[fixed] * (len(operands) - anywhere_in) + [free] * anywhere_in,
        out_specs=[fixed] * (len(outs) - anywhere_out) + [free] * anywhere_out,
        scratch_shapes=scratch,
        compiler_params=pltpu.CompilerParams(vmem_limit_bytes=VMEM_BYTES),
        cost_estimate=pl.CostEstimate(
            flops=flops, bytes_accessed=sum(o.size * o.dtype.itemsize for o in operands), transcendentals=0
        ),
    )(*operands)


def f32(*shape):
    return jax.ShapeDtypeStruct(shape, jnp.float32)


def on_device(
    points,
    probe_vectors,
    neighbours,
    leaf_pivots,
    leaf_inverse,
    local_pivots,
    local_inverse,
    upper_pivots,
    upper_inverse,
):
    group, columns, size = probe_vectors.shape
    rank = leaf_pivots.shape[1]
    leaf_total = lax.axis_size("leaf")
    parts = lax.axis_size("vec")
    share = group // parts
    total_columns = columns * parts

    up = [(i, i + 1) for i in range(leaf_total - 1)]
    down = [(j, i) for i, j in up]
    joined = call(
        join_kernel,
        [jax.ShapeDtypeStruct((group, columns + 16, size), jnp.bfloat16)],
        [],
        [points, probe_vectors],
    )[0]
    halo = (lax.ppermute(joined, "leaf", up), lax.ppermute(joined, "leaf", down))

    def vec_send(array, tier):
        return lax.ppermute(array, "vec", [(i, i ^ tier) for i in range(parts)])

    away = list(range(parts - 1, 0, -1))
    sent_rows = (parts - 1) * share

    def bf16(*shape):
        return jax.ShapeDtypeStruct(shape, jnp.bfloat16)

    started, own_far, near = near_call(
        functools.partial(own_kernel, share, away),
        [f32(group + 1, columns, size), bf16(group, DEPTH, size), bf16(group + 1, size, DEPTH)],
        [],
        [neighbours, joined],
        sent_rows,
        6,
    )
    *sent, far, vectors = near_call(
        functools.partial(halo_kernel, share, away),
        [bf16(share, columns, size)] * len(away)
        + [bf16(3 * group, DEPTH, size), bf16(3 * group, columns, size)],
        [pltpu.VMEM((group + 1, columns, size), jnp.float32)],
        [neighbours, joined, *halo, own_far, near, started],
        sent_rows,
        6,
    )
    arrived = {tier: vec_send(array, tier) for tier, array in zip(away, sent)}
    kept = near_call(
        functools.partial(kept_kernel, share),
        [bf16(share, columns, size)],
        [pltpu.VMEM((group + 1, columns, size), jnp.float32)],
        [neighbours, far, vectors, near],
        share,
        12,
    )[0]

    width = 2 * rank
    leaf_factors, own_factors, group_factors, upper_factors = call(
        functools.partial(factor_kernel, share, leaf_total),
        [
            bf16(share, width, size),
            bf16(max(1, share - 1), width, width),
            bf16(parts - 1, width, width),
            bf16(UPL, width, width),
        ],
        [],
        [
            leaf_pivots,
            leaf_inverse,
            local_pivots,
            local_inverse,
            upper_pivots,
            upper_inverse,
            kept,
        ],
        anywhere_in=1,
    )
    pack, own_up = call(
        functools.partial(device_kernel, share, group, rank),
        [f32((3 * share - 1) * rank // 2, size), f32(rank, total_columns)],
        [
            pltpu.VMEM((share, total_columns, size), jnp.bfloat16),
            pltpu.VMEM((share * rank, total_columns), jnp.float32),
        ],
        [kept] + [arrived[tier] for tier in range(1, parts)] + [leaf_factors, own_factors],
    )
    near_ups = [vec_send(own_up, tier) for tier in range(1, parts)]
    joined, own_up = call(
        functools.partial(group_kernel, share, group, rank),
        [f32((parts - 1) * rank, width), f32(rank, total_columns)],
        [pltpu.VMEM((parts * rank, total_columns), jnp.float32)],
        [own_up] + near_ups + [group_factors],
    )
    later, own_up = lax.optimization_barrier((pack, own_up))
    late = LATE if parts > max(LATE) else ()
    others = [vec_send(later if tier in late else pack, tier) for tier in range(1, parts)]

    maps = []
    for tier in range(UPL):
        partner = lax.ppermute(own_up, "leaf", [(i, i ^ (1 << tier)) for i in range(leaf_total)])
        operands = [own_up, partner, upper_factors]
        ups = pltpu.VMEM((width, total_columns), jnp.float32)
        if tier < UPL - 1:
            interp, own_up = call(
                functools.partial(upper_kernel, tier, rank),
                [f32(rank, width), f32(rank, total_columns)],
                [ups],
                operands,
                flops=ROUND_FLOPS,
            )
            maps.append(interp)
    upper_map, top, leaf_map, local_map = call(
        functools.partial(finish_kernel, UPL - 1, share, group, rank),
        [
            f32(UPL, rank, width),
            f32(columns, rank),
            f32(group * rank, size),
            f32((group - 1) * rank, width),
        ],
        [
            ups,
            pltpu.VMEM((total_columns, rank), jnp.float32),
            pltpu.SemaphoreType.DMA((parts * (share + 1) + 1,)),
        ],
        operands + maps + [pack] + others + [joined],
        flops=ROUND_FLOPS,
        anywhere_in=parts + 1,
        anywhere_out=2,
    )
    return (
        jnp.swapaxes(leaf_map.reshape(group, rank, size), 1, 2),
        jnp.swapaxes(local_map.reshape(group - 1, rank, width), 1, 2),
        jnp.swapaxes(upper_map, 1, 2)[None],
        top[None],
    )


def solution(mesh):
    placed = (
        P("leaf", None, None),
        P("leaf", "vec", None),
        P("leaf", None),
        P("leaf", None),
        P("leaf", None, None),
        P("leaf", None),
        P("leaf", None, None),
        P(),
        P(),
    )
    return jax.shard_map(
        on_device,
        mesh=mesh,
        in_specs=placed,
        out_specs=(
            P("leaf", None, None),
            P("leaf", None, None),
            P("leaf", None, None, None),
            P("leaf", "vec", None),
        ),
        check_vma=False,
    )
```

```python
import functools

import jax
import jax.numpy as jnp
from jax import lax
from jax.experimental import pallas as pl
from jax.experimental.pallas import tpu as pltpu
from jax.sharding import PartitionSpec as P

UPL = 3

SOFTEN = 0.0009
EPSILON = 1e-06
FLIGHT = 8
DEPTH = 128
CHUNK = 256
LATE = (2,)
ROUND_FLOPS = 400_000_000
VMEM_BYTES = 20 * 1024 * 1024
VMEM = pltpu.MemorySpace.VMEM
SMEM = pltpu.MemorySpace.SMEM


def nt(a, b):
    return lax.dot_general(a, b, (((1,), (1,)), ((), ())), preferred_element_type=jnp.float32)


def nn(a, b):
    return lax.dot_general(a, b, (((1,), (0,)), ((), ())), preferred_element_type=jnp.float32)


def split(a):
    high = a.astype(jnp.bfloat16)
    low = (a - high.astype(jnp.float32)).astype(jnp.bfloat16)
    return high, low


def stacked_split(a):
    high, low = split(a)
    return jnp.concatenate([high, low], axis=0)


def halves(a):
    rows = a.shape[0] // 2
    return a[:rows] + a[rows:]


def coordinates(points, extra):
    row = lax.broadcasted_iota(jnp.int32, (8, points.shape[1]), 0)
    padded = jnp.concatenate(
        [points, jnp.full((5, points.shape[1]), 0.5, jnp.float32)], axis=0
    )
    centred = padded - 0.5
    high, low = [part.astype(jnp.float32) for part in split(centred)]
    norm = jnp.sum(centred * centred, axis=0, keepdims=True) + extra
    first, rest = [part.astype(jnp.float32) for part in split(norm)]
    second, third = [part.astype(jnp.float32) for part in split(norm - first)]
    norms = jnp.where(row == 0, first, jnp.where(row == 1, second, jnp.where(row == 2, third, 0.0)))
    return high, low, norms, jnp.where(row < 3, 1.0, 0.0)


def far_features(points):
    high, low, norm, one = coordinates(points, SOFTEN)
    vacant = jnp.zeros((DEPTH - 48, points.shape[1]), jnp.float32)
    return jnp.concatenate(
        [-2.0 * high, -2.0 * low, -2.0 * high, -2.0 * low, one, norm, vacant], axis=0
    ).astype(jnp.bfloat16)


def near_features(points):
    high, low, norm, one = coordinates(points, 0.0)
    vacant = jnp.zeros((DEPTH - 48, points.shape[1]), jnp.float32)
    return jnp.transpose(
        jnp.concatenate([high, high, low, low, norm, one, vacant], axis=0)
    ).astype(jnp.bfloat16)


def add_blocks(share, tiers, base, wanted, nb_ref, far, vectors, near, total, tiles, codes):
    me = lax.axis_index("vec")
    count, slots = nb_ref.shape
    first = lax.axis_index("leaf") * count
    flight, size = tiles.shape[0], tiles.shape[1]
    idle = count * 64

    for way in range(flight):
        codes[way] = idle
    filled = jnp.int32(flight)
    for tier in tiers:
        for part in range(share):
            cluster = (me ^ tier) * share + part
            shift = cluster * 64 + count - base - first
            for slot in range(slots):
                listed = nb_ref[cluster, slot]
                codes[filled] = listed + shift
                filled += wanted(listed, first, count).astype(jnp.int32)
    for way in range(flight):
        codes[filled + way] = idle
    tiles[...] = jnp.zeros(tiles.shape, tiles.dtype)

    def multiply(code, tile):
        row = code // 64
        total[row] = total[row] + nt(vectors(code % 64), tile[...])

    def evaluate(code, tile):
        row = code // 64
        position = code % 64
        for top in range(0, size, CHUNK):
            distance = nn(near[row, top : top + CHUNK, :], far[position])
            tile[top : top + CHUNK, :] = lax.rsqrt(distance).astype(jnp.bfloat16)

    def step(index, carry):
        for way in range(flight):
            multiply(codes[index * flight + way], tiles.at[way])
            evaluate(codes[(index + 1) * flight + way], tiles.at[way])
        return carry

    steps = (filled - 1) // flight
    lax.fori_loop(0, steps, step, 0)
    for way in range(flight):
        multiply(codes[steps * flight + way], tiles.at[way])


def inside(listed, first, count):
    return (listed >= first) & (listed < first + count)


def outside(listed, first, count):
    return (listed >= 0) & ((listed < first) | (listed >= first + count))


def anywhere(listed, first, count):
    return listed >= 0


def joined_points(joined, count):
    points = joined[joined.shape[0] - 3 * count :, :].astype(jnp.float32)
    return [points[3 * cluster : 3 * cluster + 3] for cluster in range(count)]


def own_kernel(share, tiers, nb_ref, joined, total, far, near, tiles, codes):
    count, columns = far.shape[0], total.shape[1]
    for cluster, points in enumerate(joined_points(joined, count)):
        far[cluster] = far_features(points)
        near[cluster] = near_features(points)
    near[count] = near[0]
    total[...] = jnp.zeros(total.shape, total.dtype)

    def vectors(place):
        return joined[pl.ds(pl.multiple_of(place * columns, columns), columns), :]

    add_blocks(share, tiers, count, inside, nb_ref, far, vectors, near, total, tiles, codes)


def halo_kernel(share, tiers, nb_ref, joined, inner, outer, own_far, near, start, *refs):
    outs = refs[: len(tiers)]
    far, vectors, total, tiles, codes = refs[len(tiers) :]
    count, columns = own_far.shape[0], start.shape[1]
    me = lax.axis_index("vec")
    odd = lax.axis_index("leaf") & 1
    for place, source in ((2 * odd, outer), (2 - 2 * odd, inner), (1, joined)):
        for cluster in range(count):
            vectors[place * count + cluster] = source[cluster * columns : (cluster + 1) * columns, :]
        if source is joined:
            far[count : 2 * count] = own_far[...]
            continue
        for cluster, points in enumerate(joined_points(source, count)):
            far[place * count + cluster] = far_features(points)
    total[...] = start[...]

    def read(place):
        return vectors[place]

    add_blocks(share, tiers, 0, outside, nb_ref, far, read, near, total, tiles, codes)
    for tier, out in zip(tiers, outs):
        part = total[pl.ds((me ^ tier) * share, share)]
        out[...] = (part * 0.015625).astype(out.dtype)


def kept_kernel(share, nb_ref, far, vectors, near, out, total, tiles, codes):
    mine = pl.ds(lax.axis_index("vec") * share, share)
    total[mine] = jnp.zeros((share,) + total.shape[1:], total.dtype)

    def read(place):
        return vectors[place]

    add_blocks(share, (0,), 0, anywhere, nb_ref, far, read, near, total, tiles, codes)
    out[...] = (total[mine] * 0.015625).astype(out.dtype)


def join_kernel(points, probe, joined):
    count, columns, _ = probe.shape
    for cluster in range(count):
        joined[cluster * columns : (cluster + 1) * columns, :] = probe[cluster]
    joined[count * columns :, :] = jnp.concatenate(
        [points[cluster].astype(jnp.float32) for cluster in range(count)], axis=0
    ).astype(joined.dtype)


def near_call(body, outs, scratch, operands, rows, per_row):
    nb, size = operands[0], outs[0].shape[-1]
    blocks = rows * per_row
    return pl.pallas_call(
        body,
        out_shape=outs,
        in_specs=[pl.BlockSpec(memory_space=SMEM)]
        + [pl.BlockSpec(memory_space=VMEM)] * (len(operands) - 1),
        out_specs=[pl.BlockSpec(memory_space=VMEM)] * len(outs),
        scratch_shapes=scratch
        + [
            pltpu.VMEM((FLIGHT, size, size), jnp.bfloat16),
            pltpu.SMEM((rows * nb.shape[1] + 2 * FLIGHT,), jnp.int32),
        ],
        compiler_params=pltpu.CompilerParams(vmem_limit_bytes=VMEM_BYTES),
        cost_estimate=pl.CostEstimate(
            flops=blocks * size * size * 256,
            bytes_accessed=sum(o.size * o.dtype.itemsize for o in operands),
            transcendentals=blocks * size * size,
        ),
    )(*operands)


def pivot_factor(pivots, inverse, width):
    chosen = (
        lax.broadcasted_iota(jnp.int32, (width, pivots.shape[1]), 0) == pivots
    ).astype(jnp.bfloat16)
    return nt(stacked_split(jnp.transpose(inverse)), chosen).astype(jnp.bfloat16)


def leaf_node(sketch, factor):
    wide = sketch.astype(jnp.float32)
    mean_sq = jnp.sum(wide * wide, keepdims=True) / (sketch.shape[0] * sketch.shape[1]) + EPSILON
    scale = 1.0 / (sketch.shape[0] * mean_sq)
    picked = halves(nt(factor, sketch))
    raw = halves(nn(stacked_split(picked), sketch))
    interp = raw * scale
    upward = halves(nt(stacked_split(raw), sketch)) * (scale * lax.rsqrt(mean_sq))
    return interp, upward


def tree_node(sketch, factor):
    width, columns = sketch.shape
    mean_sq = jnp.sum(sketch * sketch, keepdims=True) / (width * columns) + EPSILON
    scale = 1.0 / (columns * mean_sq)
    parts = stacked_split(sketch)
    picked = halves(nn(jnp.concatenate([factor, factor], axis=1), parts))
    raw = halves(nt(stacked_split(picked), parts))
    raw = raw[:, :width] + raw[:, width:]
    interp = raw * scale
    both = stacked_split(raw)
    upward = halves(nn(jnp.concatenate([both, both], axis=1), parts)) * (scale * lax.rsqrt(mean_sq))
    return interp, upward


def own_nodes(share, group, me):
    rows, level_first, nodes = [], 0, share // 2
    while nodes >= 1:
        rows += [level_first + me * nodes + node for node in range(nodes)]
        level_first += (group // share) * nodes
        nodes //= 2
    return rows


def factor_kernel(
    share,
    leaf_total,
    leaf_pivots,
    leaf_inverse,
    local_pivots,
    local_inverse,
    upper_pivots,
    upper_inverse,
    _,
    leaf_out,
    own_out,
    group_out,
    upper_out,
):
    me = lax.axis_index("vec")
    group = leaf_pivots.shape[0]

    def put(out, index, pivots, inverse, row):
        out[index] = pivot_factor(pivots[pl.ds(row, 1), :], inverse[row], out.shape[2])

    for cluster in range(share):
        put(leaf_out, cluster, leaf_pivots, leaf_inverse, me * share + cluster)
    for index, row in enumerate(own_nodes(share, group, me)):
        put(own_out, index, local_pivots, local_inverse, row)
    for index in range(group // share - 1):
        put(group_out, index, local_pivots, local_inverse, group - group // share + index)
    heap_first = 0
    for tier in range(UPL):
        node = heap_first + (lax.axis_index("leaf") >> (tier + 1))
        put(upper_out, tier, upper_pivots, upper_inverse, node)
        heap_first += leaf_total >> (tier + 1)


def device_kernel(share, group, rank, own, *refs):
    parts = group // share
    arrived, refs = refs[: parts - 1], refs[parts - 1 :]
    leaf_factors, own_factors, pack, up_out, sketch, ups = refs
    me = lax.axis_index("vec")
    columns = own.shape[1]
    width = 2 * rank
    for tier, piece in enumerate((own,) + tuple(arrived)):
        place = pl.ds(pl.multiple_of((me ^ tier) * columns, columns), columns)
        for cluster in range(share):
            sketch[cluster, place, :] = piece[cluster]
    for cluster in range(share):
        interp, upward = leaf_node(sketch[cluster], leaf_factors[cluster])
        pack[cluster * rank : (cluster + 1) * rank, :] = interp
        ups[cluster * rank : (cluster + 1) * rank, :] = upward
    nodes, packed = share // 2, 0
    while nodes >= 1:
        results = []
        for node in range(nodes):
            interp, upward = tree_node(
                ups[2 * node * rank : 2 * (node + 1) * rank, :], own_factors[packed]
            )
            for lane, source, top, height in pack_places(packed, share, rank):
                pack[top : top + height, lane : lane + width] = interp[source : source + height]
            results.append(upward)
            packed += 1
        for node, upward in enumerate(results):
            ups[node * rank : (node + 1) * rank, :] = upward
        nodes //= 2
    up_out[...] = ups[0:rank, :]


def pack_places(index, share, rank):
    top = share * rank + index // 2 * rank
    if index < share - 2:
        return [(index % 2 * 2 * rank, 0, top, rank)]
    return [(0, 0, top, rank // 2), (2 * rank, rank // 2, top, rank // 2)]


def group_kernel(share, group, rank, own, *refs):
    parts = group // share
    arrived, refs = refs[: parts - 1], refs[parts - 1 :]
    factors, interps, up_out, ups = refs
    me = lax.axis_index("vec")
    for tier, piece in enumerate((own,) + tuple(arrived)):
        ups[pl.ds(pl.multiple_of((me ^ tier) * rank, rank), rank), :] = piece[...]
    done = 0
    nodes = parts // 2
    while nodes >= 1:
        results = []
        for node in range(nodes):
            interp, upward = tree_node(
                ups[2 * node * rank : 2 * (node + 1) * rank, :], factors[done]
            )
            interps[done * rank : (done + 1) * rank, :] = interp
            results.append(upward)
            done += 1
        for node, upward in enumerate(results):
            ups[node * rank : (node + 1) * rank, :] = upward
        nodes //= 2
    up_out[...] = ups[0:rank, :]


def upper_node(tier, rank, own, arrived, factors, ups):
    side = (lax.axis_index("leaf") >> tier) & 1
    ups[pl.ds(pl.multiple_of(side * rank, rank), rank), :] = own[...]
    ups[pl.ds(pl.multiple_of((1 - side) * rank, rank), rank), :] = arrived[...]
    return tree_node(ups[...], factors[tier])


def upper_kernel(tier, rank, own, arrived, factors, interp_out, up_out, ups):
    interp, upward = upper_node(tier, rank, own, arrived, factors, ups)
    interp_out[...] = interp
    up_out[...] = upward


def finish_kernel(tier, share, group, rank, own, arrived, factors, *refs):
    parts = group // share
    earlier, refs = refs[:tier], refs[tier:]
    packs, refs = refs[:parts], refs[parts:]
    joined, interps, top, leaf_out, local_out, ups, turned, sems = refs
    me = lax.axis_index("vec")
    copies = []

    def put(source, target):
        copies.append(pltpu.make_async_copy(source, target, sems.at[len(copies)]))
        copies[-1].start()

    def rows_at(start, height):
        return pl.ds(pl.multiple_of(start, height), height)

    for flip, piece in enumerate(packs):
        device = me ^ flip
        leaves = share * rank
        put(piece.at[0:leaves], leaf_out.at[rows_at(device * leaves, leaves)])
        for index, row in enumerate(own_nodes(share, group, device)):
            for lane, source, start, height in pack_places(index, share, rank):
                put(
                    piece.at[start : start + height, lane : lane + 2 * rank],
                    local_out.at[rows_at(row * rank + source, height)],
                )
    put(joined, local_out.at[(group - parts) * rank : (group - 1) * rank])

    interp, upward = upper_node(tier, rank, own, arrived, factors, ups)
    for index, ref in enumerate(earlier):
        interps[index] = ref[...]
    interps[tier] = interp
    turned[...] = jnp.transpose(upward)
    columns = top.shape[0]
    place = pl.multiple_of(me * columns, columns)
    top[...] = turned[pl.ds(place, columns), :]
    for copy in copies:
        copy.wait()


def call(body, outs, scratch, operands, flops=0, anywhere_in=0, anywhere_out=0):
    fixed = pl.BlockSpec(memory_space=VMEM)
    free = pl.BlockSpec(memory_space=pl.ANY)
    return pl.pallas_call(
        body,
        out_shape=outs,
        in_specs=[fixed] * (len(operands) - anywhere_in) + [free] * anywhere_in,
        out_specs=[fixed] * (len(outs) - anywhere_out) + [free] * anywhere_out,
        scratch_shapes=scratch,
        compiler_params=pltpu.CompilerParams(vmem_limit_bytes=VMEM_BYTES),
        cost_estimate=pl.CostEstimate(
            flops=flops, bytes_accessed=sum(o.size * o.dtype.itemsize for o in operands), transcendentals=0
        ),
    )(*operands)


def f32(*shape):
    return jax.ShapeDtypeStruct(shape, jnp.float32)


def on_device(
    points,
    probe_vectors,
    neighbours,
    leaf_pivots,
    leaf_inverse,
    local_pivots,
    local_inverse,
    upper_pivots,
    upper_inverse,
):
    group, columns, size = probe_vectors.shape
    rank = leaf_pivots.shape[1]
    leaf_total = lax.axis_size("leaf")
    parts = lax.axis_size("vec")
    share = group // parts
    total_columns = columns * parts

    joined = call(
        join_kernel,
        [jax.ShapeDtypeStruct((group * (columns + 3), size), jnp.bfloat16)],
        [],
        [points, probe_vectors],
    )[0]
    swaps = []
    for odd in (0, 1):
        pairs = [(i, i + 1) for i in range(odd, leaf_total - 1, 2)]
        swaps.append(lax.ppermute(joined, "leaf", pairs + [(j, i) for i, j in pairs]))
    inner, outer = swaps

    def vec_send(array, tier):
        return lax.ppermute(array, "vec", [(i, i ^ tier) for i in range(parts)])

    away = list(range(parts - 1, 0, -1))
    sent_rows = (parts - 1) * share

    def bf16(*shape):
        return jax.ShapeDtypeStruct(shape, jnp.bfloat16)

    started, own_far, near = near_call(
        functools.partial(own_kernel, share, away),
        [f32(group + 1, columns, size), bf16(group, DEPTH, size), bf16(group + 1, size, DEPTH)],
        [],
        [neighbours, joined],
        sent_rows,
        6,
    )
    *sent, far, vectors = near_call(
        functools.partial(halo_kernel, share, away),
        [bf16(share, columns, size)] * len(away)
        + [bf16(3 * group, DEPTH, size), bf16(3 * group, columns, size)],
        [pltpu.VMEM((group + 1, columns, size), jnp.float32)],
        [neighbours, joined, inner, outer, own_far, near, started],
        sent_rows,
        6,
    )
    arrived = {tier: vec_send(array, tier) for tier, array in zip(away, sent)}
    kept = near_call(
        functools.partial(kept_kernel, share),
        [bf16(share, columns, size)],
        [pltpu.VMEM((group + 1, columns, size), jnp.float32)],
        [neighbours, far, vectors, near],
        share,
        12,
    )[0]

    width = 2 * rank
    leaf_factors, own_factors, group_factors, upper_factors = call(
        functools.partial(factor_kernel, share, leaf_total),
        [
            bf16(share, width, size),
            bf16(max(1, share - 1), width, width),
            bf16(parts - 1, width, width),
            bf16(UPL, width, width),
        ],
        [],
        [
            leaf_pivots,
            leaf_inverse,
            local_pivots,
            local_inverse,
            upper_pivots,
            upper_inverse,
            kept,
        ],
        anywhere_in=1,
    )
    pack, own_up = call(
        functools.partial(device_kernel, share, group, rank),
        [f32((3 * share - 1) * rank // 2, size), f32(rank, total_columns)],
        [
            pltpu.VMEM((share, total_columns, size), jnp.bfloat16),
            pltpu.VMEM((share * rank, total_columns), jnp.float32),
        ],
        [kept] + [arrived[tier] for tier in range(1, parts)] + [leaf_factors, own_factors],
    )
    near_ups = [vec_send(own_up, tier) for tier in range(1, parts)]
    joined, own_up = call(
        functools.partial(group_kernel, share, group, rank),
        [f32((parts - 1) * rank, width), f32(rank, total_columns)],
        [pltpu.VMEM((parts * rank, total_columns), jnp.float32)],
        [own_up] + near_ups + [group_factors],
    )
    later, own_up = lax.optimization_barrier((pack, own_up))
    late = LATE if parts > max(LATE) else ()
    others = [vec_send(later if tier in late else pack, tier) for tier in range(1, parts)]

    maps = []
    for tier in range(UPL):
        partner = lax.ppermute(own_up, "leaf", [(i, i ^ (1 << tier)) for i in range(leaf_total)])
        operands = [own_up, partner, upper_factors]
        ups = pltpu.VMEM((width, total_columns), jnp.float32)
        if tier < UPL - 1:
            interp, own_up = call(
                functools.partial(upper_kernel, tier, rank),
                [f32(rank, width), f32(rank, total_columns)],
                [ups],
                operands,
                flops=ROUND_FLOPS,
            )
            maps.append(interp)
    upper_map, top, leaf_map, local_map = call(
        functools.partial(finish_kernel, UPL - 1, share, group, rank),
        [
            f32(UPL, rank, width),
            f32(columns, rank),
            f32(group * rank, size),
            f32((group - 1) * rank, width),
        ],
        [
            ups,
            pltpu.VMEM((total_columns, rank), jnp.float32),
            pltpu.SemaphoreType.DMA((parts * (share + 1) + 1,)),
        ],
        operands + maps + [pack] + others + [joined],
        flops=ROUND_FLOPS,
        anywhere_in=parts + 1,
        anywhere_out=2,
    )
    return (
        jnp.swapaxes(leaf_map.reshape(group, rank, size), 1, 2),
        jnp.swapaxes(local_map.reshape(group - 1, rank, width), 1, 2),
        jnp.swapaxes(upper_map, 1, 2)[None],
        top[None],
    )


def solution(mesh):
    placed = (
        P("leaf", None, None),
        P("leaf", "vec", None),
        P("leaf", None),
        P("leaf", None),
        P("leaf", None, None),
        P("leaf", None),
        P("leaf", None, None),
        P(),
        P(),
    )
    return jax.shard_map(
        on_device,
        mesh=mesh,
        in_specs=placed,
        out_specs=(
            P("leaf", None, None),
            P("leaf", None, None),
            P("leaf", None, None, None),
            P("leaf", "vec", None),
        ),
        check_vma=False,
    )
```

```python
import functools

import jax
import jax.numpy as jnp
from jax import lax
from jax.experimental import pallas as pl
from jax.experimental.pallas import tpu as pltpu
from jax.sharding import PartitionSpec as P

UPL = 3

SOFTEN = 0.0009
EPSILON = 1e-06
FLIGHT = 8
DEPTH = 128
CHUNK = 256
ROUND_FLOPS = 1_150_000_000
VMEM_BYTES = 20 * 1024 * 1024
VMEM = pltpu.MemorySpace.VMEM
SMEM = pltpu.MemorySpace.SMEM


def nt(a, b):
    return lax.dot_general(a, b, (((1,), (1,)), ((), ())), preferred_element_type=jnp.float32)


def nn(a, b):
    return lax.dot_general(a, b, (((1,), (0,)), ((), ())), preferred_element_type=jnp.float32)


def split(a):
    high = a.astype(jnp.bfloat16)
    low = (a - high.astype(jnp.float32)).astype(jnp.bfloat16)
    return high, low


def stacked_split(a):
    high, low = split(a)
    return jnp.concatenate([high, low], axis=0)


def halves(a):
    rows = a.shape[0] // 2
    return a[:rows] + a[rows:]


def coordinates(points, extra):
    row = lax.broadcasted_iota(jnp.int32, (8, points.shape[1]), 0)
    padded = jnp.concatenate(
        [points, jnp.full((5, points.shape[1]), 0.5, jnp.float32)], axis=0
    )
    centred = padded - 0.5
    high, low = [part.astype(jnp.float32) for part in split(centred)]
    norm = jnp.sum(centred * centred, axis=0, keepdims=True) + extra
    first, rest = [part.astype(jnp.float32) for part in split(norm)]
    second, third = [part.astype(jnp.float32) for part in split(norm - first)]
    norms = jnp.where(row == 0, first, jnp.where(row == 1, second, jnp.where(row == 2, third, 0.0)))
    return high, low, norms, jnp.where(row < 3, 1.0, 0.0)


def far_features(points):
    high, low, norm, one = coordinates(points, SOFTEN)
    vacant = jnp.zeros((DEPTH - 48, points.shape[1]), jnp.float32)
    return jnp.concatenate(
        [-2.0 * high, -2.0 * low, -2.0 * high, -2.0 * low, one, norm, vacant], axis=0
    ).astype(jnp.bfloat16)


def near_features(points):
    high, low, norm, one = coordinates(points, 0.0)
    vacant = jnp.zeros((DEPTH - 48, points.shape[1]), jnp.float32)
    return jnp.transpose(
        jnp.concatenate([high, high, low, low, norm, one, vacant], axis=0)
    ).astype(jnp.bfloat16)


def add_blocks(share, tiers, base, wanted, nb_ref, far, vectors, near, total, tiles, codes):
    me = lax.axis_index("vec")
    count, slots = nb_ref.shape
    first = lax.axis_index("leaf") * count
    flight, size = tiles.shape[0], tiles.shape[1]
    idle = count * 64

    for way in range(flight):
        codes[way] = idle
    filled = jnp.int32(flight)
    for tier in tiers:
        for part in range(share):
            cluster = (me ^ tier) * share + part
            shift = cluster * 64 + count - base - first
            for slot in range(slots):
                listed = nb_ref[cluster, slot]
                codes[filled] = listed + shift
                filled += wanted(listed, first, count).astype(jnp.int32)
    for way in range(flight):
        codes[filled + way] = idle
    tiles[...] = jnp.zeros(tiles.shape, tiles.dtype)

    def multiply(code, tile):
        row = code // 64
        total[row] = total[row] + nt(vectors(code % 64), tile[...])

    def evaluate(code, tile):
        row = code // 64
        position = code % 64
        for top in range(0, size, CHUNK):
            distance = nn(near[row, top : top + CHUNK, :], far[position])
            tile[top : top + CHUNK, :] = lax.rsqrt(distance).astype(jnp.bfloat16)

    def step(index, carry):
        for way in range(flight):
            multiply(codes[index * flight + way], tiles.at[way])
            evaluate(codes[(index + 1) * flight + way], tiles.at[way])
        return carry

    steps = (filled - 1) // flight
    lax.fori_loop(0, steps, step, 0)
    for way in range(flight):
        multiply(codes[steps * flight + way], tiles.at[way])


def inside(listed, first, count):
    return (listed >= first) & (listed < first + count)


def outside(listed, first, count):
    return (listed >= 0) & ((listed < first) | (listed >= first + count))


def anywhere(listed, first, count):
    return listed >= 0


def joined_points(joined, count):
    points = joined[joined.shape[0] - 3 * count :, :].astype(jnp.float32)
    return [points[3 * cluster : 3 * cluster + 3] for cluster in range(count)]


def own_kernel(share, tiers, nb_ref, joined, total, far, near, tiles, codes):
    count, columns = far.shape[0], total.shape[1]
    for cluster, points in enumerate(joined_points(joined, count)):
        far[cluster] = far_features(points)
        near[cluster] = near_features(points)
    near[count] = near[0]
    total[...] = jnp.zeros(total.shape, total.dtype)

    def vectors(place):
        return joined[pl.ds(pl.multiple_of(place * columns, columns), columns), :]

    add_blocks(share, tiers, count, inside, nb_ref, far, vectors, near, total, tiles, codes)


def halo_kernel(share, tiers, nb_ref, joined, inner, outer, own_far, near, start, *refs):
    outs = refs[: len(tiers)]
    far, vectors, total, tiles, codes = refs[len(tiers) :]
    count, columns = own_far.shape[0], start.shape[1]
    me = lax.axis_index("vec")
    odd = lax.axis_index("leaf") & 1
    for place, source in ((2 * odd, outer), (2 - 2 * odd, inner), (1, joined)):
        for cluster in range(count):
            vectors[place * count + cluster] = source[cluster * columns : (cluster + 1) * columns, :]
        if source is joined:
            far[count : 2 * count] = own_far[...]
            continue
        for cluster, points in enumerate(joined_points(source, count)):
            far[place * count + cluster] = far_features(points)
    total[...] = start[...]

    def read(place):
        return vectors[place]

    add_blocks(share, tiers, 0, outside, nb_ref, far, read, near, total, tiles, codes)
    for tier, out in zip(tiers, outs):
        part = total[pl.ds((me ^ tier) * share, share)]
        out[...] = (part * 0.015625).astype(out.dtype)


def kept_kernel(share, nb_ref, far, vectors, near, out, total, tiles, codes):
    mine = pl.ds(lax.axis_index("vec") * share, share)
    total[mine] = jnp.zeros((share,) + total.shape[1:], total.dtype)

    def read(place):
        return vectors[place]

    add_blocks(share, (0,), 0, anywhere, nb_ref, far, read, near, total, tiles, codes)
    out[...] = (total[mine] * 0.015625).astype(out.dtype)


def join_kernel(points, probe, joined):
    count, columns, _ = probe.shape
    for cluster in range(count):
        joined[cluster * columns : (cluster + 1) * columns, :] = probe[cluster]
    joined[count * columns :, :] = jnp.concatenate(
        [points[cluster].astype(jnp.float32) for cluster in range(count)], axis=0
    ).astype(joined.dtype)


def near_call(body, outs, scratch, operands, rows, per_row):
    nb, size = operands[0], outs[0].shape[-1]
    blocks = rows * per_row
    return pl.pallas_call(
        body,
        out_shape=outs,
        in_specs=[pl.BlockSpec(memory_space=SMEM)]
        + [pl.BlockSpec(memory_space=VMEM)] * (len(operands) - 1),
        out_specs=[pl.BlockSpec(memory_space=VMEM)] * len(outs),
        scratch_shapes=scratch
        + [
            pltpu.VMEM((FLIGHT, size, size), jnp.bfloat16),
            pltpu.SMEM((rows * nb.shape[1] + 2 * FLIGHT,), jnp.int32),
        ],
        compiler_params=pltpu.CompilerParams(vmem_limit_bytes=VMEM_BYTES),
        cost_estimate=pl.CostEstimate(
            flops=blocks * size * size * 256,
            bytes_accessed=sum(o.size * o.dtype.itemsize for o in operands),
            transcendentals=blocks * size * size,
        ),
    )(*operands)


def pivot_factor(pivots, inverse, width):
    chosen = (
        lax.broadcasted_iota(jnp.int32, (width, pivots.shape[1]), 0) == pivots
    ).astype(jnp.bfloat16)
    return nt(stacked_split(jnp.transpose(inverse)), chosen).astype(jnp.bfloat16)


def leaf_node(sketch, factor):
    wide = sketch.astype(jnp.float32)
    mean_sq = jnp.sum(wide * wide, keepdims=True) / (sketch.shape[0] * sketch.shape[1]) + EPSILON
    scale = 1.0 / (sketch.shape[0] * mean_sq)
    picked = halves(nt(factor, sketch))
    raw = halves(nn(stacked_split(picked), sketch))
    interp = raw * scale
    upward = halves(nt(stacked_split(raw), sketch)) * (scale * lax.rsqrt(mean_sq))
    return interp, upward


def tree_node(sketch, factor):
    width, columns = sketch.shape
    mean_sq = jnp.sum(sketch * sketch, keepdims=True) / (width * columns) + EPSILON
    scale = 1.0 / (columns * mean_sq)
    parts = stacked_split(sketch)
    picked = halves(nn(jnp.concatenate([factor, factor], axis=1), parts))
    raw = halves(nt(stacked_split(picked), parts))
    raw = raw[:, :width] + raw[:, width:]
    interp = raw * scale
    both = stacked_split(raw)
    upward = halves(nn(jnp.concatenate([both, both], axis=1), parts)) * (scale * lax.rsqrt(mean_sq))
    return interp, upward


def own_nodes(share, group, me):
    rows, level_first, nodes = [], 0, share // 2
    while nodes >= 1:
        rows += [level_first + me * nodes + node for node in range(nodes)]
        level_first += (group // share) * nodes
        nodes //= 2
    return rows


def factor_kernel(
    share,
    leaf_total,
    leaf_pivots,
    leaf_inverse,
    local_pivots,
    local_inverse,
    upper_pivots,
    upper_inverse,
    _,
    leaf_out,
    own_out,
    group_out,
    upper_out,
):
    me = lax.axis_index("vec")
    group = leaf_pivots.shape[0]

    def put(out, index, pivots, inverse, row):
        out[index] = pivot_factor(pivots[pl.ds(row, 1), :], inverse[row], out.shape[2])

    for cluster in range(share):
        put(leaf_out, cluster, leaf_pivots, leaf_inverse, me * share + cluster)
    for index, row in enumerate(own_nodes(share, group, me)):
        put(own_out, index, local_pivots, local_inverse, row)
    for index in range(group // share - 1):
        put(group_out, index, local_pivots, local_inverse, group - group // share + index)
    heap_first = 0
    for tier in range(UPL):
        node = heap_first + (lax.axis_index("leaf") >> (tier + 1))
        put(upper_out, tier, upper_pivots, upper_inverse, node)
        heap_first += leaf_total >> (tier + 1)


def device_kernel(share, group, rank, own, *refs):
    parts = group // share
    arrived, refs = refs[: parts - 1], refs[parts - 1 :]
    leaf_factors, own_factors, pack, up_out, sketch, ups = refs
    me = lax.axis_index("vec")
    columns = own.shape[1]
    width = 2 * rank
    for tier, piece in enumerate((own,) + tuple(arrived)):
        place = pl.ds(pl.multiple_of((me ^ tier) * columns, columns), columns)
        for cluster in range(share):
            sketch[cluster, place, :] = piece[cluster]
    for cluster in range(share):
        interp, upward = leaf_node(sketch[cluster], leaf_factors[cluster])
        pack[cluster * rank : (cluster + 1) * rank, :] = interp
        ups[cluster * rank : (cluster + 1) * rank, :] = upward
    nodes, packed = share // 2, 0
    while nodes >= 1:
        results = []
        for node in range(nodes):
            interp, upward = tree_node(
                ups[2 * node * rank : 2 * (node + 1) * rank, :], own_factors[packed]
            )
            for lane, source, top, height in pack_places(packed, share, rank):
                pack[top : top + height, lane : lane + width] = interp[source : source + height]
            results.append(upward)
            packed += 1
        for node, upward in enumerate(results):
            ups[node * rank : (node + 1) * rank, :] = upward
        nodes //= 2
    up_out[...] = ups[0:rank, :]


def pack_places(index, share, rank):
    top = share * rank + index // 2 * rank
    if index < share - 2:
        return [(index % 2 * 2 * rank, 0, top, rank)]
    return [(0, 0, top, rank // 2), (2 * rank, rank // 2, top, rank // 2)]


def group_kernel(share, group, rank, own, *refs):
    parts = group // share
    arrived, refs = refs[: parts - 1], refs[parts - 1 :]
    factors, interps, up_out, ups = refs
    me = lax.axis_index("vec")
    for tier, piece in enumerate((own,) + tuple(arrived)):
        ups[pl.ds(pl.multiple_of((me ^ tier) * rank, rank), rank), :] = piece[...]
    done = 0
    nodes = parts // 2
    while nodes >= 1:
        results = []
        for node in range(nodes):
            interp, upward = tree_node(
                ups[2 * node * rank : 2 * (node + 1) * rank, :], factors[done]
            )
            interps[done * rank : (done + 1) * rank, :] = interp
            results.append(upward)
            done += 1
        for node, upward in enumerate(results):
            ups[node * rank : (node + 1) * rank, :] = upward
        nodes //= 2
    up_out[...] = ups[0:rank, :]


def upper_node(tier, rank, own, arrived, factors, ups):
    side = (lax.axis_index("leaf") >> tier) & 1
    ups[pl.ds(pl.multiple_of(side * rank, rank), rank), :] = own[...]
    ups[pl.ds(pl.multiple_of((1 - side) * rank, rank), rank), :] = arrived[...]
    return tree_node(ups[...], factors[tier])


def upper_kernel(tier, rank, own, arrived, factors, interp_out, up_out, ups):
    interp, upward = upper_node(tier, rank, own, arrived, factors, ups)
    interp_out[...] = interp
    up_out[...] = upward


def finish_kernel(tier, share, group, rank, own, arrived, factors, *refs):
    parts = group // share
    earlier, refs = refs[:tier], refs[tier:]
    packs, refs = refs[:parts], refs[parts:]
    joined, interps, top, leaf_out, local_out, ups, turned, sems = refs
    me = lax.axis_index("vec")
    copies = []

    def put(source, target):
        copies.append(pltpu.make_async_copy(source, target, sems.at[len(copies)]))
        copies[-1].start()

    def rows_at(start, height):
        return pl.ds(pl.multiple_of(start, height), height)

    for flip, piece in enumerate(packs):
        device = me ^ flip
        leaves = share * rank
        put(piece.at[0:leaves], leaf_out.at[rows_at(device * leaves, leaves)])
        for index, row in enumerate(own_nodes(share, group, device)):
            for lane, source, start, height in pack_places(index, share, rank):
                put(
                    piece.at[start : start + height, lane : lane + 2 * rank],
                    local_out.at[rows_at(row * rank + source, height)],
                )
    put(joined, local_out.at[(group - parts) * rank : (group - 1) * rank])

    interp, upward = upper_node(tier, rank, own, arrived, factors, ups)
    for index, ref in enumerate(earlier):
        interps[index] = ref[...]
    interps[tier] = interp
    turned[...] = jnp.transpose(upward)
    columns = top.shape[0]
    place = pl.multiple_of(me * columns, columns)
    top[...] = turned[pl.ds(place, columns), :]
    for copy in copies:
        copy.wait()


def call(body, outs, scratch, operands, flops=0, anywhere_in=0, anywhere_out=0):
    fixed = pl.BlockSpec(memory_space=VMEM)
    free = pl.BlockSpec(memory_space=pl.ANY)
    return pl.pallas_call(
        body,
        out_shape=outs,
        in_specs=[fixed] * (len(operands) - anywhere_in) + [free] * anywhere_in,
        out_specs=[fixed] * (len(outs) - anywhere_out) + [free] * anywhere_out,
        scratch_shapes=scratch,
        compiler_params=pltpu.CompilerParams(vmem_limit_bytes=VMEM_BYTES),
        cost_estimate=pl.CostEstimate(
            flops=flops, bytes_accessed=sum(o.size * o.dtype.itemsize for o in operands), transcendentals=0
        ),
    )(*operands)


def f32(*shape):
    return jax.ShapeDtypeStruct(shape, jnp.float32)


def on_device(
    points,
    probe_vectors,
    neighbours,
    leaf_pivots,
    leaf_inverse,
    local_pivots,
    local_inverse,
    upper_pivots,
    upper_inverse,
):
    group, columns, size = probe_vectors.shape
    rank = leaf_pivots.shape[1]
    leaf_total = lax.axis_size("leaf")
    parts = lax.axis_size("vec")
    share = group // parts
    total_columns = columns * parts

    joined = call(
        join_kernel,
        [jax.ShapeDtypeStruct((group * (columns + 3), size), jnp.bfloat16)],
        [],
        [points, probe_vectors],
    )[0]
    swaps = []
    for odd in (0, 1):
        pairs = [(i, i + 1) for i in range(odd, leaf_total - 1, 2)]
        swaps.append(lax.ppermute(joined, "leaf", pairs + [(j, i) for i, j in pairs]))
    inner, outer = swaps

    def vec_send(array, tier):
        return lax.ppermute(array, "vec", [(i, i ^ tier) for i in range(parts)])

    away = list(range(parts - 1, 0, -1))
    sent_rows = (parts - 1) * share

    def bf16(*shape):
        return jax.ShapeDtypeStruct(shape, jnp.bfloat16)

    started, own_far, near = near_call(
        functools.partial(own_kernel, share, away),
        [f32(group + 1, columns, size), bf16(group, DEPTH, size), bf16(group + 1, size, DEPTH)],
        [],
        [neighbours, joined],
        sent_rows,
        6,
    )
    *sent, far, vectors = near_call(
        functools.partial(halo_kernel, share, away),
        [bf16(share, columns, size)] * len(away)
        + [bf16(3 * group, DEPTH, size), bf16(3 * group, columns, size)],
        [pltpu.VMEM((group + 1, columns, size), jnp.float32)],
        [neighbours, joined, inner, outer, own_far, near, started],
        sent_rows,
        6,
    )
    arrived = {tier: vec_send(array, tier) for tier, array in zip(away, sent)}
    kept = near_call(
        functools.partial(kept_kernel, share),
        [bf16(share, columns, size)],
        [pltpu.VMEM((group + 1, columns, size), jnp.float32)],
        [neighbours, far, vectors, near],
        share,
        12,
    )[0]

    width = 2 * rank
    leaf_factors, own_factors, group_factors, upper_factors = call(
        functools.partial(factor_kernel, share, leaf_total),
        [
            bf16(share, width, size),
            bf16(max(1, share - 1), width, width),
            bf16(parts - 1, width, width),
            bf16(UPL, width, width),
        ],
        [],
        [
            leaf_pivots,
            leaf_inverse,
            local_pivots,
            local_inverse,
            upper_pivots,
            upper_inverse,
            kept,
        ],
        anywhere_in=1,
    )
    pack, own_up = call(
        functools.partial(device_kernel, share, group, rank),
        [f32((3 * share - 1) * rank // 2, size), f32(rank, total_columns)],
        [
            pltpu.VMEM((share, total_columns, size), jnp.bfloat16),
            pltpu.VMEM((share * rank, total_columns), jnp.float32),
        ],
        [kept] + [arrived[tier] for tier in range(1, parts)] + [leaf_factors, own_factors],
    )
    near_ups = [vec_send(own_up, tier) for tier in range(1, parts)]
    joined, own_up = call(
        functools.partial(group_kernel, share, group, rank),
        [f32((parts - 1) * rank, width), f32(rank, total_columns)],
        [pltpu.VMEM((parts * rank, total_columns), jnp.float32)],
        [own_up] + near_ups + [group_factors],
    )
    pack, own_up = lax.optimization_barrier((pack, own_up))
    others = [vec_send(pack, tier) for tier in range(1, parts)]

    maps = []
    for tier in range(UPL):
        partner = lax.ppermute(own_up, "leaf", [(i, i ^ (1 << tier)) for i in range(leaf_total)])
        operands = [own_up, partner, upper_factors]
        ups = pltpu.VMEM((width, total_columns), jnp.float32)
        if tier < UPL - 1:
            interp, own_up = call(
                functools.partial(upper_kernel, tier, rank),
                [f32(rank, width), f32(rank, total_columns)],
                [ups],
                operands,
                flops=ROUND_FLOPS,
            )
            maps.append(interp)
    upper_map, top, leaf_map, local_map = call(
        functools.partial(finish_kernel, UPL - 1, share, group, rank),
        [
            f32(UPL, rank, width),
            f32(columns, rank),
            f32(group * rank, size),
            f32((group - 1) * rank, width),
        ],
        [
            ups,
            pltpu.VMEM((total_columns, rank), jnp.float32),
            pltpu.SemaphoreType.DMA((parts * (share + 1) + 1,)),
        ],
        operands + maps + [pack] + others + [joined],
        flops=ROUND_FLOPS,
        anywhere_in=parts + 1,
        anywhere_out=2,
    )
    return (
        jnp.swapaxes(leaf_map.reshape(group, rank, size), 1, 2),
        jnp.swapaxes(local_map.reshape(group - 1, rank, width), 1, 2),
        jnp.swapaxes(upper_map, 1, 2)[None],
        top[None],
    )


def solution(mesh):
    placed = (
        P("leaf", None, None),
        P("leaf", "vec", None),
        P("leaf", None),
        P("leaf", None),
        P("leaf", None, None),
        P("leaf", None),
        P("leaf", None, None),
        P(),
        P(),
    )
    return jax.shard_map(
        on_device,
        mesh=mesh,
        in_specs=placed,
        out_specs=(
            P("leaf", None, None),
            P("leaf", None, None),
            P("leaf", None, None, None),
            P("leaf", "vec", None),
        ),
        check_vma=False,
    )
```

```python
import functools

import jax
import jax.numpy as jnp
from jax import lax
from jax.experimental import pallas as pl
from jax.experimental.pallas import tpu as pltpu
from jax.sharding import PartitionSpec as P

UPL = 3

SOFTEN = 0.0009
EPSILON = 1e-06
FLIGHT = 8
DEPTH = 128
CHUNK = 256
ROUND_FLOPS = 950_000_000
VMEM_BYTES = 20 * 1024 * 1024
VMEM = pltpu.MemorySpace.VMEM
SMEM = pltpu.MemorySpace.SMEM


def nt(a, b):
    return lax.dot_general(a, b, (((1,), (1,)), ((), ())), preferred_element_type=jnp.float32)


def nn(a, b):
    return lax.dot_general(a, b, (((1,), (0,)), ((), ())), preferred_element_type=jnp.float32)


def split(a):
    high = a.astype(jnp.bfloat16)
    low = (a - high.astype(jnp.float32)).astype(jnp.bfloat16)
    return high, low


def stacked_split(a):
    high, low = split(a)
    return jnp.concatenate([high, low], axis=0)


def halves(a):
    rows = a.shape[0] // 2
    return a[:rows] + a[rows:]


def coordinates(points, extra):
    row = lax.broadcasted_iota(jnp.int32, (8, points.shape[1]), 0)
    padded = jnp.concatenate(
        [points, jnp.full((5, points.shape[1]), 0.5, jnp.float32)], axis=0
    )
    centred = padded - 0.5
    high, low = [part.astype(jnp.float32) for part in split(centred)]
    norm = jnp.sum(centred * centred, axis=0, keepdims=True) + extra
    first, rest = [part.astype(jnp.float32) for part in split(norm)]
    second, third = [part.astype(jnp.float32) for part in split(norm - first)]
    norms = jnp.where(row == 0, first, jnp.where(row == 1, second, jnp.where(row == 2, third, 0.0)))
    return high, low, norms, jnp.where(row < 3, 1.0, 0.0)


def far_features(points):
    high, low, norm, one = coordinates(points, SOFTEN)
    vacant = jnp.zeros((DEPTH - 48, points.shape[1]), jnp.float32)
    return jnp.concatenate(
        [-2.0 * high, -2.0 * low, -2.0 * high, -2.0 * low, one, norm, vacant], axis=0
    ).astype(jnp.bfloat16)


def near_features(points):
    high, low, norm, one = coordinates(points, 0.0)
    vacant = jnp.zeros((DEPTH - 48, points.shape[1]), jnp.float32)
    return jnp.transpose(
        jnp.concatenate([high, high, low, low, norm, one, vacant], axis=0)
    ).astype(jnp.bfloat16)


def add_blocks(share, tiers, base, wanted, nb_ref, far, vectors, near, total, tiles, codes):
    me = lax.axis_index("vec")
    count, slots = nb_ref.shape
    first = lax.axis_index("leaf") * count
    flight, size = tiles.shape[0], tiles.shape[1]
    idle = count * 64

    for way in range(flight):
        codes[way] = idle
    filled = jnp.int32(flight)
    for tier in tiers:
        for part in range(share):
            cluster = (me ^ tier) * share + part
            shift = cluster * 64 + count - base - first
            for slot in range(slots):
                listed = nb_ref[cluster, slot]
                codes[filled] = listed + shift
                filled += wanted(listed, first, count).astype(jnp.int32)
    for way in range(flight):
        codes[filled + way] = idle
    tiles[...] = jnp.zeros(tiles.shape, tiles.dtype)

    def multiply(code, tile):
        row = code // 64
        total[row] = total[row] + nt(vectors(code % 64), tile[...])

    def evaluate(code, tile):
        row = code // 64
        position = code % 64
        for top in range(0, size, CHUNK):
            distance = nn(near[row, top : top + CHUNK, :], far[position])
            tile[top : top + CHUNK, :] = lax.rsqrt(distance).astype(jnp.bfloat16)

    def step(index, carry):
        for way in range(flight):
            multiply(codes[index * flight + way], tiles.at[way])
            evaluate(codes[(index + 1) * flight + way], tiles.at[way])
        return carry

    steps = (filled - 1) // flight
    lax.fori_loop(0, steps, step, 0)
    for way in range(flight):
        multiply(codes[steps * flight + way], tiles.at[way])


def inside(listed, first, count):
    return (listed >= first) & (listed < first + count)


def outside(listed, first, count):
    return (listed >= 0) & ((listed < first) | (listed >= first + count))


def anywhere(listed, first, count):
    return listed >= 0


def joined_points(joined, count):
    points = joined[joined.shape[0] - 3 * count :, :].astype(jnp.float32)
    return [points[3 * cluster : 3 * cluster + 3] for cluster in range(count)]


def own_kernel(share, tiers, nb_ref, joined, total, far, near, tiles, codes):
    count, columns = far.shape[0], total.shape[1]
    for cluster, points in enumerate(joined_points(joined, count)):
        far[cluster] = far_features(points)
        near[cluster] = near_features(points)
    near[count] = near[0]
    total[...] = jnp.zeros(total.shape, total.dtype)

    def vectors(place):
        return joined[pl.ds(pl.multiple_of(place * columns, columns), columns), :]

    add_blocks(share, tiers, count, inside, nb_ref, far, vectors, near, total, tiles, codes)


def halo_kernel(share, tiers, nb_ref, joined, inner, outer, own_far, near, start, *refs):
    outs = refs[: len(tiers)]
    far, vectors, total, tiles, codes = refs[len(tiers) :]
    count, columns = own_far.shape[0], start.shape[1]
    me = lax.axis_index("vec")
    odd = lax.axis_index("leaf") & 1
    for place, source in ((2 * odd, outer), (2 - 2 * odd, inner), (1, joined)):
        for cluster in range(count):
            vectors[place * count + cluster] = source[cluster * columns : (cluster + 1) * columns, :]
        if source is joined:
            far[count : 2 * count] = own_far[...]
            continue
        for cluster, points in enumerate(joined_points(source, count)):
            far[place * count + cluster] = far_features(points)
    total[...] = start[...]

    def read(place):
        return vectors[place]

    add_blocks(share, tiers, 0, outside, nb_ref, far, read, near, total, tiles, codes)
    for tier, out in zip(tiers, outs):
        part = total[pl.ds((me ^ tier) * share, share)]
        out[...] = (part * 0.015625).astype(out.dtype)


def kept_kernel(share, nb_ref, far, vectors, near, out, total, tiles, codes):
    mine = pl.ds(lax.axis_index("vec") * share, share)
    total[mine] = jnp.zeros((share,) + total.shape[1:], total.dtype)

    def read(place):
        return vectors[place]

    add_blocks(share, (0,), 0, anywhere, nb_ref, far, read, near, total, tiles, codes)
    out[...] = (total[mine] * 0.015625).astype(out.dtype)


def join_kernel(points, probe, joined):
    count, columns, _ = probe.shape
    for cluster in range(count):
        joined[cluster * columns : (cluster + 1) * columns, :] = probe[cluster]
    joined[count * columns :, :] = jnp.concatenate(
        [points[cluster].astype(jnp.float32) for cluster in range(count)], axis=0
    ).astype(joined.dtype)


def near_call(body, outs, scratch, operands, rows, per_row):
    nb, size = operands[0], outs[0].shape[-1]
    blocks = rows * per_row
    return pl.pallas_call(
        body,
        out_shape=outs,
        in_specs=[pl.BlockSpec(memory_space=SMEM)]
        + [pl.BlockSpec(memory_space=VMEM)] * (len(operands) - 1),
        out_specs=[pl.BlockSpec(memory_space=VMEM)] * len(outs),
        scratch_shapes=scratch
        + [
            pltpu.VMEM((FLIGHT, size, size), jnp.bfloat16),
            pltpu.SMEM((rows * nb.shape[1] + 2 * FLIGHT,), jnp.int32),
        ],
        compiler_params=pltpu.CompilerParams(vmem_limit_bytes=VMEM_BYTES),
        cost_estimate=pl.CostEstimate(
            flops=blocks * size * size * 256,
            bytes_accessed=sum(o.size * o.dtype.itemsize for o in operands),
            transcendentals=blocks * size * size,
        ),
    )(*operands)


def pivot_factor(pivots, inverse, width):
    chosen = (
        lax.broadcasted_iota(jnp.int32, (width, pivots.shape[1]), 0) == pivots
    ).astype(jnp.bfloat16)
    return nt(stacked_split(jnp.transpose(inverse)), chosen).astype(jnp.bfloat16)


def leaf_node(sketch, factor):
    wide = sketch.astype(jnp.float32)
    mean_sq = jnp.sum(wide * wide, keepdims=True) / (sketch.shape[0] * sketch.shape[1]) + EPSILON
    scale = 1.0 / (sketch.shape[0] * mean_sq)
    picked = halves(nt(factor, sketch))
    raw = halves(nn(stacked_split(picked), sketch))
    interp = raw * scale
    upward = halves(nt(stacked_split(raw), sketch)) * (scale * lax.rsqrt(mean_sq))
    return interp, upward


def tree_node(sketch, factor):
    width, columns = sketch.shape
    mean_sq = jnp.sum(sketch * sketch, keepdims=True) / (width * columns) + EPSILON
    scale = 1.0 / (columns * mean_sq)
    parts = stacked_split(sketch)
    picked = halves(nn(jnp.concatenate([factor, factor], axis=1), parts))
    raw = halves(nt(stacked_split(picked), parts))
    raw = raw[:, :width] + raw[:, width:]
    interp = raw * scale
    both = stacked_split(raw)
    upward = halves(nn(jnp.concatenate([both, both], axis=1), parts)) * (scale * lax.rsqrt(mean_sq))
    return interp, upward


def own_nodes(share, group, me):
    rows, level_first, nodes = [], 0, share // 2
    while nodes >= 1:
        rows += [level_first + me * nodes + node for node in range(nodes)]
        level_first += (group // share) * nodes
        nodes //= 2
    return rows


def factor_kernel(
    share,
    leaf_total,
    leaf_pivots,
    leaf_inverse,
    local_pivots,
    local_inverse,
    upper_pivots,
    upper_inverse,
    _,
    leaf_out,
    own_out,
    group_out,
    upper_out,
):
    me = lax.axis_index("vec")
    group = leaf_pivots.shape[0]

    def put(out, index, pivots, inverse, row):
        out[index] = pivot_factor(pivots[pl.ds(row, 1), :], inverse[row], out.shape[2])

    for cluster in range(share):
        put(leaf_out, cluster, leaf_pivots, leaf_inverse, me * share + cluster)
    for index, row in enumerate(own_nodes(share, group, me)):
        put(own_out, index, local_pivots, local_inverse, row)
    for index in range(group // share - 1):
        put(group_out, index, local_pivots, local_inverse, group - group // share + index)
    heap_first = 0
    for tier in range(UPL):
        node = heap_first + (lax.axis_index("leaf") >> (tier + 1))
        put(upper_out, tier, upper_pivots, upper_inverse, node)
        heap_first += leaf_total >> (tier + 1)


def device_kernel(share, group, rank, own, *refs):
    parts = group // share
    arrived, refs = refs[: parts - 1], refs[parts - 1 :]
    leaf_factors, own_factors, pack, up_out, sketch, ups = refs
    me = lax.axis_index("vec")
    columns = own.shape[1]
    width = 2 * rank
    for tier, piece in enumerate((own,) + tuple(arrived)):
        place = pl.ds(pl.multiple_of((me ^ tier) * columns, columns), columns)
        for cluster in range(share):
            sketch[cluster, place, :] = piece[cluster]
    for cluster in range(share):
        interp, upward = leaf_node(sketch[cluster], leaf_factors[cluster])
        pack[cluster * rank : (cluster + 1) * rank, :] = interp
        ups[cluster * rank : (cluster + 1) * rank, :] = upward
    nodes, packed = share // 2, 0
    while nodes >= 1:
        results = []
        for node in range(nodes):
            interp, upward = tree_node(
                ups[2 * node * rank : 2 * (node + 1) * rank, :], own_factors[packed]
            )
            for lane, source, top, height in pack_places(packed, share, rank):
                pack[top : top + height, lane : lane + width] = interp[source : source + height]
            results.append(upward)
            packed += 1
        for node, upward in enumerate(results):
            ups[node * rank : (node + 1) * rank, :] = upward
        nodes //= 2
    up_out[...] = ups[0:rank, :]


def pack_places(index, share, rank):
    top = share * rank + index // 2 * rank
    if index < share - 2:
        return [(index % 2 * 2 * rank, 0, top, rank)]
    return [(0, 0, top, rank // 2), (2 * rank, rank // 2, top, rank // 2)]


def group_kernel(share, group, rank, own, *refs):
    parts = group // share
    arrived, refs = refs[: parts - 1], refs[parts - 1 :]
    factors, interps, up_out, ups = refs
    me = lax.axis_index("vec")
    for tier, piece in enumerate((own,) + tuple(arrived)):
        ups[pl.ds(pl.multiple_of((me ^ tier) * rank, rank), rank), :] = piece[...]
    done = 0
    nodes = parts // 2
    while nodes >= 1:
        results = []
        for node in range(nodes):
            interp, upward = tree_node(
                ups[2 * node * rank : 2 * (node + 1) * rank, :], factors[done]
            )
            interps[done * rank : (done + 1) * rank, :] = interp
            results.append(upward)
            done += 1
        for node, upward in enumerate(results):
            ups[node * rank : (node + 1) * rank, :] = upward
        nodes //= 2
    up_out[...] = ups[0:rank, :]


def upper_node(tier, rank, own, arrived, factors, ups):
    side = (lax.axis_index("leaf") >> tier) & 1
    ups[pl.ds(pl.multiple_of(side * rank, rank), rank), :] = own[...]
    ups[pl.ds(pl.multiple_of((1 - side) * rank, rank), rank), :] = arrived[...]
    return tree_node(ups[...], factors[tier])


def upper_kernel(tier, rank, own, arrived, factors, interp_out, up_out, ups):
    interp, upward = upper_node(tier, rank, own, arrived, factors, ups)
    interp_out[...] = interp
    up_out[...] = upward


def start_copies(pieces, share, group, rank, leaf_out, local_out, sems):
    copies = []

    def put(source, target):
        copies.append(pltpu.make_async_copy(source, target, sems.at[len(copies)]))
        copies[-1].start()

    def rows_at(start, height):
        return pl.ds(pl.multiple_of(start, height), height)

    leaves = share * rank
    for flip, first, piece in pieces:
        device = lax.axis_index("vec") ^ flip
        end = first + piece.shape[0]
        if first < leaves:
            height = min(end, leaves) - first
            step = height if height == leaves else rank
            for row in range(0, height, step):
                put(
                    piece.at[row : row + step],
                    leaf_out.at[rows_at(device * leaves + first + row, step)],
                )
        for index, node in enumerate(own_nodes(share, group, device)):
            for lane, source, start, height in pack_places(index, share, rank):
                if first <= start < end:
                    put(
                        piece.at[start - first : start - first + height, lane : lane + 2 * rank],
                        local_out.at[rows_at(node * rank + source, height)],
                    )
    return copies


def place_kernel(flips, share, group, rank, *refs):
    packs, (joined, leaf_out, local_out, sems) = refs[: len(flips)], refs[len(flips) :]
    pieces = [(flip, 0, piece) for flip, piece in zip(flips, packs)]
    copies = start_copies(pieces, share, group, rank, leaf_out, local_out, sems)
    rows = joined.shape[0]
    target = local_out.at[local_out.shape[0] - rows :]
    copies.append(pltpu.make_async_copy(joined, target, sems.at[len(copies)]))
    copies[-1].start()
    for copy in copies:
        copy.wait()


def forward_kernel(here, there, _, upper, lower):
    upper[...] = here[0 : upper.shape[0], :]
    lower[...] = there[upper.shape[0] :, :]


def finish_kernel(tier, tails, share, group, rank, own, arrived, factors, *refs):
    earlier, refs = refs[:tier], refs[tier:]
    packs, refs = refs[: len(tails)], refs[len(tails) :]
    _, _, interps, top, leaf_out, local_out, ups, turned, sems = refs
    pieces = [(flip, first, piece) for (flip, first), piece in zip(tails, packs)]
    copies = start_copies(pieces, share, group, rank, leaf_out, local_out, sems)
    interp, upward = upper_node(tier, rank, own, arrived, factors, ups)
    for index, ref in enumerate(earlier):
        interps[index] = ref[...]
    interps[tier] = interp
    turned[...] = jnp.transpose(upward)
    columns = top.shape[0]
    place = pl.multiple_of(lax.axis_index("vec") * columns, columns)
    top[...] = turned[pl.ds(place, columns), :]
    for copy in copies:
        copy.wait()


def call(body, outs, scratch, operands, flops=0, anywhere_in=0, anywhere_out=0, aliases=None):
    fixed = pl.BlockSpec(memory_space=VMEM)
    free = pl.BlockSpec(memory_space=pl.ANY)
    return pl.pallas_call(
        body,
        out_shape=outs,
        in_specs=[fixed] * (len(operands) - anywhere_in) + [free] * anywhere_in,
        out_specs=[fixed] * (len(outs) - anywhere_out) + [free] * anywhere_out,
        scratch_shapes=scratch,
        input_output_aliases=aliases or {},
        compiler_params=pltpu.CompilerParams(vmem_limit_bytes=VMEM_BYTES),
        cost_estimate=pl.CostEstimate(
            flops=flops, bytes_accessed=sum(o.size * o.dtype.itemsize for o in operands), transcendentals=0
        ),
    )(*operands)


def f32(*shape):
    return jax.ShapeDtypeStruct(shape, jnp.float32)


def on_device(
    points,
    probe_vectors,
    neighbours,
    leaf_pivots,
    leaf_inverse,
    local_pivots,
    local_inverse,
    upper_pivots,
    upper_inverse,
):
    group, columns, size = probe_vectors.shape
    rank = leaf_pivots.shape[1]
    leaf_total = lax.axis_size("leaf")
    parts = lax.axis_size("vec")
    share = group // parts
    total_columns = columns * parts

    joined = call(
        join_kernel,
        [jax.ShapeDtypeStruct((group * (columns + 3), size), jnp.bfloat16)],
        [],
        [points, probe_vectors],
    )[0]
    swaps = []
    for odd in (0, 1):
        pairs = [(i, i + 1) for i in range(odd, leaf_total - 1, 2)]
        swaps.append(lax.ppermute(joined, "leaf", pairs + [(j, i) for i, j in pairs]))
    inner, outer = swaps

    def vec_send(array, tier):
        return lax.ppermute(array, "vec", [(i, i ^ tier) for i in range(parts)])

    away = list(range(parts - 1, 0, -1))
    sent_rows = (parts - 1) * share

    def bf16(*shape):
        return jax.ShapeDtypeStruct(shape, jnp.bfloat16)

    started, own_far, near = near_call(
        functools.partial(own_kernel, share, away),
        [f32(group + 1, columns, size), bf16(group, DEPTH, size), bf16(group + 1, size, DEPTH)],
        [],
        [neighbours, joined],
        sent_rows,
        6,
    )
    *sent, far, vectors = near_call(
        functools.partial(halo_kernel, share, away),
        [bf16(share, columns, size)] * len(away)
        + [bf16(3 * group, DEPTH, size), bf16(3 * group, columns, size)],
        [pltpu.VMEM((group + 1, columns, size), jnp.float32)],
        [neighbours, joined, inner, outer, own_far, near, started],
        sent_rows,
        6,
    )
    arrived = {tier: vec_send(array, tier) for tier, array in zip(away, sent)}
    kept = near_call(
        functools.partial(kept_kernel, share),
        [bf16(share, columns, size)],
        [pltpu.VMEM((group + 1, columns, size), jnp.float32)],
        [neighbours, far, vectors, near],
        share,
        12,
    )[0]

    width = 2 * rank
    leaf_factors, own_factors, group_factors, upper_factors = call(
        functools.partial(factor_kernel, share, leaf_total),
        [
            bf16(share, width, size),
            bf16(max(1, share - 1), width, width),
            bf16(parts - 1, width, width),
            bf16(UPL, width, width),
        ],
        [],
        [
            leaf_pivots,
            leaf_inverse,
            local_pivots,
            local_inverse,
            upper_pivots,
            upper_inverse,
            kept,
        ],
        anywhere_in=1,
    )
    pack, own_up = call(
        functools.partial(device_kernel, share, group, rank),
        [f32((3 * share - 1) * rank // 2, size), f32(rank, total_columns)],
        [
            pltpu.VMEM((share, total_columns, size), jnp.bfloat16),
            pltpu.VMEM((share * rank, total_columns), jnp.float32),
        ],
        [kept] + [arrived[tier] for tier in range(1, parts)] + [leaf_factors, own_factors],
    )
    near_ups = [vec_send(own_up, tier) for tier in range(1, parts)]
    joined, own_up = call(
        functools.partial(group_kernel, share, group, rank),
        [f32((parts - 1) * rank, width), f32(rank, total_columns)],
        [pltpu.VMEM((parts * rank, total_columns), jnp.float32)],
        [own_up] + near_ups + [group_factors],
    )
    passing = parts == 4
    flips = [0] + [tier for tier in range(1, parts) if not (passing and tier == 3)]
    packs = [pack] + [vec_send(pack, tier) for tier in flips[1:]]
    tails, tail_packs = [], []

    maps = []
    for tier in range(UPL):
        partner = lax.ppermute(own_up, "leaf", [(i, i ^ (1 << tier)) for i in range(leaf_total)])
        operands = [own_up, partner, upper_factors]
        ups = pltpu.VMEM((width, total_columns), jnp.float32)
        if tier < UPL - 1:
            interp, own_up = call(
                functools.partial(upper_kernel, tier, rank),
                [f32(rank, width), f32(rank, total_columns)],
                [ups],
                operands,
                flops=ROUND_FLOPS,
            )
            maps.append(interp)
    if passing:
        upper_rows = (share - 1) * rank
        upper, lower = call(
            forward_kernel,
            [f32(upper_rows, size), f32(pack.shape[0] - upper_rows, size)],
            [],
            [packs[1], packs[2], own_up],
            anywhere_in=1,
        )
        tails = [(3, 0), (3, upper_rows)]
        tail_packs = [vec_send(upper, 2), vec_send(lower, 1)]
    leaf_map, local_map = call(
        functools.partial(place_kernel, flips, share, group, rank),
        [f32(group * rank, size), f32((group - 1) * rank, width)],
        [pltpu.SemaphoreType.DMA((len(flips) * (share + 1) + 1,))],
        packs + [joined],
        flops=ROUND_FLOPS,
        anywhere_in=len(flips) + 1,
        anywhere_out=2,
    )
    operands += maps + tail_packs + [leaf_map, local_map]
    upper_map, top, leaf_map, local_map = call(
        functools.partial(finish_kernel, UPL - 1, tails, share, group, rank),
        [
            f32(UPL, rank, width),
            f32(columns, rank),
            f32(group * rank, size),
            f32((group - 1) * rank, width),
        ],
        [
            ups,
            pltpu.VMEM((total_columns, rank), jnp.float32),
            pltpu.SemaphoreType.DMA((2 * share + 1,)),
        ],
        operands,
        flops=ROUND_FLOPS,
        anywhere_in=len(tails) + 2,
        anywhere_out=2,
        aliases={len(operands) - 2: 2, len(operands) - 1: 3},
    )
    return (
        jnp.swapaxes(leaf_map.reshape(group, rank, size), 1, 2),
        jnp.swapaxes(local_map.reshape(group - 1, rank, width), 1, 2),
        jnp.swapaxes(upper_map, 1, 2)[None],
        top[None],
    )


def solution(mesh):
    placed = (
        P("leaf", None, None),
        P("leaf", "vec", None),
        P("leaf", None),
        P("leaf", None),
        P("leaf", None, None),
        P("leaf", None),
        P("leaf", None, None),
        P(),
        P(),
    )
    return jax.shard_map(
        on_device,
        mesh=mesh,
        in_specs=placed,
        out_specs=(
            P("leaf", None, None),
            P("leaf", None, None),
            P("leaf", None, None, None),
            P("leaf", "vec", None),
        ),
        check_vma=False,
    )
```

```python
import functools

import jax
import jax.numpy as jnp
from jax import lax
from jax.experimental import pallas as pl
from jax.experimental.pallas import tpu as pltpu
from jax.sharding import PartitionSpec as P

UPL = 3

SOFTEN = 0.0009
EPSILON = 1e-06
FLIGHT = 8
DEPTH = 128
CHUNK = 256
ROUND_FLOPS = 950_000_000
VMEM_BYTES = 20 * 1024 * 1024
VMEM = pltpu.MemorySpace.VMEM
SMEM = pltpu.MemorySpace.SMEM


def nt(a, b):
    return lax.dot_general(a, b, (((1,), (1,)), ((), ())), preferred_element_type=jnp.float32)


def nn(a, b):
    return lax.dot_general(a, b, (((1,), (0,)), ((), ())), preferred_element_type=jnp.float32)


def split(a):
    high = a.astype(jnp.bfloat16)
    low = (a - high.astype(jnp.float32)).astype(jnp.bfloat16)
    return high, low


def stacked_split(a):
    high, low = split(a)
    return jnp.concatenate([high, low], axis=0)


def halves(a):
    rows = a.shape[0] // 2
    return a[:rows] + a[rows:]


def coordinates(points, extra):
    row = lax.broadcasted_iota(jnp.int32, (8, points.shape[1]), 0)
    padded = jnp.concatenate(
        [points, jnp.full((5, points.shape[1]), 0.5, jnp.float32)], axis=0
    )
    centred = padded - 0.5
    high, low = [part.astype(jnp.float32) for part in split(centred)]
    norm = jnp.sum(centred * centred, axis=0, keepdims=True) + extra
    first, rest = [part.astype(jnp.float32) for part in split(norm)]
    second, third = [part.astype(jnp.float32) for part in split(norm - first)]
    norms = jnp.where(row == 0, first, jnp.where(row == 1, second, jnp.where(row == 2, third, 0.0)))
    return high, low, norms, jnp.where(row < 3, 1.0, 0.0)


def far_features(points):
    high, low, norm, one = coordinates(points, SOFTEN)
    vacant = jnp.zeros((DEPTH - 48, points.shape[1]), jnp.float32)
    return jnp.concatenate(
        [-2.0 * high, -2.0 * low, -2.0 * high, -2.0 * low, one, norm, vacant], axis=0
    ).astype(jnp.bfloat16)


def near_features(points):
    high, low, norm, one = coordinates(points, 0.0)
    vacant = jnp.zeros((DEPTH - 48, points.shape[1]), jnp.float32)
    return jnp.transpose(
        jnp.concatenate([high, high, low, low, norm, one, vacant], axis=0)
    ).astype(jnp.bfloat16)


def add_blocks(share, tiers, base, wanted, nb_ref, far, vectors, near, total, tiles, codes):
    me = lax.axis_index("vec")
    count, slots = nb_ref.shape
    first = lax.axis_index("leaf") * count
    flight, size = tiles.shape[0], tiles.shape[1]
    idle = count * 64

    for way in range(flight):
        codes[way] = idle
    filled = jnp.int32(flight)
    for tier in tiers:
        for part in range(share):
            cluster = (me ^ tier) * share + part
            shift = cluster * 64 + count - base - first
            for slot in range(slots):
                listed = nb_ref[cluster, slot]
                codes[filled] = listed + shift
                filled += wanted(listed, first, count).astype(jnp.int32)
    for way in range(flight):
        codes[filled + way] = idle
    tiles[...] = jnp.zeros(tiles.shape, tiles.dtype)

    def multiply(code, tile):
        row = code // 64
        total[row] = total[row] + nt(vectors(code % 64), tile[...])

    def evaluate(code, tile):
        row = code // 64
        position = code % 64
        for top in range(0, size, CHUNK):
            distance = nn(near[row, top : top + CHUNK, :], far[position])
            tile[top : top + CHUNK, :] = lax.rsqrt(distance).astype(jnp.bfloat16)

    def step(index, carry):
        for way in range(flight):
            multiply(codes[index * flight + way], tiles.at[way])
            evaluate(codes[(index + 1) * flight + way], tiles.at[way])
        return carry

    def two_steps(index, carry):
        return step(2 * index + 1, step(2 * index, carry))

    steps = (filled - 1) // flight
    lax.fori_loop(0, steps // 2, two_steps, 0)
    lax.fori_loop(steps // 2 * 2, steps, step, 0)
    for way in range(flight):
        multiply(codes[steps * flight + way], tiles.at[way])


def inside(listed, first, count):
    return (listed >= first) & (listed < first + count)


def outside(listed, first, count):
    return (listed >= 0) & ((listed < first) | (listed >= first + count))


def anywhere(listed, first, count):
    return listed >= 0


def joined_points(joined, count):
    points = joined[joined.shape[0] - 3 * count :, :].astype(jnp.float32)
    return [points[3 * cluster : 3 * cluster + 3] for cluster in range(count)]


def own_kernel(share, tiers, nb_ref, joined, total, far, near, tiles, codes):
    count, columns = far.shape[0], total.shape[1]
    for cluster, points in enumerate(joined_points(joined, count)):
        far[cluster] = far_features(points)
        near[cluster] = near_features(points)
    near[count] = near[0]
    total[...] = jnp.zeros(total.shape, total.dtype)

    def vectors(place):
        return joined[pl.ds(pl.multiple_of(place * columns, columns), columns), :]

    add_blocks(share, tiers, count, inside, nb_ref, far, vectors, near, total, tiles, codes)


def halo_kernel(share, tiers, nb_ref, joined, inner, outer, own_far, near, start, *refs):
    outs = refs[: len(tiers)]
    far, vectors, total, tiles, codes = refs[len(tiers) :]
    count, columns = own_far.shape[0], start.shape[1]
    me = lax.axis_index("vec")
    odd = lax.axis_index("leaf") & 1
    for place, source in ((2 * odd, outer), (2 - 2 * odd, inner), (1, joined)):
        for cluster in range(count):
            vectors[place * count + cluster] = source[cluster * columns : (cluster + 1) * columns, :]
        if source is joined:
            far[count : 2 * count] = own_far[...]
            continue
        for cluster, points in enumerate(joined_points(source, count)):
            far[place * count + cluster] = far_features(points)
    total[...] = start[...]

    def read(place):
        return vectors[place]

    add_blocks(share, tiers, 0, outside, nb_ref, far, read, near, total, tiles, codes)
    for tier, out in zip(tiers, outs):
        part = total[pl.ds((me ^ tier) * share, share)]
        out[...] = (part * 0.015625).astype(out.dtype)


def kept_kernel(share, nb_ref, far, vectors, near, out, total, tiles, codes):
    mine = pl.ds(lax.axis_index("vec") * share, share)
    total[mine] = jnp.zeros((share,) + total.shape[1:], total.dtype)

    def read(place):
        return vectors[place]

    add_blocks(share, (0,), 0, anywhere, nb_ref, far, read, near, total, tiles, codes)
    out[...] = (total[mine] * 0.015625).astype(out.dtype)


def join_kernel(points, probe, joined):
    count, columns, _ = probe.shape
    for cluster in range(count):
        joined[cluster * columns : (cluster + 1) * columns, :] = probe[cluster]
    joined[count * columns :, :] = jnp.concatenate(
        [points[cluster].astype(jnp.float32) for cluster in range(count)], axis=0
    ).astype(joined.dtype)


def near_call(body, outs, scratch, operands, rows, per_row):
    nb, size = operands[0], outs[0].shape[-1]
    blocks = rows * per_row
    return pl.pallas_call(
        body,
        out_shape=outs,
        in_specs=[pl.BlockSpec(memory_space=SMEM)]
        + [pl.BlockSpec(memory_space=VMEM)] * (len(operands) - 1),
        out_specs=[pl.BlockSpec(memory_space=VMEM)] * len(outs),
        scratch_shapes=scratch
        + [
            pltpu.VMEM((FLIGHT, size, size), jnp.bfloat16),
            pltpu.SMEM((rows * nb.shape[1] + 2 * FLIGHT,), jnp.int32),
        ],
        compiler_params=pltpu.CompilerParams(vmem_limit_bytes=VMEM_BYTES),
        cost_estimate=pl.CostEstimate(
            flops=blocks * size * size * 256,
            bytes_accessed=sum(o.size * o.dtype.itemsize for o in operands),
            transcendentals=blocks * size * size,
        ),
    )(*operands)


def pivot_factor(pivots, inverse, width):
    chosen = (
        lax.broadcasted_iota(jnp.int32, (width, pivots.shape[1]), 0) == pivots
    ).astype(jnp.bfloat16)
    return nt(stacked_split(jnp.transpose(inverse)), chosen).astype(jnp.bfloat16)


def leaf_node(sketch, factor):
    wide = sketch.astype(jnp.float32)
    mean_sq = jnp.sum(wide * wide, keepdims=True) / (sketch.shape[0] * sketch.shape[1]) + EPSILON
    scale = 1.0 / (sketch.shape[0] * mean_sq)
    picked = halves(nt(factor, sketch))
    raw = halves(nn(stacked_split(picked), sketch))
    interp = raw * scale
    upward = halves(nt(stacked_split(raw), sketch)) * (scale * lax.rsqrt(mean_sq))
    return interp, upward


def tree_node(sketch, factor):
    width, columns = sketch.shape
    mean_sq = jnp.sum(sketch * sketch, keepdims=True) / (width * columns) + EPSILON
    scale = 1.0 / (columns * mean_sq)
    parts = stacked_split(sketch)
    picked = halves(nn(jnp.concatenate([factor, factor], axis=1), parts))
    raw = halves(nt(stacked_split(picked), parts))
    raw = raw[:, :width] + raw[:, width:]
    interp = raw * scale
    both = stacked_split(raw)
    upward = halves(nn(jnp.concatenate([both, both], axis=1), parts)) * (scale * lax.rsqrt(mean_sq))
    return interp, upward


def own_nodes(share, group, me):
    rows, level_first, nodes = [], 0, share // 2
    while nodes >= 1:
        rows += [level_first + me * nodes + node for node in range(nodes)]
        level_first += (group // share) * nodes
        nodes //= 2
    return rows


def factor_kernel(
    share,
    leaf_total,
    leaf_pivots,
    leaf_inverse,
    local_pivots,
    local_inverse,
    upper_pivots,
    upper_inverse,
    _,
    leaf_out,
    own_out,
    group_out,
    upper_out,
):
    me = lax.axis_index("vec")
    group = leaf_pivots.shape[0]

    def put(out, index, pivots, inverse, row):
        out[index] = pivot_factor(pivots[pl.ds(row, 1), :], inverse[row], out.shape[2])

    for cluster in range(share):
        put(leaf_out, cluster, leaf_pivots, leaf_inverse, me * share + cluster)
    for index, row in enumerate(own_nodes(share, group, me)):
        put(own_out, index, local_pivots, local_inverse, row)
    for index in range(group // share - 1):
        put(group_out, index, local_pivots, local_inverse, group - group // share + index)
    heap_first = 0
    for tier in range(UPL):
        node = heap_first + (lax.axis_index("leaf") >> (tier + 1))
        put(upper_out, tier, upper_pivots, upper_inverse, node)
        heap_first += leaf_total >> (tier + 1)


def device_kernel(share, group, rank, own, *refs):
    parts = group // share
    arrived, refs = refs[: parts - 1], refs[parts - 1 :]
    leaf_factors, own_factors, pack, up_out, sketch, ups = refs
    me = lax.axis_index("vec")
    columns = own.shape[1]
    width = 2 * rank
    for tier, piece in enumerate((own,) + tuple(arrived)):
        place = pl.ds(pl.multiple_of((me ^ tier) * columns, columns), columns)
        for cluster in range(share):
            sketch[cluster, place, :] = piece[cluster]
    for cluster in range(share):
        interp, upward = leaf_node(sketch[cluster], leaf_factors[cluster])
        pack[cluster * rank : (cluster + 1) * rank, :] = interp
        ups[cluster * rank : (cluster + 1) * rank, :] = upward
    nodes, packed = share // 2, 0
    while nodes >= 1:
        results = []
        for node in range(nodes):
            interp, upward = tree_node(
                ups[2 * node * rank : 2 * (node + 1) * rank, :], own_factors[packed]
            )
            for lane, source, top, height in pack_places(packed, share, rank):
                pack[top : top + height, lane : lane + width] = interp[source : source + height]
            results.append(upward)
            packed += 1
        for node, upward in enumerate(results):
            ups[node * rank : (node + 1) * rank, :] = upward
        nodes //= 2
    up_out[...] = ups[0:rank, :]


def pack_places(index, share, rank):
    top = share * rank + index // 2 * rank
    if index < share - 2:
        return [(index % 2 * 2 * rank, 0, top, rank)]
    return [(0, 0, top, rank // 2), (2 * rank, rank // 2, top, rank // 2)]


def group_kernel(share, group, rank, own, *refs):
    parts = group // share
    arrived, refs = refs[: parts - 1], refs[parts - 1 :]
    factors, interps, up_out, ups = refs
    me = lax.axis_index("vec")
    for tier, piece in enumerate((own,) + tuple(arrived)):
        ups[pl.ds(pl.multiple_of((me ^ tier) * rank, rank), rank), :] = piece[...]
    done = 0
    nodes = parts // 2
    while nodes >= 1:
        results = []
        for node in range(nodes):
            interp, upward = tree_node(
                ups[2 * node * rank : 2 * (node + 1) * rank, :], factors[done]
            )
            interps[done * rank : (done + 1) * rank, :] = interp
            results.append(upward)
            done += 1
        for node, upward in enumerate(results):
            ups[node * rank : (node + 1) * rank, :] = upward
        nodes //= 2
    up_out[...] = ups[0:rank, :]


def upper_node(tier, rank, own, arrived, factors, ups):
    side = (lax.axis_index("leaf") >> tier) & 1
    ups[pl.ds(pl.multiple_of(side * rank, rank), rank), :] = own[...]
    ups[pl.ds(pl.multiple_of((1 - side) * rank, rank), rank), :] = arrived[...]
    return tree_node(ups[...], factors[tier])


def upper_kernel(tier, rank, own, arrived, factors, interp_out, up_out, ups):
    interp, upward = upper_node(tier, rank, own, arrived, factors, ups)
    interp_out[...] = interp
    up_out[...] = upward


def start_copies(pieces, share, group, rank, leaf_out, local_out, sems):
    copies = []

    def put(source, target):
        copies.append(pltpu.make_async_copy(source, target, sems.at[len(copies)]))
        copies[-1].start()

    def rows_at(start, height):
        return pl.ds(pl.multiple_of(start, height), height)

    leaves = share * rank
    for flip, first, piece in pieces:
        device = lax.axis_index("vec") ^ flip
        end = first + piece.shape[0]
        if first < leaves:
            height = min(end, leaves) - first
            step = height if height == leaves else rank
            for row in range(0, height, step):
                put(
                    piece.at[row : row + step],
                    leaf_out.at[rows_at(device * leaves + first + row, step)],
                )
        for index, node in enumerate(own_nodes(share, group, device)):
            for lane, source, start, height in pack_places(index, share, rank):
                if first <= start < end:
                    put(
                        piece.at[start - first : start - first + height, lane : lane + 2 * rank],
                        local_out.at[rows_at(node * rank + source, height)],
                    )
    return copies


def place_kernel(flips, share, group, rank, *refs):
    packs, (joined, leaf_out, local_out, sems) = refs[: len(flips)], refs[len(flips) :]
    pieces = [(flip, 0, piece) for flip, piece in zip(flips, packs)]
    copies = start_copies(pieces, share, group, rank, leaf_out, local_out, sems)
    rows = joined.shape[0]
    target = local_out.at[local_out.shape[0] - rows :]
    copies.append(pltpu.make_async_copy(joined, target, sems.at[len(copies)]))
    copies[-1].start()
    for copy in copies:
        copy.wait()


def forward_kernel(here, there, _, upper, lower):
    upper[...] = here[0 : upper.shape[0], :]
    lower[...] = there[upper.shape[0] :, :]


def finish_kernel(tier, tails, share, group, rank, own, arrived, factors, *refs):
    earlier, refs = refs[:tier], refs[tier:]
    packs, refs = refs[: len(tails)], refs[len(tails) :]
    _, _, interps, top, leaf_out, local_out, ups, turned, sems = refs
    pieces = [(flip, first, piece) for (flip, first), piece in zip(tails, packs)]
    copies = start_copies(pieces, share, group, rank, leaf_out, local_out, sems)
    interp, upward = upper_node(tier, rank, own, arrived, factors, ups)
    for index, ref in enumerate(earlier):
        interps[index] = ref[...]
    interps[tier] = interp
    turned[...] = jnp.transpose(upward)
    columns = top.shape[0]
    place = pl.multiple_of(lax.axis_index("vec") * columns, columns)
    top[...] = turned[pl.ds(place, columns), :]
    for copy in copies:
        copy.wait()


def call(body, outs, scratch, operands, flops=0, anywhere_in=0, anywhere_out=0, aliases=None):
    fixed = pl.BlockSpec(memory_space=VMEM)
    free = pl.BlockSpec(memory_space=pl.ANY)
    return pl.pallas_call(
        body,
        out_shape=outs,
        in_specs=[fixed] * (len(operands) - anywhere_in) + [free] * anywhere_in,
        out_specs=[fixed] * (len(outs) - anywhere_out) + [free] * anywhere_out,
        scratch_shapes=scratch,
        input_output_aliases=aliases or {},
        compiler_params=pltpu.CompilerParams(vmem_limit_bytes=VMEM_BYTES),
        cost_estimate=pl.CostEstimate(
            flops=flops, bytes_accessed=sum(o.size * o.dtype.itemsize for o in operands), transcendentals=0
        ),
    )(*operands)


def f32(*shape):
    return jax.ShapeDtypeStruct(shape, jnp.float32)


def on_device(
    points,
    probe_vectors,
    neighbours,
    leaf_pivots,
    leaf_inverse,
    local_pivots,
    local_inverse,
    upper_pivots,
    upper_inverse,
):
    group, columns, size = probe_vectors.shape
    rank = leaf_pivots.shape[1]
    leaf_total = lax.axis_size("leaf")
    parts = lax.axis_size("vec")
    share = group // parts
    total_columns = columns * parts

    joined = call(
        join_kernel,
        [jax.ShapeDtypeStruct((group * (columns + 3), size), jnp.bfloat16)],
        [],
        [points, probe_vectors],
    )[0]
    swaps = []
    for odd in (0, 1):
        pairs = [(i, i + 1) for i in range(odd, leaf_total - 1, 2)]
        swaps.append(lax.ppermute(joined, "leaf", pairs + [(j, i) for i, j in pairs]))
    inner, outer = swaps

    def vec_send(array, tier):
        return lax.ppermute(array, "vec", [(i, i ^ tier) for i in range(parts)])

    away = list(range(parts - 1, 0, -1))
    sent_rows = (parts - 1) * share

    def bf16(*shape):
        return jax.ShapeDtypeStruct(shape, jnp.bfloat16)

    started, own_far, near = near_call(
        functools.partial(own_kernel, share, away),
        [f32(group + 1, columns, size), bf16(group, DEPTH, size), bf16(group + 1, size, DEPTH)],
        [],
        [neighbours, joined],
        sent_rows,
        6,
    )
    *sent, far, vectors = near_call(
        functools.partial(halo_kernel, share, away),
        [bf16(share, columns, size)] * len(away)
        + [bf16(3 * group, DEPTH, size), bf16(3 * group, columns, size)],
        [pltpu.VMEM((group + 1, columns, size), jnp.float32)],
        [neighbours, joined, inner, outer, own_far, near, started],
        sent_rows,
        6,
    )
    arrived = {tier: vec_send(array, tier) for tier, array in zip(away, sent)}
    kept = near_call(
        functools.partial(kept_kernel, share),
        [bf16(share, columns, size)],
        [pltpu.VMEM((group + 1, columns, size), jnp.float32)],
        [neighbours, far, vectors, near],
        share,
        12,
    )[0]

    width = 2 * rank
    leaf_factors, own_factors, group_factors, upper_factors = call(
        functools.partial(factor_kernel, share, leaf_total),
        [
            bf16(share, width, size),
            bf16(max(1, share - 1), width, width),
            bf16(parts - 1, width, width),
            bf16(UPL, width, width),
        ],
        [],
        [
            leaf_pivots,
            leaf_inverse,
            local_pivots,
            local_inverse,
            upper_pivots,
            upper_inverse,
            kept,
        ],
        anywhere_in=1,
    )
    pack, own_up = call(
        functools.partial(device_kernel, share, group, rank),
        [f32((3 * share - 1) * rank // 2, size), f32(rank, total_columns)],
        [
            pltpu.VMEM((share, total_columns, size), jnp.bfloat16),
            pltpu.VMEM((share * rank, total_columns), jnp.float32),
        ],
        [kept] + [arrived[tier] for tier in range(1, parts)] + [leaf_factors, own_factors],
    )
    near_ups = [vec_send(own_up, tier) for tier in range(1, parts)]
    joined, own_up = call(
        functools.partial(group_kernel, share, group, rank),
        [f32((parts - 1) * rank, width), f32(rank, total_columns)],
        [pltpu.VMEM((parts * rank, total_columns), jnp.float32)],
        [own_up] + near_ups + [group_factors],
    )
    passing = parts == 4
    flips = [0] + [tier for tier in range(1, parts) if not (passing and tier == 3)]
    packs = [pack] + [vec_send(pack, tier) for tier in flips[1:]]
    tails, tail_packs = [], []

    maps = []
    for tier in range(UPL):
        partner = lax.ppermute(own_up, "leaf", [(i, i ^ (1 << tier)) for i in range(leaf_total)])
        operands = [own_up, partner, upper_factors]
        ups = pltpu.VMEM((width, total_columns), jnp.float32)
        if tier < UPL - 1:
            interp, own_up = call(
                functools.partial(upper_kernel, tier, rank),
                [f32(rank, width), f32(rank, total_columns)],
                [ups],
                operands,
                flops=ROUND_FLOPS,
            )
            maps.append(interp)
    if passing:
        upper_rows = (share - 1) * rank
        upper, lower = call(
            forward_kernel,
            [f32(upper_rows, size), f32(pack.shape[0] - upper_rows, size)],
            [],
            [packs[1], packs[2], own_up],
            anywhere_in=1,
        )
        tails = [(3, 0), (3, upper_rows)]
        tail_packs = [vec_send(upper, 2), vec_send(lower, 1)]
    leaf_map, local_map = call(
        functools.partial(place_kernel, flips, share, group, rank),
        [f32(group * rank, size), f32((group - 1) * rank, width)],
        [pltpu.SemaphoreType.DMA((len(flips) * (share + 1) + 1,))],
        packs + [joined],
        flops=ROUND_FLOPS,
        anywhere_in=len(flips) + 1,
        anywhere_out=2,
    )
    operands += maps + tail_packs + [leaf_map, local_map]
    upper_map, top, leaf_map, local_map = call(
        functools.partial(finish_kernel, UPL - 1, tails, share, group, rank),
        [
            f32(UPL, rank, width),
            f32(columns, rank),
            f32(group * rank, size),
            f32((group - 1) * rank, width),
        ],
        [
            ups,
            pltpu.VMEM((total_columns, rank), jnp.float32),
            pltpu.SemaphoreType.DMA((2 * share + 1,)),
        ],
        operands,
        flops=ROUND_FLOPS,
        anywhere_in=len(tails) + 2,
        anywhere_out=2,
        aliases={len(operands) - 2: 2, len(operands) - 1: 3},
    )
    return (
        jnp.swapaxes(leaf_map.reshape(group, rank, size), 1, 2),
        jnp.swapaxes(local_map.reshape(group - 1, rank, width), 1, 2),
        jnp.swapaxes(upper_map, 1, 2)[None],
        top[None],
    )


def solution(mesh):
    placed = (
        P("leaf", None, None),
        P("leaf", "vec", None),
        P("leaf", None),
        P("leaf", None),
        P("leaf", None, None),
        P("leaf", None),
        P("leaf", None, None),
        P(),
        P(),
    )
    return jax.shard_map(
        on_device,
        mesh=mesh,
        in_specs=placed,
        out_specs=(
            P("leaf", None, None),
            P("leaf", None, None),
            P("leaf", None, None, None),
            P("leaf", "vec", None),
        ),
        check_vma=False,
    )
```

```python
import functools

import jax
import jax.numpy as jnp
from jax import lax
from jax.experimental import pallas as pl
from jax.experimental.pallas import tpu as pltpu
from jax.sharding import PartitionSpec as P

UPL = 3

SOFTEN = 0.0009
EPSILON = 1e-06
FLIGHT = 8
DEPTH = 128
CHUNK = 256
ROUND_FLOPS = 950_000_000
VMEM_BYTES = 20 * 1024 * 1024
VMEM = pltpu.MemorySpace.VMEM
SMEM = pltpu.MemorySpace.SMEM


def nt(a, b):
    return lax.dot_general(a, b, (((1,), (1,)), ((), ())), preferred_element_type=jnp.float32)


def nn(a, b):
    return lax.dot_general(a, b, (((1,), (0,)), ((), ())), preferred_element_type=jnp.float32)


def split(a):
    high = a.astype(jnp.bfloat16)
    low = (a - high.astype(jnp.float32)).astype(jnp.bfloat16)
    return high, low


def stacked_split(a):
    high, low = split(a)
    return jnp.concatenate([high, low], axis=0)


def halves(a):
    rows = a.shape[0] // 2
    return a[:rows] + a[rows:]


def coordinates(points, extra):
    row = lax.broadcasted_iota(jnp.int32, (8, points.shape[1]), 0)
    padded = jnp.concatenate(
        [points, jnp.full((5, points.shape[1]), 0.5, jnp.float32)], axis=0
    )
    centred = padded - 0.5
    high, low = [part.astype(jnp.float32) for part in split(centred)]
    norm = jnp.sum(centred * centred, axis=0, keepdims=True) + extra
    first, rest = [part.astype(jnp.float32) for part in split(norm)]
    second, third = [part.astype(jnp.float32) for part in split(norm - first)]
    norms = jnp.where(row == 0, first, jnp.where(row == 1, second, jnp.where(row == 2, third, 0.0)))
    return high, low, norms, jnp.where(row < 3, 1.0, 0.0)


def far_features(points):
    high, low, norm, one = coordinates(points, SOFTEN)
    vacant = jnp.zeros((DEPTH - 48, points.shape[1]), jnp.float32)
    return jnp.concatenate(
        [-2.0 * high, -2.0 * low, -2.0 * high, -2.0 * low, one, norm, vacant], axis=0
    ).astype(jnp.bfloat16)


def near_features(points):
    high, low, norm, one = coordinates(points, 0.0)
    vacant = jnp.zeros((DEPTH - 48, points.shape[1]), jnp.float32)
    return jnp.transpose(
        jnp.concatenate([high, high, low, low, norm, one, vacant], axis=0)
    ).astype(jnp.bfloat16)


def add_blocks(share, tiers, base, wanted, nb_ref, far, vectors, near, total, tiles, codes):
    me = lax.axis_index("vec")
    count, slots = nb_ref.shape
    first = lax.axis_index("leaf") * count
    flight, size = tiles.shape[0], tiles.shape[1]
    idle = count * 64

    for way in range(flight):
        codes[way] = idle
    filled = jnp.int32(flight)
    for tier in tiers:
        for part in range(share):
            cluster = (me ^ tier) * share + part
            shift = cluster * 64 + count - base - first
            for slot in range(slots):
                listed = nb_ref[cluster, slot]
                codes[filled] = listed + shift
                filled += wanted(listed, first, count).astype(jnp.int32)
    for way in range(flight):
        codes[filled + way] = idle
    tiles[...] = jnp.zeros(tiles.shape, tiles.dtype)

    def multiply(code, tile):
        row = code // 64
        total[row] = total[row] + nt(vectors(code % 64), tile[...])

    def evaluate(code, tile):
        row = code // 64
        position = code % 64
        for top in range(0, size, CHUNK):
            distance = nn(near[row, top : top + CHUNK, :], far[position])
            tile[top : top + CHUNK, :] = lax.rsqrt(distance).astype(jnp.bfloat16)

    def step(index, carry):
        for way in range(flight):
            multiply(codes[index * flight + way], tiles.at[way])
            evaluate(codes[(index + 1) * flight + way], tiles.at[way])
        return carry

    steps = (filled - 1) // flight
    done = jnp.int32(0)
    for width in (4, 2, 1):
        rounds = (steps - done) // width

        def several(index, carry, width=width, done=done):
            for offset in range(width):
                carry = step(done + index * width + offset, carry)
            return carry

        lax.fori_loop(0, rounds, several, 0)
        done = done + rounds * width
    for way in range(flight):
        multiply(codes[steps * flight + way], tiles.at[way])


def inside(listed, first, count):
    return (listed >= first) & (listed < first + count)


def outside(listed, first, count):
    return (listed >= 0) & ((listed < first) | (listed >= first + count))


def anywhere(listed, first, count):
    return listed >= 0


def joined_points(joined, count):
    points = joined[joined.shape[0] - 3 * count :, :].astype(jnp.float32)
    return [points[3 * cluster : 3 * cluster + 3] for cluster in range(count)]


def own_kernel(share, tiers, nb_ref, joined, total, far, near, tiles, codes):
    count, columns = far.shape[0], total.shape[1]
    for cluster, points in enumerate(joined_points(joined, count)):
        far[cluster] = far_features(points)
        near[cluster] = near_features(points)
    near[count] = near[0]
    total[...] = jnp.zeros(total.shape, total.dtype)

    def vectors(place):
        return joined[pl.ds(pl.multiple_of(place * columns, columns), columns), :]

    add_blocks(share, tiers, count, inside, nb_ref, far, vectors, near, total, tiles, codes)


def halo_kernel(share, tiers, nb_ref, joined, inner, outer, own_far, near, start, *refs):
    outs = refs[: len(tiers)]
    far, vectors, total, tiles, codes = refs[len(tiers) :]
    count, columns = own_far.shape[0], start.shape[1]
    me = lax.axis_index("vec")
    odd = lax.axis_index("leaf") & 1
    for place, source in ((2 * odd, outer), (2 - 2 * odd, inner), (1, joined)):
        for cluster in range(count):
            vectors[place * count + cluster] = source[cluster * columns : (cluster + 1) * columns, :]
        if source is joined:
            far[count : 2 * count] = own_far[...]
            continue
        for cluster, points in enumerate(joined_points(source, count)):
            far[place * count + cluster] = far_features(points)
    total[...] = start[...]

    def read(place):
        return vectors[place]

    add_blocks(share, tiers, 0, outside, nb_ref, far, read, near, total, tiles, codes)
    for tier, out in zip(tiers, outs):
        part = total[pl.ds((me ^ tier) * share, share)]
        out[...] = (part * 0.015625).astype(out.dtype)


def kept_kernel(share, nb_ref, far, vectors, near, out, total, tiles, codes):
    mine = pl.ds(lax.axis_index("vec") * share, share)
    total[mine] = jnp.zeros((share,) + total.shape[1:], total.dtype)

    def read(place):
        return vectors[place]

    add_blocks(share, (0,), 0, anywhere, nb_ref, far, read, near, total, tiles, codes)
    out[...] = (total[mine] * 0.015625).astype(out.dtype)


def join_kernel(points, probe, joined):
    count, columns, _ = probe.shape
    for cluster in range(count):
        joined[cluster * columns : (cluster + 1) * columns, :] = probe[cluster]
    joined[count * columns :, :] = jnp.concatenate(
        [points[cluster].astype(jnp.float32) for cluster in range(count)], axis=0
    ).astype(joined.dtype)


def near_call(body, outs, scratch, operands, rows, per_row):
    nb, size = operands[0], outs[0].shape[-1]
    blocks = rows * per_row
    return pl.pallas_call(
        body,
        out_shape=outs,
        in_specs=[pl.BlockSpec(memory_space=SMEM)]
        + [pl.BlockSpec(memory_space=VMEM)] * (len(operands) - 1),
        out_specs=[pl.BlockSpec(memory_space=VMEM)] * len(outs),
        scratch_shapes=scratch
        + [
            pltpu.VMEM((FLIGHT, size, size), jnp.bfloat16),
            pltpu.SMEM((rows * nb.shape[1] + 2 * FLIGHT,), jnp.int32),
        ],
        compiler_params=pltpu.CompilerParams(vmem_limit_bytes=VMEM_BYTES),
        cost_estimate=pl.CostEstimate(
            flops=blocks * size * size * 256,
            bytes_accessed=sum(o.size * o.dtype.itemsize for o in operands),
            transcendentals=blocks * size * size,
        ),
    )(*operands)


def pivot_factor(pivots, inverse, width):
    chosen = (
        lax.broadcasted_iota(jnp.int32, (width, pivots.shape[1]), 0) == pivots
    ).astype(jnp.bfloat16)
    return nt(stacked_split(jnp.transpose(inverse)), chosen).astype(jnp.bfloat16)


def leaf_node(sketch, factor):
    wide = sketch.astype(jnp.float32)
    mean_sq = jnp.sum(wide * wide, keepdims=True) / (sketch.shape[0] * sketch.shape[1]) + EPSILON
    scale = 1.0 / (sketch.shape[0] * mean_sq)
    picked = halves(nt(factor, sketch))
    raw = halves(nn(stacked_split(picked), sketch))
    interp = raw * scale
    upward = halves(nt(stacked_split(raw), sketch)) * (scale * lax.rsqrt(mean_sq))
    return interp, upward


def tree_node(sketch, factor):
    width, columns = sketch.shape
    mean_sq = jnp.sum(sketch * sketch, keepdims=True) / (width * columns) + EPSILON
    scale = 1.0 / (columns * mean_sq)
    parts = stacked_split(sketch)
    picked = halves(nn(jnp.concatenate([factor, factor], axis=1), parts))
    raw = halves(nt(stacked_split(picked), parts))
    raw = raw[:, :width] + raw[:, width:]
    interp = raw * scale
    both = stacked_split(raw)
    upward = halves(nn(jnp.concatenate([both, both], axis=1), parts)) * (scale * lax.rsqrt(mean_sq))
    return interp, upward


def own_nodes(share, group, me):
    rows, level_first, nodes = [], 0, share // 2
    while nodes >= 1:
        rows += [level_first + me * nodes + node for node in range(nodes)]
        level_first += (group // share) * nodes
        nodes //= 2
    return rows


def factor_kernel(
    share,
    leaf_total,
    leaf_pivots,
    leaf_inverse,
    local_pivots,
    local_inverse,
    upper_pivots,
    upper_inverse,
    _,
    leaf_out,
    own_out,
    group_out,
    upper_out,
):
    me = lax.axis_index("vec")
    group = leaf_pivots.shape[0]

    def put(out, index, pivots, inverse, row):
        out[index] = pivot_factor(pivots[pl.ds(row, 1), :], inverse[row], out.shape[2])

    for cluster in range(share):
        put(leaf_out, cluster, leaf_pivots, leaf_inverse, me * share + cluster)
    for index, row in enumerate(own_nodes(share, group, me)):
        put(own_out, index, local_pivots, local_inverse, row)
    for index in range(group // share - 1):
        put(group_out, index, local_pivots, local_inverse, group - group // share + index)
    heap_first = 0
    for tier in range(UPL):
        node = heap_first + (lax.axis_index("leaf") >> (tier + 1))
        put(upper_out, tier, upper_pivots, upper_inverse, node)
        heap_first += leaf_total >> (tier + 1)


def device_kernel(share, group, rank, own, *refs):
    parts = group // share
    arrived, refs = refs[: parts - 1], refs[parts - 1 :]
    leaf_factors, own_factors, pack, up_out, sketch, ups = refs
    me = lax.axis_index("vec")
    columns = own.shape[1]
    width = 2 * rank
    for tier, piece in enumerate((own,) + tuple(arrived)):
        place = pl.ds(pl.multiple_of((me ^ tier) * columns, columns), columns)
        for cluster in range(share):
            sketch[cluster, place, :] = piece[cluster]
    for cluster in range(share):
        interp, upward = leaf_node(sketch[cluster], leaf_factors[cluster])
        pack[cluster * rank : (cluster + 1) * rank, :] = interp
        ups[cluster * rank : (cluster + 1) * rank, :] = upward
    nodes, packed = share // 2, 0
    while nodes >= 1:
        results = []
        for node in range(nodes):
            interp, upward = tree_node(
                ups[2 * node * rank : 2 * (node + 1) * rank, :], own_factors[packed]
            )
            for lane, source, top, height in pack_places(packed, share, rank):
                pack[top : top + height, lane : lane + width] = interp[source : source + height]
            results.append(upward)
            packed += 1
        for node, upward in enumerate(results):
            ups[node * rank : (node + 1) * rank, :] = upward
        nodes //= 2
    up_out[...] = ups[0:rank, :]


def pack_places(index, share, rank):
    top = share * rank + index // 2 * rank
    if index < share - 2:
        return [(index % 2 * 2 * rank, 0, top, rank)]
    return [(0, 0, top, rank // 2), (2 * rank, rank // 2, top, rank // 2)]


def group_kernel(share, group, rank, own, *refs):
    parts = group // share
    arrived, refs = refs[: parts - 1], refs[parts - 1 :]
    factors, interps, up_out, ups = refs
    me = lax.axis_index("vec")
    for tier, piece in enumerate((own,) + tuple(arrived)):
        ups[pl.ds(pl.multiple_of((me ^ tier) * rank, rank), rank), :] = piece[...]
    done = 0
    nodes = parts // 2
    while nodes >= 1:
        results = []
        for node in range(nodes):
            interp, upward = tree_node(
                ups[2 * node * rank : 2 * (node + 1) * rank, :], factors[done]
            )
            interps[done * rank : (done + 1) * rank, :] = interp
            results.append(upward)
            done += 1
        for node, upward in enumerate(results):
            ups[node * rank : (node + 1) * rank, :] = upward
        nodes //= 2
    up_out[...] = ups[0:rank, :]


def upper_node(tier, rank, own, arrived, factors, ups):
    side = (lax.axis_index("leaf") >> tier) & 1
    ups[pl.ds(pl.multiple_of(side * rank, rank), rank), :] = own[...]
    ups[pl.ds(pl.multiple_of((1 - side) * rank, rank), rank), :] = arrived[...]
    return tree_node(ups[...], factors[tier])


def upper_kernel(tier, rank, own, arrived, factors, interp_out, up_out, ups):
    interp, upward = upper_node(tier, rank, own, arrived, factors, ups)
    interp_out[...] = interp
    up_out[...] = upward


def start_copies(pieces, share, group, rank, leaf_out, local_out, sems):
    copies = []

    def put(source, target):
        copies.append(pltpu.make_async_copy(source, target, sems.at[len(copies)]))
        copies[-1].start()

    def rows_at(start, height):
        return pl.ds(pl.multiple_of(start, height), height)

    leaves = share * rank
    for flip, first, piece in pieces:
        device = lax.axis_index("vec") ^ flip
        end = first + piece.shape[0]
        if first < leaves:
            height = min(end, leaves) - first
            step = height if height == leaves else rank
            for row in range(0, height, step):
                put(
                    piece.at[row : row + step],
                    leaf_out.at[rows_at(device * leaves + first + row, step)],
                )
        for index, node in enumerate(own_nodes(share, group, device)):
            for lane, source, start, height in pack_places(index, share, rank):
                if first <= start < end:
                    put(
                        piece.at[start - first : start - first + height, lane : lane + 2 * rank],
                        local_out.at[rows_at(node * rank + source, height)],
                    )
    return copies


def place_kernel(flips, share, group, rank, *refs):
    packs, (joined, leaf_out, local_out, sems) = refs[: len(flips)], refs[len(flips) :]
    pieces = [(flip, 0, piece) for flip, piece in zip(flips, packs)]
    copies = start_copies(pieces, share, group, rank, leaf_out, local_out, sems)
    rows = joined.shape[0]
    target = local_out.at[local_out.shape[0] - rows :]
    copies.append(pltpu.make_async_copy(joined, target, sems.at[len(copies)]))
    copies[-1].start()
    for copy in copies:
        copy.wait()


def forward_kernel(here, there, _, upper, lower):
    upper[...] = here[0 : upper.shape[0], :]
    lower[...] = there[upper.shape[0] :, :]


def finish_kernel(tier, tails, share, group, rank, own, arrived, factors, *refs):
    earlier, refs = refs[:tier], refs[tier:]
    packs, refs = refs[: len(tails)], refs[len(tails) :]
    _, _, interps, top, leaf_out, local_out, ups, turned, sems = refs
    pieces = [(flip, first, piece) for (flip, first), piece in zip(tails, packs)]
    copies = start_copies(pieces, share, group, rank, leaf_out, local_out, sems)
    interp, upward = upper_node(tier, rank, own, arrived, factors, ups)
    for index, ref in enumerate(earlier):
        interps[index] = ref[...]
    interps[tier] = interp
    turned[...] = jnp.transpose(upward)
    columns = top.shape[0]
    place = pl.multiple_of(lax.axis_index("vec") * columns, columns)
    top[...] = turned[pl.ds(place, columns), :]
    for copy in copies:
        copy.wait()


def call(body, outs, scratch, operands, flops=0, anywhere_in=0, anywhere_out=0, aliases=None):
    fixed = pl.BlockSpec(memory_space=VMEM)
    free = pl.BlockSpec(memory_space=pl.ANY)
    return pl.pallas_call(
        body,
        out_shape=outs,
        in_specs=[fixed] * (len(operands) - anywhere_in) + [free] * anywhere_in,
        out_specs=[fixed] * (len(outs) - anywhere_out) + [free] * anywhere_out,
        scratch_shapes=scratch,
        input_output_aliases=aliases or {},
        compiler_params=pltpu.CompilerParams(vmem_limit_bytes=VMEM_BYTES),
        cost_estimate=pl.CostEstimate(
            flops=flops, bytes_accessed=sum(o.size * o.dtype.itemsize for o in operands), transcendentals=0
        ),
    )(*operands)


def f32(*shape):
    return jax.ShapeDtypeStruct(shape, jnp.float32)


def on_device(
    points,
    probe_vectors,
    neighbours,
    leaf_pivots,
    leaf_inverse,
    local_pivots,
    local_inverse,
    upper_pivots,
    upper_inverse,
):
    group, columns, size = probe_vectors.shape
    rank = leaf_pivots.shape[1]
    leaf_total = lax.axis_size("leaf")
    parts = lax.axis_size("vec")
    share = group // parts
    total_columns = columns * parts

    joined = call(
        join_kernel,
        [jax.ShapeDtypeStruct((group * (columns + 3), size), jnp.bfloat16)],
        [],
        [points, probe_vectors],
    )[0]
    swaps = []
    for odd in (0, 1):
        pairs = [(i, i + 1) for i in range(odd, leaf_total - 1, 2)]
        swaps.append(lax.ppermute(joined, "leaf", pairs + [(j, i) for i, j in pairs]))
    inner, outer = swaps

    def vec_send(array, tier):
        return lax.ppermute(array, "vec", [(i, i ^ tier) for i in range(parts)])

    away = list(range(parts - 1, 0, -1))
    sent_rows = (parts - 1) * share

    def bf16(*shape):
        return jax.ShapeDtypeStruct(shape, jnp.bfloat16)

    started, own_far, near = near_call(
        functools.partial(own_kernel, share, away),
        [f32(group + 1, columns, size), bf16(group, DEPTH, size), bf16(group + 1, size, DEPTH)],
        [],
        [neighbours, joined],
        sent_rows,
        6,
    )
    *sent, far, vectors = near_call(
        functools.partial(halo_kernel, share, away),
        [bf16(share, columns, size)] * len(away)
        + [bf16(3 * group, DEPTH, size), bf16(3 * group, columns, size)],
        [pltpu.VMEM((group + 1, columns, size), jnp.float32)],
        [neighbours, joined, inner, outer, own_far, near, started],
        sent_rows,
        6,
    )
    arrived = {tier: vec_send(array, tier) for tier, array in zip(away, sent)}
    kept = near_call(
        functools.partial(kept_kernel, share),
        [bf16(share, columns, size)],
        [pltpu.VMEM((group + 1, columns, size), jnp.float32)],
        [neighbours, far, vectors, near],
        share,
        12,
    )[0]

    width = 2 * rank
    leaf_factors, own_factors, group_factors, upper_factors = call(
        functools.partial(factor_kernel, share, leaf_total),
        [
            bf16(share, width, size),
            bf16(max(1, share - 1), width, width),
            bf16(parts - 1, width, width),
            bf16(UPL, width, width),
        ],
        [],
        [
            leaf_pivots,
            leaf_inverse,
            local_pivots,
            local_inverse,
            upper_pivots,
            upper_inverse,
            kept,
        ],
        anywhere_in=1,
    )
    pack, own_up = call(
        functools.partial(device_kernel, share, group, rank),
        [f32((3 * share - 1) * rank // 2, size), f32(rank, total_columns)],
        [
            pltpu.VMEM((share, total_columns, size), jnp.bfloat16),
            pltpu.VMEM((share * rank, total_columns), jnp.float32),
        ],
        [kept] + [arrived[tier] for tier in range(1, parts)] + [leaf_factors, own_factors],
    )
    near_ups = [vec_send(own_up, tier) for tier in range(1, parts)]
    joined, own_up = call(
        functools.partial(group_kernel, share, group, rank),
        [f32((parts - 1) * rank, width), f32(rank, total_columns)],
        [pltpu.VMEM((parts * rank, total_columns), jnp.float32)],
        [own_up] + near_ups + [group_factors],
    )
    passing = parts == 4
    flips = [0] + [tier for tier in range(1, parts) if not (passing and tier == 3)]
    packs = [pack] + [vec_send(pack, tier) for tier in flips[1:]]
    tails, tail_packs = [], []

    maps = []
    for tier in range(UPL):
        partner = lax.ppermute(own_up, "leaf", [(i, i ^ (1 << tier)) for i in range(leaf_total)])
        operands = [own_up, partner, upper_factors]
        ups = pltpu.VMEM((width, total_columns), jnp.float32)
        if tier < UPL - 1:
            interp, own_up = call(
                functools.partial(upper_kernel, tier, rank),
                [f32(rank, width), f32(rank, total_columns)],
                [ups],
                operands,
                flops=ROUND_FLOPS,
            )
            maps.append(interp)
    if passing:
        upper_rows = (share - 1) * rank
        upper, lower = call(
            forward_kernel,
            [f32(upper_rows, size), f32(pack.shape[0] - upper_rows, size)],
            [],
            [packs[1], packs[2], own_up],
            anywhere_in=1,
        )
        tails = [(3, 0), (3, upper_rows)]
        tail_packs = [vec_send(upper, 2), vec_send(lower, 1)]
    leaf_map, local_map = call(
        functools.partial(place_kernel, flips, share, group, rank),
        [f32(group * rank, size), f32((group - 1) * rank, width)],
        [pltpu.SemaphoreType.DMA((len(flips) * (share + 1) + 1,))],
        packs + [joined],
        flops=ROUND_FLOPS,
        anywhere_in=len(flips) + 1,
        anywhere_out=2,
    )
    operands += maps + tail_packs + [leaf_map, local_map]
    upper_map, top, leaf_map, local_map = call(
        functools.partial(finish_kernel, UPL - 1, tails, share, group, rank),
        [
            f32(UPL, rank, width),
            f32(columns, rank),
            f32(group * rank, size),
            f32((group - 1) * rank, width),
        ],
        [
            ups,
            pltpu.VMEM((total_columns, rank), jnp.float32),
            pltpu.SemaphoreType.DMA((2 * share + 1,)),
        ],
        operands,
        flops=ROUND_FLOPS,
        anywhere_in=len(tails) + 2,
        anywhere_out=2,
        aliases={len(operands) - 2: 2, len(operands) - 1: 3},
    )
    return (
        jnp.swapaxes(leaf_map.reshape(group, rank, size), 1, 2),
        jnp.swapaxes(local_map.reshape(group - 1, rank, width), 1, 2),
        jnp.swapaxes(upper_map, 1, 2)[None],
        top[None],
    )


def solution(mesh):
    placed = (
        P("leaf", None, None),
        P("leaf", "vec", None),
        P("leaf", None),
        P("leaf", None),
        P("leaf", None, None),
        P("leaf", None),
        P("leaf", None, None),
        P(),
        P(),
    )
    return jax.shard_map(
        on_device,
        mesh=mesh,
        in_specs=placed,
        out_specs=(
            P("leaf", None, None),
            P("leaf", None, None),
            P("leaf", None, None, None),
            P("leaf", "vec", None),
        ),
        check_vma=False,
    )
```

```python
import functools

import jax
import jax.numpy as jnp
from jax import lax
from jax.experimental import pallas as pl
from jax.experimental.pallas import tpu as pltpu
from jax.sharding import PartitionSpec as P

UPL = 3

SOFTEN = 0.0009
EPSILON = 1e-06
FLIGHT = 4
DEPTH = 128
CHUNK = 256
ROUND_FLOPS = 950_000_000
VMEM_BYTES = 20 * 1024 * 1024
VMEM = pltpu.MemorySpace.VMEM
SMEM = pltpu.MemorySpace.SMEM


def nt(a, b):
    return lax.dot_general(a, b, (((1,), (1,)), ((), ())), preferred_element_type=jnp.float32)


def nn(a, b):
    return lax.dot_general(a, b, (((1,), (0,)), ((), ())), preferred_element_type=jnp.float32)


def split(a):
    high = a.astype(jnp.bfloat16)
    low = (a - high.astype(jnp.float32)).astype(jnp.bfloat16)
    return high, low


def stacked_split(a):
    high, low = split(a)
    return jnp.concatenate([high, low], axis=0)


def halves(a):
    rows = a.shape[0] // 2
    return a[:rows] + a[rows:]


def coordinates(points, extra):
    row = lax.broadcasted_iota(jnp.int32, (8, points.shape[1]), 0)
    padded = jnp.concatenate(
        [points, jnp.full((5, points.shape[1]), 0.5, jnp.float32)], axis=0
    )
    centred = padded - 0.5
    high, low = [part.astype(jnp.float32) for part in split(centred)]
    norm = jnp.sum(centred * centred, axis=0, keepdims=True) + extra
    first, rest = [part.astype(jnp.float32) for part in split(norm)]
    second, third = [part.astype(jnp.float32) for part in split(norm - first)]
    norms = jnp.where(row == 0, first, jnp.where(row == 1, second, jnp.where(row == 2, third, 0.0)))
    return high, low, norms, jnp.where(row < 3, 1.0, 0.0)


def far_features(points):
    high, low, norm, one = coordinates(points, SOFTEN)
    vacant = jnp.zeros((DEPTH - 48, points.shape[1]), jnp.float32)
    return jnp.concatenate(
        [-2.0 * high, -2.0 * low, -2.0 * high, -2.0 * low, one, norm, vacant], axis=0
    ).astype(jnp.bfloat16)


def near_features(points):
    high, low, norm, one = coordinates(points, 0.0)
    vacant = jnp.zeros((DEPTH - 48, points.shape[1]), jnp.float32)
    return jnp.transpose(
        jnp.concatenate([high, high, low, low, norm, one, vacant], axis=0)
    ).astype(jnp.bfloat16)


def add_blocks(share, tiers, base, wanted, nb_ref, far, vectors, near, total, tiles, codes):
    me = lax.axis_index("vec")
    count, slots = nb_ref.shape
    first = lax.axis_index("leaf") * count
    flight, size = tiles.shape[0], tiles.shape[1]
    idle = count * 64

    for way in range(flight):
        codes[way] = idle
    filled = jnp.int32(flight)
    for tier in tiers:
        for part in range(share):
            cluster = (me ^ tier) * share + part
            shift = cluster * 64 + count - base - first
            for slot in range(slots):
                listed = nb_ref[cluster, slot]
                codes[filled] = listed + shift
                filled += wanted(listed, first, count).astype(jnp.int32)
    for way in range(flight):
        codes[filled + way] = idle
    tiles[...] = jnp.zeros(tiles.shape, tiles.dtype)

    def multiply(code, tile):
        row = code // 64
        total[row] = total[row] + nt(vectors(code % 64), tile[...])

    def evaluate(code, tile):
        row = code // 64
        position = code % 64
        for top in range(0, size, CHUNK):
            distance = nn(near[row, top : top + CHUNK, :], far[position])
            tile[top : top + CHUNK, :] = lax.rsqrt(distance).astype(jnp.bfloat16)

    def step(index, carry):
        for way in range(flight):
            multiply(codes[index * flight + way], tiles.at[way])
            evaluate(codes[(index + 1) * flight + way], tiles.at[way])
        return carry

    steps = (filled - 1) // flight
    done = jnp.int32(0)
    for width in (8, 4, 2, 1):
        rounds = (steps - done) // width

        def several(index, carry, width=width, done=done):
            for offset in range(width):
                carry = step(done + index * width + offset, carry)
            return carry

        lax.fori_loop(0, rounds, several, 0)
        done = done + rounds * width
    for way in range(flight):
        multiply(codes[steps * flight + way], tiles.at[way])


def inside(listed, first, count):
    return (listed >= first) & (listed < first + count)


def outside(listed, first, count):
    return (listed >= 0) & ((listed < first) | (listed >= first + count))


def anywhere(listed, first, count):
    return listed >= 0


def joined_points(joined, count):
    points = joined[joined.shape[0] - 3 * count :, :].astype(jnp.float32)
    return [points[3 * cluster : 3 * cluster + 3] for cluster in range(count)]


def own_kernel(share, tiers, nb_ref, joined, total, far, near, tiles, codes):
    count, columns = far.shape[0], total.shape[1]
    for cluster, points in enumerate(joined_points(joined, count)):
        far[cluster] = far_features(points)
        near[cluster] = near_features(points)
    near[count] = near[0]
    total[...] = jnp.zeros(total.shape, total.dtype)

    def vectors(place):
        return joined[pl.ds(pl.multiple_of(place * columns, columns), columns), :]

    add_blocks(share, tiers, count, inside, nb_ref, far, vectors, near, total, tiles, codes)


def halo_kernel(share, tiers, nb_ref, joined, inner, outer, own_far, near, start, *refs):
    outs = refs[: len(tiers)]
    far, vectors, total, tiles, codes = refs[len(tiers) :]
    count, columns = own_far.shape[0], start.shape[1]
    me = lax.axis_index("vec")
    odd = lax.axis_index("leaf") & 1
    for place, source in ((2 * odd, outer), (2 - 2 * odd, inner), (1, joined)):
        for cluster in range(count):
            vectors[place * count + cluster] = source[cluster * columns : (cluster + 1) * columns, :]
        if source is joined:
            far[count : 2 * count] = own_far[...]
            continue
        for cluster, points in enumerate(joined_points(source, count)):
            far[place * count + cluster] = far_features(points)
    total[...] = start[...]

    def read(place):
        return vectors[place]

    add_blocks(share, tiers, 0, outside, nb_ref, far, read, near, total, tiles, codes)
    for tier, out in zip(tiers, outs):
        part = total[pl.ds((me ^ tier) * share, share)]
        out[...] = (part * 0.015625).astype(out.dtype)


def kept_kernel(share, nb_ref, far, vectors, near, out, total, tiles, codes):
    mine = pl.ds(lax.axis_index("vec") * share, share)
    total[mine] = jnp.zeros((share,) + total.shape[1:], total.dtype)

    def read(place):
        return vectors[place]

    add_blocks(share, (0,), 0, anywhere, nb_ref, far, read, near, total, tiles, codes)
    out[...] = (total[mine] * 0.015625).astype(out.dtype)


def join_kernel(points, probe, joined):
    count, columns, _ = probe.shape
    for cluster in range(count):
        joined[cluster * columns : (cluster + 1) * columns, :] = probe[cluster]
    joined[count * columns :, :] = jnp.concatenate(
        [points[cluster].astype(jnp.float32) for cluster in range(count)], axis=0
    ).astype(joined.dtype)


def near_call(body, outs, scratch, operands, rows, per_row):
    nb, size = operands[0], outs[0].shape[-1]
    blocks = rows * per_row
    return pl.pallas_call(
        body,
        out_shape=outs,
        in_specs=[pl.BlockSpec(memory_space=SMEM)]
        + [pl.BlockSpec(memory_space=VMEM)] * (len(operands) - 1),
        out_specs=[pl.BlockSpec(memory_space=VMEM)] * len(outs),
        scratch_shapes=scratch
        + [
            pltpu.VMEM((FLIGHT, size, size), jnp.bfloat16),
            pltpu.SMEM((rows * nb.shape[1] + 2 * FLIGHT,), jnp.int32),
        ],
        compiler_params=pltpu.CompilerParams(vmem_limit_bytes=VMEM_BYTES),
        cost_estimate=pl.CostEstimate(
            flops=blocks * size * size * 256,
            bytes_accessed=sum(o.size * o.dtype.itemsize for o in operands),
            transcendentals=blocks * size * size,
        ),
    )(*operands)


def pivot_factor(pivots, inverse, width):
    chosen = (
        lax.broadcasted_iota(jnp.int32, (width, pivots.shape[1]), 0) == pivots
    ).astype(jnp.bfloat16)
    return nt(stacked_split(jnp.transpose(inverse)), chosen).astype(jnp.bfloat16)


def leaf_node(sketch, factor):
    wide = sketch.astype(jnp.float32)
    mean_sq = jnp.sum(wide * wide, keepdims=True) / (sketch.shape[0] * sketch.shape[1]) + EPSILON
    scale = 1.0 / (sketch.shape[0] * mean_sq)
    picked = halves(nt(factor, sketch))
    raw = halves(nn(stacked_split(picked), sketch))
    interp = raw * scale
    upward = halves(nt(stacked_split(raw), sketch)) * (scale * lax.rsqrt(mean_sq))
    return interp, upward


def tree_node(sketch, factor):
    width, columns = sketch.shape
    mean_sq = jnp.sum(sketch * sketch, keepdims=True) / (width * columns) + EPSILON
    scale = 1.0 / (columns * mean_sq)
    parts = stacked_split(sketch)
    picked = halves(nn(jnp.concatenate([factor, factor], axis=1), parts))
    raw = halves(nt(stacked_split(picked), parts))
    raw = raw[:, :width] + raw[:, width:]
    interp = raw * scale
    both = stacked_split(raw)
    upward = halves(nn(jnp.concatenate([both, both], axis=1), parts)) * (scale * lax.rsqrt(mean_sq))
    return interp, upward


def own_nodes(share, group, me):
    rows, level_first, nodes = [], 0, share // 2
    while nodes >= 1:
        rows += [level_first + me * nodes + node for node in range(nodes)]
        level_first += (group // share) * nodes
        nodes //= 2
    return rows


def factor_kernel(
    share,
    leaf_total,
    leaf_pivots,
    leaf_inverse,
    local_pivots,
    local_inverse,
    upper_pivots,
    upper_inverse,
    _,
    leaf_out,
    own_out,
    group_out,
    upper_out,
):
    me = lax.axis_index("vec")
    group = leaf_pivots.shape[0]

    def put(out, index, pivots, inverse, row):
        out[index] = pivot_factor(pivots[pl.ds(row, 1), :], inverse[row], out.shape[2])

    for cluster in range(share):
        put(leaf_out, cluster, leaf_pivots, leaf_inverse, me * share + cluster)
    for index, row in enumerate(own_nodes(share, group, me)):
        put(own_out, index, local_pivots, local_inverse, row)
    for index in range(group // share - 1):
        put(group_out, index, local_pivots, local_inverse, group - group // share + index)
    heap_first = 0
    for tier in range(UPL):
        node = heap_first + (lax.axis_index("leaf") >> (tier + 1))
        put(upper_out, tier, upper_pivots, upper_inverse, node)
        heap_first += leaf_total >> (tier + 1)


def device_kernel(share, group, rank, own, *refs):
    parts = group // share
    arrived, refs = refs[: parts - 1], refs[parts - 1 :]
    leaf_factors, own_factors, pack, up_out, sketch, ups = refs
    me = lax.axis_index("vec")
    columns = own.shape[1]
    width = 2 * rank
    for tier, piece in enumerate((own,) + tuple(arrived)):
        place = pl.ds(pl.multiple_of((me ^ tier) * columns, columns), columns)
        for cluster in range(share):
            sketch[cluster, place, :] = piece[cluster]
    for cluster in range(share):
        interp, upward = leaf_node(sketch[cluster], leaf_factors[cluster])
        pack[cluster * rank : (cluster + 1) * rank, :] = interp
        ups[cluster * rank : (cluster + 1) * rank, :] = upward
    nodes, packed = share // 2, 0
    while nodes >= 1:
        results = []
        for node in range(nodes):
            interp, upward = tree_node(
                ups[2 * node * rank : 2 * (node + 1) * rank, :], own_factors[packed]
            )
            for lane, source, top, height in pack_places(packed, share, rank):
                pack[top : top + height, lane : lane + width] = interp[source : source + height]
            results.append(upward)
            packed += 1
        for node, upward in enumerate(results):
            ups[node * rank : (node + 1) * rank, :] = upward
        nodes //= 2
    up_out[...] = ups[0:rank, :]


def pack_places(index, share, rank):
    top = share * rank + index // 2 * rank
    if index < share - 2:
        return [(index % 2 * 2 * rank, 0, top, rank)]
    return [(0, 0, top, rank // 2), (2 * rank, rank // 2, top, rank // 2)]


def group_kernel(share, group, rank, own, *refs):
    parts = group // share
    arrived, refs = refs[: parts - 1], refs[parts - 1 :]
    factors, interps, up_out, ups = refs
    me = lax.axis_index("vec")
    for tier, piece in enumerate((own,) + tuple(arrived)):
        ups[pl.ds(pl.multiple_of((me ^ tier) * rank, rank), rank), :] = piece[...]
    done = 0
    nodes = parts // 2
    while nodes >= 1:
        results = []
        for node in range(nodes):
            interp, upward = tree_node(
                ups[2 * node * rank : 2 * (node + 1) * rank, :], factors[done]
            )
            interps[done * rank : (done + 1) * rank, :] = interp
            results.append(upward)
            done += 1
        for node, upward in enumerate(results):
            ups[node * rank : (node + 1) * rank, :] = upward
        nodes //= 2
    up_out[...] = ups[0:rank, :]


def upper_node(tier, rank, own, arrived, factors, ups):
    side = (lax.axis_index("leaf") >> tier) & 1
    ups[pl.ds(pl.multiple_of(side * rank, rank), rank), :] = own[...]
    ups[pl.ds(pl.multiple_of((1 - side) * rank, rank), rank), :] = arrived[...]
    return tree_node(ups[...], factors[tier])


def upper_kernel(tier, rank, own, arrived, factors, interp_out, up_out, ups):
    interp, upward = upper_node(tier, rank, own, arrived, factors, ups)
    interp_out[...] = interp
    up_out[...] = upward


def start_copies(pieces, share, group, rank, leaf_out, local_out, sems):
    copies = []

    def put(source, target):
        copies.append(pltpu.make_async_copy(source, target, sems.at[len(copies)]))
        copies[-1].start()

    def rows_at(start, height):
        return pl.ds(pl.multiple_of(start, height), height)

    leaves = share * rank
    for flip, first, piece in pieces:
        device = lax.axis_index("vec") ^ flip
        end = first + piece.shape[0]
        if first < leaves:
            height = min(end, leaves) - first
            step = height if height == leaves else rank
            for row in range(0, height, step):
                put(
                    piece.at[row : row + step],
                    leaf_out.at[rows_at(device * leaves + first + row, step)],
                )
        for index, node in enumerate(own_nodes(share, group, device)):
            for lane, source, start, height in pack_places(index, share, rank):
                if first <= start < end:
                    put(
                        piece.at[start - first : start - first + height, lane : lane + 2 * rank],
                        local_out.at[rows_at(node * rank + source, height)],
                    )
    return copies


def place_kernel(flips, share, group, rank, *refs):
    packs, (joined, leaf_out, local_out, sems) = refs[: len(flips)], refs[len(flips) :]
    pieces = [(flip, 0, piece) for flip, piece in zip(flips, packs)]
    copies = start_copies(pieces, share, group, rank, leaf_out, local_out, sems)
    rows = joined.shape[0]
    target = local_out.at[local_out.shape[0] - rows :]
    copies.append(pltpu.make_async_copy(joined, target, sems.at[len(copies)]))
    copies[-1].start()
    for copy in copies:
        copy.wait()


def forward_kernel(here, there, _, upper, lower):
    upper[...] = here[0 : upper.shape[0], :]
    lower[...] = there[upper.shape[0] :, :]


def finish_kernel(tier, tails, share, group, rank, own, arrived, factors, *refs):
    earlier, refs = refs[:tier], refs[tier:]
    packs, refs = refs[: len(tails)], refs[len(tails) :]
    _, _, interps, top, leaf_out, local_out, ups, turned, sems = refs
    pieces = [(flip, first, piece) for (flip, first), piece in zip(tails, packs)]
    copies = start_copies(pieces, share, group, rank, leaf_out, local_out, sems)
    interp, upward = upper_node(tier, rank, own, arrived, factors, ups)
    for index, ref in enumerate(earlier):
        interps[index] = ref[...]
    interps[tier] = interp
    turned[...] = jnp.transpose(upward)
    columns = top.shape[0]
    place = pl.multiple_of(lax.axis_index("vec") * columns, columns)
    top[...] = turned[pl.ds(place, columns), :]
    for copy in copies:
        copy.wait()


def call(body, outs, scratch, operands, flops=0, anywhere_in=0, anywhere_out=0, aliases=None):
    fixed = pl.BlockSpec(memory_space=VMEM)
    free = pl.BlockSpec(memory_space=pl.ANY)
    return pl.pallas_call(
        body,
        out_shape=outs,
        in_specs=[fixed] * (len(operands) - anywhere_in) + [free] * anywhere_in,
        out_specs=[fixed] * (len(outs) - anywhere_out) + [free] * anywhere_out,
        scratch_shapes=scratch,
        input_output_aliases=aliases or {},
        compiler_params=pltpu.CompilerParams(vmem_limit_bytes=VMEM_BYTES),
        cost_estimate=pl.CostEstimate(
            flops=flops, bytes_accessed=sum(o.size * o.dtype.itemsize for o in operands), transcendentals=0
        ),
    )(*operands)


def f32(*shape):
    return jax.ShapeDtypeStruct(shape, jnp.float32)


def on_device(
    points,
    probe_vectors,
    neighbours,
    leaf_pivots,
    leaf_inverse,
    local_pivots,
    local_inverse,
    upper_pivots,
    upper_inverse,
):
    group, columns, size = probe_vectors.shape
    rank = leaf_pivots.shape[1]
    leaf_total = lax.axis_size("leaf")
    parts = lax.axis_size("vec")
    share = group // parts
    total_columns = columns * parts

    joined = call(
        join_kernel,
        [jax.ShapeDtypeStruct((group * (columns + 3), size), jnp.bfloat16)],
        [],
        [points, probe_vectors],
    )[0]
    swaps = []
    for odd in (0, 1):
        pairs = [(i, i + 1) for i in range(odd, leaf_total - 1, 2)]
        swaps.append(lax.ppermute(joined, "leaf", pairs + [(j, i) for i, j in pairs]))
    inner, outer = swaps

    def vec_send(array, tier):
        return lax.ppermute(array, "vec", [(i, i ^ tier) for i in range(parts)])

    away = list(range(parts - 1, 0, -1))
    sent_rows = (parts - 1) * share

    def bf16(*shape):
        return jax.ShapeDtypeStruct(shape, jnp.bfloat16)

    started, own_far, near = near_call(
        functools.partial(own_kernel, share, away),
        [f32(group + 1, columns, size), bf16(group, DEPTH, size), bf16(group + 1, size, DEPTH)],
        [],
        [neighbours, joined],
        sent_rows,
        6,
    )
    *sent, far, vectors = near_call(
        functools.partial(halo_kernel, share, away),
        [bf16(share, columns, size)] * len(away)
        + [bf16(3 * group, DEPTH, size), bf16(3 * group, columns, size)],
        [pltpu.VMEM((group + 1, columns, size), jnp.float32)],
        [neighbours, joined, inner, outer, own_far, near, started],
        sent_rows,
        6,
    )
    arrived = {tier: vec_send(array, tier) for tier, array in zip(away, sent)}
    kept = near_call(
        functools.partial(kept_kernel, share),
        [bf16(share, columns, size)],
        [pltpu.VMEM((group + 1, columns, size), jnp.float32)],
        [neighbours, far, vectors, near],
        share,
        12,
    )[0]

    width = 2 * rank
    leaf_factors, own_factors, group_factors, upper_factors = call(
        functools.partial(factor_kernel, share, leaf_total),
        [
            bf16(share, width, size),
            bf16(max(1, share - 1), width, width),
            bf16(parts - 1, width, width),
            bf16(UPL, width, width),
        ],
        [],
        [
            leaf_pivots,
            leaf_inverse,
            local_pivots,
            local_inverse,
            upper_pivots,
            upper_inverse,
            kept,
        ],
        anywhere_in=1,
    )
    pack, own_up = call(
        functools.partial(device_kernel, share, group, rank),
        [f32((3 * share - 1) * rank // 2, size), f32(rank, total_columns)],
        [
            pltpu.VMEM((share, total_columns, size), jnp.bfloat16),
            pltpu.VMEM((share * rank, total_columns), jnp.float32),
        ],
        [kept] + [arrived[tier] for tier in range(1, parts)] + [leaf_factors, own_factors],
    )
    near_ups = [vec_send(own_up, tier) for tier in range(1, parts)]
    joined, own_up = call(
        functools.partial(group_kernel, share, group, rank),
        [f32((parts - 1) * rank, width), f32(rank, total_columns)],
        [pltpu.VMEM((parts * rank, total_columns), jnp.float32)],
        [own_up] + near_ups + [group_factors],
    )
    passing = parts == 4
    flips = [0] + [tier for tier in range(1, parts) if not (passing and tier == 3)]
    packs = [pack] + [vec_send(pack, tier) for tier in flips[1:]]
    tails, tail_packs = [], []

    maps = []
    for tier in range(UPL):
        partner = lax.ppermute(own_up, "leaf", [(i, i ^ (1 << tier)) for i in range(leaf_total)])
        operands = [own_up, partner, upper_factors]
        ups = pltpu.VMEM((width, total_columns), jnp.float32)
        if tier < UPL - 1:
            interp, own_up = call(
                functools.partial(upper_kernel, tier, rank),
                [f32(rank, width), f32(rank, total_columns)],
                [ups],
                operands,
                flops=ROUND_FLOPS,
            )
            maps.append(interp)
    if passing:
        upper_rows = (share - 1) * rank
        upper, lower = call(
            forward_kernel,
            [f32(upper_rows, size), f32(pack.shape[0] - upper_rows, size)],
            [],
            [packs[1], packs[2], own_up],
            anywhere_in=1,
        )
        tails = [(3, 0), (3, upper_rows)]
        tail_packs = [vec_send(upper, 2), vec_send(lower, 1)]
    leaf_map, local_map = call(
        functools.partial(place_kernel, flips, share, group, rank),
        [f32(group * rank, size), f32((group - 1) * rank, width)],
        [pltpu.SemaphoreType.DMA((len(flips) * (share + 1) + 1,))],
        packs + [joined],
        flops=ROUND_FLOPS,
        anywhere_in=len(flips) + 1,
        anywhere_out=2,
    )
    operands += maps + tail_packs + [leaf_map, local_map]
    upper_map, top, leaf_map, local_map = call(
        functools.partial(finish_kernel, UPL - 1, tails, share, group, rank),
        [
            f32(UPL, rank, width),
            f32(columns, rank),
            f32(group * rank, size),
            f32((group - 1) * rank, width),
        ],
        [
            ups,
            pltpu.VMEM((total_columns, rank), jnp.float32),
            pltpu.SemaphoreType.DMA((2 * share + 1,)),
        ],
        operands,
        flops=ROUND_FLOPS,
        anywhere_in=len(tails) + 2,
        anywhere_out=2,
        aliases={len(operands) - 2: 2, len(operands) - 1: 3},
    )
    return (
        jnp.swapaxes(leaf_map.reshape(group, rank, size), 1, 2),
        jnp.swapaxes(local_map.reshape(group - 1, rank, width), 1, 2),
        jnp.swapaxes(upper_map, 1, 2)[None],
        top[None],
    )


def solution(mesh):
    placed = (
        P("leaf", None, None),
        P("leaf", "vec", None),
        P("leaf", None),
        P("leaf", None),
        P("leaf", None, None),
        P("leaf", None),
        P("leaf", None, None),
        P(),
        P(),
    )
    return jax.shard_map(
        on_device,
        mesh=mesh,
        in_specs=placed,
        out_specs=(
            P("leaf", None, None),
            P("leaf", None, None),
            P("leaf", None, None, None),
            P("leaf", "vec", None),
        ),
        check_vma=False,
    )
```

```python
import functools

import jax
import jax.numpy as jnp
from jax import lax
from jax.experimental import pallas as pl
from jax.experimental.pallas import tpu as pltpu
from jax.sharding import PartitionSpec as P

UPL = 3

SOFTEN = 0.0009
EPSILON = 1e-06
FLIGHT = 4
DEPTH = 128
CHUNK = 256
ROUND_FLOPS = 950_000_000
VMEM_BYTES = 20 * 1024 * 1024
VMEM = pltpu.MemorySpace.VMEM
SMEM = pltpu.MemorySpace.SMEM


def nt(a, b):
    return lax.dot_general(a, b, (((1,), (1,)), ((), ())), preferred_element_type=jnp.float32)


def nn(a, b):
    return lax.dot_general(a, b, (((1,), (0,)), ((), ())), preferred_element_type=jnp.float32)


def split(a):
    high = a.astype(jnp.bfloat16)
    low = (a - high.astype(jnp.float32)).astype(jnp.bfloat16)
    return high, low


def stacked_split(a):
    high, low = split(a)
    return jnp.concatenate([high, low], axis=0)


def halves(a):
    rows = a.shape[0] // 2
    return a[:rows] + a[rows:]


def coordinates(points, extra):
    row = lax.broadcasted_iota(jnp.int32, (8, points.shape[1]), 0)
    padded = jnp.concatenate(
        [points, jnp.full((5, points.shape[1]), 0.5, jnp.float32)], axis=0
    )
    centred = padded - 0.5
    high, low = [part.astype(jnp.float32) for part in split(centred)]
    norm = jnp.sum(centred * centred, axis=0, keepdims=True) + extra
    first, rest = [part.astype(jnp.float32) for part in split(norm)]
    second, third = [part.astype(jnp.float32) for part in split(norm - first)]
    norms = jnp.where(row == 0, first, jnp.where(row == 1, second, jnp.where(row == 2, third, 0.0)))
    return high, low, norms, jnp.where(row < 3, 1.0, 0.0)


def far_features(points):
    high, low, norm, one = coordinates(points, SOFTEN)
    vacant = jnp.zeros((DEPTH - 48, points.shape[1]), jnp.float32)
    return jnp.concatenate(
        [-2.0 * high, -2.0 * low, -2.0 * high, -2.0 * low, one, norm, vacant], axis=0
    ).astype(jnp.bfloat16)


def near_features(points):
    high, low, norm, one = coordinates(points, 0.0)
    vacant = jnp.zeros((DEPTH - 48, points.shape[1]), jnp.float32)
    return jnp.transpose(
        jnp.concatenate([high, high, low, low, norm, one, vacant], axis=0)
    ).astype(jnp.bfloat16)


def add_blocks(share, tiers, base, wanted, nb_ref, far, vectors, near, total, tiles, codes):
    me = lax.axis_index("vec")
    count, slots = nb_ref.shape
    first = lax.axis_index("leaf") * count
    flight, size = tiles.shape[0], tiles.shape[1]
    idle = count * 64

    for way in range(flight):
        codes[way] = idle
    filled = jnp.int32(flight)
    for tier in tiers:
        for part in range(share):
            cluster = (me ^ tier) * share + part
            shift = cluster * 64 + count - base - first
            for slot in range(slots):
                listed = nb_ref[cluster, slot]
                codes[filled] = listed + shift
                filled += wanted(listed, first, count).astype(jnp.int32)
    for way in range(flight):
        codes[filled + way] = idle

    def multiply(code, tile):
        row = code // 64
        total[row] = total[row] + nt(vectors(code % 64), tile[...])

    def evaluate(code, tile):
        row = code // 64
        position = code % 64
        for top in range(0, size, CHUNK):
            distance = nn(near[row, top : top + CHUNK, :], far[position])
            tile[top : top + CHUNK, :] = lax.rsqrt(distance).astype(jnp.bfloat16)

    def step(index, carry):
        for way in range(flight):
            multiply(codes[index * flight + way], tiles.at[way])
            evaluate(codes[(index + 1) * flight + way], tiles.at[way])
        return carry

    steps = (filled - 1) // flight
    done = jnp.int32(0)
    for width in (8, 4, 2, 1):
        rounds = (steps - done) // width

        def several(index, carry, width=width, done=done):
            for offset in range(width):
                carry = step(done + index * width + offset, carry)
            return carry

        lax.fori_loop(0, rounds, several, 0)
        done = done + rounds * width
    for way in range(flight):
        multiply(codes[steps * flight + way], tiles.at[way])


def inside(listed, first, count):
    return (listed >= first) & (listed < first + count)


def outside(listed, first, count):
    return (listed >= 0) & ((listed < first) | (listed >= first + count))


def anywhere(listed, first, count):
    return listed >= 0


def joined_points(joined, count):
    points = joined[joined.shape[0] - 3 * count :, :].astype(jnp.float32)
    return [points[3 * cluster : 3 * cluster + 3] for cluster in range(count)]


def own_kernel(share, tiers, nb_ref, joined, total, far, near, tiles, codes):
    count, columns = far.shape[0], total.shape[1]
    for cluster, points in enumerate(joined_points(joined, count)):
        far[cluster] = far_features(points)
        near[cluster] = near_features(points)
    near[count] = near[0]
    total[...] = jnp.zeros(total.shape, total.dtype)

    def vectors(place):
        return joined[pl.ds(pl.multiple_of(place * columns, columns), columns), :]

    add_blocks(share, tiers, count, inside, nb_ref, far, vectors, near, total, tiles, codes)


def halo_kernel(share, tiers, nb_ref, joined, inner, outer, own_far, near, start, *refs):
    outs = refs[: len(tiers)]
    far, vectors, total, tiles, codes = refs[len(tiers) :]
    count, columns = own_far.shape[0], start.shape[1]
    me = lax.axis_index("vec")
    odd = lax.axis_index("leaf") & 1
    for place, source in ((2 * odd, outer), (2 - 2 * odd, inner), (1, joined)):
        for cluster in range(count):
            vectors[place * count + cluster] = source[cluster * columns : (cluster + 1) * columns, :]
        if source is joined:
            far[count : 2 * count] = own_far[...]
            continue
        for cluster, points in enumerate(joined_points(source, count)):
            far[place * count + cluster] = far_features(points)
    total[...] = start[...]

    def read(place):
        return vectors[place]

    add_blocks(share, tiers, 0, outside, nb_ref, far, read, near, total, tiles, codes)
    for tier, out in zip(tiers, outs):
        part = total[pl.ds((me ^ tier) * share, share)]
        out[...] = (part * 0.015625).astype(out.dtype)


def kept_kernel(share, nb_ref, far, vectors, near, out, total, tiles, codes):
    mine = pl.ds(lax.axis_index("vec") * share, share)
    total[mine] = jnp.zeros((share,) + total.shape[1:], total.dtype)

    def read(place):
        return vectors[place]

    add_blocks(share, (0,), 0, anywhere, nb_ref, far, read, near, total, tiles, codes)
    out[...] = (total[mine] * 0.015625).astype(out.dtype)


def join_kernel(points, probe, joined):
    count, columns, _ = probe.shape
    for cluster in range(count):
        joined[cluster * columns : (cluster + 1) * columns, :] = probe[cluster]
    joined[count * columns :, :] = jnp.concatenate(
        [points[cluster].astype(jnp.float32) for cluster in range(count)], axis=0
    ).astype(joined.dtype)


def near_call(body, outs, scratch, operands, rows, per_row):
    nb, size = operands[0], outs[0].shape[-1]
    blocks = rows * per_row
    return pl.pallas_call(
        body,
        out_shape=outs,
        in_specs=[pl.BlockSpec(memory_space=SMEM)]
        + [pl.BlockSpec(memory_space=VMEM)] * (len(operands) - 1),
        out_specs=[pl.BlockSpec(memory_space=VMEM)] * len(outs),
        scratch_shapes=scratch
        + [
            pltpu.VMEM((FLIGHT, size, size), jnp.bfloat16),
            pltpu.SMEM((rows * nb.shape[1] + 2 * FLIGHT,), jnp.int32),
        ],
        compiler_params=pltpu.CompilerParams(vmem_limit_bytes=VMEM_BYTES),
        cost_estimate=pl.CostEstimate(
            flops=blocks * size * size * 256,
            bytes_accessed=sum(o.size * o.dtype.itemsize for o in operands),
            transcendentals=blocks * size * size,
        ),
    )(*operands)


def pivot_factor(pivots, inverse, width):
    chosen = (
        lax.broadcasted_iota(jnp.int32, (width, pivots.shape[1]), 0) == pivots
    ).astype(jnp.bfloat16)
    return nt(stacked_split(jnp.transpose(inverse)), chosen).astype(jnp.bfloat16)


def leaf_node(sketch, factor):
    wide = sketch.astype(jnp.float32)
    mean_sq = jnp.sum(wide * wide, keepdims=True) / (sketch.shape[0] * sketch.shape[1]) + EPSILON
    scale = 1.0 / (sketch.shape[0] * mean_sq)
    picked = halves(nt(factor, sketch))
    raw = halves(nn(stacked_split(picked), sketch))
    interp = raw * scale
    upward = halves(nt(stacked_split(raw), sketch)) * (scale * lax.rsqrt(mean_sq))
    return interp, upward


def tree_node(sketch, factor):
    width, columns = sketch.shape
    mean_sq = jnp.sum(sketch * sketch, keepdims=True) / (width * columns) + EPSILON
    scale = 1.0 / (columns * mean_sq)
    parts = stacked_split(sketch)
    picked = halves(nn(jnp.concatenate([factor, factor], axis=1), parts))
    raw = halves(nt(stacked_split(picked), parts))
    raw = raw[:, :width] + raw[:, width:]
    interp = raw * scale
    both = stacked_split(raw)
    upward = halves(nn(jnp.concatenate([both, both], axis=1), parts)) * (scale * lax.rsqrt(mean_sq))
    return interp, upward


def own_nodes(share, group, me):
    rows, level_first, nodes = [], 0, share // 2
    while nodes >= 1:
        rows += [level_first + me * nodes + node for node in range(nodes)]
        level_first += (group // share) * nodes
        nodes //= 2
    return rows


def factor_kernel(
    share,
    leaf_total,
    leaf_pivots,
    leaf_inverse,
    local_pivots,
    local_inverse,
    upper_pivots,
    upper_inverse,
    _,
    leaf_out,
    own_out,
    group_out,
    upper_out,
):
    me = lax.axis_index("vec")
    group = leaf_pivots.shape[0]

    def put(out, index, pivots, inverse, row):
        out[index] = pivot_factor(pivots[pl.ds(row, 1), :], inverse[row], out.shape[2])

    for cluster in range(share):
        put(leaf_out, cluster, leaf_pivots, leaf_inverse, me * share + cluster)
    for index, row in enumerate(own_nodes(share, group, me)):
        put(own_out, index, local_pivots, local_inverse, row)
    for index in range(group // share - 1):
        put(group_out, index, local_pivots, local_inverse, group - group // share + index)
    heap_first = 0
    for tier in range(UPL):
        node = heap_first + (lax.axis_index("leaf") >> (tier + 1))
        put(upper_out, tier, upper_pivots, upper_inverse, node)
        heap_first += leaf_total >> (tier + 1)


def device_kernel(share, group, rank, own, *refs):
    parts = group // share
    arrived, refs = refs[: parts - 1], refs[parts - 1 :]
    leaf_factors, own_factors, pack, up_out, sketch, ups = refs
    me = lax.axis_index("vec")
    columns = own.shape[1]
    width = 2 * rank
    for tier, piece in enumerate((own,) + tuple(arrived)):
        place = pl.ds(pl.multiple_of((me ^ tier) * columns, columns), columns)
        for cluster in range(share):
            sketch[cluster, place, :] = piece[cluster]
    for cluster in range(share):
        interp, upward = leaf_node(sketch[cluster], leaf_factors[cluster])
        pack[cluster * rank : (cluster + 1) * rank, :] = interp
        ups[cluster * rank : (cluster + 1) * rank, :] = upward
    nodes, packed = share // 2, 0
    while nodes >= 1:
        results = []
        for node in range(nodes):
            interp, upward = tree_node(
                ups[2 * node * rank : 2 * (node + 1) * rank, :], own_factors[packed]
            )
            for lane, source, top, height in pack_places(packed, share, rank):
                pack[top : top + height, lane : lane + width] = interp[source : source + height]
            results.append(upward)
            packed += 1
        for node, upward in enumerate(results):
            ups[node * rank : (node + 1) * rank, :] = upward
        nodes //= 2
    up_out[...] = ups[0:rank, :]


def pack_places(index, share, rank):
    top = share * rank + index // 2 * rank
    if index < share - 2:
        return [(index % 2 * 2 * rank, 0, top, rank)]
    return [(0, 0, top, rank // 2), (2 * rank, rank // 2, top, rank // 2)]


def group_kernel(share, group, rank, own, *refs):
    parts = group // share
    arrived, refs = refs[: parts - 1], refs[parts - 1 :]
    factors, interps, up_out, ups = refs
    me = lax.axis_index("vec")
    for tier, piece in enumerate((own,) + tuple(arrived)):
        ups[pl.ds(pl.multiple_of((me ^ tier) * rank, rank), rank), :] = piece[...]
    done = 0
    nodes = parts // 2
    while nodes >= 1:
        results = []
        for node in range(nodes):
            interp, upward = tree_node(
                ups[2 * node * rank : 2 * (node + 1) * rank, :], factors[done]
            )
            interps[done * rank : (done + 1) * rank, :] = interp
            results.append(upward)
            done += 1
        for node, upward in enumerate(results):
            ups[node * rank : (node + 1) * rank, :] = upward
        nodes //= 2
    up_out[...] = ups[0:rank, :]


def upper_node(tier, rank, own, arrived, factors, ups):
    side = (lax.axis_index("leaf") >> tier) & 1
    ups[pl.ds(pl.multiple_of(side * rank, rank), rank), :] = own[...]
    ups[pl.ds(pl.multiple_of((1 - side) * rank, rank), rank), :] = arrived[...]
    return tree_node(ups[...], factors[tier])


def upper_kernel(tier, rank, own, arrived, factors, interp_out, up_out, ups):
    interp, upward = upper_node(tier, rank, own, arrived, factors, ups)
    interp_out[...] = interp
    up_out[...] = upward


def start_copies(pieces, share, group, rank, leaf_out, local_out, sems):
    copies = []

    def put(source, target):
        copies.append(pltpu.make_async_copy(source, target, sems.at[len(copies)]))
        copies[-1].start()

    def rows_at(start, height):
        return pl.ds(pl.multiple_of(start, height), height)

    leaves = share * rank
    for flip, first, piece in pieces:
        device = lax.axis_index("vec") ^ flip
        end = first + piece.shape[0]
        if first < leaves:
            height = min(end, leaves) - first
            step = height if height == leaves else rank
            for row in range(0, height, step):
                put(
                    piece.at[row : row + step],
                    leaf_out.at[rows_at(device * leaves + first + row, step)],
                )
        for index, node in enumerate(own_nodes(share, group, device)):
            for lane, source, start, height in pack_places(index, share, rank):
                if first <= start < end:
                    put(
                        piece.at[start - first : start - first + height, lane : lane + 2 * rank],
                        local_out.at[rows_at(node * rank + source, height)],
                    )
    return copies


def place_kernel(flips, share, group, rank, *refs):
    packs, (joined, leaf_out, local_out, sems) = refs[: len(flips)], refs[len(flips) :]
    pieces = [(flip, 0, piece) for flip, piece in zip(flips, packs)]
    copies = start_copies(pieces, share, group, rank, leaf_out, local_out, sems)
    rows = joined.shape[0]
    target = local_out.at[local_out.shape[0] - rows :]
    copies.append(pltpu.make_async_copy(joined, target, sems.at[len(copies)]))
    copies[-1].start()
    for copy in copies:
        copy.wait()


def forward_kernel(here, there, _, upper, lower):
    upper[...] = here[0 : upper.shape[0], :]
    lower[...] = there[upper.shape[0] :, :]


def finish_kernel(tier, tails, share, group, rank, own, arrived, factors, *refs):
    earlier, refs = refs[:tier], refs[tier:]
    packs, refs = refs[: len(tails)], refs[len(tails) :]
    _, _, interps, top, leaf_out, local_out, ups, turned, sems = refs
    pieces = [(flip, first, piece) for (flip, first), piece in zip(tails, packs)]
    copies = start_copies(pieces, share, group, rank, leaf_out, local_out, sems)
    interp, upward = upper_node(tier, rank, own, arrived, factors, ups)
    for index, ref in enumerate(earlier):
        interps[index] = ref[...]
    interps[tier] = interp
    turned[...] = jnp.transpose(upward)
    columns = top.shape[0]
    place = pl.multiple_of(lax.axis_index("vec") * columns, columns)
    top[...] = turned[pl.ds(place, columns), :]
    for copy in copies:
        copy.wait()


def call(body, outs, scratch, operands, flops=0, anywhere_in=0, anywhere_out=0, aliases=None):
    fixed = pl.BlockSpec(memory_space=VMEM)
    free = pl.BlockSpec(memory_space=pl.ANY)
    return pl.pallas_call(
        body,
        out_shape=outs,
        in_specs=[fixed] * (len(operands) - anywhere_in) + [free] * anywhere_in,
        out_specs=[fixed] * (len(outs) - anywhere_out) + [free] * anywhere_out,
        scratch_shapes=scratch,
        input_output_aliases=aliases or {},
        compiler_params=pltpu.CompilerParams(vmem_limit_bytes=VMEM_BYTES),
        cost_estimate=pl.CostEstimate(
            flops=flops, bytes_accessed=sum(o.size * o.dtype.itemsize for o in operands), transcendentals=0
        ),
    )(*operands)


def f32(*shape):
    return jax.ShapeDtypeStruct(shape, jnp.float32)


def on_device(
    points,
    probe_vectors,
    neighbours,
    leaf_pivots,
    leaf_inverse,
    local_pivots,
    local_inverse,
    upper_pivots,
    upper_inverse,
):
    group, columns, size = probe_vectors.shape
    rank = leaf_pivots.shape[1]
    leaf_total = lax.axis_size("leaf")
    parts = lax.axis_size("vec")
    share = group // parts
    total_columns = columns * parts

    joined = call(
        join_kernel,
        [jax.ShapeDtypeStruct((group * (columns + 3), size), jnp.bfloat16)],
        [],
        [points, probe_vectors],
    )[0]
    swaps = []
    for odd in (0, 1):
        pairs = [(i, i + 1) for i in range(odd, leaf_total - 1, 2)]
        swaps.append(lax.ppermute(joined, "leaf", pairs + [(j, i) for i, j in pairs]))
    inner, outer = swaps

    def vec_send(array, tier):
        return lax.ppermute(array, "vec", [(i, i ^ tier) for i in range(parts)])

    away = list(range(parts - 1, 0, -1))
    sent_rows = (parts - 1) * share

    def bf16(*shape):
        return jax.ShapeDtypeStruct(shape, jnp.bfloat16)

    started, own_far, near = near_call(
        functools.partial(own_kernel, share, away),
        [f32(group + 1, columns, size), bf16(group, DEPTH, size), bf16(group + 1, size, DEPTH)],
        [],
        [neighbours, joined],
        sent_rows,
        6,
    )
    *sent, far, vectors = near_call(
        functools.partial(halo_kernel, share, away),
        [bf16(share, columns, size)] * len(away)
        + [bf16(3 * group, DEPTH, size), bf16(3 * group, columns, size)],
        [pltpu.VMEM((group + 1, columns, size), jnp.float32)],
        [neighbours, joined, inner, outer, own_far, near, started],
        sent_rows,
        6,
    )
    arrived = {tier: vec_send(array, tier) for tier, array in zip(away, sent)}
    kept = near_call(
        functools.partial(kept_kernel, share),
        [bf16(share, columns, size)],
        [pltpu.VMEM((group + 1, columns, size), jnp.float32)],
        [neighbours, far, vectors, near],
        share,
        12,
    )[0]

    width = 2 * rank
    leaf_factors, own_factors, group_factors, upper_factors = call(
        functools.partial(factor_kernel, share, leaf_total),
        [
            bf16(share, width, size),
            bf16(max(1, share - 1), width, width),
            bf16(parts - 1, width, width),
            bf16(UPL, width, width),
        ],
        [],
        [
            leaf_pivots,
            leaf_inverse,
            local_pivots,
            local_inverse,
            upper_pivots,
            upper_inverse,
            kept,
        ],
        anywhere_in=1,
    )
    pack, own_up = call(
        functools.partial(device_kernel, share, group, rank),
        [f32((3 * share - 1) * rank // 2, size), f32(rank, total_columns)],
        [
            pltpu.VMEM((share, total_columns, size), jnp.bfloat16),
            pltpu.VMEM((share * rank, total_columns), jnp.float32),
        ],
        [kept] + [arrived[tier] for tier in range(1, parts)] + [leaf_factors, own_factors],
    )
    near_ups = [vec_send(own_up, tier) for tier in range(1, parts)]
    joined, own_up = call(
        functools.partial(group_kernel, share, group, rank),
        [f32((parts - 1) * rank, width), f32(rank, total_columns)],
        [pltpu.VMEM((parts * rank, total_columns), jnp.float32)],
        [own_up] + near_ups + [group_factors],
    )
    passing = parts == 4
    flips = [0] + [tier for tier in range(1, parts) if not (passing and tier == 3)]
    packs = [pack] + [vec_send(pack, tier) for tier in flips[1:]]
    tails, tail_packs = [], []

    maps = []
    for tier in range(UPL):
        partner = lax.ppermute(own_up, "leaf", [(i, i ^ (1 << tier)) for i in range(leaf_total)])
        operands = [own_up, partner, upper_factors]
        ups = pltpu.VMEM((width, total_columns), jnp.float32)
        if tier < UPL - 1:
            interp, own_up = call(
                functools.partial(upper_kernel, tier, rank),
                [f32(rank, width), f32(rank, total_columns)],
                [ups],
                operands,
                flops=ROUND_FLOPS,
            )
            maps.append(interp)
    if passing:
        upper_rows = (share - 1) * rank
        upper, lower = call(
            forward_kernel,
            [f32(upper_rows, size), f32(pack.shape[0] - upper_rows, size)],
            [],
            [packs[1], packs[2], own_up],
            anywhere_in=1,
        )
        tails = [(3, 0), (3, upper_rows)]
        tail_packs = [vec_send(upper, 2), vec_send(lower, 1)]
    leaf_map, local_map = call(
        functools.partial(place_kernel, flips, share, group, rank),
        [f32(group * rank, size), f32((group - 1) * rank, width)],
        [pltpu.SemaphoreType.DMA((len(flips) * (share + 1) + 1,))],
        packs + [joined],
        flops=ROUND_FLOPS,
        anywhere_in=len(flips) + 1,
        anywhere_out=2,
    )
    operands += maps + tail_packs + [leaf_map, local_map]
    upper_map, top, leaf_map, local_map = call(
        functools.partial(finish_kernel, UPL - 1, tails, share, group, rank),
        [
            f32(UPL, rank, width),
            f32(columns, rank),
            f32(group * rank, size),
            f32((group - 1) * rank, width),
        ],
        [
            ups,
            pltpu.VMEM((total_columns, rank), jnp.float32),
            pltpu.SemaphoreType.DMA((2 * share + 1,)),
        ],
        operands,
        flops=ROUND_FLOPS,
        anywhere_in=len(tails) + 2,
        anywhere_out=2,
        aliases={len(operands) - 2: 2, len(operands) - 1: 3},
    )
    return (
        jnp.swapaxes(leaf_map.reshape(group, rank, size), 1, 2),
        jnp.swapaxes(local_map.reshape(group - 1, rank, width), 1, 2),
        jnp.swapaxes(upper_map, 1, 2)[None],
        top[None],
    )


def solution(mesh):
    placed = (
        P("leaf", None, None),
        P("leaf", "vec", None),
        P("leaf", None),
        P("leaf", None),
        P("leaf", None, None),
        P("leaf", None),
        P("leaf", None, None),
        P(),
        P(),
    )
    return jax.shard_map(
        on_device,
        mesh=mesh,
        in_specs=placed,
        out_specs=(
            P("leaf", None, None),
            P("leaf", None, None),
            P("leaf", None, None, None),
            P("leaf", "vec", None),
        ),
        check_vma=False,
    )
```
